32 devices in a mesh: batch: 8 (over z, x), chan: 4 (over y, core).
Axes of the slice: x: 2, y: 2, z: 4, core: 2. Of those that a mesh axis runs over, the one named last changes fastest.
Arguments:
- images: bfloat16 [32, 16, 24, 1024], P('batch', None, None, 'chan'), may hold values from -12 to 12
- heights: int32 [32], replicated, may hold values from 4 to 8
- widths: int32 [32], replicated, may hold values from 6 to 12
- reduce_first: bfloat16 [1024, 512], P(None, 'chan'), may hold values from -0.1875 to 0.1875
- spatial_first: bfloat16 [3, 3, 512, 512], P(None, None, None, 'chan'), may hold values from -0.09375 to 0.09375
- expand_first: bfloat16 [512, 2048], P(None, 'chan'), may hold values from -0.25 to 0.25
- shortcut: bfloat16 [1024, 2048], P(None, 'chan'), may hold values from -0.1875 to 0.1875
- reduce_second: bfloat16 [2048, 512], P(None, 'chan'), may hold values from -0.125 to 0.125
- spatial_second: bfloat16 [3, 3, 512, 512], P(None, None, None, 'chan'), may hold values from -0.09375 to 0.09375
- expand_second: bfloat16 [512, 2048], P(None, 'chan'), may hold values from -0.25 to 0.25
- gain_mid: float32 [4, 512], P(None, 'chan'), may hold values from 0.5 to 1.5
- bias_mid: float32 [4, 512], P(None, 'chan'), may hold values from -3 to 3
- gain_out: float32 [3, 2048], P(None, 'chan'), may hold values from 0.5 to 1.5
- bias_out: float32 [3, 2048], P(None, 'chan'), may hold values from -3 to 3
- cotangent: bfloat16 [32, 8, 12, 2048], P('batch', None, None, 'chan'), may hold values from -6 to 6
Outputs:
- block_out: float32 [32, 8, 12, 2048], P('batch', None, None, 'chan')
- images_grad: float32 [32, 16, 24, 1024], P('batch', None, None, 'chan')
- reduce_first_grad: float32 [1024, 512], P(None, 'chan')
- spatial_first_grad: float32 [3, 3, 512, 512], P(None, None, None, 'chan')
- expand_first_grad: float32 [512, 2048], P(None, 'chan')
- shortcut_grad: float32 [1024, 2048], P(None, 'chan')
- reduce_second_grad: float32 [2048, 512], P(None, 'chan')
- spatial_second_grad: float32 [3, 3, 512, 512], P(None, None, None, 'chan')
- expand_second_grad: float32 [512, 2048], P(None, 'chan')
- gain_mid_grad: float32 [4, 512], P(None, 'chan')
- bias_mid_grad: float32 [4, 512], P(None, 'chan')
- gain_out_grad: float32 [3, 2048], P(None, 'chan')
- bias_out_grad: float32 [3, 2048], P(None, 'chan')
- mean_mid_batch: float32 [4, 512], P(None, 'chan')
- var_mid_batch: float32 [4, 512], P(None, 'chan')
- mean_out_batch: float32 [3, 2048], P(None, 'chan')
- var_out_batch: float32 [3, 2048], P(None, 'chan')
The draws below stay inside these ranges and needn't reach their ends.
All inputs are finite; a program needn't handle non-finite values.
Results may differ from the reference program's by a relative error of at most 0.029.
Values may be sent and summed in bfloat16 or wider, within the bound.
A program may use at most 192 MiB of HBM per device.

```python
import math
import jax
import jax.numpy as jnp
from jax import lax

CIN = 1024
MID = 512
COUT = 2048
HO = 8
WO = 12
IMAGES = 32


def draw_images(key, part):
    key = jax.random.fold_in(key, 11)
    base_key, scale_key = jax.random.split(key, 2)
    shape = (IMAGES, 2 * HO, 2 * WO, CIN)
    place = jnp.arange(IMAGES, dtype=jnp.float32) / float(max(IMAGES - 1, 1))
    rough = jax.random.uniform(scale_key, (IMAGES,), jnp.float32, 0.7, 1.4)
    values = jnp.clip(jax.random.normal(base_key, shape, jnp.float32), -4.0, 4.0)
    scale = jnp.exp((place - 0.5) * math.log(3.0)) * rough
    values = values * scale[:, None, None, None]
    return values.astype(jnp.bfloat16)


def place_ends(array, stream_key, smallest, largest):
    shape = array.shape
    spot = [jax.random.randint(jax.random.fold_in(stream_key, axis), (), 0, shape[axis]) for axis in range(len(shape))]
    array = array.at[tuple(spot)].set(smallest)
    longest = shape.index(max(shape))
    spot[longest] = (spot[longest] + 1) % shape[longest]
    return array.at[tuple(spot)].set(largest)


def level_of(key, shape, cuts, least, high):
    factor_of = 1.0
    for position, shards_of in cuts:
        steps = jax.random.uniform(jax.random.fold_in(jax.random.fold_in(key, 6), position), (shards_of,), jnp.float32, least / len(cuts), high / len(cuts))
        factor_of = factor_of * jnp.repeat(jnp.exp(steps), shape[position] // shards_of).reshape((-1,) + (1,) * (len(shape) - 1 - position))
    return factor_of


def normal_values(rng, dims, scale, reach, shards=(), kind=jnp.bfloat16):
    drawn = jax.random.normal(rng, dims, jnp.float32) * scale
    if len(shards) > 0:
        drawn = level_of(rng, dims, shards, -0.22, 0.18) * drawn
    return jnp.clip(drawn, min=-reach, max=reach).astype(kind)


def setup_inputs(seed: int = 0) -> dict:
    seeds = jax.random.split(jax.random.key(seed), 16)
    images = draw_images(jax.random.fold_in(seeds[15], 71), 0)
    heights = place_ends(jax.random.randint(seeds[1], (IMAGES,), HO // 2, HO + 1), jax.random.fold_in(seeds[1], 1), HO // 2, HO).astype(jnp.int32)
    widths = place_ends(jax.random.randint(seeds[2], (IMAGES,), WO // 2, WO + 1), jax.random.fold_in(seeds[2], 1), WO // 2, WO).astype(jnp.int32)
    reduce_first = normal_values(seeds[3], (CIN, MID), CIN ** -0.5, 0.1875, ((1, 4),))
    spatial_first = normal_values(seeds[4], (3, 3, MID, MID), (9 * MID) ** -0.5, 0.09375, ((3, 4),))
    expand_first = normal_values(seeds[5], (MID, COUT), MID ** -0.5, 0.25, ((1, 4),))
    shortcut = normal_values(seeds[6], (CIN, COUT), CIN ** -0.5, 0.1875, ((1, 4),))
    reduce_second = normal_values(seeds[7], (COUT, MID), COUT ** -0.5, 0.125, ((1, 4),))
    spatial_second = normal_values(seeds[8], (3, 3, MID, MID), (9 * MID) ** -0.5, 0.09375, ((3, 4),))
    expand_second = normal_values(seeds[9], (MID, COUT), MID ** -0.5, 0.25, ((1, 4),))
    gain_mid = jnp.clip(1.0 + 0.1 * jax.random.normal(seeds[10], (4, MID), jnp.float32), 0.5, 1.5)
    bias_mid = normal_values(seeds[11], (4, MID), 0.5, 3.0, ((1, 4),), jnp.float32)
    gain_out = jnp.clip(1.0 + 0.1 * jax.random.normal(seeds[12], (3, COUT), jnp.float32), 0.5, 1.5)
    bias_out = normal_values(seeds[13], (3, COUT), 0.5, 3.0, ((1, 4),), jnp.float32)
    cotangent = normal_values(seeds[14], (IMAGES, HO, WO, COUT), 1.0, 6.0, ((0, 8), (3, 4)))
    return dict(images=images, heights=heights, widths=widths, reduce_first=reduce_first, spatial_first=spatial_first, expand_first=expand_first, shortcut=shortcut, reduce_second=reduce_second, spatial_second=spatial_second, expand_second=expand_second, gain_mid=gain_mid, bias_mid=bias_mid, gain_out=gain_out, bias_out=bias_out, cotangent=cotangent)


@jax.custom_vjp
def low(v):
    return lax.optimization_barrier(v.astype(jnp.bfloat16)).astype(jnp.float32)

@jax.custom_vjp
def low_back(v):
    return v

def low_keep(v):
    return (low(v), None)

def low_pass(kept, grad):
    return (grad,)

def back_keep(v):
    return (v, None)

def back_low(kept, grad):
    return (low(grad),)
low.defvjp(low_keep, low_pass)
low_back.defvjp(back_keep, back_low)
EPS = 1e-05

def frame_masks(heights, widths):
    tall = heights[:, None, None]
    broad = widths[:, None, None]
    row_in = jnp.arange(2 * HO, dtype=jnp.int32)[None, :, None]
    col_in = jnp.arange(2 * WO, dtype=jnp.int32)[None, None, :]
    row_out = jnp.arange(HO, dtype=jnp.int32)[None, :, None]
    col_out = jnp.arange(WO, dtype=jnp.int32)[None, None, :]
    inner = ((row_in < 2 * tall) & (col_in < 2 * broad)).astype(jnp.float32)[..., None]
    outer = ((row_out < tall) & (col_out < broad)).astype(jnp.float32)[..., None]
    return (inner, outer)

def one_conv(source, kernel, stride):
    return jnp.einsum('nhwc,cd->nhwd', source[:, ::stride, ::stride, :], kernel, precision=lax.Precision.HIGHEST)

def three_conv(source, kernel, stride):
    return lax.conv_general_dilated(source, kernel, (stride, stride), ((1, 1), (1, 1)), dimension_numbers=('NHWC', 'HWIO', 'NHWC'), precision=lax.Precision.HIGHEST)

def batch_norm(pre, mask, count, gain, bias):
    mean = lax.optimization_barrier(jnp.sum(pre * mask, axis=(0, 1, 2))) / count
    centered = (pre - mean) * mask
    spread = lax.optimization_barrier(jnp.sum(centered * centered, axis=(0, 1, 2))) / count
    return ((pre - mean) * lax.rsqrt(spread + EPS) * gain + bias, mean, spread)

def forward(images, reduce_first, spatial_first, expand_first, shortcut, reduce_second, spatial_second, expand_second, gain_mid, bias_mid, gain_out, bias_out, inner, outer, count_in, count_out):
    source = images * inner
    pre_one = low_back(one_conv(source, reduce_first, 1))
    normed_one, mean_one, spread_one = batch_norm(pre_one, inner, count_in, gain_mid[0], bias_mid[0])
    feat_one = low(jax.nn.silu(normed_one) * inner)
    pre_two = low_back(three_conv(feat_one, spatial_first, 2))
    normed_two, mean_two, spread_two = batch_norm(pre_two, outer, count_out, gain_mid[1], bias_mid[1])
    feat_two = low(jax.nn.silu(normed_two) * outer)
    pre_three = low_back(one_conv(feat_two, expand_first, 1))
    normed_three, mean_three, spread_three = batch_norm(pre_three, outer, count_out, gain_out[0], bias_out[0])
    pre_side = low_back(one_conv(source, shortcut, 2))
    normed_side, mean_side, spread_side = batch_norm(pre_side, outer, count_out, gain_out[1], bias_out[1])
    block_mid = jax.nn.silu(normed_three + normed_side) * outer
    feat_mid = low(block_mid)
    pre_four = low_back(one_conv(feat_mid, reduce_second, 1))
    normed_four, mean_four, spread_four = batch_norm(pre_four, outer, count_out, gain_mid[2], bias_mid[2])
    feat_four = low(jax.nn.silu(normed_four) * outer)
    pre_five = low_back(three_conv(feat_four, spatial_second, 1))
    normed_five, mean_five, spread_five = batch_norm(pre_five, outer, count_out, gain_mid[3], bias_mid[3])
    feat_five = low(jax.nn.silu(normed_five) * outer)
    pre_six = low_back(one_conv(feat_five, expand_second, 1))
    normed_six, mean_six, spread_six = batch_norm(pre_six, outer, count_out, gain_out[2], bias_out[2])
    result = jax.nn.silu(normed_six + block_mid) * outer
    stats = (jnp.stack([mean_one, mean_two, mean_four, mean_five]), jnp.stack([spread_one, spread_two, spread_four, spread_five]), jnp.stack([mean_three, mean_side, mean_six]), jnp.stack([spread_three, spread_side, spread_six]))
    return (result, stats)

def reference(images, heights, widths, reduce_first, spatial_first, expand_first, shortcut, reduce_second, spatial_second, expand_second, gain_mid, bias_mid, gain_out, bias_out, cotangent):
    inner, outer = frame_masks(heights, widths)
    count_out = jnp.sum(outer)
    count_in = jnp.sum(inner)
    params = tuple((item.astype(jnp.float32) for item in (images, reduce_first, spatial_first, expand_first, shortcut, reduce_second, spatial_second, expand_second, gain_mid, bias_mid, gain_out, bias_out)))

    def layer(*values):
        return forward(*values, inner, outer, count_in, count_out)
    result, pullback, stats = jax.vjp(layer, *params, has_aux=True)
    grads = pullback(cotangent.astype(jnp.float32))
    batch_mean_mid, batch_var_mid, batch_mean_out, batch_var_out = stats
    counts_mid = jnp.stack([count_in, count_out, count_out, count_out])[:, None]
    var_mid_batch = batch_var_mid * counts_mid / (counts_mid - 1.0)
    var_out_batch = batch_var_out * count_out / (count_out - 1.0)
    return (result, grads[0], grads[1], grads[2], grads[3], grads[4], grads[5], grads[6], grads[7], grads[8], grads[9], grads[10], grads[11], batch_mean_mid, var_mid_batch, batch_mean_out, var_out_batch)
```

```python
import functools
import types

import jax
import jax.numpy as jnp
import ml_dtypes
import numpy as np
from jax import lax
from jax.experimental import pallas as pl
from jax.experimental.pallas import tpu as pltpu
from jax.sharding import PartitionSpec as P

EPS = 1e-05
VMEM_LIMIT = 60 * 1024 * 1024


def shortened(shard):
    return jax.tree.map(lambda a: a.astype(jnp.bfloat16) if a.dtype == jnp.float32 else a, shard)


def frame_masks(heights, widths, rows, cols):
    tall = heights[:, None, None]
    broad = widths[:, None, None]
    row_in = jnp.arange(2 * rows, dtype=jnp.int32)[None, :, None]
    col_in = jnp.arange(2 * cols, dtype=jnp.int32)[None, None, :]
    row_out = jnp.arange(rows, dtype=jnp.int32)[None, :, None]
    col_out = jnp.arange(cols, dtype=jnp.int32)[None, None, :]
    inner = ((row_in < 2 * tall) & (col_in < 2 * broad)).astype(jnp.float32)[..., None]
    outer = ((row_out < tall) & (col_out < broad)).astype(jnp.float32)[..., None]
    return (inner, outer)


def silu_slope(value):
    sig = jax.nn.sigmoid(value)
    return sig * (1.0 + value * (1.0 - sig))


def convolve(source, kernel, stride, rows, cols):
    taps = kernel.shape[0]
    margin = taps // 2
    padded = jnp.pad(source, ((0, 0), (margin, margin), (margin, margin), (0, 0)))
    total = None
    for top in range(taps):
        for left in range(taps):
            window = padded[
                :, top : top + stride * rows : stride, left : left + stride * cols : stride, :
            ]
            term = jnp.einsum(
                "nhwc,cd->nhwd", window, kernel[top, left], preferred_element_type=jnp.float32
            )
            total = term if total is None else total + term
    return total


def kernel_grad(source, grad, stride, taps):
    rows, cols = (grad.shape[1], grad.shape[2])
    margin = taps // 2
    padded = jnp.pad(source, ((0, 0), (margin, margin), (margin, margin), (0, 0)))
    return jnp.stack(
        [
            jnp.stack(
                [
                    jnp.einsum(
                        "nhwc,nhwd->cd",
                        padded[
                            :,
                            top : top + stride * rows : stride,
                            left : left + stride * cols : stride,
                            :,
                        ],
                        grad,
                        preferred_element_type=jnp.float32,
                    )
                    for left in range(taps)
                ]
            )
            for top in range(taps)
        ]
    )


def spread_back(grad, kernel, stride):
    taps = kernel.shape[0]
    margin = taps // 2
    total = None
    for top in range(taps):
        for left in range(taps):
            term = jnp.einsum(
                "nhwd,cd->nhwc", grad, kernel[top, left], preferred_element_type=jnp.float32
            )
            placed = lax.pad(
                term,
                jnp.float32(0.0),
                (
                    (0, 0, 0),
                    (top, 2 * margin - top + stride - 1, stride - 1),
                    (left, 2 * margin - left + stride - 1, stride - 1),
                    (0, 0, 0),
                ),
            )
            total = placed if total is None else total + placed
    rows, cols = (grad.shape[1], grad.shape[2])
    return total[:, margin : margin + stride * rows, margin : margin + stride * cols, :]


def norm_forward(pre, mask, count, gain, bias):
    mean = lax.psum(jnp.sum(pre * mask, axis=(0, 1, 2)), "batch") / count
    centered = (pre - mean) * mask
    spread = lax.psum(jnp.sum(centered * centered, axis=(0, 1, 2)), "batch") / count
    inv = lax.rsqrt(spread + EPS)
    hat = (pre - mean) * inv
    return (hat * gain + bias, hat, inv, mean, spread)


def norm_backward(grad, hat, mask, count, gain, inv):
    masked = grad * mask
    bias_grad, gain_grad = lax.psum(
        (jnp.sum(masked, axis=(0, 1, 2)), jnp.sum(masked * hat, axis=(0, 1, 2))), "batch"
    )
    pre_grad = mask * gain * inv * (grad - (bias_grad + hat * gain_grad) / count)
    return (pre_grad.astype(jnp.bfloat16), gain_grad, bias_grad)


def widen(feature):
    return lax.all_gather(feature, "chan", axis=3, tiled=True)


def input_grad(grad, kernel, stride):
    return jax.tree.map(
        lambda part: part.astype(jnp.float32),
        lax.psum_scatter(
            shortened(spread_back(grad, kernel, stride)), "chan", scatter_dimension=3, tiled=True
        ),
    )


def image_back(grad_one, grad_side, kernels):
    summands = spread_back(grad_one, kernels[0], 1) + spread_back(grad_side, kernels[3], 2)
    return lax.psum_scatter(
        summands.astype(jnp.bfloat16), "chan", scatter_dimension=3, tiled=True
    ).astype(jnp.float32)


def on_device(
    images,
    heights,
    widths,
    reduce_first,
    spatial_first,
    expand_first,
    shortcut,
    reduce_second,
    spatial_second,
    expand_second,
    gain_mid,
    bias_mid,
    gain_out,
    bias_out,
    cotangent,
):
    local = images.shape[0]
    rows, cols = (cotangent.shape[1], cotangent.shape[2])
    offset = lax.axis_index("batch") * local
    inner, outer = frame_masks(
        lax.dynamic_slice_in_dim(heights, offset, local),
        lax.dynamic_slice_in_dim(widths, offset, local),
        rows,
        cols,
    )
    count_out = jnp.sum(heights * widths).astype(jnp.float32)
    count_in = 4.0 * count_out
    kernels = (
        reduce_first[None, None],
        spatial_first,
        expand_first[None, None],
        shortcut[None, None],
        reduce_second[None, None],
        spatial_second,
        expand_second[None, None],
    )
    source = images * inner.astype(jnp.bfloat16)
    whole_source = lax.all_gather(source, "chan", axis=3, tiled=True)
    pre_one = convolve(whole_source, kernels[0], 1, 2 * rows, 2 * cols)
    normed_one, hat_one, inv_one, mean_one, spread_one = norm_forward(
        pre_one, inner, count_in, gain_mid[0], bias_mid[0]
    )
    whole_one = widen((jax.nn.silu(normed_one) * inner).astype(jnp.bfloat16))
    pre_two = convolve(whole_one, kernels[1], 2, rows, cols)
    normed_two, hat_two, inv_two, mean_two, spread_two = norm_forward(
        pre_two, outer, count_out, gain_mid[1], bias_mid[1]
    )
    whole_two = widen((jax.nn.silu(normed_two) * outer).astype(jnp.bfloat16))
    pre_three = convolve(whole_two, kernels[2], 1, rows, cols)
    normed_three, hat_three, inv_three, mean_three, spread_three = norm_forward(
        pre_three, outer, count_out, gain_out[0], bias_out[0]
    )
    pre_side = convolve(whole_source, kernels[3], 2, rows, cols)
    normed_side, hat_side, inv_side, mean_side, spread_side = norm_forward(
        pre_side, outer, count_out, gain_out[1], bias_out[1]
    )
    block_mid = jax.nn.silu(normed_three + normed_side) * outer
    whole_mid = widen(block_mid.astype(jnp.bfloat16))
    pre_four = convolve(whole_mid, kernels[4], 1, rows, cols)
    normed_four, hat_four, inv_four, mean_four, spread_four = norm_forward(
        pre_four, outer, count_out, gain_mid[2], bias_mid[2]
    )
    whole_four = widen((jax.nn.silu(normed_four) * outer).astype(jnp.bfloat16))
    pre_five = convolve(whole_four, kernels[5], 1, rows, cols)
    normed_five, hat_five, inv_five, mean_five, spread_five = norm_forward(
        pre_five, outer, count_out, gain_mid[3], bias_mid[3]
    )
    whole_five = widen((jax.nn.silu(normed_five) * outer).astype(jnp.bfloat16))
    pre_six = convolve(whole_five, kernels[6], 1, rows, cols)
    normed_six, hat_six, inv_six, mean_six, spread_six = norm_forward(
        pre_six, outer, count_out, gain_out[2], bias_out[2]
    )
    result = jax.nn.silu(normed_six + block_mid) * outer
    grad_sum_b = cotangent.astype(jnp.float32) * outer * silu_slope(normed_six + block_mid)
    grad_six, gain_six, bias_six = norm_backward(
        grad_sum_b, hat_six, outer, count_out, gain_out[2], inv_six
    )
    kern_six = kernel_grad(whole_five, grad_six, 1, 1)
    grad_feat_five = input_grad(grad_six, kernels[6], 1)
    grad_five, gain_five, bias_five = norm_backward(
        grad_feat_five * outer * silu_slope(normed_five),
        hat_five,
        outer,
        count_out,
        gain_mid[3],
        inv_five,
    )
    kern_five = kernel_grad(whole_four, grad_five, 1, 3)
    grad_feat_four = input_grad(grad_five, kernels[5], 1)
    grad_four, gain_four, bias_four = norm_backward(
        grad_feat_four * outer * silu_slope(normed_four),
        hat_four,
        outer,
        count_out,
        gain_mid[2],
        inv_four,
    )
    kern_four = kernel_grad(whole_mid, grad_four, 1, 1)
    grad_mid = grad_sum_b + input_grad(grad_four, kernels[4], 1)
    grad_sum_a = grad_mid * outer * silu_slope(normed_three + normed_side)
    grad_three, gain_three, bias_three = norm_backward(
        grad_sum_a, hat_three, outer, count_out, gain_out[0], inv_three
    )
    grad_side, gain_side, bias_side = norm_backward(
        grad_sum_a, hat_side, outer, count_out, gain_out[1], inv_side
    )
    kern_three = kernel_grad(whole_two, grad_three, 1, 1)
    kern_side = kernel_grad(whole_source, grad_side, 2, 1)
    grad_feat_two = input_grad(grad_three, kernels[2], 1)
    grad_two, gain_two, bias_two = norm_backward(
        grad_feat_two * outer * silu_slope(normed_two),
        hat_two,
        outer,
        count_out,
        gain_mid[1],
        inv_two,
    )
    kern_two = kernel_grad(whole_one, grad_two, 2, 3)
    grad_feat_one = input_grad(grad_two, kernels[1], 2)
    grad_one, gain_one, bias_one = norm_backward(
        grad_feat_one * inner * silu_slope(normed_one),
        hat_one,
        inner,
        count_in,
        gain_mid[0],
        inv_one,
    )
    kern_one = kernel_grad(whole_source, grad_one, 1, 1)
    images_grad = image_back(grad_one, grad_side, kernels) * inner
    summed = (
        lax.psum(kern_one.astype(jnp.bfloat16), "batch").astype(jnp.float32),
        lax.psum(kern_two.astype(jnp.bfloat16), "batch").astype(jnp.float32),
        lax.psum(kern_three.astype(jnp.bfloat16), "batch").astype(jnp.float32),
        lax.psum(kern_side.astype(jnp.bfloat16), "batch").astype(jnp.float32),
        lax.psum(kern_four.astype(jnp.bfloat16), "batch").astype(jnp.float32),
        lax.psum(kern_five.astype(jnp.bfloat16), "batch").astype(jnp.float32),
        lax.psum(kern_six.astype(jnp.bfloat16), "batch").astype(jnp.float32),
    )
    counts_mid = jnp.stack([count_in, count_out, count_out, count_out])[:, None]
    mean_mid_batch = jnp.stack([mean_one, mean_two, mean_four, mean_five])
    var_mid_batch = (
        jnp.stack([spread_one, spread_two, spread_four, spread_five])
        * counts_mid
        / (counts_mid - 1.0)
    )
    mean_out_batch = jnp.stack([mean_three, mean_side, mean_six])
    var_out_batch = (
        jnp.stack([spread_three, spread_side, spread_six]) * count_out / (count_out - 1.0)
    )
    return (
        result,
        images_grad,
        summed[0][0, 0],
        summed[1],
        summed[2][0, 0],
        summed[3][0, 0],
        summed[4][0, 0],
        summed[5],
        summed[6][0, 0],
        jnp.stack([gain_one, gain_two, gain_four, gain_five]),
        jnp.stack([bias_one, bias_two, bias_four, bias_five]),
        jnp.stack([gain_three, gain_side, gain_six]),
        jnp.stack([bias_three, bias_side, bias_six]),
        mean_mid_batch,
        var_mid_batch,
        mean_out_batch,
        var_out_batch,
    )


MESH = pl.DeviceIdType.MESH
BF = jnp.bfloat16
F32 = jnp.float32


def flip(value, bit):
    return value + bit - 2 * bit * lax.rem(lax.div(value, bit), 2)


def gate(value):
    return 0.5 * jnp.tanh(0.5 * value) + 0.5


def tree(parts):
    while len(parts) > 1:
        parts = [parts[k] + parts[k + 1] for k in range(0, len(parts), 2)]
    return parts[0]


def wide_row(block):
    return jnp.concatenate([block[j : j + 1] for j in range(block.shape[0])], axis=1)


def fold(value):
    return jnp.sum(value.reshape(value.shape[0] // 8, 8, value.shape[1]), axis=0)


def mm(a, b):
    return jnp.dot(a, b, preferred_element_type=F32)


def mm_nt(a, b):
    return lax.dot_general(a, b, (((1,), (1,)), ((), ())), preferred_element_type=F32)


def mm_tn(a, b):
    return lax.dot_general(a, b, (((0,), (0,)), ((), ())), preferred_element_type=F32)


class Traffic:
    def __init__(self, sems):
        self.sems, self.used, self.sent = sems, 0, []

    def take(self):
        self.used += 1
        return self.sems.at[self.used - 1]

    def push(self, src, dst, device):
        copy = pltpu.make_async_remote_copy(
            src_ref=src,
            dst_ref=dst,
            send_sem=self.take(),
            recv_sem=self.take(),
            device_id=device,
            device_id_type=MESH,
        )
        copy.start()
        self.sent.append(copy)
        return copy

    def local(self, src, dst):
        copy = pltpu.make_async_copy(src, dst, self.take())
        copy.start()
        return copy


SEMS = 480


def block_kernel(geo, names, *refs):
    g = types.SimpleNamespace(**dict(zip(names, refs)))
    R, QS, PS = geo.R, geo.QS, geo.PS
    CI, MI, CO = geo.CI, geo.MI, geo.CO
    NB = geo.NB
    r = lax.axis_index("chan")
    b = lax.axis_index("batch")
    r1, r2 = flip(r, 1), flip(r, 2)
    r3 = flip(r1, 2)
    ranks = (r, r1, r2, r3)
    core, far = (b, r1), (b, r2)
    peers = []
    for k in range(1, NB):
        other = b
        bit = 1
        while bit < NB:
            if k & bit:
                other = flip(other, bit)
            bit *= 2
        peers.append((other, r))
    net = Traffic(g.sems)

    bar = pltpu.get_barrier_semaphore()
    everyone = [core, far] + peers
    for device in everyone:
        pl.semaphore_signal(bar, 1, device_id=device, device_id_type=MESH)

    def rows_of(ref, rank, size):
        return ref.at[pl.ds(pl.multiple_of(rank * size, size), size)]

    def taps_of(ref, rank, size):
        return ref.at[:, pl.ds(pl.multiple_of(rank * size, size), size), :]

    ld_src = net.local(g.src, g.SRC.at[0])
    ld_w1 = [
        net.local(rows_of(g.w1, rank, CI), g.W1C.at[pl.ds(s * CI, CI), pl.ds(MI, MI)])
        for s, rank in enumerate((r, r1))
    ]
    ld_sc = [net.local(rows_of(g.wsc, rank, CI), g.WS.at[s]) for s, rank in enumerate(ranks)]
    ld_w2 = [net.local(taps_of(g.w2, rank, MI), g.W2.at[:, s]) for s, rank in enumerate(ranks)]
    ld_w3 = [net.local(rows_of(g.w3, rank, MI), g.W3.at[s]) for s, rank in enumerate(ranks)]
    ld_w4 = [
        net.local(rows_of(g.w4, rank, CO), g.W4C.at[pl.ds(s * CO, CO), pl.ds(MI, MI)])
        for s, rank in enumerate((r, r1))
    ]
    ld_w5 = [net.local(taps_of(g.w5, rank, MI), g.W5.at[:, s]) for s, rank in enumerate(ranks)]
    ld_w6 = [net.local(rows_of(g.w6, rank, MI), g.W6.at[s]) for s, rank in enumerate(ranks)]
    ld_cot = net.local(g.cot, g.COT)

    pl.semaphore_wait(bar, len(everyone))

    rm_src = net.push(g.src, g.SRC.at[1], core)
    rm_w1 = [
        net.push(rows_of(g.w1, rank, CI), g.W1C.at[pl.ds(s * CI, CI), pl.ds(0, MI)], far)
        for s, rank in enumerate((r2, r3))
    ]
    for ph in (1, 3):
        for s in range(4):
            g.F1[s, ph, 0:QS, :] = jnp.zeros((QS, MI), BF)
    for s in range(4):
        g.D1[1, s, 0:QS, :] = jnp.zeros((QS, MI), BF)
        g.F4[s, 0:QS, :] = jnp.zeros((QS, MI), BF)
        g.F4[s, QS + R :, :] = jnp.zeros((QS, MI), BF)
        for d in range(2):
            g.D4[d, s, 0:QS, :] = jnp.zeros((QS, MI), BF)
            g.D4[d, s, QS + R :, :] = jnp.zeros((QS, MI), BF)
    for d in range(3):
        for s in range(2):
            g.E5[d, s, 0:QS, :] = jnp.zeros((QS, MI), BF)
            g.E5[d, s, QS + R :, :] = jnp.zeros((QS, MI), BF)
    for d in range(2):
        for s in range(2):
            g.E2[d, s, R:, :] = jnp.zeros((QS, MI), BF)

    ld_src.wait()
    for copy in ld_w1:
        copy.wait()
    rm_src.wait_recv()
    for copy in rm_w1:
        copy.wait_recv()
    rm_p1 = []
    for ph in range(4):
        span = slice(ph * R, (ph + 1) * R)
        both = jnp.concatenate([g.SRC[0, span, :], g.SRC[1, span, :]], axis=1)
        part = mm(both, g.W1C[...])
        g.P1S[ph] = part[:, :MI].astype(BF)
        rm_p1.append(net.push(g.P1S.at[ph], g.P1R.at[ph], far))
        g.PRE1[span, :] = part[:, MI:]

    rm_back = []
    for s, rank in enumerate((r1, r3)):
        rm_back.append(net.push(rows_of(g.w6, rank, MI), g.W6P.at[s], core))
        rm_back.append(net.push(taps_of(g.w5, rank, MI), g.W5P.at[:, s], core))
        rm_back.append(net.push(rows_of(g.w3, rank, MI), g.W3P.at[s], core))
        rm_back.append(net.push(rows_of(g.wsc, rank, CI), g.WSP.at[s], core))
        rm_back.append(net.push(taps_of(g.w2, rank, MI), g.W2P.at[:, s], core))
    rm_back.append(net.push(rows_of(g.w4, r1, CO), g.W4P.at[0], core))
    rm_back.append(net.push(rows_of(g.w1, r1, CI), g.W1P.at[0], core))
    rm_back.append(
        net.push(g.W1C.at[pl.ds(CI, CI), pl.ds(0, MI)], g.W1P.at[1], core)
    )

    aux = g.aux
    inv_out = aux[16:17, :]
    unb_out, unb_in = aux[17:18, :], aux[18:19, :]

    def mask_rows(at, size):
        return g.mask[pl.ds(at, size), :]

    def over(total, size, body, init):
        def step(i, carry):
            return body(pl.multiple_of(i * size, size), carry)

        return lax.fori_loop(0, total // size, step, init)

    NCH = 128 if R % 128 == 0 else QS
    WCH = QS

    def bc(mask, width):
        return jnp.concatenate([mask] * (width // 128), axis=1)

    def exchange(slots, payload_rows):
        return [net.push(slots.at[0], slots.at[k], peers[k - 1]) for k in range(1, NB)]

    def narrow_local(pre, phases, prepare=None):
        total = jnp.zeros((8, MI), F32)
        for ph in range(phases):
            if prepare is not None:
                prepare(ph)

            def add(at, acc, ph=ph):
                return acc + fold(pre[pl.ds(ph * R + at, NCH), :] * mask_rows(at, NCH))

            total = over(R, NCH, add, total)
        total = jnp.sum(total, axis=0, keepdims=True)
        mean = total * (aux[8:9, :] * (1.0 / phases))
        squares = jnp.zeros((8, MI), F32)
        for ph in range(phases):

            def add2(at, acc, ph=ph):
                d = (pre[pl.ds(ph * R + at, NCH), :] - mean) * mask_rows(at, NCH)
                return acc + fold(d * d)

            squares = over(R, NCH, add2, squares)
        return total, jnp.sum(squares, axis=0, keepdims=True)

    def narrow_send(idx, first, second):
        slots = g.SN.at[idx]
        g.SN[idx, 0, 0:1, :] = first
        g.SN[idx, 0, 1:2, :] = second
        return exchange(slots, 2)

    def narrow_merge(idx, copies, phases):
        for copy in copies:
            copy.wait_recv()
        sums = [g.SN[idx, k, 0:1, :] for k in range(NB)]
        squares = [g.SN[idx, k, 1:2, :] for k in range(NB)]
        return moments(sums, squares, phases)

    def moments(sums, squares, phases):
        inv_count = inv_out * (1.0 / phases)
        mean = tree(list(sums)) * inv_count
        terms = []
        for k in range(NB):
            d = sums[k] * (aux[8 + k : 9 + k, :] * (1.0 / phases)) - mean
            terms.append(squares[k] + aux[k : k + 1, :] * float(phases) * d * d)
        spread = tree(terms) * inv_count
        return mean, spread

    def wide_local(pre):
        def add(at, acc):
            m = bc(mask_rows(at, WCH), CO)
            return acc + fold(pre[pl.ds(at, WCH), :] * m)

        total = jnp.sum(over(R, WCH, add, jnp.zeros((8, CO), F32)), axis=0, keepdims=True)
        mean = total * bc(aux[8:9, :], CO)

        def add2(at, acc):
            m = bc(mask_rows(at, WCH), CO)
            d = (pre[pl.ds(at, WCH), :] - mean) * m
            return acc + fold(d * d)

        squares = jnp.sum(over(R, WCH, add2, jnp.zeros((8, CO), F32)), axis=0, keepdims=True)
        return total, squares

    NW = CO // 128

    def wide_put(slots, row, value):
        for j in range(NW):
            slots[0, row + j : row + j + 1, :] = value[:, j * 128 : (j + 1) * 128]

    def wide_send(idx, first, second):
        slots = g.SW.at[idx]
        wide_put(slots, 0, first)
        wide_put(slots, NW, second)
        return exchange(slots, 2 * NW)

    def wide_merge(idx, copies):
        for copy in copies:
            copy.wait_recv()
        sums = [g.SW[idx, k, 0:NW, :] for k in range(NB)]
        squares = [g.SW[idx, k, NW : 2 * NW, :] for k in range(NB)]
        mean, spread = moments(sums, squares, 1)
        return wide_row(mean), wide_row(spread)

    def gather(buf, at, size):
        here = [buf(s).at[pl.ds(at, size)] for s in range(4)]
        near = net.push(here[0], here[1], core)
        away = net.push(here[0], here[2], far)
        return [near, away, here]

    def relay(chunk):
        near, away, here = chunk
        away.wait_recv()
        chunk.append(net.push(here[2], here[3], core))

    def landed(chunk):
        chunk[0].wait_recv()
        chunk[3].wait_recv()

    def lanes(parts):
        return jnp.concatenate(parts, axis=1)

    place = lax.broadcasted_iota(jnp.int32, (QS, 128), 0)
    keep_down = place >= PS
    keep_up = place < QS - PS

    def shifted(value, step):
        if step < 0:
            return jnp.where(keep_down, pltpu.roll(value, PS, 0), 0.0)
        return jnp.where(keep_up, pltpu.roll(value, QS - PS, 0), 0.0)

    def take_p1(ph):
        rm_p1[ph].wait_recv()

        def add(at, carry):
            rows = pl.ds(ph * R + at, NCH)
            g.PRE1[rows, :] = g.PRE1[rows, :] + g.P1R[ph, pl.ds(at, NCH), :].astype(F32)
            return carry

        over(R, NCH, add, 0)

    sum_one, sq_one = narrow_local(g.PRE1, 4, take_p1)
    st_one = narrow_send(0, sum_one, sq_one)
    rm_xs = net.push(g.SRC.at[0, pl.ds(0, R)], g.XS.at[0], far)

    def scale_of(spread, gain):
        inv = lax.rsqrt(spread + EPS)
        return inv, inv * gain

    mean_one, spread_one = narrow_merge(0, st_one, 4)
    inv_one, scale_one = scale_of(spread_one, g.gm[0:1, :])

    def narrow_feature(pre, mean, scale, bias, out, ph, at0):
        def body(at, carry):
            v = (pre[pl.ds(ph * R + at, NCH), :] - mean) * scale + bias
            out[pl.ds(at0 + at, NCH), :] = (v * gate(v) * mask_rows(at, NCH)).astype(BF)
            return carry

        over(R, NCH, body, 0)

    ch_one = []
    for ph in range(4):
        narrow_feature(
            g.PRE1, mean_one, scale_one, g.bm[0:1, :], g.F1.at[0, ph], ph, QS
        )
        ch_one.append(gather(lambda s, ph=ph: g.F1.at[s, ph], QS, R))

    rm_xs.wait_recv()
    rm_xs2 = net.push(g.XS.at[0], g.XS.at[1], core)
    for copy in ld_sc:
        copy.wait()
    rm_xs2.wait_recv()

    def strided():
        return [g.SRC[0, 0:R, :], g.SRC[1, 0:R, :], g.XS[0], g.XS[1]]

    pre_side = None
    for s, block in enumerate(strided()):
        term = mm(block, g.WS[s])
        pre_side = term if pre_side is None else pre_side + term
    g.PRES[...] = pre_side
    st_side = wide_send(0, *wide_local(g.PRES))

    for copy in ld_w2:
        copy.wait()

    def whole_one(ph, down, left):
        rows = slice(0, R) if left else slice(QS, QS + R)
        if down:
            return lanes([g.D1[ph - 2, s, rows, :] for s in range(4)])
        return lanes([g.F1[s, ph, rows, :] for s in range(4)])

    def kernel_rows(ref, tap):
        return jnp.concatenate([ref[tap, s] for s in range(4)], axis=0)

    def taps_two(ph):
        top = (1,) if ph < 2 else (0, 2)
        left = (1,) if ph % 2 == 0 else (0, 2)
        return [(t, l) for t in top for l in left]

    relay(ch_one[0])
    pre_two = None
    for ph in range(4):
        if ph < 3:
            relay(ch_one[ph + 1])
        landed(ch_one[ph])
        if ph >= 2:

            def move(at, carry, ph=ph):
                for s in range(4):
                    v = g.F1[s, ph, pl.ds(QS + at, QS), :].astype(F32)
                    g.D1[ph - 2, s, pl.ds(QS + at, QS), :] = shifted(v, -1).astype(BF)
                return carry

            over(R, QS, move, 0)
        for t, l in taps_two(ph):
            term = mm(whole_one(ph, t == 0, l == 0), kernel_rows(g.W2, 3 * t + l))
            pre_two = term if pre_two is None else pre_two + term
    g.PRE2[...] = pre_two
    rm_w4 = [
        net.push(rows_of(g.w4, rank, CO), g.W4C.at[pl.ds(s * CO, CO), pl.ds(0, MI)], far)
        for s, rank in enumerate((r2, r3))
    ]
    st_two = narrow_send(1, *narrow_local(g.PRE2, 1))
    mean_two, spread_two = narrow_merge(1, st_two, 1)
    inv_two, scale_two = scale_of(spread_two, g.gm[1:2, :])
    narrow_feature(g.PRE2, mean_two, scale_two, g.bm[1:2, :], g.F2.at[0], 0, 0)
    ch_two = gather(lambda s: g.F2.at[s], 0, R)
    for copy in ld_w3:
        copy.wait()
    mean_side, spread_side = wide_merge(0, st_side)
    inv_side, scale_side = scale_of(spread_side, g.go[1:2, :])
    relay(ch_two)
    landed(ch_two)

    def four(ref):
        return lanes([ref[s] for s in range(4)])

    g.PRE3[...] = mm(four(g.F2), g.W3[...].reshape(4 * MI, CO))
    st_three = wide_send(1, *wide_local(g.PRE3))
    mean_three, spread_three = wide_merge(1, st_three)
    inv_three, scale_three = scale_of(spread_three, g.go[0:1, :])
    bias_three, bias_side = g.bo[0:1, :], g.bo[1:2, :]

    def mid_value(rows):
        return (
            (g.PRE3[rows, :] - mean_three) * scale_three
            + bias_three
            + (g.PRES[rows, :] - mean_side) * scale_side
            + bias_side
        )

    def mid_body(at, carry):
        rows = pl.ds(at, WCH)
        v = mid_value(rows)
        out = v * gate(v) * bc(mask_rows(at, WCH), CO)
        g.BM[rows, :] = out
        g.MIDC[0, rows, :] = out.astype(BF)
        return carry

    over(R, WCH, mid_body, 0)
    rm_mid = net.push(g.MIDC.at[0], g.MIDC.at[1], core)

    for copy in ld_w4:
        copy.wait()
    for copy in rm_w4:
        copy.wait_recv()
    rm_back.append(net.push(g.W4C.at[pl.ds(CO, CO), pl.ds(0, MI)], g.W4P.at[1], core))
    rm_mid.wait_recv()
    part = mm(lanes([g.MIDC[0], g.MIDC[1]]), g.W4C[...])
    g.P4S[...] = part[:, :MI].astype(BF)
    rm_p4 = net.push(g.P4S, g.P4R, far)
    g.PRE4[...] = part[:, MI:]

    def take_p4(ph):
        rm_p4.wait_recv()

        def add(at, carry):
            rows = pl.ds(at, NCH)
            g.PRE4[rows, :] = g.PRE4[rows, :] + g.P4R[rows, :].astype(F32)
            return carry

        over(R, NCH, add, 0)

    st_four = narrow_send(2, *narrow_local(g.PRE4, 1, take_p4))
    mean_four, spread_four = narrow_merge(2, st_four, 1)
    inv_four, scale_four = scale_of(spread_four, g.gm[2:3, :])
    narrow_feature(g.PRE4, mean_four, scale_four, g.bm[2:3, :], g.F4.at[0], 0, QS)
    ch_four = gather(lambda s: g.F4.at[s], QS, R)
    for copy in ld_w5:
        copy.wait()

    def spread_rows(src, dst_up, dst_down):
        def body(at, carry):
            rows = pl.ds(QS + at, QS)
            v = src[rows, :].astype(F32)
            dst_up[rows, :] = shifted(v, -1).astype(BF)
            dst_down[rows, :] = shifted(v, 1).astype(BF)
            return carry

        over(R, QS, body, 0)

    def fill_four(s):
        spread_rows(g.F4.at[s], g.D4.at[0, s], g.D4.at[1, s])

    fill_four(0)
    relay(ch_four)
    ch_four[0].wait_recv()
    fill_four(1)
    fill_four(2)
    ch_four[3].wait_recv()
    fill_four(3)

    def whole_four(t, l):
        rows = slice(l * QS, l * QS + R)
        if t == 1:
            return lanes([g.F4[s, rows, :] for s in range(4)])
        return lanes([g.D4[t // 2, s, rows, :] for s in range(4)])

    pre_five = None
    for t in range(3):
        for l in range(3):
            term = mm(whole_four(t, l), kernel_rows(g.W5, 3 * t + l))
            pre_five = term if pre_five is None else pre_five + term
    g.PRE5[...] = pre_five
    st_five = narrow_send(3, *narrow_local(g.PRE5, 1))
    mean_five, spread_five = narrow_merge(3, st_five, 1)
    inv_five, scale_five = scale_of(spread_five, g.gm[3:4, :])
    narrow_feature(g.PRE5, mean_five, scale_five, g.bm[3:4, :], g.F5.at[0], 0, 0)
    ch_five = gather(lambda s: g.F5.at[s], 0, R)
    for copy in ld_w6:
        copy.wait()
    ld_cot.wait()
    relay(ch_five)
    landed(ch_five)
    g.PRE6[...] = mm(four(g.F5), g.W6[...].reshape(4 * MI, CO))
    st_six = wide_send(2, *wide_local(g.PRE6))
    mean_six, spread_six = wide_merge(2, st_six)
    inv_six, scale_six = scale_of(spread_six, g.go[2:3, :])
    bias_six = g.bo[2:3, :]

    def last_body(at, carry):
        acc_b, acc_g = carry
        rows = pl.ds(at, WCH)
        m = bc(mask_rows(at, WCH), CO)
        hat = (g.PRE6[rows, :] - mean_six) * inv_six
        v = (g.PRE6[rows, :] - mean_six) * scale_six + bias_six + g.BM[rows, :]
        s = gate(v)
        g.OUT[rows, :] = v * s * m
        grad = g.COT[rows, :].astype(F32) * m * (s * (1.0 + v * (1.0 - s)))
        g.GSB[rows, :] = grad
        return acc_b + fold(grad), acc_g + fold(grad * hat)

    zero_w = jnp.zeros((8, CO), F32)
    acc_b, acc_g = over(R, WCH, last_body, (zero_w, zero_w))

    def down(value):
        return jnp.sum(value, axis=0, keepdims=True)

    st = wide_send(3, down(acc_b), down(acc_g))

    out = g.OUT[...]
    high = out.astype(BF)
    low = (out - high.astype(F32)).astype(BF)
    g.OUTP[...] = mm(g.po[...], high) + mm(g.po[...], low)
    out_block = net.local(g.OUTP, g.block_out)

    def wide_sums(ref, copies, count):
        for copy in copies:
            copy.wait_recv()
        return [
            wide_row(tree([ref[k, j * NW : (j + 1) * NW, :] for k in range(NB)]))
            for j in range(count)
        ]

    def narrow_sums(idx, copies):
        for copy in copies:
            copy.wait_recv()
        return [tree([g.SN[idx, k, j : j + 1, :] for k in range(NB)]) for j in range(2)]

    bsum_six, gsum_six = wide_sums(g.SW.at[3], st, 2)
    inv_wide = bc(inv_out, CO)

    def wide_pre_grad(grad, pre, mean, inv, scale, bsum, gsum, out):
        mb, mg = bsum * inv_wide, gsum * inv_wide

        def body(at, carry):
            rows = pl.ds(at, WCH)
            hat = (pre[rows, :] - mean) * inv
            e = bc(mask_rows(at, WCH), CO) * scale * (grad[rows, :] - (mb + hat * mg))
            out[rows, :] = e.astype(BF)
            return carry

        over(R, WCH, body, 0)

    wide_pre_grad(
        g.GSB, g.PRE6, mean_six, inv_six, scale_six, bsum_six, gsum_six, g.E6.at[0]
    )
    for copy in rm_back:
        copy.wait_recv()

    def swap(ref):
        return net.push(ref.at[0], ref.at[1], core)

    def reduce_back(part, sent, got):
        sent[...] = part[:, MI:].astype(BF)
        return net.push(sent, got, far)

    def wide_back(e, own, other):
        near = lanes([own[0], other[0]])
        away = lanes([own[2], other[1]])
        return mm_nt(lanes([e[0], e[1]]), jnp.concatenate([near, away], axis=0))

    def narrow_back(idx, near, got, copy, phases, pre, mean, inv, scale, bias, order=None):
        acc_b = jnp.zeros((8, MI), F32)
        acc_g = jnp.zeros((8, MI), F32)
        for ph in range(phases):
            copy[ph].wait_recv()

            def body(at, carry, ph=ph):
                b_acc, g_acc = carry
                rows = pl.ds(ph * R + at, NCH)
                hat = (pre[rows, :] - mean) * inv
                v = (pre[rows, :] - mean) * scale + bias
                s = gate(v)
                feat = near[rows, :] + got[rows, :].astype(F32)
                grad = feat * mask_rows(at, NCH) * (s * (1.0 + v * (1.0 - s)))
                near[rows, :] = grad
                return b_acc + fold(grad), g_acc + fold(grad * hat)

            acc_b, acc_g = over(R, NCH, body, (acc_b, acc_g))
        return narrow_send(idx, down(acc_b), down(acc_g))

    def narrow_pre_grad(grad, pre, mean, inv, scale, bsum, gsum, phases, ph, out, at0):
        inv_count = inv_out * (1.0 / phases)
        mb, mg = bsum * inv_count, gsum * inv_count

        def body(at, carry):
            rows = pl.ds(ph * R + at, NCH)
            hat = (pre[rows, :] - mean) * inv
            e = mask_rows(at, NCH) * scale * (grad[rows, :] - (mb + hat * mg))
            out[pl.ds(at0 + at, NCH), :] = e.astype(BF)
            return carry

        over(R, NCH, body, 0)

    outs = []

    def give(src, dst):
        outs.append(net.local(src, dst))

    cp = swap(g.E6)
    cp.wait_recv()
    part = wide_back(g.E6, g.W6, g.W6P)
    cp = [reduce_back(part, g.B5S, g.B5R)]
    g.GF5[...] = part[:, :MI]
    for s in range(4):
        g.K6[s] = mm_tn(g.F5[s], g.E6[0]).astype(BF)
        give(g.K6.at[s], rows_of(g.k6, ranks[s], MI))
    st = narrow_back(
        4, g.GF5, g.B5R, cp, 1, g.PRE5, mean_five, inv_five, scale_five, g.bm[3:4, :]
    )
    bsum_five, gsum_five = narrow_sums(4, st)
    narrow_pre_grad(
        g.GF5, g.PRE5, mean_five, inv_five, scale_five, bsum_five, gsum_five, 1, 0,
        g.E5.at[1, 0], QS,
    )
    cp = net.push(g.E5.at[1, 0, pl.ds(QS, R)], g.E5.at[1, 1, pl.ds(QS, R)], core)
    spread_rows(g.E5.at[1, 0], g.E5.at[0, 0], g.E5.at[2, 0])
    cp.wait_recv()
    spread_rows(g.E5.at[1, 1], g.E5.at[0, 1], g.E5.at[2, 1])

    def taps_back(own, other, tap):
        near = lanes([own[tap, 0], other[tap, 0]])
        away = lanes([own[tap, 2], other[tap, 1]])
        return jnp.concatenate([near, away], axis=0)

    part = None
    for t in range(3):
        for l in range(3):
            rows = slice((2 - l) * QS, (2 - l) * QS + R)
            e = lanes([g.E5[2 - t, s, rows, :] for s in range(2)])
            term = mm_nt(e, taps_back(g.W5, g.W5P, 3 * t + l))
            part = term if part is None else part + term
    cp = [reduce_back(part, g.B4S, g.B4R)]
    g.GF4[...] = part[:, :MI]
    own_five = g.E5[1, 0, QS : QS + R, :]
    for t in range(3):
        for l in range(3):
            g.K5[3 * t + l] = mm_tn(whole_four(t, l), own_five).astype(BF)
    for s in range(4):
        give(g.K5.at[:, pl.ds(s * MI, MI), :], taps_of(g.k5, ranks[s], MI))
    st = narrow_back(
        5, g.GF4, g.B4R, cp, 1, g.PRE4, mean_four, inv_four, scale_four, g.bm[2:3, :]
    )
    bsum_four, gsum_four = narrow_sums(5, st)
    narrow_pre_grad(
        g.GF4, g.PRE4, mean_four, inv_four, scale_four, bsum_four, gsum_four, 1, 0,
        g.G4.at[0], 0,
    )
    ch = gather(lambda s: g.G4.at[s], 0, R)
    relay(ch)
    landed(ch)
    mid_back = mm_nt(
        four(g.G4),
        lanes([g.W4C[0:CO, MI:], g.W4P[0], g.W4C[0:CO, :MI], g.W4P[1]]),
    )
    g.GMID[...] = mid_back

    def mid_back_body(at, carry):
        a_b, a_3, a_s = carry
        rows = pl.ds(at, WCH)
        v = mid_value(rows)
        s = gate(v)
        grad = (g.GSB[rows, :] + g.GMID[rows, :]) * bc(mask_rows(at, WCH), CO)
        grad = grad * (s * (1.0 + v * (1.0 - s)))
        g.GMID[rows, :] = grad
        hat3 = (g.PRE3[rows, :] - mean_three) * inv_three
        hats = (g.PRES[rows, :] - mean_side) * inv_side
        return a_b + fold(grad), a_3 + fold(grad * hat3), a_s + fold(grad * hats)

    a_b, a_3, a_s = over(R, WCH, mid_back_body, (zero_w, zero_w, zero_w))
    for j, value in enumerate((a_b, a_3, a_s, zero_w)):
        wide_put(g.SA, j * NW, down(value))
    st = exchange(g.SA, 4 * NW)
    e4 = lanes([g.G4[0], g.G4[2]])
    for s in range(2):
        k4 = mm_tn(g.MIDC[s], e4)
        g.K4[0, s] = k4[:, :MI].astype(BF)
        g.K4[1, s] = k4[:, MI:].astype(BF)
    cp_k4 = net.push(g.K4.at[1], g.K4R, far)
    bsum_a, gsum_three, gsum_side = wide_sums(g.SA, st, 3)
    wide_pre_grad(
        g.GMID, g.PRE3, mean_three, inv_three, scale_three, bsum_a, gsum_three,
        g.E3.at[0],
    )
    cp = swap(g.E3)
    wide_pre_grad(
        g.GMID, g.PRES, mean_side, inv_side, scale_side, bsum_a, gsum_side, g.ES.at[0]
    )
    cp_side = swap(g.ES)
    cp.wait_recv()
    part = wide_back(g.E3, g.W3, g.W3P)
    cp = [reduce_back(part, g.B2S, g.B2R)]
    g.GF2[...] = part[:, :MI]
    for s in range(4):
        g.K3[s] = mm_tn(g.F2[s], g.E3[0]).astype(BF)
        give(g.K3.at[s], rows_of(g.k3, ranks[s], MI))
    st = narrow_back(
        6, g.GF2, g.B2R, cp, 1, g.PRE2, mean_two, inv_two, scale_two, g.bm[1:2, :]
    )
    cp_side.wait_recv()
    es = lanes([g.ES[0], g.ES[1]])
    g.IGS[...] = mm_nt(es, lanes([g.WS[0], g.WSP[0]]))
    bsum_two, gsum_two = narrow_sums(6, st)
    narrow_pre_grad(
        g.GF2, g.PRE2, mean_two, inv_two, scale_two, bsum_two, gsum_two, 1, 0,
        g.E2.at[0, 0], 0,
    )
    cp = net.push(g.E2.at[0, 0, pl.ds(0, R)], g.E2.at[0, 1, pl.ds(0, R)], core)

    def lift(s):
        def body(at, carry):
            rows = pl.ds(at, QS)
            v = g.E2[0, s, rows, :].astype(F32)
            g.E2[1, s, rows, :] = shifted(v, 1).astype(BF)
            return carry

        over(R, QS, body, 0)

    lift(0)
    cp.wait_recv()
    lift(1)
    cp = []
    for ph in range(4):
        part = None
        for t, l in taps_two(ph):
            rows = slice(QS, QS + R) if l == 0 else slice(0, R)
            e = lanes([g.E2[1 if t == 0 else 0, s, rows, :] for s in range(2)])
            term = mm_nt(e, taps_back(g.W2, g.W2P, 3 * t + l))
            part = term if part is None else part + term
        cp.append(
            reduce_back(part, g.B1S.at[pl.ds(ph * R, R)], g.B1R.at[pl.ds(ph * R, R)])
        )
        g.GF1[ph * R : (ph + 1) * R, :] = part[:, :MI]
    own_two = g.E2[0, 0, 0:R, :]
    for ph in range(4):
        for t, l in taps_two(ph):
            g.K2[3 * t + l] = mm_tn(whole_one(ph, t == 0, l == 0), own_two).astype(BF)
    for s in range(4):
        give(g.K2.at[:, pl.ds(s * MI, MI), :], taps_of(g.k2, ranks[s], MI))
    st = narrow_back(
        7, g.GF1, g.B1R, cp, 4, g.PRE1, mean_one, inv_one, scale_one, g.bm[0:1, :]
    )
    side_far = mm_nt(es, lanes([g.WS[2], g.WSP[1]]))
    g.BSS[...] = side_far.astype(BF)
    cp_bs = net.push(g.BSS, g.BSR, far)
    bsum_one, gsum_one = narrow_sums(7, st)
    ch = []
    for ph in range(4):
        narrow_pre_grad(
            g.GF1, g.PRE1, mean_one, inv_one, scale_one, bsum_one, gsum_one, 4, ph,
            g.G1.at[0, ph], 0,
        )
        ch.append(gather(lambda s, ph=ph: g.G1.at[s, ph], 0, R))
    for s, block in enumerate(strided()):
        g.KS[s] = mm_tn(block, g.ES[0]).astype(BF)
        give(g.KS.at[s], rows_of(g.ks, ranks[s], CI))
    w1_own = lanes([g.W1C[0:CI, MI:], g.W1P[0], g.W1C[0:CI, :MI], g.W1P[1]])
    relay(ch[0])
    for ph in range(4):
        if ph < 3:
            relay(ch[ph + 1])
        landed(ch[ph])
        whole = lanes([g.G1[s, ph] for s in range(4)])
        g.IG[ph * R : (ph + 1) * R, :] = mm_nt(whole, w1_own)
    cp_bs.wait_recv()
    g.IG[0:R, :] = g.IG[0:R, :] + g.IGS[...] + g.BSR[...].astype(F32)
    for a in range(2):
        both = jnp.concatenate(
            [
                g.IG[(2 * a + h) * R : (2 * a + h + 1) * R, :] * bc(g.mask[...], CI)
                for h in range(2)
            ],
            axis=0,
        )
        high = both.astype(BF)
        low = (both - high.astype(F32)).astype(BF)
        g.IGP[a] = (mm(g.pi[...], high) + mm(g.pi[...], low)).reshape(g.IGP.shape[1:])
        give(g.IGP.at[a], g.images_grad.at[:, a])
    for s in range(2):
        k1 = None
        for ph in range(4):
            e1 = lanes([g.G1[0, ph], g.G1[2, ph]])
            term = mm_tn(g.SRC[s, ph * R : (ph + 1) * R, :], e1)
            k1 = term if k1 is None else k1 + term
        g.K1[0, s] = k1[:, :MI].astype(BF)
        g.K1[1, s] = k1[:, MI:].astype(BF)
    cp_k1 = net.push(g.K1.at[1], g.K1R, far)
    cp_k4.wait_recv()
    cp_k1.wait_recv()
    for s in range(2):
        give(g.K4.at[0, s], rows_of(g.k4, ranks[s], CO))
        give(g.K1.at[0, s], rows_of(g.k1, ranks[s], CI))
        give(g.K4R.at[s], rows_of(g.k4, ranks[2 + s], CO))
        give(g.K1R.at[s], rows_of(g.k1, ranks[2 + s], CI))

    g.gain_mid_grad[...] = jnp.concatenate([gsum_one, gsum_two, gsum_four, gsum_five], axis=0)
    g.bias_mid_grad[...] = jnp.concatenate([bsum_one, bsum_two, bsum_four, bsum_five], axis=0)
    g.gain_out_grad[...] = jnp.concatenate([gsum_three, gsum_side, gsum_six], axis=0)
    g.bias_out_grad[...] = jnp.concatenate([bsum_a, bsum_a, bsum_six], axis=0)
    g.mean_mid[...] = jnp.concatenate([mean_one, mean_two, mean_four, mean_five], axis=0)
    g.var_mid[...] = jnp.concatenate(
        [spread_one * unb_in, spread_two * unb_out, spread_four * unb_out, spread_five * unb_out],
        axis=0,
    )
    g.mean_out[...] = jnp.concatenate([mean_three, mean_side, mean_six], axis=0)
    g.var_out[...] = jnp.concatenate([spread_three, spread_side, spread_six], axis=0) * bc(
        unb_out, CO
    )
    out_block.wait()
    for copy in outs:
        copy.wait()
    for copy in net.sent:
        copy.wait_send()


def fused_on_device(
    images, heights, widths, reduce_first, spatial_first, expand_first, shortcut, reduce_second,
    spatial_second, expand_second, gain_mid, bias_mid, gain_out, bias_out, cotangent,
):
    n, rows, cols, CO = cotangent.shape
    CI, MI = images.shape[3], reduce_first.shape[1]
    NB = heights.shape[0] // n
    R, QS = n * rows * cols, n * rows
    batch = lax.axis_index("batch")
    valid = heights * widths
    local_h = lax.dynamic_slice_in_dim(heights, batch * n, n)
    local_w = lax.dynamic_slice_in_dim(widths, batch * n, n)
    q, p, i = np.meshgrid(np.arange(cols), np.arange(rows), np.arange(n), indexing="ij")
    q, p, i = (v.reshape(-1) for v in (q, p, i))
    mask = (
        (jnp.asarray(p)[:, None] < jnp.tile(local_h, rows * cols)[:, None])
        & (jnp.asarray(q)[:, None] < jnp.tile(local_w, rows * cols)[:, None])
    ).astype(F32)
    where_out = (i * rows + p) * cols + q
    pick_out = np.zeros((R, R), np.float32)
    pick_out[np.arange(R), where_out] = 1.0
    pick_in = np.zeros((2 * R, 2 * R), np.float32)
    for h in range(2):
        pick_in[h * R + np.arange(R), (i * rows + p) * 2 * cols + 2 * q + h] = 1.0
    po = jnp.asarray(pick_out.T.astype(ml_dtypes.bfloat16))
    pi = jnp.asarray(pick_in.T.astype(ml_dtypes.bfloat16))
    mask_bf = mask.astype(BF)
    cot = jnp.einsum(
        "mk,kc->mc", po.T * mask_bf, cotangent.reshape(R, CO), preferred_element_type=F32
    ).astype(BF)
    parity = images.reshape(n, rows, 2, 2 * cols, CI).transpose(2, 0, 1, 3, 4).reshape(2, 2 * R, CI)
    src = jnp.einsum(
        "mk,akc->amc", pi.T * jnp.tile(mask_bf, (2, 1)), parity, preferred_element_type=F32
    ).astype(BF).reshape(4 * R, CI)
    order = np.arange(NB)
    by_rank = jnp.sum(valid.reshape(NB, n), axis=1)
    relative = jnp.take(by_rank, jnp.bitwise_xor(order, batch)).astype(F32)
    count_out = jnp.sum(valid).astype(F32)
    count_in = 4.0 * count_out
    aux = jnp.concatenate(
        [
            relative,
            1.0 / relative,
            jnp.stack(
                [1.0 / count_out, count_out / (count_out - 1.0), count_in / (count_in - 1.0)]
            ),
            jnp.zeros((5,), F32),
        ]
    )
    aux = jnp.broadcast_to(aux[:, None], (24, 128))
    ANY, VM = pl.BlockSpec(memory_space=pl.ANY), pl.BlockSpec(memory_space=pltpu.VMEM)
    CM, MC = 4 * MI, 4 * CI
    ins = dict(
        src=(src, ANY),
        cot=(cot, ANY),
        w1=(reduce_first, ANY),
        w2=(spatial_first.reshape(9, CM, MI), ANY),
        w3=(expand_first, ANY),
        wsc=(shortcut, ANY),
        w4=(reduce_second, ANY),
        w5=(spatial_second.reshape(9, CM, MI), ANY),
        w6=(expand_second, ANY),
        mask=(jnp.broadcast_to(mask, (R, 128)), VM),
        aux=(aux, VM),
        gm=(gain_mid, VM),
        bm=(bias_mid, VM),
        go=(gain_out, VM),
        bo=(bias_out, VM),
        po=(po, VM),
        pi=(pi, VM),
    )
    outs = dict(
        block_out=((R, CO), F32, ANY),
        images_grad=((n * rows, 2, 2 * cols, CI), F32, ANY),
        k1=((MC, MI), BF, ANY),
        k2=((9, CM, MI), BF, ANY),
        k3=((CM, CO), BF, ANY),
        ks=((MC, CO), BF, ANY),
        k4=((4 * CO, MI), BF, ANY),
        k5=((9, CM, MI), BF, ANY),
        k6=((CM, CO), BF, ANY),
        gain_mid_grad=((4, MI), F32, VM),
        bias_mid_grad=((4, MI), F32, VM),
        gain_out_grad=((3, CO), F32, VM),
        bias_out_grad=((3, CO), F32, VM),
        mean_mid=((4, MI), F32, VM),
        var_mid=((4, MI), F32, VM),
        mean_out=((3, CO), F32, VM),
        var_out=((3, CO), F32, VM),
    )
    NW = CO // 128
    scratch = dict(
        SRC=((2, 4 * R, CI), BF),
        XS=((2, R, CI), BF),
        W1C=((2 * CI, 2 * MI), BF),
        W1P=((2, CI, MI), BF),
        W2=((9, 4, MI, MI), BF),
        W2P=((9, 2, MI, MI), BF),
        W3=((4, MI, CO), BF),
        W3P=((2, MI, CO), BF),
        WS=((4, CI, CO), BF),
        WSP=((2, CI, CO), BF),
        W4C=((2 * CO, 2 * MI), BF),
        W4P=((2, CO, MI), BF),
        W5=((9, 4, MI, MI), BF),
        W5P=((9, 2, MI, MI), BF),
        W6=((4, MI, CO), BF),
        W6P=((2, MI, CO), BF),
        COT=((R, CO), BF),
        P1S=((4, R, MI), BF),
        P1R=((4, R, MI), BF),
        P4S=((R, MI), BF),
        P4R=((R, MI), BF),
        PRE1=((4 * R, MI), F32),
        PRE2=((R, MI), F32),
        PRE3=((R, CO), F32),
        PRES=((R, CO), F32),
        PRE4=((R, MI), F32),
        PRE5=((R, MI), F32),
        PRE6=((R, CO), F32),
        F1=((4, 4, QS + R, MI), BF),
        D1=((2, 4, QS + R, MI), BF),
        F2=((4, R, MI), BF),
        BM=((R, CO), F32),
        MIDC=((2, R, CO), BF),
        F4=((4, R + 2 * QS, MI), BF),
        D4=((2, 4, R + 2 * QS, MI), BF),
        F5=((4, R, MI), BF),
        OUT=((R, CO), F32),
        OUTP=((R, CO), F32),
        GSB=((R, CO), F32),
        E6=((2, R, CO), BF),
        B5S=((R, MI), BF),
        B5R=((R, MI), BF),
        GF5=((R, MI), F32),
        E5=((3, 2, R + 2 * QS, MI), BF),
        B4S=((R, MI), BF),
        B4R=((R, MI), BF),
        GF4=((R, MI), F32),
        G4=((4, R, MI), BF),
        GMID=((R, CO), F32),
        E3=((2, R, CO), BF),
        ES=((2, R, CO), BF),
        B2S=((R, MI), BF),
        B2R=((R, MI), BF),
        GF2=((R, MI), F32),
        E2=((2, 2, R + QS, MI), BF),
        B1S=((4 * R, MI), BF),
        B1R=((4 * R, MI), BF),
        GF1=((4 * R, MI), F32),
        G1=((4, 4, R, MI), BF),
        IGS=((R, CI), F32),
        BSS=((R, CI), BF),
        BSR=((R, CI), BF),
        IG=((4 * R, CI), F32),
        IGP=((2, n * rows, 2 * cols, CI), F32),
        K1=((2, 2, CI, MI), BF),
        K1R=((2, CI, MI), BF),
        K2=((9, CM, MI), BF),
        K3=((4, MI, CO), BF),
        KS=((4, CI, CO), BF),
        K4=((2, 2, CO, MI), BF),
        K4R=((2, CO, MI), BF),
        K5=((9, CM, MI), BF),
        K6=((4, MI, CO), BF),
        SN=((8, NB, 2, MI), F32),
        SW=((4, NB, 2 * NW, 128), F32),
        SA=((NB, 4 * NW, 128), F32),
    )
    names = [*ins, *outs, *scratch, "sems"]
    geo = types.SimpleNamespace(R=R, QS=QS, PS=n, CI=CI, MI=MI, CO=CO, NB=NB)
    got = pl.pallas_call(
        functools.partial(block_kernel, geo, names),
        out_shape=[jax.ShapeDtypeStruct(s, d) for s, d, _ in outs.values()],
        in_specs=[spec for _, spec in ins.values()],
        out_specs=[spec for _, _, spec in outs.values()],
        scratch_shapes=[pltpu.VMEM(s, d) for s, d in scratch.values()]
        + [pltpu.SemaphoreType.DMA((SEMS,))],
        compiler_params=pltpu.CompilerParams(
            collective_id=0, has_side_effects=True, vmem_limit_bytes=VMEM_LIMIT
        ),
    )(*[value for value, _ in ins.values()])
    o = types.SimpleNamespace(**dict(zip(outs, got)))
    k1, k2, k3, ks, k4, k5, k6 = (
        lax.psum(k, "batch").astype(F32) for k in (o.k1, o.k2, o.k3, o.ks, o.k4, o.k5, o.k6)
    )
    return (
        o.block_out.reshape(n, rows, cols, CO),
        o.images_grad.reshape(n, 2 * rows, 2 * cols, CI),
        k1,
        k2.reshape(3, 3, CM, MI),
        k3,
        ks,
        k4,
        k5.reshape(3, 3, CM, MI),
        k6,
        o.gain_mid_grad,
        o.bias_mid_grad,
        o.gain_out_grad,
        o.bias_out_grad,
        o.mean_mid,
        o.var_mid,
        o.mean_out,
        o.var_out,
    )


def solution(mesh):
    in_specs = (
        P("batch", None, None, "chan"),
        P(),
        P(),
        P(None, "chan"),
        P(None, None, None, "chan"),
        P(None, "chan"),
        P(None, "chan"),
        P(None, "chan"),
        P(None, None, None, "chan"),
        P(None, "chan"),
        P(None, "chan"),
        P(None, "chan"),
        P(None, "chan"),
        P(None, "chan"),
        P("batch", None, None, "chan"),
    )
    out_specs = (
        P("batch", None, None, "chan"),
        P("batch", None, None, "chan"),
        P(None, "chan"),
        P(None, None, None, "chan"),
        P(None, "chan"),
        P(None, "chan"),
        P(None, "chan"),
        P(None, None, None, "chan"),
        P(None, "chan"),
        P(None, "chan"),
        P(None, "chan"),
        P(None, "chan"),
        P(None, "chan"),
        P(None, "chan"),
        P(None, "chan"),
        P(None, "chan"),
        P(None, "chan"),
    )
    fused = mesh.shape["chan"] == 4 and mesh.shape["batch"] == 8
    return jax.shard_map(
        fused_on_device if fused else on_device, mesh=mesh, in_specs=in_specs, out_specs=out_specs, check_vma=False
    )
```

```python
import functools
import types

import jax
import jax.numpy as jnp
import ml_dtypes
import numpy as np
from jax import lax
from jax.experimental import pallas as pl
from jax.experimental.pallas import tpu as pltpu
from jax.sharding import PartitionSpec as P

EPS = 1e-05
VMEM_LIMIT = 60 * 1024 * 1024


def shortened(shard):
    return jax.tree.map(lambda a: a.astype(jnp.bfloat16) if a.dtype == jnp.float32 else a, shard)


def frame_masks(heights, widths, rows, cols):
    tall = heights[:, None, None]
    broad = widths[:, None, None]
    row_in = jnp.arange(2 * rows, dtype=jnp.int32)[None, :, None]
    col_in = jnp.arange(2 * cols, dtype=jnp.int32)[None, None, :]
    row_out = jnp.arange(rows, dtype=jnp.int32)[None, :, None]
    col_out = jnp.arange(cols, dtype=jnp.int32)[None, None, :]
    inner = ((row_in < 2 * tall) & (col_in < 2 * broad)).astype(jnp.float32)[..., None]
    outer = ((row_out < tall) & (col_out < broad)).astype(jnp.float32)[..., None]
    return (inner, outer)


def silu_slope(value):
    sig = jax.nn.sigmoid(value)
    return sig * (1.0 + value * (1.0 - sig))


def convolve(source, kernel, stride, rows, cols):
    taps = kernel.shape[0]
    margin = taps // 2
    padded = jnp.pad(source, ((0, 0), (margin, margin), (margin, margin), (0, 0)))
    total = None
    for top in range(taps):
        for left in range(taps):
            window = padded[
                :, top : top + stride * rows : stride, left : left + stride * cols : stride, :
            ]
            term = jnp.einsum(
                "nhwc,cd->nhwd", window, kernel[top, left], preferred_element_type=jnp.float32
            )
            total = term if total is None else total + term
    return total


def kernel_grad(source, grad, stride, taps):
    rows, cols = (grad.shape[1], grad.shape[2])
    margin = taps // 2
    padded = jnp.pad(source, ((0, 0), (margin, margin), (margin, margin), (0, 0)))
    return jnp.stack(
        [
            jnp.stack(
                [
                    jnp.einsum(
                        "nhwc,nhwd->cd",
                        padded[
                            :,
                            top : top + stride * rows : stride,
                            left : left + stride * cols : stride,
                            :,
                        ],
                        grad,
                        preferred_element_type=jnp.float32,
                    )
                    for left in range(taps)
                ]
            )
            for top in range(taps)
        ]
    )


def spread_back(grad, kernel, stride):
    taps = kernel.shape[0]
    margin = taps // 2
    total = None
    for top in range(taps):
        for left in range(taps):
            term = jnp.einsum(
                "nhwd,cd->nhwc", grad, kernel[top, left], preferred_element_type=jnp.float32
            )
            placed = lax.pad(
                term,
                jnp.float32(0.0),
                (
                    (0, 0, 0),
                    (top, 2 * margin - top + stride - 1, stride - 1),
                    (left, 2 * margin - left + stride - 1, stride - 1),
                    (0, 0, 0),
                ),
            )
            total = placed if total is None else total + placed
    rows, cols = (grad.shape[1], grad.shape[2])
    return total[:, margin : margin + stride * rows, margin : margin + stride * cols, :]


def norm_forward(pre, mask, count, gain, bias):
    mean = lax.psum(jnp.sum(pre * mask, axis=(0, 1, 2)), "batch") / count
    centered = (pre - mean) * mask
    spread = lax.psum(jnp.sum(centered * centered, axis=(0, 1, 2)), "batch") / count
    inv = lax.rsqrt(spread + EPS)
    hat = (pre - mean) * inv
    return (hat * gain + bias, hat, inv, mean, spread)


def norm_backward(grad, hat, mask, count, gain, inv):
    masked = grad * mask
    bias_grad, gain_grad = lax.psum(
        (jnp.sum(masked, axis=(0, 1, 2)), jnp.sum(masked * hat, axis=(0, 1, 2))), "batch"
    )
    pre_grad = mask * gain * inv * (grad - (bias_grad + hat * gain_grad) / count)
    return (pre_grad.astype(jnp.bfloat16), gain_grad, bias_grad)


def widen(feature):
    return lax.all_gather(feature, "chan", axis=3, tiled=True)


def input_grad(grad, kernel, stride):
    return jax.tree.map(
        lambda part: part.astype(jnp.float32),
        lax.psum_scatter(
            shortened(spread_back(grad, kernel, stride)), "chan", scatter_dimension=3, tiled=True
        ),
    )


def image_back(grad_one, grad_side, kernels):
    summands = spread_back(grad_one, kernels[0], 1) + spread_back(grad_side, kernels[3], 2)
    return lax.psum_scatter(
        summands.astype(jnp.bfloat16), "chan", scatter_dimension=3, tiled=True
    ).astype(jnp.float32)


def on_device(
    images,
    heights,
    widths,
    reduce_first,
    spatial_first,
    expand_first,
    shortcut,
    reduce_second,
    spatial_second,
    expand_second,
    gain_mid,
    bias_mid,
    gain_out,
    bias_out,
    cotangent,
):
    local = images.shape[0]
    rows, cols = (cotangent.shape[1], cotangent.shape[2])
    offset = lax.axis_index("batch") * local
    inner, outer = frame_masks(
        lax.dynamic_slice_in_dim(heights, offset, local),
        lax.dynamic_slice_in_dim(widths, offset, local),
        rows,
        cols,
    )
    count_out = jnp.sum(heights * widths).astype(jnp.float32)
    count_in = 4.0 * count_out
    kernels = (
        reduce_first[None, None],
        spatial_first,
        expand_first[None, None],
        shortcut[None, None],
        reduce_second[None, None],
        spatial_second,
        expand_second[None, None],
    )
    source = images * inner.astype(jnp.bfloat16)
    whole_source = lax.all_gather(source, "chan", axis=3, tiled=True)
    pre_one = convolve(whole_source, kernels[0], 1, 2 * rows, 2 * cols)
    normed_one, hat_one, inv_one, mean_one, spread_one = norm_forward(
        pre_one, inner, count_in, gain_mid[0], bias_mid[0]
    )
    whole_one = widen((jax.nn.silu(normed_one) * inner).astype(jnp.bfloat16))
    pre_two = convolve(whole_one, kernels[1], 2, rows, cols)
    normed_two, hat_two, inv_two, mean_two, spread_two = norm_forward(
        pre_two, outer, count_out, gain_mid[1], bias_mid[1]
    )
    whole_two = widen((jax.nn.silu(normed_two) * outer).astype(jnp.bfloat16))
    pre_three = convolve(whole_two, kernels[2], 1, rows, cols)
    normed_three, hat_three, inv_three, mean_three, spread_three = norm_forward(
        pre_three, outer, count_out, gain_out[0], bias_out[0]
    )
    pre_side = convolve(whole_source, kernels[3], 2, rows, cols)
    normed_side, hat_side, inv_side, mean_side, spread_side = norm_forward(
        pre_side, outer, count_out, gain_out[1], bias_out[1]
    )
    block_mid = jax.nn.silu(normed_three + normed_side) * outer
    whole_mid = widen(block_mid.astype(jnp.bfloat16))
    pre_four = convolve(whole_mid, kernels[4], 1, rows, cols)
    normed_four, hat_four, inv_four, mean_four, spread_four = norm_forward(
        pre_four, outer, count_out, gain_mid[2], bias_mid[2]
    )
    whole_four = widen((jax.nn.silu(normed_four) * outer).astype(jnp.bfloat16))
    pre_five = convolve(whole_four, kernels[5], 1, rows, cols)
    normed_five, hat_five, inv_five, mean_five, spread_five = norm_forward(
        pre_five, outer, count_out, gain_mid[3], bias_mid[3]
    )
    whole_five = widen((jax.nn.silu(normed_five) * outer).astype(jnp.bfloat16))
    pre_six = convolve(whole_five, kernels[6], 1, rows, cols)
    normed_six, hat_six, inv_six, mean_six, spread_six = norm_forward(
        pre_six, outer, count_out, gain_out[2], bias_out[2]
    )
    result = jax.nn.silu(normed_six + block_mid) * outer
    grad_sum_b = cotangent.astype(jnp.float32) * outer * silu_slope(normed_six + block_mid)
    grad_six, gain_six, bias_six = norm_backward(
        grad_sum_b, hat_six, outer, count_out, gain_out[2], inv_six
    )
    kern_six = kernel_grad(whole_five, grad_six, 1, 1)
    grad_feat_five = input_grad(grad_six, kernels[6], 1)
    grad_five, gain_five, bias_five = norm_backward(
        grad_feat_five * outer * silu_slope(normed_five),
        hat_five,
        outer,
        count_out,
        gain_mid[3],
        inv_five,
    )
    kern_five = kernel_grad(whole_four, grad_five, 1, 3)
    grad_feat_four = input_grad(grad_five, kernels[5], 1)
    grad_four, gain_four, bias_four = norm_backward(
        grad_feat_four * outer * silu_slope(normed_four),
        hat_four,
        outer,
        count_out,
        gain_mid[2],
        inv_four,
    )
    kern_four = kernel_grad(whole_mid, grad_four, 1, 1)
    grad_mid = grad_sum_b + input_grad(grad_four, kernels[4], 1)
    grad_sum_a = grad_mid * outer * silu_slope(normed_three + normed_side)
    grad_three, gain_three, bias_three = norm_backward(
        grad_sum_a, hat_three, outer, count_out, gain_out[0], inv_three
    )
    grad_side, gain_side, bias_side = norm_backward(
        grad_sum_a, hat_side, outer, count_out, gain_out[1], inv_side
    )
    kern_three = kernel_grad(whole_two, grad_three, 1, 1)
    kern_side = kernel_grad(whole_source, grad_side, 2, 1)
    grad_feat_two = input_grad(grad_three, kernels[2], 1)
    grad_two, gain_two, bias_two = norm_backward(
        grad_feat_two * outer * silu_slope(normed_two),
        hat_two,
        outer,
        count_out,
        gain_mid[1],
        inv_two,
    )
    kern_two = kernel_grad(whole_one, grad_two, 2, 3)
    grad_feat_one = input_grad(grad_two, kernels[1], 2)
    grad_one, gain_one, bias_one = norm_backward(
        grad_feat_one * inner * silu_slope(normed_one),
        hat_one,
        inner,
        count_in,
        gain_mid[0],
        inv_one,
    )
    kern_one = kernel_grad(whole_source, grad_one, 1, 1)
    images_grad = image_back(grad_one, grad_side, kernels) * inner
    summed = (
        lax.psum(kern_one.astype(jnp.bfloat16), "batch").astype(jnp.float32),
        lax.psum(kern_two.astype(jnp.bfloat16), "batch").astype(jnp.float32),
        lax.psum(kern_three.astype(jnp.bfloat16), "batch").astype(jnp.float32),
        lax.psum(kern_side.astype(jnp.bfloat16), "batch").astype(jnp.float32),
        lax.psum(kern_four.astype(jnp.bfloat16), "batch").astype(jnp.float32),
        lax.psum(kern_five.astype(jnp.bfloat16), "batch").astype(jnp.float32),
        lax.psum(kern_six.astype(jnp.bfloat16), "batch").astype(jnp.float32),
    )
    counts_mid = jnp.stack([count_in, count_out, count_out, count_out])[:, None]
    mean_mid_batch = jnp.stack([mean_one, mean_two, mean_four, mean_five])
    var_mid_batch = (
        jnp.stack([spread_one, spread_two, spread_four, spread_five])
        * counts_mid
        / (counts_mid - 1.0)
    )
    mean_out_batch = jnp.stack([mean_three, mean_side, mean_six])
    var_out_batch = (
        jnp.stack([spread_three, spread_side, spread_six]) * count_out / (count_out - 1.0)
    )
    return (
        result,
        images_grad,
        summed[0][0, 0],
        summed[1],
        summed[2][0, 0],
        summed[3][0, 0],
        summed[4][0, 0],
        summed[5],
        summed[6][0, 0],
        jnp.stack([gain_one, gain_two, gain_four, gain_five]),
        jnp.stack([bias_one, bias_two, bias_four, bias_five]),
        jnp.stack([gain_three, gain_side, gain_six]),
        jnp.stack([bias_three, bias_side, bias_six]),
        mean_mid_batch,
        var_mid_batch,
        mean_out_batch,
        var_out_batch,
    )


MESH = pl.DeviceIdType.MESH
BF = jnp.bfloat16
F32 = jnp.float32


def flip(value, bit):
    return value + bit - 2 * bit * lax.rem(lax.div(value, bit), 2)


def gate(value):
    return 0.5 * jnp.tanh(0.5 * value) + 0.5


def tree(parts):
    while len(parts) > 1:
        parts = [parts[k] + parts[k + 1] for k in range(0, len(parts), 2)]
    return parts[0]


def wide_row(block):
    return jnp.concatenate([block[j : j + 1] for j in range(block.shape[0])], axis=1)


def fold(value):
    return jnp.sum(value.reshape(value.shape[0] // 8, 8, value.shape[1]), axis=0)


def mm(a, b):
    return jnp.dot(a, b, preferred_element_type=F32)


def mm_nt(a, b):
    return lax.dot_general(a, b, (((1,), (1,)), ((), ())), preferred_element_type=F32)


def mm_tn(a, b):
    return lax.dot_general(a, b, (((0,), (0,)), ((), ())), preferred_element_type=F32)


class Traffic:
    def __init__(self, sems):
        self.sems, self.used, self.sent = sems, 0, []

    def take(self):
        self.used += 1
        return self.sems.at[self.used - 1]

    def push(self, src, dst, device):
        copy = pltpu.make_async_remote_copy(
            src_ref=src,
            dst_ref=dst,
            send_sem=self.take(),
            recv_sem=self.take(),
            device_id=device,
            device_id_type=MESH,
        )
        copy.start()
        self.sent.append(copy)
        return copy

    def local(self, src, dst):
        copy = pltpu.make_async_copy(src, dst, self.take())
        copy.start()
        return copy


class Summed:
    def __init__(self, net, part, got, done, coords, across=None):
        self.net, self.part, self.got, self.done = net, part, got, done
        (self.i0, self.p0), (self.i1, self.p1), (self.i2, self.p2) = coords
        self.across = across
        self.todo = [self.halves, self.quarters, self.eighths, self.finish]
        if across is not None:
            self.todo.append(self.crossed)
        self.todo += [self.pairs, self.fours, self.last]

    def step(self):
        self.todo.pop(0)()

    def halves(self):
        self.copy = self.net.push(self.part.at[:, :, 1 - self.i0], self.got[0], self.p0)

    def quarters(self):
        self.copy.wait_recv()
        for k in range(2):
            for j in range(2):
                self.got[0][k, j] = self.got[0][k, j] + self.part[k, j, self.i0]
        self.copy = self.net.push(self.got[0].at[:, 1 - self.i1], self.got[1], self.p1)

    def eighths(self):
        self.copy.wait_recv()
        for k in range(2):
            self.got[1][k] = self.got[1][k] + self.got[0][k, self.i1]
        self.copy = self.net.push(self.got[1].at[1 - self.i2], self.got[2], self.p2)

    def mine(self):
        return self.done.at[self.i2, self.i1, self.i0]

    def finish(self):
        self.copy.wait_recv()
        total = self.got[2][...] + self.got[1][self.i2]
        if self.across is None:
            self.done[self.i2, self.i1, self.i0] = total
            self.copy = self.net.push(self.mine(), self.mine(), self.p2)
        else:
            self.done[self.i2, self.i1, self.i0, 0] = total[0]
            self.got[2][1] = total[1]
            self.copy = self.net.push(self.got[2].at[1], self.mine().at[1], self.across)

    def crossed(self):
        self.copy.wait_recv()
        self.copy = self.net.push(self.mine(), self.mine(), self.p2)

    def pairs(self):
        self.copy.wait_recv()
        block = self.done.at[:, self.i1, self.i0]
        self.copy = self.net.push(block, block, self.p1)

    def fours(self):
        self.copy.wait_recv()
        block = self.done.at[:, :, self.i0]
        self.copy = self.net.push(block, block, self.p0)

    def last(self):
        self.copy.wait_recv()


SEMS = 700


def block_kernel(geo, names, *refs):
    g = types.SimpleNamespace(**dict(zip(names, refs)))
    R, QS, PS = geo.R, geo.QS, geo.PS
    CI, MI, CO = geo.CI, geo.MI, geo.CO
    NB = geo.NB
    r = lax.axis_index("chan")
    b = lax.axis_index("batch")
    r1, r2 = flip(r, 1), flip(r, 2)
    r3 = flip(r1, 2)
    ranks = (r, r1, r2, r3)
    core, far = (b, r1), (b, r2)
    peers = []
    for k in range(1, NB):
        other = b
        bit = 1
        while bit < NB:
            if k & bit:
                other = flip(other, bit)
            bit *= 2
        peers.append((other, r))
    net = Traffic(g.sems)
    x_way = (lax.rem(b, 2), (flip(b, 1), r))
    z_way = (lax.rem(lax.div(b, 2), 2), (flip(b, 2), r))
    s_way = (lax.div(b, 4), (flip(b, 4), r))
    x_first, z_first = (x_way, z_way, s_way), (z_way, x_way, s_way)

    bar = pltpu.get_barrier_semaphore()
    everyone = [core, far] + peers
    for device in everyone:
        pl.semaphore_signal(bar, 1, device_id=device, device_id_type=MESH)

    def rows_of(ref, rank, size):
        return ref.at[pl.ds(pl.multiple_of(rank * size, size), size)]

    def taps_of(ref, rank, size):
        return ref.at[:, pl.ds(pl.multiple_of(rank * size, size), size), :]

    ld_src = net.local(g.src, g.SRC.at[0])
    ld_w1 = [
        net.local(rows_of(g.w1, rank, CI), g.W1C.at[pl.ds(s * CI, CI), pl.ds(MI, MI)])
        for s, rank in enumerate((r, r1))
    ]
    ld_sc = [net.local(rows_of(g.wsc, rank, CI), g.WS.at[s]) for s, rank in enumerate(ranks)]
    ld_w2 = [net.local(taps_of(g.w2, rank, MI), g.W2.at[:, s]) for s, rank in enumerate(ranks)]
    ld_w3 = [net.local(rows_of(g.w3, rank, MI), g.W3.at[s]) for s, rank in enumerate(ranks)]
    ld_w4 = [
        net.local(rows_of(g.w4, rank, CO), g.W4C.at[pl.ds(s * CO, CO), pl.ds(MI, MI)])
        for s, rank in enumerate((r, r1))
    ]
    ld_w5 = [net.local(taps_of(g.w5, rank, MI), g.W5.at[:, s]) for s, rank in enumerate(ranks)]
    ld_w6 = [net.local(rows_of(g.w6, rank, MI), g.W6.at[s]) for s, rank in enumerate(ranks)]
    ld_cot = net.local(g.cot, g.COT)

    pl.semaphore_wait(bar, len(everyone))

    rm_src = net.push(g.src, g.SRC.at[1], core)
    rm_w1 = [
        net.push(rows_of(g.w1, rank, CI), g.W1C.at[pl.ds(s * CI, CI), pl.ds(0, MI)], far)
        for s, rank in enumerate((r2, r3))
    ]
    for ph in (1, 3):
        for s in range(4):
            g.F1[s, ph, 0:QS, :] = jnp.zeros((QS, MI), BF)
    for s in range(4):
        g.D1[1, s, 0:QS, :] = jnp.zeros((QS, MI), BF)
        g.F4[s, 0:QS, :] = jnp.zeros((QS, MI), BF)
        g.F4[s, QS + R :, :] = jnp.zeros((QS, MI), BF)
        for d in range(2):
            g.D4[d, s, 0:QS, :] = jnp.zeros((QS, MI), BF)
            g.D4[d, s, QS + R :, :] = jnp.zeros((QS, MI), BF)
    for d in range(3):
        for s in range(2):
            g.E5[d, s, 0:QS, :] = jnp.zeros((QS, MI), BF)
            g.E5[d, s, QS + R :, :] = jnp.zeros((QS, MI), BF)
    for d in range(2):
        for s in range(2):
            g.E2[d, s, R:, :] = jnp.zeros((QS, MI), BF)

    ld_src.wait()
    for copy in ld_w1:
        copy.wait()
    rm_src.wait_recv()
    for copy in rm_w1:
        copy.wait_recv()
    rm_p1 = []
    for ph in range(4):
        span = slice(ph * R, (ph + 1) * R)
        both = jnp.concatenate([g.SRC[0, span, :], g.SRC[1, span, :]], axis=1)
        part = mm(both, g.W1C[...])
        g.P1S[ph] = part[:, :MI].astype(BF)
        rm_p1.append(net.push(g.P1S.at[ph], g.P1R.at[ph], far))
        g.PRE1[span, :] = part[:, MI:]

    rm_back = []
    for s, rank in enumerate((r1, r3)):
        rm_back.append(net.push(rows_of(g.w6, rank, MI), g.W6P.at[s], core))
        rm_back.append(net.push(taps_of(g.w5, rank, MI), g.W5P.at[:, s], core))
        rm_back.append(net.push(rows_of(g.w3, rank, MI), g.W3P.at[s], core))
        rm_back.append(net.push(rows_of(g.wsc, rank, CI), g.WSP.at[s], core))
        rm_back.append(net.push(taps_of(g.w2, rank, MI), g.W2P.at[:, s], core))
    rm_back.append(net.push(rows_of(g.w4, r1, CO), g.W4P.at[0], core))
    rm_back.append(net.push(rows_of(g.w1, r1, CI), g.W1P.at[0], core))
    rm_back.append(
        net.push(g.W1C.at[pl.ds(CI, CI), pl.ds(0, MI)], g.W1P.at[1], core)
    )

    aux = g.aux
    inv_out = aux[16:17, :]
    unb_out, unb_in = aux[17:18, :], aux[18:19, :]

    def mask_rows(at, size):
        return g.mask[pl.ds(at, size), :]

    def over(total, size, body, init):
        def step(i, carry):
            return body(pl.multiple_of(i * size, size), carry)

        return lax.fori_loop(0, total // size, step, init)

    NCH = 128 if R % 128 == 0 else QS
    WCH = QS

    def bc(mask, width):
        return jnp.concatenate([mask] * (width // 128), axis=1)

    def exchange(slots, payload_rows):
        return [net.push(slots.at[0], slots.at[k], peers[k - 1]) for k in range(1, NB)]

    def narrow_local(pre, phases, prepare=None):
        total = jnp.zeros((8, MI), F32)
        for ph in range(phases):
            if prepare is not None:
                prepare(ph)

            def add(at, acc, ph=ph):
                return acc + fold(pre[pl.ds(ph * R + at, NCH), :] * mask_rows(at, NCH))

            total = over(R, NCH, add, total)
        total = jnp.sum(total, axis=0, keepdims=True)
        mean = total * (aux[8:9, :] * (1.0 / phases))
        squares = jnp.zeros((8, MI), F32)
        for ph in range(phases):

            def add2(at, acc, ph=ph):
                d = (pre[pl.ds(ph * R + at, NCH), :] - mean) * mask_rows(at, NCH)
                return acc + fold(d * d)

            squares = over(R, NCH, add2, squares)
        return total, jnp.sum(squares, axis=0, keepdims=True)

    def narrow_send(idx, first, second):
        slots = g.SN.at[idx]
        g.SN[idx, 0, 0:1, :] = first
        g.SN[idx, 0, 1:2, :] = second
        return exchange(slots, 2)

    def narrow_merge(idx, copies, phases):
        for copy in copies:
            copy.wait_recv()
        sums = [g.SN[idx, k, 0:1, :] for k in range(NB)]
        squares = [g.SN[idx, k, 1:2, :] for k in range(NB)]
        return moments(sums, squares, phases)

    def moments(sums, squares, phases):
        inv_count = inv_out * (1.0 / phases)
        mean = tree(list(sums)) * inv_count
        terms = []
        for k in range(NB):
            d = sums[k] * (aux[8 + k : 9 + k, :] * (1.0 / phases)) - mean
            terms.append(squares[k] + aux[k : k + 1, :] * float(phases) * d * d)
        spread = tree(terms) * inv_count
        return mean, spread

    def wide_local(pre):
        def add(at, acc):
            m = bc(mask_rows(at, WCH), CO)
            return acc + fold(pre[pl.ds(at, WCH), :] * m)

        total = jnp.sum(over(R, WCH, add, jnp.zeros((8, CO), F32)), axis=0, keepdims=True)
        mean = total * bc(aux[8:9, :], CO)

        def add2(at, acc):
            m = bc(mask_rows(at, WCH), CO)
            d = (pre[pl.ds(at, WCH), :] - mean) * m
            return acc + fold(d * d)

        squares = jnp.sum(over(R, WCH, add2, jnp.zeros((8, CO), F32)), axis=0, keepdims=True)
        return total, squares

    NW = CO // 128

    def wide_put(slots, row, value):
        for j in range(NW):
            slots[0, row + j : row + j + 1, :] = value[:, j * 128 : (j + 1) * 128]

    def wide_send(idx, first, second):
        slots = g.SW.at[idx]
        wide_put(slots, 0, first)
        wide_put(slots, NW, second)
        return exchange(slots, 2 * NW)

    def wide_merge(idx, copies):
        for copy in copies:
            copy.wait_recv()
        sums = [g.SW[idx, k, 0:NW, :] for k in range(NB)]
        squares = [g.SW[idx, k, NW : 2 * NW, :] for k in range(NB)]
        mean, spread = moments(sums, squares, 1)
        return wide_row(mean), wide_row(spread)

    def gather(buf, at, size):
        here = [buf(s).at[pl.ds(at, size)] for s in range(4)]
        near = net.push(here[0], here[1], core)
        away = net.push(here[0], here[2], far)
        return [near, away, here]

    def relay(chunk):
        near, away, here = chunk
        away.wait_recv()
        chunk.append(net.push(here[2], here[3], core))

    def landed(chunk):
        chunk[0].wait_recv()
        chunk[3].wait_recv()

    def lanes(parts):
        return jnp.concatenate(parts, axis=1)

    place = lax.broadcasted_iota(jnp.int32, (QS, 128), 0)
    keep_down = place >= PS
    keep_up = place < QS - PS

    def shifted(value, step):
        if step < 0:
            return jnp.where(keep_down, pltpu.roll(value, PS, 0), 0.0)
        return jnp.where(keep_up, pltpu.roll(value, QS - PS, 0), 0.0)

    def take_p1(ph):
        rm_p1[ph].wait_recv()

        def add(at, carry):
            rows = pl.ds(ph * R + at, NCH)
            g.PRE1[rows, :] = g.PRE1[rows, :] + g.P1R[ph, pl.ds(at, NCH), :].astype(F32)
            return carry

        over(R, NCH, add, 0)

    sum_one, sq_one = narrow_local(g.PRE1, 4, take_p1)
    st_one = narrow_send(0, sum_one, sq_one)
    rm_xs = net.push(g.SRC.at[0, pl.ds(0, R)], g.XS.at[0], far)

    def scale_of(spread, gain):
        inv = lax.rsqrt(spread + EPS)
        return inv, inv * gain

    mean_one, spread_one = narrow_merge(0, st_one, 4)
    inv_one, scale_one = scale_of(spread_one, g.gm[0:1, :])

    def narrow_feature(pre, mean, scale, bias, out, ph, at0):
        def body(at, carry):
            v = (pre[pl.ds(ph * R + at, NCH), :] - mean) * scale + bias
            out[pl.ds(at0 + at, NCH), :] = (v * gate(v) * mask_rows(at, NCH)).astype(BF)
            return carry

        over(R, NCH, body, 0)

    ch_one = []
    for ph in range(4):
        narrow_feature(
            g.PRE1, mean_one, scale_one, g.bm[0:1, :], g.F1.at[0, ph], ph, QS
        )
        ch_one.append(gather(lambda s, ph=ph: g.F1.at[s, ph], QS, R))

    rm_xs.wait_recv()
    rm_xs2 = net.push(g.XS.at[0], g.XS.at[1], core)
    for copy in ld_sc:
        copy.wait()
    rm_xs2.wait_recv()

    def strided():
        return [g.SRC[0, 0:R, :], g.SRC[1, 0:R, :], g.XS[0], g.XS[1]]

    pre_side = None
    for s, block in enumerate(strided()):
        term = mm(block, g.WS[s])
        pre_side = term if pre_side is None else pre_side + term
    g.PRES[...] = pre_side
    st_side = wide_send(0, *wide_local(g.PRES))

    for copy in ld_w2:
        copy.wait()

    def whole_one(ph, down, left):
        rows = slice(0, R) if left else slice(QS, QS + R)
        if down:
            return lanes([g.D1[ph - 2, s, rows, :] for s in range(4)])
        return lanes([g.F1[s, ph, rows, :] for s in range(4)])

    def kernel_rows(ref, tap):
        return jnp.concatenate([ref[tap, s] for s in range(4)], axis=0)

    def taps_two(ph):
        top = (1,) if ph < 2 else (0, 2)
        left = (1,) if ph % 2 == 0 else (0, 2)
        return [(t, l) for t in top for l in left]

    relay(ch_one[0])
    pre_two = None
    for ph in range(4):
        if ph < 3:
            relay(ch_one[ph + 1])
        landed(ch_one[ph])
        if ph >= 2:

            def move(at, carry, ph=ph):
                for s in range(4):
                    v = g.F1[s, ph, pl.ds(QS + at, QS), :].astype(F32)
                    g.D1[ph - 2, s, pl.ds(QS + at, QS), :] = shifted(v, -1).astype(BF)
                return carry

            over(R, QS, move, 0)
        for t, l in taps_two(ph):
            term = mm(whole_one(ph, t == 0, l == 0), kernel_rows(g.W2, 3 * t + l))
            pre_two = term if pre_two is None else pre_two + term
    g.PRE2[...] = pre_two
    rm_w4 = [
        net.push(rows_of(g.w4, rank, CO), g.W4C.at[pl.ds(s * CO, CO), pl.ds(0, MI)], far)
        for s, rank in enumerate((r2, r3))
    ]
    st_two = narrow_send(1, *narrow_local(g.PRE2, 1))
    mean_two, spread_two = narrow_merge(1, st_two, 1)
    inv_two, scale_two = scale_of(spread_two, g.gm[1:2, :])
    narrow_feature(g.PRE2, mean_two, scale_two, g.bm[1:2, :], g.F2.at[0], 0, 0)
    ch_two = gather(lambda s: g.F2.at[s], 0, R)
    for copy in ld_w3:
        copy.wait()
    mean_side, spread_side = wide_merge(0, st_side)
    inv_side, scale_side = scale_of(spread_side, g.go[1:2, :])
    relay(ch_two)
    landed(ch_two)

    def four(ref):
        return lanes([ref[s] for s in range(4)])

    g.PRE3[...] = mm(four(g.F2), g.W3[...].reshape(4 * MI, CO))
    st_three = wide_send(1, *wide_local(g.PRE3))
    mean_three, spread_three = wide_merge(1, st_three)
    inv_three, scale_three = scale_of(spread_three, g.go[0:1, :])
    bias_three, bias_side = g.bo[0:1, :], g.bo[1:2, :]

    def mid_value(rows):
        return (
            (g.PRE3[rows, :] - mean_three) * scale_three
            + bias_three
            + (g.PRES[rows, :] - mean_side) * scale_side
            + bias_side
        )

    def mid_body(at, carry):
        rows = pl.ds(at, WCH)
        v = mid_value(rows)
        out = v * gate(v) * bc(mask_rows(at, WCH), CO)
        g.BM[rows, :] = out
        g.MIDC[0, rows, :] = out.astype(BF)
        return carry

    over(R, WCH, mid_body, 0)
    rm_mid = net.push(g.MIDC.at[0], g.MIDC.at[1], core)

    for copy in ld_w4:
        copy.wait()
    for copy in rm_w4:
        copy.wait_recv()
    rm_back.append(net.push(g.W4C.at[pl.ds(CO, CO), pl.ds(0, MI)], g.W4P.at[1], core))
    rm_mid.wait_recv()
    part = mm(lanes([g.MIDC[0], g.MIDC[1]]), g.W4C[...])
    g.P4S[...] = part[:, :MI].astype(BF)
    rm_p4 = net.push(g.P4S, g.P4R, far)
    g.PRE4[...] = part[:, MI:]

    def take_p4(ph):
        rm_p4.wait_recv()

        def add(at, carry):
            rows = pl.ds(at, NCH)
            g.PRE4[rows, :] = g.PRE4[rows, :] + g.P4R[rows, :].astype(F32)
            return carry

        over(R, NCH, add, 0)

    st_four = narrow_send(2, *narrow_local(g.PRE4, 1, take_p4))
    mean_four, spread_four = narrow_merge(2, st_four, 1)
    inv_four, scale_four = scale_of(spread_four, g.gm[2:3, :])
    narrow_feature(g.PRE4, mean_four, scale_four, g.bm[2:3, :], g.F4.at[0], 0, QS)
    ch_four = gather(lambda s: g.F4.at[s], QS, R)
    for copy in ld_w5:
        copy.wait()

    def spread_rows(src, dst_up, dst_down):
        def body(at, carry):
            rows = pl.ds(QS + at, QS)
            v = src[rows, :].astype(F32)
            dst_up[rows, :] = shifted(v, -1).astype(BF)
            dst_down[rows, :] = shifted(v, 1).astype(BF)
            return carry

        over(R, QS, body, 0)

    def fill_four(s):
        spread_rows(g.F4.at[s], g.D4.at[0, s], g.D4.at[1, s])

    fill_four(0)
    relay(ch_four)
    ch_four[0].wait_recv()
    fill_four(1)
    fill_four(2)
    ch_four[3].wait_recv()
    fill_four(3)

    def whole_four(t, l):
        rows = slice(l * QS, l * QS + R)
        if t == 1:
            return lanes([g.F4[s, rows, :] for s in range(4)])
        return lanes([g.D4[t // 2, s, rows, :] for s in range(4)])

    pre_five = None
    for t in range(3):
        for l in range(3):
            term = mm(whole_four(t, l), kernel_rows(g.W5, 3 * t + l))
            pre_five = term if pre_five is None else pre_five + term
    g.PRE5[...] = pre_five
    st_five = narrow_send(3, *narrow_local(g.PRE5, 1))
    mean_five, spread_five = narrow_merge(3, st_five, 1)
    inv_five, scale_five = scale_of(spread_five, g.gm[3:4, :])
    narrow_feature(g.PRE5, mean_five, scale_five, g.bm[3:4, :], g.F5.at[0], 0, 0)
    ch_five = gather(lambda s: g.F5.at[s], 0, R)
    for copy in ld_w6:
        copy.wait()
    ld_cot.wait()
    relay(ch_five)
    landed(ch_five)
    g.PRE6[...] = mm(four(g.F5), g.W6[...].reshape(4 * MI, CO))
    st_six = wide_send(2, *wide_local(g.PRE6))
    mean_six, spread_six = wide_merge(2, st_six)
    inv_six, scale_six = scale_of(spread_six, g.go[2:3, :])
    bias_six = g.bo[2:3, :]

    def last_body(at, carry):
        acc_b, acc_g = carry
        rows = pl.ds(at, WCH)
        m = bc(mask_rows(at, WCH), CO)
        hat = (g.PRE6[rows, :] - mean_six) * inv_six
        v = (g.PRE6[rows, :] - mean_six) * scale_six + bias_six + g.BM[rows, :]
        s = gate(v)
        g.OUT[rows, :] = v * s * m
        grad = g.COT[rows, :].astype(F32) * m * (s * (1.0 + v * (1.0 - s)))
        g.GSB[rows, :] = grad
        return acc_b + fold(grad), acc_g + fold(grad * hat)

    zero_w = jnp.zeros((8, CO), F32)
    acc_b, acc_g = over(R, WCH, last_body, (zero_w, zero_w))

    def down(value):
        return jnp.sum(value, axis=0, keepdims=True)

    st = wide_send(3, down(acc_b), down(acc_g))

    out = g.OUT[...]
    high = out.astype(BF)
    low = (out - high.astype(F32)).astype(BF)
    g.OUTP[...] = mm(g.po[...], high) + mm(g.po[...], low)
    out_block = net.local(g.OUTP, g.block_out)

    def wide_sums(ref, copies, count):
        for copy in copies:
            copy.wait_recv()
        return [
            wide_row(tree([ref[k, j * NW : (j + 1) * NW, :] for k in range(NB)]))
            for j in range(count)
        ]

    def narrow_sums(idx, copies):
        for copy in copies:
            copy.wait_recv()
        return [tree([g.SN[idx, k, j : j + 1, :] for k in range(NB)]) for j in range(2)]

    bsum_six, gsum_six = wide_sums(g.SW.at[3], st, 2)
    inv_wide = bc(inv_out, CO)

    def wide_pre_grad(grad, pre, mean, inv, scale, bsum, gsum, out):
        mb, mg = bsum * inv_wide, gsum * inv_wide

        def body(at, carry):
            rows = pl.ds(at, WCH)
            hat = (pre[rows, :] - mean) * inv
            e = bc(mask_rows(at, WCH), CO) * scale * (grad[rows, :] - (mb + hat * mg))
            out[rows, :] = e.astype(BF)
            return carry

        over(R, WCH, body, 0)

    wide_pre_grad(
        g.GSB, g.PRE6, mean_six, inv_six, scale_six, bsum_six, gsum_six, g.E6.at[0]
    )
    for copy in rm_back:
        copy.wait_recv()

    def swap(ref):
        return net.push(ref.at[0], ref.at[1], core)

    def reduce_back(part, sent, got):
        sent[...] = part[:, MI:].astype(BF)
        return net.push(sent, got, far)

    def wide_back(e, own, other):
        near = lanes([own[0], other[0]])
        away = lanes([own[2], other[1]])
        return mm_nt(lanes([e[0], e[1]]), jnp.concatenate([near, away], axis=0))

    def narrow_back(idx, near, got, copy, phases, pre, mean, inv, scale, bias, order=None):
        acc_b = jnp.zeros((8, MI), F32)
        acc_g = jnp.zeros((8, MI), F32)
        for ph in range(phases):
            copy[ph].wait_recv()

            def body(at, carry, ph=ph):
                b_acc, g_acc = carry
                rows = pl.ds(ph * R + at, NCH)
                hat = (pre[rows, :] - mean) * inv
                v = (pre[rows, :] - mean) * scale + bias
                s = gate(v)
                feat = near[rows, :] + got[rows, :].astype(F32)
                grad = feat * mask_rows(at, NCH) * (s * (1.0 + v * (1.0 - s)))
                near[rows, :] = grad
                return b_acc + fold(grad), g_acc + fold(grad * hat)

            acc_b, acc_g = over(R, NCH, body, (acc_b, acc_g))
        return narrow_send(idx, down(acc_b), down(acc_g))

    def narrow_pre_grad(grad, pre, mean, inv, scale, bsum, gsum, phases, ph, out, at0):
        inv_count = inv_out * (1.0 / phases)
        mb, mg = bsum * inv_count, gsum * inv_count

        def body(at, carry):
            rows = pl.ds(ph * R + at, NCH)
            hat = (pre[rows, :] - mean) * inv
            e = mask_rows(at, NCH) * scale * (grad[rows, :] - (mb + hat * mg))
            out[pl.ds(at0 + at, NCH), :] = e.astype(BF)
            return carry

        over(R, NCH, body, 0)

    outs = []

    def give(src, dst):
        outs.append(net.local(src, dst))

    cp = swap(g.E6)
    cp.wait_recv()
    part = wide_back(g.E6, g.W6, g.W6P)
    cp = [reduce_back(part, g.B5S, g.B5R)]
    g.GF5[...] = part[:, :MI]
    def rows_grad(part, value, s):
        half = value.shape[0] // 2
        for h in range(2):
            part[s // 2, s % 2, h] = value[h * half : (h + 1) * half].astype(BF)

    def taps_grad(part, tap, value):
        half = MI // 2
        for p in range(8):
            part[p // 4, p // 2 % 2, p % 2, tap] = value[p * half : (p + 1) * half].astype(BF)

    def job(part, got, done, coords, across=None):
        work = Summed(net, part, got, done, coords, across)
        jobs.append(work)
        return work

    jobs = []

    for s in range(4):
        rows_grad(g.K6, mm_tn(g.F5[s], g.E6[0]), s)
    six = job(g.K6, (g.K6X, g.K6Z, g.K6E), g.A6, x_first)
    six.step()
    st = narrow_back(
        4, g.GF5, g.B5R, cp, 1, g.PRE5, mean_five, inv_five, scale_five, g.bm[3:4, :]
    )
    bsum_five, gsum_five = narrow_sums(4, st)
    narrow_pre_grad(
        g.GF5, g.PRE5, mean_five, inv_five, scale_five, bsum_five, gsum_five, 1, 0,
        g.E5.at[1, 0], QS,
    )
    cp = net.push(g.E5.at[1, 0, pl.ds(QS, R)], g.E5.at[1, 1, pl.ds(QS, R)], core)
    spread_rows(g.E5.at[1, 0], g.E5.at[0, 0], g.E5.at[2, 0])
    cp.wait_recv()
    spread_rows(g.E5.at[1, 1], g.E5.at[0, 1], g.E5.at[2, 1])

    def taps_back(own, other, tap):
        near = lanes([own[tap, 0], other[tap, 0]])
        away = lanes([own[tap, 2], other[tap, 1]])
        return jnp.concatenate([near, away], axis=0)

    part = None
    for t in range(3):
        for l in range(3):
            rows = slice((2 - l) * QS, (2 - l) * QS + R)
            e = lanes([g.E5[2 - t, s, rows, :] for s in range(2)])
            term = mm_nt(e, taps_back(g.W5, g.W5P, 3 * t + l))
            part = term if part is None else part + term
    cp = [reduce_back(part, g.B4S, g.B4R)]
    g.GF4[...] = part[:, :MI]
    six.step()
    own_five = g.E5[1, 0, QS : QS + R, :]

    def five_grad(part, first, last):
        for tap in range(first, last):
            taps_grad(part, tap - first, mm_tn(whole_four(tap // 3, tap % 3), own_five))

    five_grad(g.K5A, 0, 5)
    five_a = job(g.K5A, (g.K5AX, g.K5AZ, g.K5AE), g.A5A, x_first)
    five_a.step()
    five_grad(g.K5B, 5, 9)
    five_b = job(g.K5B, (g.K5BX, g.K5BZ, g.K5BE), g.A5B, z_first)
    five_b.step()
    st = narrow_back(
        5, g.GF4, g.B4R, cp, 1, g.PRE4, mean_four, inv_four, scale_four, g.bm[2:3, :]
    )
    bsum_four, gsum_four = narrow_sums(5, st)
    narrow_pre_grad(
        g.GF4, g.PRE4, mean_four, inv_four, scale_four, bsum_four, gsum_four, 1, 0,
        g.G4.at[0], 0,
    )
    ch = gather(lambda s: g.G4.at[s], 0, R)
    relay(ch)
    six.step()
    landed(ch)
    mid_back = mm_nt(
        four(g.G4),
        lanes([g.W4C[0:CO, MI:], g.W4P[0], g.W4C[0:CO, :MI], g.W4P[1]]),
    )
    g.GMID[...] = mid_back

    def mid_back_body(at, carry):
        a_b, a_3, a_s = carry
        rows = pl.ds(at, WCH)
        v = mid_value(rows)
        s = gate(v)
        grad = (g.GSB[rows, :] + g.GMID[rows, :]) * bc(mask_rows(at, WCH), CO)
        grad = grad * (s * (1.0 + v * (1.0 - s)))
        g.GMID[rows, :] = grad
        hat3 = (g.PRE3[rows, :] - mean_three) * inv_three
        hats = (g.PRES[rows, :] - mean_side) * inv_side
        return a_b + fold(grad), a_3 + fold(grad * hat3), a_s + fold(grad * hats)

    a_b, a_3, a_s = over(R, WCH, mid_back_body, (zero_w, zero_w, zero_w))
    for j, value in enumerate((a_b, a_3, a_s, zero_w)):
        wide_put(g.SA, j * NW, down(value))
    st = exchange(g.SA, 4 * NW)
    e4 = lanes([g.G4[0], g.G4[2]])

    def chip_grad(part, s, value):
        size = value.shape[0] // 4
        for p in range(4):
            for w in range(2):
                block = value[p * size : (p + 1) * size, w * MI : (w + 1) * MI]
                part[s, p // 2, p % 2, w] = block.astype(BF)

    for s in range(2):
        chip_grad(g.K4, s, mm_tn(g.MIDC[s], e4))
    four_w = job(g.K4, (g.K4X, g.K4Z, g.K4E), g.A4, x_first, far)
    five_b.step()
    four_w.step()
    bsum_a, gsum_three, gsum_side = wide_sums(g.SA, st, 3)
    wide_pre_grad(
        g.GMID, g.PRE3, mean_three, inv_three, scale_three, bsum_a, gsum_three,
        g.E3.at[0],
    )
    cp = swap(g.E3)
    wide_pre_grad(
        g.GMID, g.PRES, mean_side, inv_side, scale_side, bsum_a, gsum_side, g.ES.at[0]
    )
    cp_side = swap(g.ES)
    cp.wait_recv()
    part = wide_back(g.E3, g.W3, g.W3P)
    cp = [reduce_back(part, g.B2S, g.B2R)]
    g.GF2[...] = part[:, :MI]
    six.step()
    five_a.step()
    for s in range(4):
        rows_grad(g.K3, mm_tn(g.F2[s], g.E3[0]), s)
    three_w = job(g.K3, (g.K3X, g.K3Z, g.K3E), g.A3, x_first)
    three_w.step()
    st = narrow_back(
        6, g.GF2, g.B2R, cp, 1, g.PRE2, mean_two, inv_two, scale_two, g.bm[1:2, :]
    )
    cp_side.wait_recv()
    es = lanes([g.ES[0], g.ES[1]])
    g.IGS[...] = mm_nt(es, lanes([g.WS[0], g.WSP[0]]))
    half = CO // 2
    for s, block in enumerate(strided()):
        grad = mm_tn(block, g.ES[0])
        rows_grad(g.KSA, grad[:, :half], s)
        rows_grad(g.KSB, grad[:, half:], s)
    five_b.step()
    bsum_two, gsum_two = narrow_sums(6, st)
    narrow_pre_grad(
        g.GF2, g.PRE2, mean_two, inv_two, scale_two, bsum_two, gsum_two, 1, 0,
        g.E2.at[0, 0], 0,
    )
    cp = net.push(g.E2.at[0, 0, pl.ds(0, R)], g.E2.at[0, 1, pl.ds(0, R)], core)

    def lift(s):
        def body(at, carry):
            rows = pl.ds(at, QS)
            v = g.E2[0, s, rows, :].astype(F32)
            g.E2[1, s, rows, :] = shifted(v, 1).astype(BF)
            return carry

        over(R, QS, body, 0)

    lift(0)
    cp.wait_recv()
    lift(1)
    cp = []
    for ph in range(4):
        part = None
        for t, l in taps_two(ph):
            rows = slice(QS, QS + R) if l == 0 else slice(0, R)
            e = lanes([g.E2[1 if t == 0 else 0, s, rows, :] for s in range(2)])
            term = mm_nt(e, taps_back(g.W2, g.W2P, 3 * t + l))
            part = term if part is None else part + term
        cp.append(
            reduce_back(part, g.B1S.at[pl.ds(ph * R, R)], g.B1R.at[pl.ds(ph * R, R)])
        )
        g.GF1[ph * R : (ph + 1) * R, :] = part[:, :MI]
    side_a = job(g.KSA, (g.KSAX, g.KSAZ, g.KSAE), g.ASA, x_first)
    side_a.step()
    side_b = job(g.KSB, (g.KSBX, g.KSBZ, g.KSBE), g.ASB, z_first)
    side_b.step()
    six.step()
    five_a.step()
    four_w.step()
    five_b.step()
    own_two = g.E2[0, 0, 0:R, :]

    def two_grad(part, first, last):
        for ph in range(4):
            for t, l in taps_two(ph):
                tap = 3 * t + l
                if first <= tap < last:
                    grad = mm_tn(whole_one(ph, t == 0, l == 0), own_two)
                    taps_grad(part, tap - first, grad)

    two_grad(g.K2A, 0, 5)
    two_grad(g.K2B, 5, 9)
    three_w.step()
    six.step()
    five_a.step()
    four_w.step()
    st = narrow_back(
        7, g.GF1, g.B1R, cp, 4, g.PRE1, mean_one, inv_one, scale_one, g.bm[0:1, :]
    )
    side_far = mm_nt(es, lanes([g.WS[2], g.WSP[1]]))
    g.BSS[...] = side_far.astype(BF)
    cp_bs = net.push(g.BSS, g.BSR, far)
    bsum_one, gsum_one = narrow_sums(7, st)
    ch = []
    for ph in range(4):
        narrow_pre_grad(
            g.GF1, g.PRE1, mean_one, inv_one, scale_one, bsum_one, gsum_one, 4, ph,
            g.G1.at[0, ph], 0,
        )
        ch.append(gather(lambda s, ph=ph: g.G1.at[s, ph], 0, R))
    two_a = job(g.K2A, (g.K2AX, g.K2AZ, g.K2AE), g.A2A, x_first)
    two_a.step()
    two_b = job(g.K2B, (g.K2BX, g.K2BZ, g.K2BE), g.A2B, z_first)
    two_b.step()
    w1_own = lanes([g.W1C[0:CI, MI:], g.W1P[0], g.W1C[0:CI, :MI], g.W1P[1]])
    relay(ch[0])
    for ph in range(4):
        if ph < 3:
            relay(ch[ph + 1])
        landed(ch[ph])
        side_b.step() if ph == 1 else None
        side_a.step() if ph == 2 else None
        five_b.step() if ph == 3 else None
        whole = lanes([g.G1[s, ph] for s in range(4)])
        g.IG[ph * R : (ph + 1) * R, :] = mm_nt(whole, w1_own)
    for s in range(2):
        k1 = None
        for ph in range(4):
            e1 = lanes([g.G1[0, ph], g.G1[2, ph]])
            term = mm_tn(g.SRC[s, ph * R : (ph + 1) * R, :], e1)
            k1 = term if k1 is None else k1 + term
        chip_grad(g.K1, s, k1)
    one_w = job(g.K1, (g.K1X, g.K1Z, g.K1E), g.A1, x_first, far)
    one_w.step()
    three_w.step()
    six.step()
    cp_bs.wait_recv()
    g.IG[0:R, :] = g.IG[0:R, :] + g.IGS[...] + g.BSR[...].astype(F32)
    for a in range(2):
        both = jnp.concatenate(
            [
                g.IG[(2 * a + h) * R : (2 * a + h + 1) * R, :] * bc(g.mask[...], CI)
                for h in range(2)
            ],
            axis=0,
        )
        high = both.astype(BF)
        low = (both - high.astype(F32)).astype(BF)
        g.IGP[a] = (mm(g.pi[...], high) + mm(g.pi[...], low)).reshape(g.IGP.shape[1:])
        give(g.IGP.at[a], g.images_grad.at[:, a])
    while any(work.todo for work in jobs):
        for work in jobs:
            if work.todo:
                work.step()
    for s in range(4):
        for done, out in ((g.A6, g.k6), (g.A3, g.k3)):
            give(done.at[s // 2, s % 2], out.at[ranks[s]])
        for w, done in enumerate((g.ASA, g.ASB)):
            give(done.at[s // 2, s % 2], g.ks.at[ranks[s], :, :, pl.ds(w * half, half)])
        for h in range(2):
            for done, out, first, last in (
                (g.A5A, g.k5, 0, 5),
                (g.A5B, g.k5, 5, 9),
                (g.A2A, g.k2, 0, 5),
                (g.A2B, g.k2, 5, 9),
            ):
                give(done.at[s // 2, s % 2, h], out.at[pl.ds(first, last - first), ranks[s], h])
    for done, out in ((g.A4, g.k4), (g.A1, g.k1)):
        for s in range(2):
            for w in range(2):
                give(done.at[s, :, :, w], out.at[ranks[2 * w + s]])

    g.gain_mid_grad[...] = jnp.concatenate([gsum_one, gsum_two, gsum_four, gsum_five], axis=0)
    g.bias_mid_grad[...] = jnp.concatenate([bsum_one, bsum_two, bsum_four, bsum_five], axis=0)
    g.gain_out_grad[...] = jnp.concatenate([gsum_three, gsum_side, gsum_six], axis=0)
    g.bias_out_grad[...] = jnp.concatenate([bsum_a, bsum_a, bsum_six], axis=0)
    g.mean_mid[...] = jnp.concatenate([mean_one, mean_two, mean_four, mean_five], axis=0)
    g.var_mid[...] = jnp.concatenate(
        [spread_one * unb_in, spread_two * unb_out, spread_four * unb_out, spread_five * unb_out],
        axis=0,
    )
    g.mean_out[...] = jnp.concatenate([mean_three, mean_side, mean_six], axis=0)
    g.var_out[...] = jnp.concatenate([spread_three, spread_side, spread_six], axis=0) * bc(
        unb_out, CO
    )
    out_block.wait()
    for copy in outs:
        copy.wait()
    for copy in net.sent:
        copy.wait_send()


def fused_on_device(
    images, heights, widths, reduce_first, spatial_first, expand_first, shortcut, reduce_second,
    spatial_second, expand_second, gain_mid, bias_mid, gain_out, bias_out, cotangent,
):
    n, rows, cols, CO = cotangent.shape
    CI, MI = images.shape[3], reduce_first.shape[1]
    NB = heights.shape[0] // n
    R, QS = n * rows * cols, n * rows
    batch = lax.axis_index("batch")
    valid = heights * widths
    local_h = lax.dynamic_slice_in_dim(heights, batch * n, n)
    local_w = lax.dynamic_slice_in_dim(widths, batch * n, n)
    q, p, i = np.meshgrid(np.arange(cols), np.arange(rows), np.arange(n), indexing="ij")
    q, p, i = (v.reshape(-1) for v in (q, p, i))
    mask = (
        (jnp.asarray(p)[:, None] < jnp.tile(local_h, rows * cols)[:, None])
        & (jnp.asarray(q)[:, None] < jnp.tile(local_w, rows * cols)[:, None])
    ).astype(F32)
    where_out = (i * rows + p) * cols + q
    pick_out = np.zeros((R, R), np.float32)
    pick_out[np.arange(R), where_out] = 1.0
    pick_in = np.zeros((2 * R, 2 * R), np.float32)
    for h in range(2):
        pick_in[h * R + np.arange(R), (i * rows + p) * 2 * cols + 2 * q + h] = 1.0
    po = jnp.asarray(pick_out.T.astype(ml_dtypes.bfloat16))
    pi = jnp.asarray(pick_in.T.astype(ml_dtypes.bfloat16))
    mask_bf = mask.astype(BF)
    cot = jnp.einsum(
        "mk,kc->mc", po.T * mask_bf, cotangent.reshape(R, CO), preferred_element_type=F32
    ).astype(BF)
    parity = images.reshape(n, rows, 2, 2 * cols, CI).transpose(2, 0, 1, 3, 4).reshape(2, 2 * R, CI)
    src = jnp.einsum(
        "mk,akc->amc", pi.T * jnp.tile(mask_bf, (2, 1)), parity, preferred_element_type=F32
    ).astype(BF).reshape(4 * R, CI)
    order = np.arange(NB)
    by_rank = jnp.sum(valid.reshape(NB, n), axis=1)
    relative = jnp.take(by_rank, jnp.bitwise_xor(order, batch)).astype(F32)
    count_out = jnp.sum(valid).astype(F32)
    count_in = 4.0 * count_out
    aux = jnp.concatenate(
        [
            relative,
            1.0 / relative,
            jnp.stack(
                [1.0 / count_out, count_out / (count_out - 1.0), count_in / (count_in - 1.0)]
            ),
            jnp.zeros((5,), F32),
        ]
    )
    aux = jnp.broadcast_to(aux[:, None], (24, 128))
    ANY, VM = pl.BlockSpec(memory_space=pl.ANY), pl.BlockSpec(memory_space=pltpu.VMEM)
    CM, MC = 4 * MI, 4 * CI
    ins = dict(
        src=(src, ANY),
        cot=(cot, ANY),
        w1=(reduce_first, ANY),
        w2=(spatial_first.reshape(9, CM, MI), ANY),
        w3=(expand_first, ANY),
        wsc=(shortcut, ANY),
        w4=(reduce_second, ANY),
        w5=(spatial_second.reshape(9, CM, MI), ANY),
        w6=(expand_second, ANY),
        mask=(jnp.broadcast_to(mask, (R, 128)), VM),
        aux=(aux, VM),
        gm=(gain_mid, VM),
        bm=(bias_mid, VM),
        go=(gain_out, VM),
        bo=(bias_out, VM),
        po=(po, VM),
        pi=(pi, VM),
    )
    outs = dict(
        block_out=((R, CO), F32, ANY),
        images_grad=((n * rows, 2, 2 * cols, CI), F32, ANY),
        k1=((4, 2, 2, CI // 4, MI), BF, ANY),
        k2=((9, 4, 2, MI // 2, MI), BF, ANY),
        k3=((4, 2, MI // 2, CO), BF, ANY),
        ks=((4, 2, CI // 2, CO), BF, ANY),
        k4=((4, 2, 2, CO // 4, MI), BF, ANY),
        k5=((9, 4, 2, MI // 2, MI), BF, ANY),
        k6=((4, 2, MI // 2, CO), BF, ANY),
        gain_mid_grad=((4, MI), F32, VM),
        bias_mid_grad=((4, MI), F32, VM),
        gain_out_grad=((3, CO), F32, VM),
        bias_out_grad=((3, CO), F32, VM),
        mean_mid=((4, MI), F32, VM),
        var_mid=((4, MI), F32, VM),
        mean_out=((3, CO), F32, VM),
        var_out=((3, CO), F32, VM),
    )
    NW = CO // 128
    scratch = dict(
        SRC=((2, 4 * R, CI), BF),
        XS=((2, R, CI), BF),
        W1C=((2 * CI, 2 * MI), BF),
        W1P=((2, CI, MI), BF),
        W2=((9, 4, MI, MI), BF),
        W2P=((9, 2, MI, MI), BF),
        W3=((4, MI, CO), BF),
        W3P=((2, MI, CO), BF),
        WS=((4, CI, CO), BF),
        WSP=((2, CI, CO), BF),
        W4C=((2 * CO, 2 * MI), BF),
        W4P=((2, CO, MI), BF),
        W5=((9, 4, MI, MI), BF),
        W5P=((9, 2, MI, MI), BF),
        W6=((4, MI, CO), BF),
        W6P=((2, MI, CO), BF),
        COT=((R, CO), BF),
        P1S=((4, R, MI), BF),
        P1R=((4, R, MI), BF),
        P4S=((R, MI), BF),
        P4R=((R, MI), BF),
        PRE1=((4 * R, MI), F32),
        PRE2=((R, MI), F32),
        PRE3=((R, CO), F32),
        PRES=((R, CO), F32),
        PRE4=((R, MI), F32),
        PRE5=((R, MI), F32),
        PRE6=((R, CO), F32),
        F1=((4, 4, QS + R, MI), BF),
        D1=((2, 4, QS + R, MI), BF),
        F2=((4, R, MI), BF),
        BM=((R, CO), F32),
        MIDC=((2, R, CO), BF),
        F4=((4, R + 2 * QS, MI), BF),
        D4=((2, 4, R + 2 * QS, MI), BF),
        F5=((4, R, MI), BF),
        OUT=((R, CO), F32),
        OUTP=((R, CO), F32),
        GSB=((R, CO), F32),
        E6=((2, R, CO), BF),
        B5S=((R, MI), BF),
        B5R=((R, MI), BF),
        GF5=((R, MI), F32),
        E5=((3, 2, R + 2 * QS, MI), BF),
        B4S=((R, MI), BF),
        B4R=((R, MI), BF),
        GF4=((R, MI), F32),
        G4=((4, R, MI), BF),
        GMID=((R, CO), F32),
        E3=((2, R, CO), BF),
        ES=((2, R, CO), BF),
        B2S=((R, MI), BF),
        B2R=((R, MI), BF),
        GF2=((R, MI), F32),
        E2=((2, 2, R + QS, MI), BF),
        B1S=((4 * R, MI), BF),
        B1R=((4 * R, MI), BF),
        GF1=((4 * R, MI), F32),
        G1=((4, 4, R, MI), BF),
        IGS=((R, CI), F32),
        BSS=((R, CI), BF),
        BSR=((R, CI), BF),
        IG=((4 * R, CI), F32),
        IGP=((2, n * rows, 2 * cols, CI), F32),
        SN=((8, NB, 2, MI), F32),
        SW=((4, NB, 2 * NW, 128), F32),
        SA=((NB, 4 * NW, 128), F32),
    )
    for name, piece in dict(
        K1=(2, CI // 4, MI),
        K2A=(5, MI // 2, MI),
        K2B=(4, MI // 2, MI),
        K3=(MI // 2, CO),
        KSA=(CI // 2, CO // 2),
        KSB=(CI // 2, CO // 2),
        K4=(2, CO // 4, MI),
        K5A=(5, MI // 2, MI),
        K5B=(4, MI // 2, MI),
        K6=(MI // 2, CO),
    ).items():
        scratch[name] = ((2, 2, 2, *piece), BF)
        scratch[name + "X"] = ((2, 2, *piece), BF)
        scratch[name + "Z"] = ((2, *piece), BF)
        scratch[name + "E"] = (piece, BF)
        scratch["A" + name[1:]] = ((2, 2, 2, *piece), BF)
    names = [*ins, *outs, *scratch, "sems"]
    geo = types.SimpleNamespace(R=R, QS=QS, PS=n, CI=CI, MI=MI, CO=CO, NB=NB)
    got = pl.pallas_call(
        functools.partial(block_kernel, geo, names),
        out_shape=[jax.ShapeDtypeStruct(s, d) for s, d, _ in outs.values()],
        in_specs=[spec for _, spec in ins.values()],
        out_specs=[spec for _, _, spec in outs.values()],
        scratch_shapes=[pltpu.VMEM(s, d) for s, d in scratch.values()]
        + [pltpu.SemaphoreType.DMA((SEMS,))],
        compiler_params=pltpu.CompilerParams(
            collective_id=0, has_side_effects=True, vmem_limit_bytes=VMEM_LIMIT
        ),
    )(*[value for value, _ in ins.values()])
    o = types.SimpleNamespace(**dict(zip(outs, got)))
    k1, k2, k3, ks, k4, k5, k6 = (
        k.astype(F32) for k in (o.k1, o.k2, o.k3, o.ks, o.k4, o.k5, o.k6)
    )
    return (
        o.block_out.reshape(n, rows, cols, CO),
        o.images_grad.reshape(n, 2 * rows, 2 * cols, CI),
        k1.reshape(MC, MI),
        k2.reshape(3, 3, CM, MI),
        k3.reshape(CM, CO),
        ks.reshape(MC, CO),
        k4.reshape(4 * CO, MI),
        k5.reshape(3, 3, CM, MI),
        k6.reshape(CM, CO),
        o.gain_mid_grad,
        o.bias_mid_grad,
        o.gain_out_grad,
        o.bias_out_grad,
        o.mean_mid,
        o.var_mid,
        o.mean_out,
        o.var_out,
    )


def solution(mesh):
    in_specs = (
        P("batch", None, None, "chan"),
        P(),
        P(),
        P(None, "chan"),
        P(None, None, None, "chan"),
        P(None, "chan"),
        P(None, "chan"),
        P(None, "chan"),
        P(None, None, None, "chan"),
        P(None, "chan"),
        P(None, "chan"),
        P(None, "chan"),
        P(None, "chan"),
        P(None, "chan"),
        P("batch", None, None, "chan"),
    )
    out_specs = (
        P("batch", None, None, "chan"),
        P("batch", None, None, "chan"),
        P(None, "chan"),
        P(None, None, None, "chan"),
        P(None, "chan"),
        P(None, "chan"),
        P(None, "chan"),
        P(None, None, None, "chan"),
        P(None, "chan"),
        P(None, "chan"),
        P(None, "chan"),
        P(None, "chan"),
        P(None, "chan"),
        P(None, "chan"),
        P(None, "chan"),
        P(None, "chan"),
        P(None, "chan"),
    )
    fused = mesh.shape["chan"] == 4 and mesh.shape["batch"] == 8
    return jax.shard_map(
        fused_on_device if fused else on_device, mesh=mesh, in_specs=in_specs, out_specs=out_specs, check_vma=False
    )
```

```python
import functools
import math
import types

import jax
import jax.numpy as jnp
import ml_dtypes
import numpy as np
from jax import lax
from jax.experimental import pallas as pl
from jax.experimental.pallas import tpu as pltpu
from jax.sharding import PartitionSpec as P

EPS = 1e-05
VMEM_LIMIT = 60 * 1024 * 1024


def shortened(shard):
    return jax.tree.map(lambda a: a.astype(jnp.bfloat16) if a.dtype == jnp.float32 else a, shard)


def frame_masks(heights, widths, rows, cols):
    tall = heights[:, None, None]
    broad = widths[:, None, None]
    row_in = jnp.arange(2 * rows, dtype=jnp.int32)[None, :, None]
    col_in = jnp.arange(2 * cols, dtype=jnp.int32)[None, None, :]
    row_out = jnp.arange(rows, dtype=jnp.int32)[None, :, None]
    col_out = jnp.arange(cols, dtype=jnp.int32)[None, None, :]
    inner = ((row_in < 2 * tall) & (col_in < 2 * broad)).astype(jnp.float32)[..., None]
    outer = ((row_out < tall) & (col_out < broad)).astype(jnp.float32)[..., None]
    return (inner, outer)


def silu_slope(value):
    sig = jax.nn.sigmoid(value)
    return sig * (1.0 + value * (1.0 - sig))


def convolve(source, kernel, stride, rows, cols):
    taps = kernel.shape[0]
    margin = taps // 2
    padded = jnp.pad(source, ((0, 0), (margin, margin), (margin, margin), (0, 0)))
    total = None
    for top in range(taps):
        for left in range(taps):
            window = padded[
                :, top : top + stride * rows : stride, left : left + stride * cols : stride, :
            ]
            term = jnp.einsum(
                "nhwc,cd->nhwd", window, kernel[top, left], preferred_element_type=jnp.float32
            )
            total = term if total is None else total + term
    return total


def kernel_grad(source, grad, stride, taps):
    rows, cols = (grad.shape[1], grad.shape[2])
    margin = taps // 2
    padded = jnp.pad(source, ((0, 0), (margin, margin), (margin, margin), (0, 0)))
    return jnp.stack(
        [
            jnp.stack(
                [
                    jnp.einsum(
                        "nhwc,nhwd->cd",
                        padded[
                            :,
                            top : top + stride * rows : stride,
                            left : left + stride * cols : stride,
                            :,
                        ],
                        grad,
                        preferred_element_type=jnp.float32,
                    )
                    for left in range(taps)
                ]
            )
            for top in range(taps)
        ]
    )


def spread_back(grad, kernel, stride):
    taps = kernel.shape[0]
    margin = taps // 2
    total = None
    for top in range(taps):
        for left in range(taps):
            term = jnp.einsum(
                "nhwd,cd->nhwc", grad, kernel[top, left], preferred_element_type=jnp.float32
            )
            placed = lax.pad(
                term,
                jnp.float32(0.0),
                (
                    (0, 0, 0),
                    (top, 2 * margin - top + stride - 1, stride - 1),
                    (left, 2 * margin - left + stride - 1, stride - 1),
                    (0, 0, 0),
                ),
            )
            total = placed if total is None else total + placed
    rows, cols = (grad.shape[1], grad.shape[2])
    return total[:, margin : margin + stride * rows, margin : margin + stride * cols, :]


def norm_forward(pre, mask, count, gain, bias):
    mean = lax.psum(jnp.sum(pre * mask, axis=(0, 1, 2)), "batch") / count
    centered = (pre - mean) * mask
    spread = lax.psum(jnp.sum(centered * centered, axis=(0, 1, 2)), "batch") / count
    inv = lax.rsqrt(spread + EPS)
    hat = (pre - mean) * inv
    return (hat * gain + bias, hat, inv, mean, spread)


def norm_backward(grad, hat, mask, count, gain, inv):
    masked = grad * mask
    bias_grad, gain_grad = lax.psum(
        (jnp.sum(masked, axis=(0, 1, 2)), jnp.sum(masked * hat, axis=(0, 1, 2))), "batch"
    )
    pre_grad = mask * gain * inv * (grad - (bias_grad + hat * gain_grad) / count)
    return (pre_grad.astype(jnp.bfloat16), gain_grad, bias_grad)


def widen(feature):
    return lax.all_gather(feature, "chan", axis=3, tiled=True)


def input_grad(grad, kernel, stride):
    return jax.tree.map(
        lambda part: part.astype(jnp.float32),
        lax.psum_scatter(
            shortened(spread_back(grad, kernel, stride)), "chan", scatter_dimension=3, tiled=True
        ),
    )


def image_back(grad_one, grad_side, kernels):
    summands = spread_back(grad_one, kernels[0], 1) + spread_back(grad_side, kernels[3], 2)
    return lax.psum_scatter(
        summands.astype(jnp.bfloat16), "chan", scatter_dimension=3, tiled=True
    ).astype(jnp.float32)


def on_device(
    images,
    heights,
    widths,
    reduce_first,
    spatial_first,
    expand_first,
    shortcut,
    reduce_second,
    spatial_second,
    expand_second,
    gain_mid,
    bias_mid,
    gain_out,
    bias_out,
    cotangent,
):
    local = images.shape[0]
    rows, cols = (cotangent.shape[1], cotangent.shape[2])
    offset = lax.axis_index("batch") * local
    inner, outer = frame_masks(
        lax.dynamic_slice_in_dim(heights, offset, local),
        lax.dynamic_slice_in_dim(widths, offset, local),
        rows,
        cols,
    )
    count_out = jnp.sum(heights * widths).astype(jnp.float32)
    count_in = 4.0 * count_out
    kernels = (
        reduce_first[None, None],
        spatial_first,
        expand_first[None, None],
        shortcut[None, None],
        reduce_second[None, None],
        spatial_second,
        expand_second[None, None],
    )
    source = images * inner.astype(jnp.bfloat16)
    whole_source = lax.all_gather(source, "chan", axis=3, tiled=True)
    pre_one = convolve(whole_source, kernels[0], 1, 2 * rows, 2 * cols)
    normed_one, hat_one, inv_one, mean_one, spread_one = norm_forward(
        pre_one, inner, count_in, gain_mid[0], bias_mid[0]
    )
    whole_one = widen((jax.nn.silu(normed_one) * inner).astype(jnp.bfloat16))
    pre_two = convolve(whole_one, kernels[1], 2, rows, cols)
    normed_two, hat_two, inv_two, mean_two, spread_two = norm_forward(
        pre_two, outer, count_out, gain_mid[1], bias_mid[1]
    )
    whole_two = widen((jax.nn.silu(normed_two) * outer).astype(jnp.bfloat16))
    pre_three = convolve(whole_two, kernels[2], 1, rows, cols)
    normed_three, hat_three, inv_three, mean_three, spread_three = norm_forward(
        pre_three, outer, count_out, gain_out[0], bias_out[0]
    )
    pre_side = convolve(whole_source, kernels[3], 2, rows, cols)
    normed_side, hat_side, inv_side, mean_side, spread_side = norm_forward(
        pre_side, outer, count_out, gain_out[1], bias_out[1]
    )
    block_mid = jax.nn.silu(normed_three + normed_side) * outer
    whole_mid = widen(block_mid.astype(jnp.bfloat16))
    pre_four = convolve(whole_mid, kernels[4], 1, rows, cols)
    normed_four, hat_four, inv_four, mean_four, spread_four = norm_forward(
        pre_four, outer, count_out, gain_mid[2], bias_mid[2]
    )
    whole_four = widen((jax.nn.silu(normed_four) * outer).astype(jnp.bfloat16))
    pre_five = convolve(whole_four, kernels[5], 1, rows, cols)
    normed_five, hat_five, inv_five, mean_five, spread_five = norm_forward(
        pre_five, outer, count_out, gain_mid[3], bias_mid[3]
    )
    whole_five = widen((jax.nn.silu(normed_five) * outer).astype(jnp.bfloat16))
    pre_six = convolve(whole_five, kernels[6], 1, rows, cols)
    normed_six, hat_six, inv_six, mean_six, spread_six = norm_forward(
        pre_six, outer, count_out, gain_out[2], bias_out[2]
    )
    result = jax.nn.silu(normed_six + block_mid) * outer
    grad_sum_b = cotangent.astype(jnp.float32) * outer * silu_slope(normed_six + block_mid)
    grad_six, gain_six, bias_six = norm_backward(
        grad_sum_b, hat_six, outer, count_out, gain_out[2], inv_six
    )
    kern_six = kernel_grad(whole_five, grad_six, 1, 1)
    grad_feat_five = input_grad(grad_six, kernels[6], 1)
    grad_five, gain_five, bias_five = norm_backward(
        grad_feat_five * outer * silu_slope(normed_five),
        hat_five,
        outer,
        count_out,
        gain_mid[3],
        inv_five,
    )
    kern_five = kernel_grad(whole_four, grad_five, 1, 3)
    grad_feat_four = input_grad(grad_five, kernels[5], 1)
    grad_four, gain_four, bias_four = norm_backward(
        grad_feat_four * outer * silu_slope(normed_four),
        hat_four,
        outer,
        count_out,
        gain_mid[2],
        inv_four,
    )
    kern_four = kernel_grad(whole_mid, grad_four, 1, 1)
    grad_mid = grad_sum_b + input_grad(grad_four, kernels[4], 1)
    grad_sum_a = grad_mid * outer * silu_slope(normed_three + normed_side)
    grad_three, gain_three, bias_three = norm_backward(
        grad_sum_a, hat_three, outer, count_out, gain_out[0], inv_three
    )
    grad_side, gain_side, bias_side = norm_backward(
        grad_sum_a, hat_side, outer, count_out, gain_out[1], inv_side
    )
    kern_three = kernel_grad(whole_two, grad_three, 1, 1)
    kern_side = kernel_grad(whole_source, grad_side, 2, 1)
    grad_feat_two = input_grad(grad_three, kernels[2], 1)
    grad_two, gain_two, bias_two = norm_backward(
        grad_feat_two * outer * silu_slope(normed_two),
        hat_two,
        outer,
        count_out,
        gain_mid[1],
        inv_two,
    )
    kern_two = kernel_grad(whole_one, grad_two, 2, 3)
    grad_feat_one = input_grad(grad_two, kernels[1], 2)
    grad_one, gain_one, bias_one = norm_backward(
        grad_feat_one * inner * silu_slope(normed_one),
        hat_one,
        inner,
        count_in,
        gain_mid[0],
        inv_one,
    )
    kern_one = kernel_grad(whole_source, grad_one, 1, 1)
    images_grad = image_back(grad_one, grad_side, kernels) * inner
    summed = (
        lax.psum(kern_one.astype(jnp.bfloat16), "batch").astype(jnp.float32),
        lax.psum(kern_two.astype(jnp.bfloat16), "batch").astype(jnp.float32),
        lax.psum(kern_three.astype(jnp.bfloat16), "batch").astype(jnp.float32),
        lax.psum(kern_side.astype(jnp.bfloat16), "batch").astype(jnp.float32),
        lax.psum(kern_four.astype(jnp.bfloat16), "batch").astype(jnp.float32),
        lax.psum(kern_five.astype(jnp.bfloat16), "batch").astype(jnp.float32),
        lax.psum(kern_six.astype(jnp.bfloat16), "batch").astype(jnp.float32),
    )
    counts_mid = jnp.stack([count_in, count_out, count_out, count_out])[:, None]
    mean_mid_batch = jnp.stack([mean_one, mean_two, mean_four, mean_five])
    var_mid_batch = (
        jnp.stack([spread_one, spread_two, spread_four, spread_five])
        * counts_mid
        / (counts_mid - 1.0)
    )
    mean_out_batch = jnp.stack([mean_three, mean_side, mean_six])
    var_out_batch = (
        jnp.stack([spread_three, spread_side, spread_six]) * count_out / (count_out - 1.0)
    )
    return (
        result,
        images_grad,
        summed[0][0, 0],
        summed[1],
        summed[2][0, 0],
        summed[3][0, 0],
        summed[4][0, 0],
        summed[5],
        summed[6][0, 0],
        jnp.stack([gain_one, gain_two, gain_four, gain_five]),
        jnp.stack([bias_one, bias_two, bias_four, bias_five]),
        jnp.stack([gain_three, gain_side, gain_six]),
        jnp.stack([bias_three, bias_side, bias_six]),
        mean_mid_batch,
        var_mid_batch,
        mean_out_batch,
        var_out_batch,
    )


MESH = pl.DeviceIdType.MESH
BF = jnp.bfloat16
F32 = jnp.float32


def flip(value, bit):
    return value + bit - 2 * bit * lax.rem(lax.div(value, bit), 2)


def gate(value):
    return 0.5 * jnp.tanh(0.5 * value) + 0.5


def tree(parts):
    while len(parts) > 1:
        parts = [parts[k] + parts[k + 1] for k in range(0, len(parts), 2)]
    return parts[0]


def wide_row(block):
    return jnp.concatenate([block[j : j + 1] for j in range(block.shape[0])], axis=1)


def fold(value):
    return jnp.sum(value.reshape(value.shape[0] // 8, 8, value.shape[1]), axis=0)


def mm(a, b):
    return jnp.dot(a, b, preferred_element_type=F32)


def mm_nt(a, b):
    return lax.dot_general(a, b, (((1,), (1,)), ((), ())), preferred_element_type=F32)


def mm_tn(a, b):
    return lax.dot_general(a, b, (((0,), (0,)), ((), ())), preferred_element_type=F32)


class Traffic:
    def __init__(self, sems):
        self.sems, self.used, self.sent = sems, 0, []

    def take(self):
        self.used += 1
        return self.sems.at[self.used - 1]

    def plan(self, src, dst, device, recv_sem=None):
        return pltpu.make_async_remote_copy(
            src_ref=src,
            dst_ref=dst,
            send_sem=self.take(),
            recv_sem=self.take() if recv_sem is None else recv_sem,
            device_id=device,
            device_id_type=MESH,
        )

    def push(self, src, dst, device):
        copy = self.plan(src, dst, device)
        copy.start()
        self.sent.append(copy)
        return copy

    def plan_local(self, src, dst):
        return pltpu.make_async_copy(src, dst, self.take())

    def local(self, src, dst):
        copy = self.plan_local(src, dst)
        copy.start()
        return copy


class Summed:
    def __init__(self, net, part, got, done, ring, spill, across=None):
        at, ahead = ring
        self.part, self.got, self.done, self.at, self.spill = part, got, done, at, spill
        self.out = [net.plan(part.at[at[0]], got.at[0], ahead)]
        self.out += [net.plan(got.at[k - 1], got.at[k], ahead) for k in range(1, 7)]
        self.back = [
            net.plan(done.at[at[(k + 7) % 8]], done.at[at[(k + 7) % 8]], ahead) for k in range(7)
        ]
        self.across = across is not None
        if self.across:
            self.crossing = net.plan(got.at[6, 1], done.at[at[7], 1], across)
        self.todo = [self.begin] + [functools.partial(self.add, k) for k in range(6)]
        self.todo += [self.finish] + ([self.crossed] if self.across else [])
        self.todo += [functools.partial(self.pass_on, k) for k in range(6)] + [self.last]

    def step(self):
        self.todo.pop(0)()

    def begin(self):
        self.out[0].start()

    def add(self, k):
        self.out[k].wait_recv()
        self.got[k] = self.got[k] + self.part[self.at[k + 1]]
        self.out[k + 1].start()

    def finish(self):
        self.out[6].wait_recv()
        total = self.got[6] + self.part[self.at[7]]
        if self.across:
            self.done[self.at[7], 0] = total[0]
            self.got[6, 1] = total[1]
            self.crossing.start()
        else:
            self.done[self.at[7]] = total
            self.back[0].start()

    def crossed(self):
        self.crossing.wait_recv()
        self.back[0].start()

    def pass_on(self, k):
        self.back[k].wait_recv()
        self.back[k + 1].start()

    def last(self):
        self.back[6].wait_recv()
        for copy in self.spill:
            copy.start()

    def drain(self):
        for copy in self.out + self.back + ([self.crossing] if self.across else []):
            copy.wait_send()
        for copy in self.spill:
            copy.wait()


class Direct:
    def __init__(self, net, part, got, done, place, peers, spill, across):
        self.part, self.got, self.done, self.place, self.spill = part, got, done, place, spill
        n = len(peers)
        self.out = [net.plan(part.at[peers[k][0]], got.at[k], peers[k]) for k in range(n)]
        self.back = [net.plan(done.at[place], done.at[place], peers[k]) for k in range(n)]
        self.crossing = net.plan(got.at[n, 1], done.at[place, 1], across)
        self.todo = [self.begin, self.finish, self.crossed, self.last]

    def step(self):
        self.todo.pop(0)()

    def begin(self):
        for copy in self.out:
            copy.start()

    def finish(self):
        total = self.part[self.place].astype(F32)
        for k, copy in enumerate(self.out):
            copy.wait_recv()
            total = total + self.got[k].astype(F32)
        self.done[self.place, 0] = total[0].astype(BF)
        self.got[len(self.out), 1] = total[1].astype(BF)
        self.crossing.start()

    def crossed(self):
        self.crossing.wait_recv()
        for copy in self.back:
            copy.start()

    def last(self):
        for copy in self.back:
            copy.wait_recv()
        for copy in self.spill:
            copy.start()

    def drain(self):
        for copy in self.out + self.back + [self.crossing]:
            copy.wait_send()
        for copy in self.spill:
            copy.wait()


SEMS = 900


def block_kernel(geo, names, *refs):
    g = types.SimpleNamespace(**dict(zip(names, refs)))
    R, QS, PS = geo.R, geo.QS, geo.PS
    CI, MI, CO = geo.CI, geo.MI, geo.CO
    NB = geo.NB
    r = lax.axis_index("chan")
    b = lax.axis_index("batch")
    r1, r3 = flip(r, 1), flip(r, 2)
    r2 = flip(r1, 2)
    ranks = (r, r1, r2, r3)
    core, far = (b, r1), (b, r2)
    peers = []
    for k in range(1, NB):
        other = b
        bit = 1
        while bit < NB:
            if k & bit:
                other = flip(other, bit)
            bit *= 2
        peers.append((other, r))
    net = Traffic(g.sems)
    def seat(batch):
        x, z = lax.rem(batch, 2), lax.div(batch, 2)
        return z + x * (7 - 2 * z)

    def batch_at(place):
        x = lax.div(place, 4)
        return 2 * (place + x * (7 - 2 * place)) + x

    way = 1 - 2 * lax.rem(lax.rem(r, 2) + lax.div(r, 2), 2)
    pieces = [lax.rem(seat(b) - way * k + 16, 8) for k in range(8)]
    ring = (pieces, (batch_at(pieces[7]), r))

    bar = pltpu.get_barrier_semaphore()
    everyone = [core, far] + peers
    for device in everyone:
        pl.semaphore_signal(bar, 1, device_id=device, device_id_type=MESH)

    def rows_of(ref, rank, size):
        return ref.at[pl.ds(pl.multiple_of(rank * size, size), size)]

    def taps_of(ref, rank, size):
        return ref.at[:, pl.ds(pl.multiple_of(rank * size, size), size), :]

    ld_img = net.local(g.img, g.IMG)
    ld_w1 = [
        net.local(rows_of(g.w1, rank, CI), g.W1C.at[pl.ds(s * CI, CI), pl.ds(MI, MI)])
        for s, rank in enumerate((r, r1))
    ]
    ld_sc = [net.local(rows_of(g.wsc, rank, CI), g.WS.at[s]) for s, rank in enumerate(ranks)]
    ld_w2 = [net.local(taps_of(g.w2, rank, MI), g.W2.at[:, s]) for s, rank in enumerate(ranks)]
    ld_w3 = [net.local(rows_of(g.w3, rank, MI), g.W3.at[s]) for s, rank in enumerate(ranks)]
    ld_w4 = [
        net.local(rows_of(g.w4, rank, CO), g.W4C.at[pl.ds(s * CO, CO), pl.ds(MI, MI)])
        for s, rank in enumerate((r, r1))
    ]
    ld_w5 = [net.local(taps_of(g.w5, rank, MI), g.W5.at[:, s]) for s, rank in enumerate(ranks)]
    ld_w6 = [net.local(rows_of(g.w6, rank, MI), g.W6.at[s]) for s, rank in enumerate(ranks)]
    ld_cot = net.local(g.cot, g.COT)

    area = [g.heights[k] * g.widths[k] for k in range(NB * PS)]
    first = lax.broadcasted_iota(jnp.int32, (R, 128), 0)

    def of_image(ref, image):
        value = jnp.full(image.shape, ref[b * PS], jnp.int32)
        for k in range(1, PS):
            value = jnp.where(image == k, ref[b * PS + k], value)
        return value

    def pixel(m):
        image, row, column = lax.rem(m, PS), lax.rem(lax.div(m, PS), geo.rows), lax.div(m, QS)
        good = (row < of_image(g.heights, image)) & (column < of_image(g.widths, image))
        return column, row, image, good

    g.mask[...] = jnp.where(pixel(first)[3], 1.0, 0.0)

    def row(scalar):
        return jnp.full((1, 128), scalar.astype(F32), F32)

    for k in range(NB):
        other = b if k == 0 else peers[k - 1][0]
        own = 0
        for j in range(PS):
            own = own + g.heights[other * PS + j] * g.widths[other * PS + j]
        g.aux[k : k + 1, :] = row(own)
        g.aux[NB + k : NB + k + 1, :] = 1.0 / row(own)
    count = row(sum(area))
    g.aux[16:17, :] = 1.0 / count
    g.aux[17:18, :] = count / (count - 1.0)
    g.aux[18:19, :] = 4.0 * count / (4.0 * count - 1.0)

    ld_img.wait()
    lane = lax.broadcasted_iota(jnp.int32, (R, 4 * R), 1)
    column, line, image, good = pixel(lax.broadcasted_iota(jnp.int32, (R, 1), 0))
    corner = image * 4 * geo.rows * geo.cols + 2 * line * 2 * geo.cols + 2 * column
    for ph in range(4):
        source = jnp.where(good, corner + (ph // 2) * 2 * geo.cols + ph % 2, -1)
        pick = jnp.where(lane == source, 1.0, 0.0).astype(BF)
        g.SRC[0, ph * R : (ph + 1) * R, :] = mm(pick, g.IMG[...]).astype(BF)

    pl.semaphore_wait(bar, len(everyone))

    rm_src = net.push(g.SRC.at[0], g.SRC.at[1], core)
    rm_w1 = [
        net.push(rows_of(g.w1, rank, CI), g.W1C.at[pl.ds(s * CI, CI), pl.ds(0, MI)], far)
        for s, rank in enumerate((r2, r3))
    ]
    for ph in (1, 3):
        for s in range(4):
            g.F1[s, ph, 0:QS, :] = jnp.zeros((QS, MI), BF)
    for s in range(4):
        g.D1[1, s, 0:QS, :] = jnp.zeros((QS, MI), BF)
        g.F4[s, 0:QS, :] = jnp.zeros((QS, MI), BF)
        g.F4[s, QS + R :, :] = jnp.zeros((QS, MI), BF)
        for d in range(2):
            g.D4[d, s, 0:QS, :] = jnp.zeros((QS, MI), BF)
            g.D4[d, s, QS + R :, :] = jnp.zeros((QS, MI), BF)
    for d in range(3):
        for s in range(2):
            g.E5[d, s, 0:QS, :] = jnp.zeros((QS, MI), BF)
            g.E5[d, s, QS + R :, :] = jnp.zeros((QS, MI), BF)
    for d in range(2):
        for s in range(2):
            g.E2[d, s, R:, :] = jnp.zeros((QS, MI), BF)

    for copy in ld_w1:
        copy.wait()
    rm_src.wait_recv()
    for copy in rm_w1:
        copy.wait_recv()
    rm_p1 = []
    for ph in range(4):
        span = slice(ph * R, (ph + 1) * R)
        both = jnp.concatenate([g.SRC[0, span, :], g.SRC[1, span, :]], axis=1)
        part = mm(both, g.W1C[...])
        g.P1S[ph] = part[:, :MI].astype(BF)
        rm_p1.append(net.push(g.P1S.at[ph], g.P1R.at[ph], far))
        g.PRE1[span, :] = part[:, MI:]

    rm_back = []
    for s, rank in enumerate((r1, r3)):
        rm_back.append(net.push(rows_of(g.w6, rank, MI), g.W6P.at[s], core))
        rm_back.append(net.push(taps_of(g.w5, rank, MI), g.W5P.at[:, s], core))
        rm_back.append(net.push(rows_of(g.w3, rank, MI), g.W3P.at[s], core))
        rm_back.append(net.push(rows_of(g.wsc, rank, CI), g.WSP.at[s], core))
        rm_back.append(net.push(taps_of(g.w2, rank, MI), g.W2P.at[:, s], core))
    rm_back.append(net.push(rows_of(g.w4, r1, CO), g.W4P.at[0], core))
    rm_back.append(net.push(rows_of(g.w1, r1, CI), g.W1P.at[0], core))
    rm_back.append(
        net.push(g.W1C.at[pl.ds(CI, CI), pl.ds(0, MI)], g.W1P.at[1], core)
    )

    aux = g.aux
    inv_out = aux[16:17, :]
    unb_out, unb_in = aux[17:18, :], aux[18:19, :]

    def mask_rows(at, size):
        return g.mask[pl.ds(at, size), :]

    def over(total, size, body, init):
        def step(i, carry):
            return body(pl.multiple_of(i * size, size), carry)

        return lax.fori_loop(0, total // size, step, init)

    NCH = 128 if R % 128 == 0 else QS
    WCH = QS

    def bc(mask, width):
        return jnp.concatenate([mask] * (width // 128), axis=1)

    def exchange(slots, payload_rows):
        return [net.push(slots.at[0], slots.at[k], peers[k - 1]) for k in range(1, NB)]

    def narrow_local(pre, phases, prepare=None):
        total = jnp.zeros((8, MI), F32)
        for ph in range(phases):
            if prepare is not None:
                prepare(ph)

            def add(at, acc, ph=ph):
                return acc + fold(pre[pl.ds(ph * R + at, NCH), :] * mask_rows(at, NCH))

            total = over(R, NCH, add, total)
        total = jnp.sum(total, axis=0, keepdims=True)
        mean = total * (aux[8:9, :] * (1.0 / phases))
        squares = jnp.zeros((8, MI), F32)
        for ph in range(phases):

            def add2(at, acc, ph=ph):
                d = (pre[pl.ds(ph * R + at, NCH), :] - mean) * mask_rows(at, NCH)
                return acc + fold(d * d)

            squares = over(R, NCH, add2, squares)
        return total, jnp.sum(squares, axis=0, keepdims=True)

    def narrow_send(idx, first, second):
        slots = g.SN.at[idx]
        g.SN[idx, 0, 0:1, :] = first
        g.SN[idx, 0, 1:2, :] = second
        return exchange(slots, 2)

    def narrow_merge(idx, copies, phases):
        for copy in copies:
            copy.wait_recv()
        sums = [g.SN[idx, k, 0:1, :] for k in range(NB)]
        squares = [g.SN[idx, k, 1:2, :] for k in range(NB)]
        return moments(sums, squares, phases)

    def moments(sums, squares, phases):
        inv_count = inv_out * (1.0 / phases)
        mean = tree(list(sums)) * inv_count
        terms = []
        for k in range(NB):
            d = sums[k] * (aux[8 + k : 9 + k, :] * (1.0 / phases)) - mean
            terms.append(squares[k] + aux[k : k + 1, :] * float(phases) * d * d)
        spread = tree(terms) * inv_count
        return mean, spread

    def wide_local(pre):
        def add(at, acc):
            m = bc(mask_rows(at, WCH), CO)
            return acc + fold(pre[pl.ds(at, WCH), :] * m)

        total = jnp.sum(over(R, WCH, add, jnp.zeros((8, CO), F32)), axis=0, keepdims=True)
        mean = total * bc(aux[8:9, :], CO)

        def add2(at, acc):
            m = bc(mask_rows(at, WCH), CO)
            d = (pre[pl.ds(at, WCH), :] - mean) * m
            return acc + fold(d * d)

        squares = jnp.sum(over(R, WCH, add2, jnp.zeros((8, CO), F32)), axis=0, keepdims=True)
        return total, squares

    NW = CO // 128

    def wide_put(slots, row, value):
        for j in range(NW):
            slots[0, row + j : row + j + 1, :] = value[:, j * 128 : (j + 1) * 128]

    def wide_send(idx, first, second):
        slots = g.SW.at[idx]
        wide_put(slots, 0, first)
        wide_put(slots, NW, second)
        return exchange(slots, 2 * NW)

    def wide_merge(idx, copies):
        for copy in copies:
            copy.wait_recv()
        sums = [g.SW[idx, k, 0:NW, :] for k in range(NB)]
        squares = [g.SW[idx, k, NW : 2 * NW, :] for k in range(NB)]
        mean, spread = moments(sums, squares, 1)
        return wide_row(mean), wide_row(spread)

    def gather(buf, at, size):
        here = [buf(s).at[pl.ds(at, size)] for s in range(4)]
        near = net.push(here[0], here[1], core)
        away = net.push(here[0], here[2], far)
        return [near, away, here]

    def relay(chunk):
        near, away, here = chunk
        away.wait_recv()
        chunk.append(net.push(here[2], here[3], core))

    def landed(chunk):
        chunk[0].wait_recv()
        chunk[3].wait_recv()

    def lanes(parts):
        return jnp.concatenate(parts, axis=1)

    place = lax.broadcasted_iota(jnp.int32, (QS, 128), 0)
    keep_down = place >= PS
    keep_up = place < QS - PS

    def shifted(value, step):
        if step < 0:
            return jnp.where(keep_down, pltpu.roll(value, PS, 0), 0.0)
        return jnp.where(keep_up, pltpu.roll(value, QS - PS, 0), 0.0)

    def take_p1(ph):
        rm_p1[ph].wait_recv()

        def add(at, carry):
            rows = pl.ds(ph * R + at, NCH)
            g.PRE1[rows, :] = g.PRE1[rows, :] + g.P1R[ph, pl.ds(at, NCH), :].astype(F32)
            return carry

        over(R, NCH, add, 0)

    sum_one, sq_one = narrow_local(g.PRE1, 4, take_p1)
    st_one = narrow_send(0, sum_one, sq_one)
    rm_xs = net.push(g.SRC.at[0, pl.ds(0, R)], g.XS.at[0], far)

    def scale_of(spread, gain):
        inv = lax.rsqrt(spread + EPS)
        return inv, inv * gain

    mean_one, spread_one = narrow_merge(0, st_one, 4)
    inv_one, scale_one = scale_of(spread_one, g.gm[0:1, :])

    def narrow_feature(pre, mean, scale, bias, out, ph, at0):
        def body(at, carry):
            v = (pre[pl.ds(ph * R + at, NCH), :] - mean) * scale + bias
            out[pl.ds(at0 + at, NCH), :] = (v * gate(v) * mask_rows(at, NCH)).astype(BF)
            return carry

        over(R, NCH, body, 0)

    ch_one = []
    for ph in range(4):
        narrow_feature(
            g.PRE1, mean_one, scale_one, g.bm[0:1, :], g.F1.at[0, ph], ph, QS
        )
        ch_one.append(gather(lambda s, ph=ph: g.F1.at[s, ph], QS, R))

    rm_xs.wait_recv()
    rm_xs2 = net.push(g.XS.at[0], g.XS.at[1], core)
    for copy in ld_sc:
        copy.wait()
    rm_xs2.wait_recv()

    def strided():
        return [g.SRC[0, 0:R, :], g.SRC[1, 0:R, :], g.XS[0], g.XS[1]]

    pre_side = None
    for s, block in enumerate(strided()):
        term = mm(block, g.WS[s])
        pre_side = term if pre_side is None else pre_side + term
    g.PRES[...] = pre_side
    st_side = wide_send(0, *wide_local(g.PRES))

    for copy in ld_w2:
        copy.wait()

    def whole_one(ph, down, left):
        rows = slice(0, R) if left else slice(QS, QS + R)
        if down:
            return lanes([g.D1[ph - 2, s, rows, :] for s in range(4)])
        return lanes([g.F1[s, ph, rows, :] for s in range(4)])

    def kernel_rows(ref, tap):
        return jnp.concatenate([ref[tap, s] for s in range(4)], axis=0)

    def taps_two(ph):
        top = (1,) if ph < 2 else (0, 2)
        left = (1,) if ph % 2 == 0 else (0, 2)
        return [(t, l) for t in top for l in left]

    relay(ch_one[0])
    pre_two = None
    for ph in range(4):
        if ph < 3:
            relay(ch_one[ph + 1])
        landed(ch_one[ph])
        if ph >= 2:

            def move(at, carry, ph=ph):
                for s in range(4):
                    v = g.F1[s, ph, pl.ds(QS + at, QS), :].astype(F32)
                    g.D1[ph - 2, s, pl.ds(QS + at, QS), :] = shifted(v, -1).astype(BF)
                return carry

            over(R, QS, move, 0)
        for t, l in taps_two(ph):
            term = mm(whole_one(ph, t == 0, l == 0), kernel_rows(g.W2, 3 * t + l))
            pre_two = term if pre_two is None else pre_two + term
    g.PRE2[...] = pre_two
    rm_w4 = [
        net.push(rows_of(g.w4, rank, CO), g.W4C.at[pl.ds(s * CO, CO), pl.ds(0, MI)], far)
        for s, rank in enumerate((r2, r3))
    ]
    st_two = narrow_send(1, *narrow_local(g.PRE2, 1))
    mean_two, spread_two = narrow_merge(1, st_two, 1)
    inv_two, scale_two = scale_of(spread_two, g.gm[1:2, :])
    narrow_feature(g.PRE2, mean_two, scale_two, g.bm[1:2, :], g.F2.at[0], 0, 0)
    ch_two = gather(lambda s: g.F2.at[s], 0, R)
    for copy in ld_w3:
        copy.wait()
    mean_side, spread_side = wide_merge(0, st_side)
    inv_side, scale_side = scale_of(spread_side, g.go[1:2, :])
    relay(ch_two)
    landed(ch_two)

    def four(ref):
        return lanes([ref[s] for s in range(4)])

    g.PRE3[...] = mm(four(g.F2), g.W3[...].reshape(4 * MI, CO))
    st_three = wide_send(1, *wide_local(g.PRE3))
    mean_three, spread_three = wide_merge(1, st_three)
    inv_three, scale_three = scale_of(spread_three, g.go[0:1, :])
    bias_three, bias_side = g.bo[0:1, :], g.bo[1:2, :]

    def mid_value(rows):
        return (
            (g.PRE3[rows, :] - mean_three) * scale_three
            + bias_three
            + (g.PRES[rows, :] - mean_side) * scale_side
            + bias_side
        )

    def mid_body(at, carry):
        rows = pl.ds(at, WCH)
        v = mid_value(rows)
        out = v * gate(v) * bc(mask_rows(at, WCH), CO)
        g.BM[rows, :] = out
        g.MIDC[0, rows, :] = out.astype(BF)
        return carry

    over(R, WCH, mid_body, 0)
    rm_mid = net.push(g.MIDC.at[0], g.MIDC.at[1], core)

    for copy in ld_w4:
        copy.wait()
    for copy in rm_w4:
        copy.wait_recv()
    rm_back.append(net.push(g.W4C.at[pl.ds(CO, CO), pl.ds(0, MI)], g.W4P.at[1], core))
    rm_mid.wait_recv()
    part = mm(lanes([g.MIDC[0], g.MIDC[1]]), g.W4C[...])
    g.P4S[...] = part[:, :MI].astype(BF)
    rm_p4 = net.push(g.P4S, g.P4R, far)
    g.PRE4[...] = part[:, MI:]

    def take_p4(ph):
        rm_p4.wait_recv()

        def add(at, carry):
            rows = pl.ds(at, NCH)
            g.PRE4[rows, :] = g.PRE4[rows, :] + g.P4R[rows, :].astype(F32)
            return carry

        over(R, NCH, add, 0)

    st_four = narrow_send(2, *narrow_local(g.PRE4, 1, take_p4))
    mean_four, spread_four = narrow_merge(2, st_four, 1)
    inv_four, scale_four = scale_of(spread_four, g.gm[2:3, :])
    narrow_feature(g.PRE4, mean_four, scale_four, g.bm[2:3, :], g.F4.at[0], 0, QS)
    ch_four = gather(lambda s: g.F4.at[s], QS, R)
    for copy in ld_w5:
        copy.wait()

    def spread_rows(src, dst_up, dst_down):
        def body(at, carry):
            rows = pl.ds(QS + at, QS)
            v = src[rows, :].astype(F32)
            dst_up[rows, :] = shifted(v, -1).astype(BF)
            dst_down[rows, :] = shifted(v, 1).astype(BF)
            return carry

        over(R, QS, body, 0)

    def fill_four(s):
        spread_rows(g.F4.at[s], g.D4.at[0, s], g.D4.at[1, s])

    fill_four(0)
    relay(ch_four)
    ch_four[0].wait_recv()
    fill_four(1)
    fill_four(2)
    ch_four[3].wait_recv()
    fill_four(3)

    def whole_four(t, l):
        rows = slice(l * QS, l * QS + R)
        if t == 1:
            return lanes([g.F4[s, rows, :] for s in range(4)])
        return lanes([g.D4[t // 2, s, rows, :] for s in range(4)])

    pre_five = None
    for t in range(3):
        for l in range(3):
            term = mm(whole_four(t, l), kernel_rows(g.W5, 3 * t + l))
            pre_five = term if pre_five is None else pre_five + term
    g.PRE5[...] = pre_five
    st_five = narrow_send(3, *narrow_local(g.PRE5, 1))
    mean_five, spread_five = narrow_merge(3, st_five, 1)
    inv_five, scale_five = scale_of(spread_five, g.gm[3:4, :])
    narrow_feature(g.PRE5, mean_five, scale_five, g.bm[3:4, :], g.F5.at[0], 0, 0)
    ch_five = gather(lambda s: g.F5.at[s], 0, R)
    for copy in ld_w6:
        copy.wait()
    ld_cot.wait()
    g.COTP[...] = mm_tn(g.po[...], g.COT[...])
    relay(ch_five)
    landed(ch_five)
    g.PRE6[...] = mm(four(g.F5), g.W6[...].reshape(4 * MI, CO))
    st_six = wide_send(2, *wide_local(g.PRE6))
    mean_six, spread_six = wide_merge(2, st_six)
    inv_six, scale_six = scale_of(spread_six, g.go[2:3, :])
    bias_six = g.bo[2:3, :]

    def last_body(at, carry):
        acc_b, acc_g = carry
        rows = pl.ds(at, WCH)
        m = bc(mask_rows(at, WCH), CO)
        hat = (g.PRE6[rows, :] - mean_six) * inv_six
        v = (g.PRE6[rows, :] - mean_six) * scale_six + bias_six + g.BM[rows, :]
        s = gate(v)
        g.OUT[rows, :] = v * s * m
        grad = g.COTP[rows, :] * m * (s * (1.0 + v * (1.0 - s)))
        g.GSB[rows, :] = grad
        return acc_b + fold(grad), acc_g + fold(grad * hat)

    zero_w = jnp.zeros((8, CO), F32)
    acc_b, acc_g = over(R, WCH, last_body, (zero_w, zero_w))

    def down(value):
        return jnp.sum(value, axis=0, keepdims=True)

    st = wide_send(3, down(acc_b), down(acc_g))

    out_block = net.local(g.OUT, g.block_out)

    def wide_sums(ref, copies, count):
        for copy in copies:
            copy.wait_recv()
        return [
            wide_row(tree([ref[k, j * NW : (j + 1) * NW, :] for k in range(NB)]))
            for j in range(count)
        ]

    def narrow_sums(idx, copies):
        for copy in copies:
            copy.wait_recv()
        return [tree([g.SN[idx, k, j : j + 1, :] for k in range(NB)]) for j in range(2)]

    bsum_six, gsum_six = wide_sums(g.SW.at[3], st, 2)
    inv_wide = bc(inv_out, CO)

    def wide_pre_grad(grad, pre, mean, inv, scale, bsum, gsum, out):
        mb, mg = bsum * inv_wide, gsum * inv_wide

        def body(at, carry):
            rows = pl.ds(at, WCH)
            hat = (pre[rows, :] - mean) * inv
            e = bc(mask_rows(at, WCH), CO) * scale * (grad[rows, :] - (mb + hat * mg))
            out[rows, :] = e.astype(BF)
            return carry

        over(R, WCH, body, 0)

    wide_pre_grad(
        g.GSB, g.PRE6, mean_six, inv_six, scale_six, bsum_six, gsum_six, g.E6.at[0]
    )
    for copy in rm_back:
        copy.wait_recv()

    def swap(ref):
        return net.push(ref.at[0], ref.at[1], core)

    def reduce_back(part, sent, got):
        sent[...] = part[:, MI:].astype(BF)
        return net.push(sent, got, far)

    def wide_back(e, own, other):
        near = lanes([own[0], other[0]])
        away = lanes([own[2], other[1]])
        return mm_nt(lanes([e[0], e[1]]), jnp.concatenate([near, away], axis=0))

    def narrow_back(idx, near, got, copy, phases, pre, mean, inv, scale, bias, order=None):
        acc_b = jnp.zeros((8, MI), F32)
        acc_g = jnp.zeros((8, MI), F32)
        for ph in range(phases):
            if ph:
                pump(5)
            copy[ph].wait_recv()

            def body(at, carry, ph=ph):
                b_acc, g_acc = carry
                rows = pl.ds(ph * R + at, NCH)
                hat = (pre[rows, :] - mean) * inv
                v = (pre[rows, :] - mean) * scale + bias
                s = gate(v)
                feat = near[rows, :] + got[rows, :].astype(F32)
                grad = feat * mask_rows(at, NCH) * (s * (1.0 + v * (1.0 - s)))
                near[rows, :] = grad
                return b_acc + fold(grad), g_acc + fold(grad * hat)

            acc_b, acc_g = over(R, NCH, body, (acc_b, acc_g))
        return narrow_send(idx, down(acc_b), down(acc_g))

    def narrow_pre_grad(grad, pre, mean, inv, scale, bsum, gsum, phases, ph, out, at0):
        inv_count = inv_out * (1.0 / phases)
        mb, mg = bsum * inv_count, gsum * inv_count

        def body(at, carry):
            rows = pl.ds(ph * R + at, NCH)
            hat = (pre[rows, :] - mean) * inv
            e = mask_rows(at, NCH) * scale * (grad[rows, :] - (mb + hat * mg))
            out[pl.ds(at0 + at, NCH), :] = e.astype(BF)
            return carry

        over(R, NCH, body, 0)

    outs = [out_block]

    def give(src, dst):
        outs.append(net.local(src, dst))

    cp = swap(g.E6)
    cp.wait_recv()
    part = wide_back(g.E6, g.W6, g.W6P)
    cp = [reduce_back(part, g.B5S, g.B5R)]
    g.GF5[...] = part[:, :MI]
    def rows_grad(part, value, s):
        half = value.shape[0] // 2
        for h in range(2):
            part[2 * s + h] = value[h * half : (h + 1) * half].astype(BF)

    def taps_grad(part, tap, value):
        half = MI // 2
        for p in range(8):
            part[p, tap] = value[p * half : (p + 1) * half].astype(BF)

    jobs = []

    def job(part, got, done, targets, across=None):
        spill = [net.plan_local(source, place) for source, place in targets]
        jobs.append(Summed(net, part, got, done, ring, spill, across))

    def pump(most=99):
        left = sorted((work for work in jobs if work.todo), key=lambda work: -len(work.todo))
        for work in left[:most]:
            work.step()

    def slots_to(part, place):
        return [(part.at[pl.ds(2 * s, 2)], place(ranks[s])) for s in range(4)]

    def chips_to(part, out):
        return [
            (part.at[pl.ds(4 * s, 4), v], out.at[ranks[2 * v + s]])
            for s in range(2)
            for v in range(2)
        ]

    for s in range(4):
        rows_grad(g.K6, mm_tn(g.F5[s], g.E6[0]), s)
    job(g.K6, g.K6R, g.K6D, slots_to(g.K6D, lambda rank: g.k6.at[rank]))
    pump()
    st = narrow_back(
        4, g.GF5, g.B5R, cp, 1, g.PRE5, mean_five, inv_five, scale_five, g.bm[3:4, :]
    )
    pump()
    bsum_five, gsum_five = narrow_sums(4, st)
    narrow_pre_grad(
        g.GF5, g.PRE5, mean_five, inv_five, scale_five, bsum_five, gsum_five, 1, 0,
        g.E5.at[1, 0], QS,
    )
    cp = net.push(g.E5.at[1, 0, pl.ds(QS, R)], g.E5.at[1, 1, pl.ds(QS, R)], core)
    spread_rows(g.E5.at[1, 0], g.E5.at[0, 0], g.E5.at[2, 0])
    cp.wait_recv()
    spread_rows(g.E5.at[1, 1], g.E5.at[0, 1], g.E5.at[2, 1])
    pump()

    def taps_back(own, other, tap):
        near = lanes([own[tap, 0], other[tap, 0]])
        away = lanes([own[tap, 2], other[tap, 1]])
        return jnp.concatenate([near, away], axis=0)

    part = None
    for t in range(3):
        for l in range(3):
            rows = slice((2 - l) * QS, (2 - l) * QS + R)
            e = lanes([g.E5[2 - t, s, rows, :] for s in range(2)])
            term = mm_nt(e, taps_back(g.W5, g.W5P, 3 * t + l))
            part = term if part is None else part + term
    cp = [reduce_back(part, g.B4S, g.B4R)]
    g.GF4[...] = part[:, :MI]
    pump()
    own_five = g.E5[1, 0, QS : QS + R, :]

    def five_grad(part, first, last):
        for tap in range(first, last):
            taps_grad(part, tap - first, mm_tn(whole_four(tap // 3, tap % 3), own_five))

    five_grad(g.K5A, 0, 5)
    job(g.K5A, g.K5AR, g.K5AD, slots_to(g.K5AD, lambda rank: g.k5.at[rank, :, pl.ds(0, 5)]))
    five_grad(g.K5B, 5, 9)
    job(g.K5B, g.K5BR, g.K5BD, slots_to(g.K5BD, lambda rank: g.k5.at[rank, :, pl.ds(5, 4)]))
    pump()
    st = narrow_back(
        5, g.GF4, g.B4R, cp, 1, g.PRE4, mean_four, inv_four, scale_four, g.bm[2:3, :]
    )
    pump()
    bsum_four, gsum_four = narrow_sums(5, st)
    narrow_pre_grad(
        g.GF4, g.PRE4, mean_four, inv_four, scale_four, bsum_four, gsum_four, 1, 0,
        g.G4.at[0], 0,
    )
    ch = gather(lambda s: g.G4.at[s], 0, R)
    relay(ch)
    pump()
    landed(ch)
    mid_back = mm_nt(
        four(g.G4),
        lanes([g.W4C[0:CO, MI:], g.W4P[0], g.W4C[0:CO, :MI], g.W4P[1]]),
    )
    g.GMID[...] = mid_back

    def mid_back_body(at, carry):
        a_b, a_3, a_s = carry
        rows = pl.ds(at, WCH)
        v = mid_value(rows)
        s = gate(v)
        grad = (g.GSB[rows, :] + g.GMID[rows, :]) * bc(mask_rows(at, WCH), CO)
        grad = grad * (s * (1.0 + v * (1.0 - s)))
        g.GMID[rows, :] = grad
        hat3 = (g.PRE3[rows, :] - mean_three) * inv_three
        hats = (g.PRES[rows, :] - mean_side) * inv_side
        return a_b + fold(grad), a_3 + fold(grad * hat3), a_s + fold(grad * hats)

    a_b, a_3, a_s = over(R, WCH, mid_back_body, (zero_w, zero_w, zero_w))
    for j, value in enumerate((a_b, a_3, a_s, zero_w)):
        wide_put(g.SA, j * NW, down(value))
    st = exchange(g.SA, 4 * NW)
    e4 = lanes([g.G4[0], g.G4[2]])

    def chip_grad(part, s, value):
        size = value.shape[0] // 4
        for p in range(4):
            for w in range(2):
                block = value[p * size : (p + 1) * size, w * MI : (w + 1) * MI]
                part[4 * s + p, w] = block.astype(BF)

    for s in range(2):
        chip_grad(g.K4, s, mm_tn(g.MIDC[s], e4))
    job(g.K4, g.K4R, g.K4D, chips_to(g.K4D, g.k4), far)
    pump()
    bsum_a, gsum_three, gsum_side = wide_sums(g.SA, st, 3)
    wide_pre_grad(
        g.GMID, g.PRE3, mean_three, inv_three, scale_three, bsum_a, gsum_three,
        g.E3.at[0],
    )
    cp = swap(g.E3)
    wide_pre_grad(
        g.GMID, g.PRES, mean_side, inv_side, scale_side, bsum_a, gsum_side, g.ES.at[0]
    )
    cp_side = swap(g.ES)
    pump()
    cp.wait_recv()
    part = wide_back(g.E3, g.W3, g.W3P)
    cp = [reduce_back(part, g.B2S, g.B2R)]
    g.GF2[...] = part[:, :MI]
    for s in range(4):
        rows_grad(g.K3, mm_tn(g.F2[s], g.E3[0]), s)
    job(g.K3, g.K3R, g.K3D, slots_to(g.K3D, lambda rank: g.k3.at[rank]))
    pump()
    st = narrow_back(
        6, g.GF2, g.B2R, cp, 1, g.PRE2, mean_two, inv_two, scale_two, g.bm[1:2, :]
    )
    pump()
    cp_side.wait_recv()
    es = lanes([g.ES[0], g.ES[1]])
    g.IGS[...] = mm_nt(es, lanes([g.WS[0], g.WSP[0]]))
    half = CO // 2
    for s, block in enumerate(strided()):
        grad = mm_tn(block, g.ES[0])
        rows_grad(g.KSA, grad[:, :half], s)
        rows_grad(g.KSB, grad[:, half:], s)
    job(g.KSA, g.KSAR, g.KSAD, slots_to(g.KSAD, lambda rank: g.ks.at[rank, :, :, pl.ds(0, half)]))
    job(g.KSB, g.KSBR, g.KSBD, slots_to(g.KSBD, lambda rank: g.ks.at[rank, :, :, pl.ds(half, half)]))
    pump()
    pump()
    bsum_two, gsum_two = narrow_sums(6, st)
    narrow_pre_grad(
        g.GF2, g.PRE2, mean_two, inv_two, scale_two, bsum_two, gsum_two, 1, 0,
        g.E2.at[0, 0], 0,
    )
    cp = net.push(g.E2.at[0, 0, pl.ds(0, R)], g.E2.at[0, 1, pl.ds(0, R)], core)

    def lift(s):
        def body(at, carry):
            rows = pl.ds(at, QS)
            v = g.E2[0, s, rows, :].astype(F32)
            g.E2[1, s, rows, :] = shifted(v, 1).astype(BF)
            return carry

        over(R, QS, body, 0)

    lift(0)
    cp.wait_recv()
    lift(1)
    cp = []
    for ph in range(4):
        part = None
        for t, l in taps_two(ph):
            rows = slice(QS, QS + R) if l == 0 else slice(0, R)
            e = lanes([g.E2[1 if t == 0 else 0, s, rows, :] for s in range(2)])
            term = mm_nt(e, taps_back(g.W2, g.W2P, 3 * t + l))
            part = term if part is None else part + term
        cp.append(
            reduce_back(part, g.B1S.at[pl.ds(ph * R, R)], g.B1R.at[pl.ds(ph * R, R)])
        )
        g.GF1[ph * R : (ph + 1) * R, :] = part[:, :MI]
    pump()
    own_two = g.E2[0, 0, 0:R, :]

    def two_grad(part, first, last):
        for ph in range(4):
            for t, l in taps_two(ph):
                tap = 3 * t + l
                if first <= tap < last:
                    grad = mm_tn(whole_one(ph, t == 0, l == 0), own_two)
                    taps_grad(part, tap - first, grad)

    two_grad(g.K2A, 0, 5)
    pump()
    job(g.K2A, g.K2AR, g.K2AD, slots_to(g.K2AD, lambda rank: g.k2.at[rank, :, pl.ds(0, 5)]))
    two_grad(g.K2B, 5, 9)
    job(g.K2B, g.K2BR, g.K2BD, slots_to(g.K2BD, lambda rank: g.k2.at[rank, :, pl.ds(5, 4)]))
    pump()
    st = narrow_back(
        7, g.GF1, g.B1R, cp, 4, g.PRE1, mean_one, inv_one, scale_one, g.bm[0:1, :]
    )
    side_far = mm_nt(es, lanes([g.WS[2], g.WSP[1]]))
    g.BSS[...] = side_far.astype(BF)
    cp_bs = net.push(g.BSS, g.BSR, far)
    pump(5)
    bsum_one, gsum_one = narrow_sums(7, st)
    ch = []
    for ph in range(4):
        narrow_pre_grad(
            g.GF1, g.PRE1, mean_one, inv_one, scale_one, bsum_one, gsum_one, 4, ph,
            g.G1.at[0, ph], 0,
        )
        ch.append(gather(lambda s, ph=ph: g.G1.at[s, ph], 0, R))
    pump()
    w1_own = lanes([g.W1C[0:CI, MI:], g.W1P[0], g.W1C[0:CI, :MI], g.W1P[1]])
    relay(ch[0])
    for ph in range(4):
        if ph < 3:
            relay(ch[ph + 1])
        landed(ch[ph])
        pump()
        whole = lanes([g.G1[s, ph] for s in range(4)])
        g.IG[ph * R : (ph + 1) * R, :] = mm_nt(whole, w1_own)
    for s in range(2):
        k1 = None
        for ph in range(4):
            e1 = lanes([g.G1[0, ph], g.G1[2, ph]])
            term = mm_tn(g.SRC[s, ph * R : (ph + 1) * R, :], e1)
            k1 = term if k1 is None else k1 + term
        chip_grad(g.K1, s, k1)
    spill = [net.plan_local(source, place) for source, place in chips_to(g.K1D, g.k1)]
    jobs.append(Direct(net, g.K1, g.K1R, g.K1D, b, peers, spill, far))
    jobs[-1].step()
    pump(5)
    cp_bs.wait_recv()
    g.IG[0:R, :] = g.IG[0:R, :] + g.IGS[...] + g.BSR[...].astype(F32)
    for ph in range(4):
        rows = slice(ph * R, (ph + 1) * R)
        g.IG[rows, :] = g.IG[rows, :] * bc(g.mask[...], CI)
    give(g.IG, g.images_grad)
    while any(work.todo for work in jobs):
        if jobs[-1].todo:
            jobs[-1].step()
        pump(5)

    g.gain_mid_grad[...] = jnp.concatenate([gsum_one, gsum_two, gsum_four, gsum_five], axis=0)
    g.bias_mid_grad[...] = jnp.concatenate([bsum_one, bsum_two, bsum_four, bsum_five], axis=0)
    g.gain_out_grad[...] = jnp.concatenate([gsum_three, gsum_side, gsum_six], axis=0)
    g.bias_out_grad[...] = jnp.concatenate([bsum_a, bsum_a, bsum_six], axis=0)
    g.mean_mid[...] = jnp.concatenate([mean_one, mean_two, mean_four, mean_five], axis=0)
    g.var_mid[...] = jnp.concatenate(
        [spread_one * unb_in, spread_two * unb_out, spread_four * unb_out, spread_five * unb_out],
        axis=0,
    )
    g.mean_out[...] = jnp.concatenate([mean_three, mean_side, mean_six], axis=0)
    g.var_out[...] = jnp.concatenate([spread_three, spread_side, spread_six], axis=0) * bc(
        unb_out, CO
    )
    for copy in outs:
        copy.wait()
    for copy in net.sent:
        copy.wait_send()

    for work in jobs:
        work.drain()


def fused_on_device(
    images, heights, widths, reduce_first, spatial_first, expand_first, shortcut, reduce_second,
    spatial_second, expand_second, gain_mid, bias_mid, gain_out, bias_out, cotangent,
):
    n, rows, cols, CO = cotangent.shape
    CI, MI = images.shape[3], reduce_first.shape[1]
    NB = heights.shape[0] // n
    R, QS = n * rows * cols, n * rows
    q, p, i = np.meshgrid(np.arange(cols), np.arange(rows), np.arange(n), indexing="ij")
    q, p, i = (v.reshape(-1) for v in (q, p, i))
    pick_out = np.zeros((R, R), np.float32)
    pick_out[np.arange(R), (i * cols + q) * rows + p] = 1.0
    pick_in = np.zeros((2 * R, 2 * R), np.float32)
    for h in range(2):
        pick_in[h * R + np.arange(R), (i * rows + p) * 2 * cols + 2 * q + h] = 1.0
    po = jnp.asarray(pick_out.T.astype(ml_dtypes.bfloat16))
    pi = jnp.asarray(pick_in.T.astype(ml_dtypes.bfloat16))
    cot = cotangent.transpose(0, 2, 1, 3).reshape(R, CO)
    ANY, VM = pl.BlockSpec(memory_space=pl.ANY), pl.BlockSpec(memory_space=pltpu.VMEM)
    SM = pl.BlockSpec(memory_space=pltpu.SMEM)
    CM, MC = 4 * MI, 4 * CI
    ins = dict(
        img=(images.reshape(4 * R, CI), ANY),
        cot=(cot, ANY),
        w1=(reduce_first, ANY),
        w2=(spatial_first.reshape(9, CM, MI), ANY),
        w3=(expand_first, ANY),
        wsc=(shortcut, ANY),
        w4=(reduce_second, ANY),
        w5=(spatial_second.reshape(9, CM, MI), ANY),
        w6=(expand_second, ANY),
        heights=(heights, SM),
        widths=(widths, SM),
        po=(po, VM),
        gm=(gain_mid, VM),
        bm=(bias_mid, VM),
        go=(gain_out, VM),
        bo=(bias_out, VM),
    )
    outs = dict(
        block_out=((R, CO), F32, ANY),
        images_grad=((4 * R, CI), F32, ANY),
        k1=((4, 4, CI // 4, MI), BF, ANY),
        k2=((4, 2, 9, MI // 2, MI), BF, ANY),
        k3=((4, 2, MI // 2, CO), BF, ANY),
        ks=((4, 2, CI // 2, CO), BF, ANY),
        k4=((4, 4, CO // 4, MI), BF, ANY),
        k5=((4, 2, 9, MI // 2, MI), BF, ANY),
        k6=((4, 2, MI // 2, CO), BF, ANY),
        gain_mid_grad=((4, MI), F32, VM),
        bias_mid_grad=((4, MI), F32, VM),
        gain_out_grad=((3, CO), F32, VM),
        bias_out_grad=((3, CO), F32, VM),
        mean_mid=((4, MI), F32, VM),
        var_mid=((4, MI), F32, VM),
        mean_out=((3, CO), F32, VM),
        var_out=((3, CO), F32, VM),
    )
    NW = CO // 128
    scratch = dict(
        IMG=((4 * R, CI), BF),
        mask=((R, 128), F32),
        aux=((24, 128), F32),
        SRC=((2, 4 * R, CI), BF),
        XS=((2, R, CI), BF),
        W1C=((2 * CI, 2 * MI), BF),
        W1P=((2, CI, MI), BF),
        W2=((9, 4, MI, MI), BF),
        W2P=((9, 2, MI, MI), BF),
        W3=((4, MI, CO), BF),
        W3P=((2, MI, CO), BF),
        WS=((4, CI, CO), BF),
        WSP=((2, CI, CO), BF),
        W4C=((2 * CO, 2 * MI), BF),
        W4P=((2, CO, MI), BF),
        W5=((9, 4, MI, MI), BF),
        W5P=((9, 2, MI, MI), BF),
        W6=((4, MI, CO), BF),
        W6P=((2, MI, CO), BF),
        COT=((R, CO), BF),
        COTP=((R, CO), F32),
        P1S=((4, R, MI), BF),
        P1R=((4, R, MI), BF),
        P4S=((R, MI), BF),
        P4R=((R, MI), BF),
        PRE1=((4 * R, MI), F32),
        PRE2=((R, MI), F32),
        PRE3=((R, CO), F32),
        PRES=((R, CO), F32),
        PRE4=((R, MI), F32),
        PRE5=((R, MI), F32),
        PRE6=((R, CO), F32),
        F1=((4, 4, QS + R, MI), BF),
        D1=((2, 4, QS + R, MI), BF),
        F2=((4, R, MI), BF),
        BM=((R, CO), F32),
        MIDC=((2, R, CO), BF),
        F4=((4, R + 2 * QS, MI), BF),
        D4=((2, 4, R + 2 * QS, MI), BF),
        F5=((4, R, MI), BF),
        OUT=((R, CO), F32),
        GSB=((R, CO), F32),
        E6=((2, R, CO), BF),
        B5S=((R, MI), BF),
        B5R=((R, MI), BF),
        GF5=((R, MI), F32),
        E5=((3, 2, R + 2 * QS, MI), BF),
        B4S=((R, MI), BF),
        B4R=((R, MI), BF),
        GF4=((R, MI), F32),
        G4=((4, R, MI), BF),
        GMID=((R, CO), F32),
        E3=((2, R, CO), BF),
        ES=((2, R, CO), BF),
        B2S=((R, MI), BF),
        B2R=((R, MI), BF),
        GF2=((R, MI), F32),
        E2=((2, 2, R + QS, MI), BF),
        B1S=((4 * R, MI), BF),
        B1R=((4 * R, MI), BF),
        GF1=((4 * R, MI), F32),
        G1=((4, 4, R, MI), BF),
        IGS=((R, CI), F32),
        BSS=((R, CI), BF),
        BSR=((R, CI), BF),
        IG=((4 * R, CI), F32),
        SN=((8, NB, 2, MI), F32),
        SW=((4, NB, 2 * NW, 128), F32),
        SA=((NB, 4 * NW, 128), F32),
    )
    for name, piece in dict(
        K1=(2, CI // 4, MI),
        K2A=(5, MI // 2, MI),
        K2B=(4, MI // 2, MI),
        K3=(MI // 2, CO),
        KSA=(CI // 2, CO // 2),
        KSB=(CI // 2, CO // 2),
        K4=(2, CO // 4, MI),
        K5A=(5, MI // 2, MI),
        K5B=(4, MI // 2, MI),
        K6=(MI // 2, CO),
    ).items():
        scratch[name] = ((8, *piece), BF)
        scratch[name + "D"] = ((8, *piece), BF)
        scratch[name + "R"] = ((8 if name == "K1" else 7, *piece), BF)
    names = [*ins, *outs, *scratch, "sems"]
    geo = types.SimpleNamespace(
        R=R, QS=QS, PS=n, CI=CI, MI=MI, CO=CO, NB=NB, rows=rows, cols=cols
    )
    got = pl.pallas_call(
        functools.partial(block_kernel, geo, names),
        out_shape=[jax.ShapeDtypeStruct(s, d) for s, d, _ in outs.values()],
        in_specs=[spec for _, spec in ins.values()],
        out_specs=[spec for _, _, spec in outs.values()],
        scratch_shapes=[pltpu.VMEM(s, d) for s, d in scratch.values()]
        + [pltpu.SemaphoreType.DMA((SEMS,))],
        compiler_params=pltpu.CompilerParams(
            collective_id=0, has_side_effects=True, vmem_limit_bytes=VMEM_LIMIT
        ),
    )(*[value for value, _ in ins.values()])
    o = types.SimpleNamespace(**dict(zip(outs, got)))
    passed = [
        o.gain_mid_grad, o.bias_mid_grad, o.gain_out_grad, o.bias_out_grad,
        o.mean_mid, o.var_mid, o.mean_out, o.var_out,
    ]
    finals = [
        jax.ShapeDtypeStruct(shape, F32)
        for shape in (
            (R, CO), (n, 2 * rows, 2 * cols, CI), (MC, MI), (3, 3, CM, MI), (CM, CO),
            (MC, CO), (4 * CO, MI), (3, 3, CM, MI), (CM, CO),
        )
    ]
    ks = (o.k1, o.k2, o.k3, o.ks, o.k4, o.k5, o.k6)
    res = pl.pallas_call(
        finish_kernel,
        out_shape=finals + [jax.ShapeDtypeStruct(v.shape, F32) for v in passed],
        in_specs=[ANY] * 9 + [VM] * 10,
        out_specs=[ANY] * 9 + [VM] * 8,
        scratch_shapes=[pltpu.VMEM((R, CO), F32), pltpu.VMEM((4 * R, CI), F32)]
        + [pltpu.VMEM(k.shape, BF) for k in ks]
        + [pltpu.VMEM(f.shape, F32) for f in finals]
        + [pltpu.SemaphoreType.DMA((18,))],
        compiler_params=pltpu.CompilerParams(vmem_limit_bytes=VMEM_LIMIT),
    )(o.block_out, o.images_grad, *ks, po, pi, *passed)
    block_out = res[0].reshape(n, cols, rows, CO).transpose(0, 2, 1, 3)
    return (block_out, *res[1:])


def exact(pick, value):
    high = value.astype(BF)
    low = (value - high.astype(F32)).astype(BF)
    return mm(pick, high) + mm(pick, low)


def finish_kernel(*refs):
    ins, po, pi, small = refs[:9], refs[9], refs[10], refs[11:19]
    outs, small_outs = refs[19:28], refs[28:36]
    held, made, sems = refs[36:45], refs[45:54], refs[54]
    loads = [pltpu.make_async_copy(a, v, sems.at[k]) for k, (a, v) in enumerate(zip(ins, held))]
    stores = [
        pltpu.make_async_copy(v, a, sems.at[9 + k]) for k, (v, a) in enumerate(zip(made, outs))
    ]
    for copy in loads:
        copy.start()
    for a, v in zip(small, small_outs):
        v[...] = a[...]

    def rows_of(k):
        src, dst = held[k], made[k]
        size = math.prod(src.shape[1:-1])
        for rank in range(4):
            dst[rank * size : (rank + 1) * size, :] = (
                src[rank].reshape(size, src.shape[-1]).astype(F32)
            )

    def taps_of(k):
        src, dst = held[k], made[k]
        size = src.shape[3]

        def tap(t):
            for rank in range(4):
                for h in range(2):
                    at = (2 * rank + h) * size
                    dst[t // 3, t % 3, at : at + size, :] = src[rank, h, t].astype(F32)

        for t in range(src.shape[2]):
            tap(t)

    def block():
        made[0][...] = exact(po[...], held[0][...])

    def images():
        half = held[1].shape[0] // 2
        for a in range(2):
            value = exact(pi[...], held[1][a * half : (a + 1) * half, :])
            value = value.reshape(-1, *made[1].shape[2:])
            rows = made[1].shape[1] // 2
            for at in range(value.shape[0]):
                made[1][at // rows, 2 * (at % rows) + a] = value[at]

    for k in (3, 7, 5, 2, 4, 6, 8, 0, 1):
        loads[k].wait()
        if k == 0:
            block()
        elif k == 1:
            images()
        elif k in (3, 7):
            taps_of(k)
        else:
            rows_of(k)
        stores[k].start()
    for copy in stores:
        copy.wait()


def solution(mesh):
    in_specs = (
        P("batch", None, None, "chan"),
        P(),
        P(),
        P(None, "chan"),
        P(None, None, None, "chan"),
        P(None, "chan"),
        P(None, "chan"),
        P(None, "chan"),
        P(None, None, None, "chan"),
        P(None, "chan"),
        P(None, "chan"),
        P(None, "chan"),
        P(None, "chan"),
        P(None, "chan"),
        P("batch", None, None, "chan"),
    )
    out_specs = (
        P("batch", None, None, "chan"),
        P("batch", None, None, "chan"),
        P(None, "chan"),
        P(None, None, None, "chan"),
        P(None, "chan"),
        P(None, "chan"),
        P(None, "chan"),
        P(None, None, None, "chan"),
        P(None, "chan"),
        P(None, "chan"),
        P(None, "chan"),
        P(None, "chan"),
        P(None, "chan"),
        P(None, "chan"),
        P(None, "chan"),
        P(None, "chan"),
        P(None, "chan"),
    )
    fused = mesh.shape["chan"] == 4 and mesh.shape["batch"] == 8
    return jax.shard_map(
        fused_on_device if fused else on_device, mesh=mesh, in_specs=in_specs, out_specs=out_specs, check_vma=False
    )
```

```python
import functools
import math
import types

import jax
import jax.numpy as jnp
import ml_dtypes
import numpy as np
from jax import lax
from jax.experimental import pallas as pl
from jax.experimental.pallas import tpu as pltpu
from jax.sharding import PartitionSpec as P

EPS = 1e-05
VMEM_LIMIT = 60 * 1024 * 1024


def shortened(shard):
    return jax.tree.map(lambda a: a.astype(jnp.bfloat16) if a.dtype == jnp.float32 else a, shard)


def frame_masks(heights, widths, rows, cols):
    tall = heights[:, None, None]
    broad = widths[:, None, None]
    row_in = jnp.arange(2 * rows, dtype=jnp.int32)[None, :, None]
    col_in = jnp.arange(2 * cols, dtype=jnp.int32)[None, None, :]
    row_out = jnp.arange(rows, dtype=jnp.int32)[None, :, None]
    col_out = jnp.arange(cols, dtype=jnp.int32)[None, None, :]
    inner = ((row_in < 2 * tall) & (col_in < 2 * broad)).astype(jnp.float32)[..., None]
    outer = ((row_out < tall) & (col_out < broad)).astype(jnp.float32)[..., None]
    return (inner, outer)


def silu_slope(value):
    sig = jax.nn.sigmoid(value)
    return sig * (1.0 + value * (1.0 - sig))


def convolve(source, kernel, stride, rows, cols):
    taps = kernel.shape[0]
    margin = taps // 2
    padded = jnp.pad(source, ((0, 0), (margin, margin), (margin, margin), (0, 0)))
    total = None
    for top in range(taps):
        for left in range(taps):
            window = padded[
                :, top : top + stride * rows : stride, left : left + stride * cols : stride, :
            ]
            term = jnp.einsum(
                "nhwc,cd->nhwd", window, kernel[top, left], preferred_element_type=jnp.float32
            )
            total = term if total is None else total + term
    return total


def kernel_grad(source, grad, stride, taps):
    rows, cols = (grad.shape[1], grad.shape[2])
    margin = taps // 2
    padded = jnp.pad(source, ((0, 0), (margin, margin), (margin, margin), (0, 0)))
    return jnp.stack(
        [
            jnp.stack(
                [
                    jnp.einsum(
                        "nhwc,nhwd->cd",
                        padded[
                            :,
                            top : top + stride * rows : stride,
                            left : left + stride * cols : stride,
                            :,
                        ],
                        grad,
                        preferred_element_type=jnp.float32,
                    )
                    for left in range(taps)
                ]
            )
            for top in range(taps)
        ]
    )


def spread_back(grad, kernel, stride):
    taps = kernel.shape[0]
    margin = taps // 2
    total = None
    for top in range(taps):
        for left in range(taps):
            term = jnp.einsum(
                "nhwd,cd->nhwc", grad, kernel[top, left], preferred_element_type=jnp.float32
            )
            placed = lax.pad(
                term,
                jnp.float32(0.0),
                (
                    (0, 0, 0),
                    (top, 2 * margin - top + stride - 1, stride - 1),
                    (left, 2 * margin - left + stride - 1, stride - 1),
                    (0, 0, 0),
                ),
            )
            total = placed if total is None else total + placed
    rows, cols = (grad.shape[1], grad.shape[2])
    return total[:, margin : margin + stride * rows, margin : margin + stride * cols, :]


def norm_forward(pre, mask, count, gain, bias):
    mean = lax.psum(jnp.sum(pre * mask, axis=(0, 1, 2)), "batch") / count
    centered = (pre - mean) * mask
    spread = lax.psum(jnp.sum(centered * centered, axis=(0, 1, 2)), "batch") / count
    inv = lax.rsqrt(spread + EPS)
    hat = (pre - mean) * inv
    return (hat * gain + bias, hat, inv, mean, spread)


def norm_backward(grad, hat, mask, count, gain, inv):
    masked = grad * mask
    bias_grad, gain_grad = lax.psum(
        (jnp.sum(masked, axis=(0, 1, 2)), jnp.sum(masked * hat, axis=(0, 1, 2))), "batch"
    )
    pre_grad = mask * gain * inv * (grad - (bias_grad + hat * gain_grad) / count)
    return (pre_grad.astype(jnp.bfloat16), gain_grad, bias_grad)


def widen(feature):
    return lax.all_gather(feature, "chan", axis=3, tiled=True)


def input_grad(grad, kernel, stride):
    return jax.tree.map(
        lambda part: part.astype(jnp.float32),
        lax.psum_scatter(
            shortened(spread_back(grad, kernel, stride)), "chan", scatter_dimension=3, tiled=True
        ),
    )


def image_back(grad_one, grad_side, kernels):
    summands = spread_back(grad_one, kernels[0], 1) + spread_back(grad_side, kernels[3], 2)
    return lax.psum_scatter(
        summands.astype(jnp.bfloat16), "chan", scatter_dimension=3, tiled=True
    ).astype(jnp.float32)


def on_device(
    images,
    heights,
    widths,
    reduce_first,
    spatial_first,
    expand_first,
    shortcut,
    reduce_second,
    spatial_second,
    expand_second,
    gain_mid,
    bias_mid,
    gain_out,
    bias_out,
    cotangent,
):
    local = images.shape[0]
    rows, cols = (cotangent.shape[1], cotangent.shape[2])
    offset = lax.axis_index("batch") * local
    inner, outer = frame_masks(
        lax.dynamic_slice_in_dim(heights, offset, local),
        lax.dynamic_slice_in_dim(widths, offset, local),
        rows,
        cols,
    )
    count_out = jnp.sum(heights * widths).astype(jnp.float32)
    count_in = 4.0 * count_out
    kernels = (
        reduce_first[None, None],
        spatial_first,
        expand_first[None, None],
        shortcut[None, None],
        reduce_second[None, None],
        spatial_second,
        expand_second[None, None],
    )
    source = images * inner.astype(jnp.bfloat16)
    whole_source = lax.all_gather(source, "chan", axis=3, tiled=True)
    pre_one = convolve(whole_source, kernels[0], 1, 2 * rows, 2 * cols)
    normed_one, hat_one, inv_one, mean_one, spread_one = norm_forward(
        pre_one, inner, count_in, gain_mid[0], bias_mid[0]
    )
    whole_one = widen((jax.nn.silu(normed_one) * inner).astype(jnp.bfloat16))
    pre_two = convolve(whole_one, kernels[1], 2, rows, cols)
    normed_two, hat_two, inv_two, mean_two, spread_two = norm_forward(
        pre_two, outer, count_out, gain_mid[1], bias_mid[1]
    )
    whole_two = widen((jax.nn.silu(normed_two) * outer).astype(jnp.bfloat16))
    pre_three = convolve(whole_two, kernels[2], 1, rows, cols)
    normed_three, hat_three, inv_three, mean_three, spread_three = norm_forward(
        pre_three, outer, count_out, gain_out[0], bias_out[0]
    )
    pre_side = convolve(whole_source, kernels[3], 2, rows, cols)
    normed_side, hat_side, inv_side, mean_side, spread_side = norm_forward(
        pre_side, outer, count_out, gain_out[1], bias_out[1]
    )
    block_mid = jax.nn.silu(normed_three + normed_side) * outer
    whole_mid = widen(block_mid.astype(jnp.bfloat16))
    pre_four = convolve(whole_mid, kernels[4], 1, rows, cols)
    normed_four, hat_four, inv_four, mean_four, spread_four = norm_forward(
        pre_four, outer, count_out, gain_mid[2], bias_mid[2]
    )
    whole_four = widen((jax.nn.silu(normed_four) * outer).astype(jnp.bfloat16))
    pre_five = convolve(whole_four, kernels[5], 1, rows, cols)
    normed_five, hat_five, inv_five, mean_five, spread_five = norm_forward(
        pre_five, outer, count_out, gain_mid[3], bias_mid[3]
    )
    whole_five = widen((jax.nn.silu(normed_five) * outer).astype(jnp.bfloat16))
    pre_six = convolve(whole_five, kernels[6], 1, rows, cols)
    normed_six, hat_six, inv_six, mean_six, spread_six = norm_forward(
        pre_six, outer, count_out, gain_out[2], bias_out[2]
    )
    result = jax.nn.silu(normed_six + block_mid) * outer
    grad_sum_b = cotangent.astype(jnp.float32) * outer * silu_slope(normed_six + block_mid)
    grad_six, gain_six, bias_six = norm_backward(
        grad_sum_b, hat_six, outer, count_out, gain_out[2], inv_six
    )
    kern_six = kernel_grad(whole_five, grad_six, 1, 1)
    grad_feat_five = input_grad(grad_six, kernels[6], 1)
    grad_five, gain_five, bias_five = norm_backward(
        grad_feat_five * outer * silu_slope(normed_five),
        hat_five,
        outer,
        count_out,
        gain_mid[3],
        inv_five,
    )
    kern_five = kernel_grad(whole_four, grad_five, 1, 3)
    grad_feat_four = input_grad(grad_five, kernels[5], 1)
    grad_four, gain_four, bias_four = norm_backward(
        grad_feat_four * outer * silu_slope(normed_four),
        hat_four,
        outer,
        count_out,
        gain_mid[2],
        inv_four,
    )
    kern_four = kernel_grad(whole_mid, grad_four, 1, 1)
    grad_mid = grad_sum_b + input_grad(grad_four, kernels[4], 1)
    grad_sum_a = grad_mid * outer * silu_slope(normed_three + normed_side)
    grad_three, gain_three, bias_three = norm_backward(
        grad_sum_a, hat_three, outer, count_out, gain_out[0], inv_three
    )
    grad_side, gain_side, bias_side = norm_backward(
        grad_sum_a, hat_side, outer, count_out, gain_out[1], inv_side
    )
    kern_three = kernel_grad(whole_two, grad_three, 1, 1)
    kern_side = kernel_grad(whole_source, grad_side, 2, 1)
    grad_feat_two = input_grad(grad_three, kernels[2], 1)
    grad_two, gain_two, bias_two = norm_backward(
        grad_feat_two * outer * silu_slope(normed_two),
        hat_two,
        outer,
        count_out,
        gain_mid[1],
        inv_two,
    )
    kern_two = kernel_grad(whole_one, grad_two, 2, 3)
    grad_feat_one = input_grad(grad_two, kernels[1], 2)
    grad_one, gain_one, bias_one = norm_backward(
        grad_feat_one * inner * silu_slope(normed_one),
        hat_one,
        inner,
        count_in,
        gain_mid[0],
        inv_one,
    )
    kern_one = kernel_grad(whole_source, grad_one, 1, 1)
    images_grad = image_back(grad_one, grad_side, kernels) * inner
    summed = (
        lax.psum(kern_one.astype(jnp.bfloat16), "batch").astype(jnp.float32),
        lax.psum(kern_two.astype(jnp.bfloat16), "batch").astype(jnp.float32),
        lax.psum(kern_three.astype(jnp.bfloat16), "batch").astype(jnp.float32),
        lax.psum(kern_side.astype(jnp.bfloat16), "batch").astype(jnp.float32),
        lax.psum(kern_four.astype(jnp.bfloat16), "batch").astype(jnp.float32),
        lax.psum(kern_five.astype(jnp.bfloat16), "batch").astype(jnp.float32),
        lax.psum(kern_six.astype(jnp.bfloat16), "batch").astype(jnp.float32),
    )
    counts_mid = jnp.stack([count_in, count_out, count_out, count_out])[:, None]
    mean_mid_batch = jnp.stack([mean_one, mean_two, mean_four, mean_five])
    var_mid_batch = (
        jnp.stack([spread_one, spread_two, spread_four, spread_five])
        * counts_mid
        / (counts_mid - 1.0)
    )
    mean_out_batch = jnp.stack([mean_three, mean_side, mean_six])
    var_out_batch = (
        jnp.stack([spread_three, spread_side, spread_six]) * count_out / (count_out - 1.0)
    )
    return (
        result,
        images_grad,
        summed[0][0, 0],
        summed[1],
        summed[2][0, 0],
        summed[3][0, 0],
        summed[4][0, 0],
        summed[5],
        summed[6][0, 0],
        jnp.stack([gain_one, gain_two, gain_four, gain_five]),
        jnp.stack([bias_one, bias_two, bias_four, bias_five]),
        jnp.stack([gain_three, gain_side, gain_six]),
        jnp.stack([bias_three, bias_side, bias_six]),
        mean_mid_batch,
        var_mid_batch,
        mean_out_batch,
        var_out_batch,
    )


MESH = pl.DeviceIdType.MESH
BF = jnp.bfloat16
F32 = jnp.float32


def flip(value, bit):
    return value + bit - 2 * bit * lax.rem(lax.div(value, bit), 2)


def gate(value):
    return 0.5 * jnp.tanh(0.5 * value) + 0.5


def tree(parts):
    while len(parts) > 1:
        parts = [parts[k] + parts[k + 1] for k in range(0, len(parts), 2)]
    return parts[0]


def wide_row(block):
    return jnp.concatenate([block[j : j + 1] for j in range(block.shape[0])], axis=1)


def fold(value):
    return jnp.sum(value.reshape(value.shape[0] // 8, 8, value.shape[1]), axis=0)


def mm(a, b):
    return jnp.dot(a, b, preferred_element_type=F32)


def mm_nt(a, b):
    return lax.dot_general(a, b, (((1,), (1,)), ((), ())), preferred_element_type=F32)


def mm_tn(a, b):
    return lax.dot_general(a, b, (((0,), (0,)), ((), ())), preferred_element_type=F32)


class Traffic:
    def __init__(self, sems):
        self.sems, self.used, self.sent = sems, 0, []

    def take(self):
        self.used += 1
        return self.sems.at[self.used - 1]

    def plan(self, src, dst, device, send_sem=None, recv_sem=None):
        return pltpu.make_async_remote_copy(
            src_ref=src,
            dst_ref=dst,
            send_sem=self.take() if send_sem is None else send_sem,
            recv_sem=self.take() if recv_sem is None else recv_sem,
            device_id=device,
            device_id_type=MESH,
        )

    def spread(self, src, dst, peers, all_of):
        sems = self.take(), self.take()
        copies = [self.plan(a, d, p, *sems) for a, d, p in zip(src, dst, peers)]
        return copies, self.plan(all_of, all_of, peers[0], *sems)

    def push(self, src, dst, device):
        copy = self.plan(src, dst, device)
        copy.start()
        self.sent.append(copy)
        return copy

    def plan_local(self, src, dst, sem=None):
        return pltpu.make_async_copy(src, dst, self.take() if sem is None else sem)

    def local(self, src, dst):
        copy = self.plan_local(src, dst)
        copy.start()
        return copy

    def load(self, pairs, all_of):
        sem = self.take()
        for src, dst in pairs:
            pltpu.make_async_copy(src, dst, sem).start()
        return pltpu.make_async_copy(all_of, all_of, sem)


class Summed:
    def __init__(self, net, part, got, done, ring, spill, across=None):
        at, ahead, behind = ring
        self.part, self.got, self.done, self.at = part, got, done, at
        self.spill, self.spill_wait = spill
        legs, legs_back = net.take(), net.take()
        up = [part.at[at(4)]] + [got.at[k] for k in range(4)]
        down = [part.at[at(-3)]] + [got.at[k] for k in range(4, 7)]
        self.out = [
            [net.plan(up[k], up[k + 1], ahead, legs)]
            + ([net.plan(down[k], down[k + 1], behind, legs)] if k < 3 else [])
            for k in range(4)
        ]
        self.back = [
            ([net.plan(done.at[at(-k)], done.at[at(-k)], ahead, legs_back)] if k < 3 else [])
            + [net.plan(done.at[at(k)], done.at[at(k)], behind, legs_back)]
            for k in range(4)
        ]
        self.left = [
            net.plan(got, got, ahead, legs, legs),
            net.plan(done.at[pl.ds(0, 7)], done.at[pl.ds(0, 7)], ahead, legs_back, legs_back),
        ]
        self.across = across is not None
        if self.across:
            self.crossing = net.plan(got.at[3, 1], done.at[at(0), 1], across)
            self.left.append(self.crossing)
        self.todo = [self.begin] + [functools.partial(self.add, k) for k in range(3)]
        self.todo += [self.finish] + ([self.crossed] if self.across else [])
        self.todo += [functools.partial(self.pass_on, k) for k in range(3)] + [self.last]

    def step(self):
        self.todo.pop(0)()

    def start(self, copies):
        for copy in copies:
            copy.start()

    def arrived(self, copies):
        for copy in copies:
            copy.wait_recv()

    def begin(self):
        self.start(self.out[0])

    def add(self, k):
        self.arrived(self.out[k])
        self.got[k] = self.got[k] + self.part[self.at(3 - k)]
        if k < 2:
            self.got[4 + k] = self.got[4 + k] + self.part[self.at(k - 2)]
        self.start(self.out[k + 1])

    def finish(self):
        self.arrived(self.out[3])
        total = self.got[3] + self.got[6] + self.part[self.at(0)]
        if self.across:
            self.done[self.at(0), 0] = total[0]
            self.got[3, 1] = total[1]
            self.crossing.start()
        else:
            self.done[self.at(0)] = total
            self.start(self.back[0])

    def crossed(self):
        self.crossing.wait_recv()
        self.start(self.back[0])

    def pass_on(self, k):
        self.arrived(self.back[k])
        self.start(self.back[k + 1])

    def last(self):
        self.arrived(self.back[3])
        self.start(self.spill)

    def drain(self):
        for copy in self.left:
            copy.wait_send()
        self.spill_wait.wait()


class Direct:
    def __init__(self, net, part, got, done, place, peers, spill, across):
        self.part, self.got, self.done, self.place = part, got, done, place
        self.spill, self.spill_wait = spill
        n = len(peers)
        self.out, self.whole = net.spread(
            [part.at[peer[0]] for peer in peers],
            [got.at[k] for k in range(n)],
            peers,
            got.at[pl.ds(0, n)],
        )
        self.back, self.whole_back = net.spread(
            [done.at[place]] * n, [done.at[place]] * n, peers, done.at[pl.ds(0, n)]
        )
        self.crossing = net.plan(got.at[n, 1], done.at[place, 1], across)
        self.todo = [self.begin, self.finish, self.crossed, self.last]

    def step(self):
        self.todo.pop(0)()

    def begin(self):
        for copy in self.out:
            copy.start()

    def finish(self):
        total = self.part[self.place].astype(F32)
        self.whole.wait_recv()
        for k in range(len(self.out)):
            total = total + self.got[k].astype(F32)
        self.done[self.place, 0] = total[0].astype(BF)
        self.got[len(self.out), 1] = total[1].astype(BF)
        self.crossing.start()

    def crossed(self):
        self.crossing.wait_recv()
        for copy in self.back:
            copy.start()

    def last(self):
        self.whole_back.wait_recv()
        for copy in self.spill:
            copy.start()

    def drain(self):
        for copy in (self.whole, self.whole_back, self.crossing):
            copy.wait_send()
        self.spill_wait.wait()


SEMS = 344


def block_kernel(geo, names, *refs):
    g = types.SimpleNamespace(**dict(zip(names, refs)))
    R, QS, PS = geo.R, geo.QS, geo.PS
    CI, MI, CO = geo.CI, geo.MI, geo.CO
    NB = geo.NB
    r = lax.axis_index("chan")
    b = lax.axis_index("batch")
    r1, r3 = flip(r, 1), flip(r, 2)
    r2 = flip(r1, 2)
    ranks = (r, r1, r2, r3)
    core, far = (b, r1), (b, r2)
    peers = []
    for k in range(1, NB):
        other = b
        bit = 1
        while bit < NB:
            if k & bit:
                other = flip(other, bit)
            bit *= 2
        peers.append((other, r))
    net = Traffic(g.sems)
    def seat(batch):
        x, z = lax.rem(batch, 2), lax.div(batch, 2)
        return z + x * (7 - 2 * z)

    def batch_at(place):
        x = lax.div(place, 4)
        return 2 * (place + x * (7 - 2 * place)) + x

    way = 1 - 2 * lax.rem(lax.rem(r, 2) + lax.div(r, 2), 2)
    places = {k: lax.rem(seat(b) + way * k + 16, 8) for k in range(-3, 5)}
    ring = (places.get, (batch_at(places[1]), r), (batch_at(places[-1]), r))

    bar = pltpu.get_barrier_semaphore()
    everyone = [core, far] + peers
    for device in everyone:
        pl.semaphore_signal(bar, 1, device_id=device, device_id_type=MESH)

    def everywhere(src, dst, all_of):
        copies, whole = net.spread(src, dst, peers, all_of)
        for copy in copies:
            copy.start()
        net.sent.append(whole)
        return whole

    def rows_of(ref, rank, size):
        return ref.at[pl.ds(pl.multiple_of(rank * size, size), size)]

    def taps_of(ref, rank, size):
        return ref.at[:, pl.ds(pl.multiple_of(rank * size, size), size), :]

    ld_img = net.local(g.img, g.IMG)
    ld_w1 = [
        net.local(rows_of(g.w1, rank, CI), g.W1C.at[pl.ds(s * CI, CI), pl.ds(MI, MI)])
        for s, rank in enumerate((r, r1))
    ]

    area = [g.heights[k] * g.widths[k] for k in range(NB * PS)]
    first = lax.broadcasted_iota(jnp.int32, (R, 128), 0)

    def of_image(ref, image):
        value = jnp.full(image.shape, ref[b * PS], jnp.int32)
        for k in range(1, PS):
            value = jnp.where(image == k, ref[b * PS + k], value)
        return value

    def pixel(m):
        image, row, column = lax.rem(m, PS), lax.rem(lax.div(m, PS), geo.rows), lax.div(m, QS)
        good = (row < of_image(g.heights, image)) & (column < of_image(g.widths, image))
        return column, row, image, good

    g.mask[...] = jnp.where(pixel(first)[3], 1.0, 0.0)

    def row(scalar):
        return jnp.full((1, 128), scalar.astype(F32), F32)

    for k in range(NB):
        other = b if k == 0 else peers[k - 1][0]
        own = 0
        for j in range(PS):
            own = own + g.heights[other * PS + j] * g.widths[other * PS + j]
        g.aux[k : k + 1, :] = row(own)
        g.aux[NB + k : NB + k + 1, :] = 1.0 / row(own)
    count = row(sum(area))
    g.aux[16:17, :] = 1.0 / count
    g.aux[17:18, :] = count / (count - 1.0)
    g.aux[18:19, :] = 4.0 * count / (4.0 * count - 1.0)

    ld_img.wait()
    lane = lax.broadcasted_iota(jnp.int32, (R, 4 * R), 1)
    column, line, image, good = pixel(lax.broadcasted_iota(jnp.int32, (R, 1), 0))
    corner = image * 4 * geo.rows * geo.cols + 2 * line * 2 * geo.cols + 2 * column
    for ph in range(4):
        source = jnp.where(good, corner + (ph // 2) * 2 * geo.cols + ph % 2, -1)
        pick = jnp.where(lane == source, 1.0, 0.0).astype(BF)
        g.SRC[0, ph * R : (ph + 1) * R, :] = mm(pick, g.IMG[...]).astype(BF)

    pl.semaphore_wait(bar, len(everyone))

    rm_src = net.push(g.SRC.at[0], g.SRC.at[1], core)
    rm_w1 = [
        net.push(rows_of(g.w1, rank, CI), g.W1C.at[pl.ds(s * CI, CI), pl.ds(0, MI)], far)
        for s, rank in enumerate((r2, r3))
    ]
    piece = MI // 4
    rank = jnp.where(b < 4, r2, r3)
    at = pl.multiple_of(rank * MI + lax.rem(b, 4) * piece, piece)
    rm_w2 = net.push(g.w2.at[:, pl.ds(at, piece), :], g.W2F.at[b], far)
    ld_sc = net.load([(rows_of(g.wsc, rank, CI), g.WS.at[s]) for s, rank in enumerate(ranks)], g.WS)
    ld_w2 = net.load([(taps_of(g.w2, rank, MI), g.W2.at[:, s]) for s, rank in enumerate((r, r1))], g.W2)
    ld_w3 = net.load([(rows_of(g.w3, rank, MI), g.W3.at[s]) for s, rank in enumerate(ranks)], g.W3)
    ld_w4 = [
        net.local(rows_of(g.w4, rank, CO), g.W4C.at[pl.ds(s * CO, CO), pl.ds(MI, MI)])
        for s, rank in enumerate((r, r1))
    ]
    ld_w5 = net.load([(taps_of(g.w5, rank, MI), g.W5.at[:, s]) for s, rank in enumerate(ranks)], g.W5)
    ld_w6 = net.load([(rows_of(g.w6, rank, MI), g.W6.at[s]) for s, rank in enumerate(ranks)], g.W6)
    ld_cot = net.local(g.cot, g.COT)

    for ph in (1, 3):
        for s in range(2):
            g.F1[s, ph, 0:QS, :] = jnp.zeros((QS, MI), BF)
    for s in range(2):
        g.D1[1, s, 0:QS, :] = jnp.zeros((QS, MI), BF)
    for s in range(4):
        g.F4[s, 0:QS, :] = jnp.zeros((QS, MI), BF)
        g.F4[s, QS + R :, :] = jnp.zeros((QS, MI), BF)
        for d in range(2):
            g.D4[d, s, 0:QS, :] = jnp.zeros((QS, MI), BF)
            g.D4[d, s, QS + R :, :] = jnp.zeros((QS, MI), BF)
    for d in range(3):
        for s in range(2):
            g.E5[d, s, 0:QS, :] = jnp.zeros((QS, MI), BF)
            g.E5[d, s, QS + R :, :] = jnp.zeros((QS, MI), BF)
    for d in range(2):
        for s in range(4):
            g.E2[d, s, R:, :] = jnp.zeros((QS, MI), BF)

    for copy in ld_w1:
        copy.wait()
    rm_src.wait_recv()
    for copy in rm_w1:
        copy.wait_recv()
    rm_p1 = []
    for ph in range(4):
        span = slice(ph * R, (ph + 1) * R)
        both = jnp.concatenate([g.SRC[0, span, :], g.SRC[1, span, :]], axis=1)
        part = mm(both, g.W1C[...])
        g.P1S[ph] = part[:, :MI].astype(BF)
        rm_p1.append(net.push(g.P1S.at[ph], g.P1R.at[ph], far))
        g.PRE1[span, :] = part[:, MI:]

    rm_w2.wait_recv()
    rm_w2s = everywhere([g.W2F.at[b]] * (NB - 1), [g.W2F.at[b]] * (NB - 1), g.W2F.at[pl.ds(0, NB - 1)])

    rm_back = []
    for s, rank in enumerate((r1, r3)):
        rm_back.append(net.push(rows_of(g.w6, rank, MI), g.W6P.at[s], core))
        rm_back.append(net.push(taps_of(g.w5, rank, MI), g.W5P.at[:, s], core))
        rm_back.append(net.push(rows_of(g.w3, rank, MI), g.W3P.at[s], core))
        rm_back.append(net.push(rows_of(g.wsc, rank, CI), g.WSP.at[s], core))
    rm_back.append(net.push(taps_of(g.w2, r1, MI), g.W2P, core))
    rm_back.append(net.push(rows_of(g.w4, r1, CO), g.W4P.at[0], core))
    rm_back.append(net.push(rows_of(g.w1, r1, CI), g.W1P.at[0], core))
    rm_back.append(
        net.push(g.W1C.at[pl.ds(CI, CI), pl.ds(0, MI)], g.W1P.at[1], core)
    )

    aux = g.aux
    inv_out = aux[16:17, :]
    unb_out, unb_in = aux[17:18, :], aux[18:19, :]

    def mask_rows(at, size):
        return g.mask[pl.ds(at, size), :]

    def over(total, size, body, init):
        def step(i, carry):
            return body(pl.multiple_of(i * size, size), carry)

        return lax.fori_loop(0, total // size, step, init)

    NCH = 128 if R % 128 == 0 else QS
    WCH = QS

    def bc(mask, width):
        return jnp.concatenate([mask] * (width // 128), axis=1)

    def exchange(slots, payload_rows):
        others = range(1, NB)
        return everywhere(
            [slots.at[0] for _ in others],
            [slots.at[k] for k in others],
            slots.at[pl.ds(1, NB - 1)],
        )

    def narrow_local(pre, phases, prepare=None):
        total = jnp.zeros((8, MI), F32)
        for ph in range(phases):
            if prepare is not None:
                prepare(ph)

            def add(at, acc, ph=ph):
                return acc + fold(pre[pl.ds(ph * R + at, NCH), :] * mask_rows(at, NCH))

            total = over(R, NCH, add, total)
        total = jnp.sum(total, axis=0, keepdims=True)
        mean = total * (aux[8:9, :] * (1.0 / phases))
        squares = jnp.zeros((8, MI), F32)
        for ph in range(phases):

            def add2(at, acc, ph=ph):
                d = (pre[pl.ds(ph * R + at, NCH), :] - mean) * mask_rows(at, NCH)
                return acc + fold(d * d)

            squares = over(R, NCH, add2, squares)
        return total, jnp.sum(squares, axis=0, keepdims=True)

    def narrow_send(idx, first, second):
        slots = g.SN.at[idx]
        g.SN[idx, 0, 0:1, :] = first
        g.SN[idx, 0, 1:2, :] = second
        return exchange(slots, 2)

    def narrow_merge(idx, copies, phases):
        copies.wait_recv()
        sums = [g.SN[idx, k, 0:1, :] for k in range(NB)]
        squares = [g.SN[idx, k, 1:2, :] for k in range(NB)]
        return moments(sums, squares, phases)

    def moments(sums, squares, phases):
        inv_count = inv_out * (1.0 / phases)
        mean = tree(list(sums)) * inv_count
        terms = []
        for k in range(NB):
            d = sums[k] * (aux[8 + k : 9 + k, :] * (1.0 / phases)) - mean
            terms.append(squares[k] + aux[k : k + 1, :] * float(phases) * d * d)
        spread = tree(terms) * inv_count
        return mean, spread

    def wide_local(pre):
        def add(at, acc):
            m = bc(mask_rows(at, WCH), CO)
            return acc + fold(pre[pl.ds(at, WCH), :] * m)

        total = jnp.sum(over(R, WCH, add, jnp.zeros((8, CO), F32)), axis=0, keepdims=True)
        mean = total * bc(aux[8:9, :], CO)

        def add2(at, acc):
            m = bc(mask_rows(at, WCH), CO)
            d = (pre[pl.ds(at, WCH), :] - mean) * m
            return acc + fold(d * d)

        squares = jnp.sum(over(R, WCH, add2, jnp.zeros((8, CO), F32)), axis=0, keepdims=True)
        return total, squares

    NW = CO // 128

    def wide_put(slots, row, value):
        for j in range(NW):
            slots[0, row + j : row + j + 1, :] = value[:, j * 128 : (j + 1) * 128]

    def wide_send(idx, first, second):
        slots = g.SW.at[idx]
        wide_put(slots, 0, first)
        wide_put(slots, NW, second)
        return exchange(slots, 2 * NW)

    def wide_merge(idx, copies):
        copies.wait_recv()
        sums = [g.SW[idx, k, 0:NW, :] for k in range(NB)]
        squares = [g.SW[idx, k, NW : 2 * NW, :] for k in range(NB)]
        mean, spread = moments(sums, squares, 1)
        return wide_row(mean), wide_row(spread)

    def gather(buf, at, size):
        here = [buf(s).at[pl.ds(at, size)] for s in range(4)]
        near = net.push(here[0], here[1], core)
        away = net.push(here[0], here[2], far)
        return [near, away, here]

    def relay(chunk):
        near, away, here = chunk
        away.wait_recv()
        chunk.append(net.push(here[2], here[3], core))

    def landed(chunk):
        chunk[0].wait_recv()
        chunk[3].wait_recv()

    def lanes(parts):
        return jnp.concatenate(parts, axis=1)

    place = lax.broadcasted_iota(jnp.int32, (QS, 128), 0)
    keep_down = place >= PS
    keep_up = place < QS - PS

    def shifted(value, step):
        if step < 0:
            return jnp.where(keep_down, pltpu.roll(value, PS, 0), 0.0)
        return jnp.where(keep_up, pltpu.roll(value, QS - PS, 0), 0.0)

    def take_p1(ph):
        rm_p1[ph].wait_recv()

        def add(at, carry):
            rows = pl.ds(ph * R + at, NCH)
            g.PRE1[rows, :] = g.PRE1[rows, :] + g.P1R[ph, pl.ds(at, NCH), :].astype(F32)
            return carry

        over(R, NCH, add, 0)

    sum_one, sq_one = narrow_local(g.PRE1, 4, take_p1)
    st_one = narrow_send(0, sum_one, sq_one)
    rm_xs = net.push(g.SRC.at[0, pl.ds(0, R)], g.XS.at[0], far)

    def scale_of(spread, gain):
        inv = lax.rsqrt(spread + EPS)
        return inv, inv * gain

    mean_one, spread_one = narrow_merge(0, st_one, 4)
    inv_one, scale_one = scale_of(spread_one, g.gm[0:1, :])

    def narrow_feature(pre, mean, scale, bias, out, ph, at0):
        def body(at, carry):
            v = (pre[pl.ds(ph * R + at, NCH), :] - mean) * scale + bias
            out[pl.ds(at0 + at, NCH), :] = (v * gate(v) * mask_rows(at, NCH)).astype(BF)
            return carry

        over(R, NCH, body, 0)

    ch_one = []
    for ph in range(4):
        narrow_feature(
            g.PRE1, mean_one, scale_one, g.bm[0:1, :], g.F1.at[0, ph], ph, QS
        )
        span = pl.ds(QS, R)
        ch_one.append(net.push(g.F1.at[0, ph, span], g.F1.at[1, ph, span], core))

    def taking(copy, pre, got):
        def take(ph):
            copy.wait_recv()

            def add(at, carry):
                rows = pl.ds(at, NCH)
                pre[rows, :] = pre[rows, :] + got[rows, :].astype(F32)
                return carry

            over(R, NCH, add, 0)

        return take

    rm_xs.wait_recv()
    rm_xs2 = net.push(g.XS.at[0], g.XS.at[1], core)
    ld_sc.wait()
    rm_xs2.wait_recv()

    def strided():
        return [g.SRC[0, 0:R, :], g.SRC[1, 0:R, :], g.XS[0], g.XS[1]]

    pre_side = None
    for s, block in enumerate(strided()):
        term = mm(block, g.WS[s])
        pre_side = term if pre_side is None else pre_side + term
    g.PRES[...] = pre_side
    st_side = wide_send(0, *wide_local(g.PRES))

    ld_w2.wait()

    def chip_one(s, ph, down, left):
        rows = slice(0, R) if left else slice(QS, QS + R)
        return g.D1[ph - 2, s, rows, :] if down else g.F1[s, ph, rows, :]

    def far_two(tap, first):
        return jnp.concatenate([g.W2F[first + k, tap] for k in range(4)], axis=0)

    def both_two(tap):
        near = jnp.concatenate([g.W2[tap, s] for s in range(2)], axis=0)
        away = jnp.concatenate([far_two(tap, 0), far_two(tap, 4)], axis=0)
        return lanes([away, near])

    def taps_two(ph):
        top = (1,) if ph < 2 else (0, 2)
        left = (1,) if ph % 2 == 0 else (0, 2)
        return [(t, l) for t in top for l in left]

    def lower(ph, s):
        def move(at, carry):
            v = g.F1[s, ph, pl.ds(QS + at, QS), :].astype(F32)
            g.D1[ph - 2, s, pl.ds(QS + at, QS), :] = shifted(v, -1).astype(BF)
            return carry

        over(R, QS, move, 0)

    rm_w2s.wait_recv()
    rm_back.append(net.push(g.W2F.at[pl.ds(4, 4)], g.W2Q, core))
    part = None
    for ph in range(4):
        if ph >= 2:
            lower(ph, 0)
        ch_one[ph].wait_recv()
        if ph >= 2:
            lower(ph, 1)
        for t, l in taps_two(ph):
            term = mm(lanes([chip_one(s, ph, t == 0, l == 0) for s in range(2)]), both_two(3 * t + l))
            part = term if part is None else part + term
    g.P2S[...] = part[:, :MI].astype(BF)
    rm_p2 = net.push(g.P2S, g.P2R, far)
    g.PRE2[...] = part[:, MI:]
    rm_w4 = [
        net.push(rows_of(g.w4, rank, CO), g.W4C.at[pl.ds(s * CO, CO), pl.ds(0, MI)], far)
        for s, rank in enumerate((r2, r3))
    ]
    st_two = narrow_send(1, *narrow_local(g.PRE2, 1, taking(rm_p2, g.PRE2, g.P2R)))
    mean_two, spread_two = narrow_merge(1, st_two, 1)
    inv_two, scale_two = scale_of(spread_two, g.gm[1:2, :])
    narrow_feature(g.PRE2, mean_two, scale_two, g.bm[1:2, :], g.F2.at[0], 0, 0)
    ch_two = gather(lambda s: g.F2.at[s], 0, R)
    ld_w3.wait()
    mean_side, spread_side = wide_merge(0, st_side)
    inv_side, scale_side = scale_of(spread_side, g.go[1:2, :])

    def four(ref):
        return lanes([ref[s] for s in range(4)])

    def chip_product(chunk, ref, weight):
        chunk[0].wait_recv()
        value = mm(lanes([ref[0], ref[1]]), weight[0:2].reshape(2 * MI, CO))
        relay(chunk)
        chunk[3].wait_recv()
        return value + mm(lanes([ref[2], ref[3]]), weight[2:4].reshape(2 * MI, CO))

    g.PRE3[...] = chip_product(ch_two, g.F2, g.W3)
    st_three = wide_send(1, *wide_local(g.PRE3))
    mean_three, spread_three = wide_merge(1, st_three)
    inv_three, scale_three = scale_of(spread_three, g.go[0:1, :])
    bias_three, bias_side = g.bo[0:1, :], g.bo[1:2, :]

    def mid_value(rows):
        return (
            (g.PRE3[rows, :] - mean_three) * scale_three
            + bias_three
            + (g.PRES[rows, :] - mean_side) * scale_side
            + bias_side
        )

    def mid_body(at, carry):
        rows = pl.ds(at, WCH)
        v = mid_value(rows)
        out = v * gate(v) * bc(mask_rows(at, WCH), CO)
        g.BM[rows, :] = out
        g.MIDC[0, rows, :] = out.astype(BF)
        return carry

    over(R, WCH, mid_body, 0)
    rm_mid = net.push(g.MIDC.at[0], g.MIDC.at[1], core)

    for copy in ld_w4:
        copy.wait()
    for copy in rm_w4:
        copy.wait_recv()
    rm_back.append(net.push(g.W4C.at[pl.ds(CO, CO), pl.ds(0, MI)], g.W4P.at[1], core))
    rm_mid.wait_recv()
    part = mm(lanes([g.MIDC[0], g.MIDC[1]]), g.W4C[...])
    g.P4S[...] = part[:, :MI].astype(BF)
    rm_p4 = net.push(g.P4S, g.P4R, far)
    g.PRE4[...] = part[:, MI:]

    st_four = narrow_send(2, *narrow_local(g.PRE4, 1, taking(rm_p4, g.PRE4, g.P4R)))
    mean_four, spread_four = narrow_merge(2, st_four, 1)
    inv_four, scale_four = scale_of(spread_four, g.gm[2:3, :])
    narrow_feature(g.PRE4, mean_four, scale_four, g.bm[2:3, :], g.F4.at[0], 0, QS)
    ch_four = gather(lambda s: g.F4.at[s], QS, R)
    ld_w5.wait()

    def kernel_rows(ref, tap, first=0):
        return jnp.concatenate([ref[tap, s] for s in range(first, first + 2)], axis=0)

    def spread_rows(src, dst_up, dst_down):
        def body(at, carry):
            rows = pl.ds(QS + at, QS)
            v = src[rows, :].astype(F32)
            dst_up[rows, :] = shifted(v, -1).astype(BF)
            dst_down[rows, :] = shifted(v, 1).astype(BF)
            return carry

        over(R, QS, body, 0)

    def fill_four(s):
        spread_rows(g.F4.at[s], g.D4.at[0, s], g.D4.at[1, s])

    fill_four(0)
    ch_four[0].wait_recv()
    fill_four(1)

    def four_blocks(t, l, slots):
        rows = slice(l * QS, l * QS + R)
        if t == 1:
            return lanes([g.F4[s, rows, :] for s in slots])
        return lanes([g.D4[t // 2, s, rows, :] for s in slots])

    def whole_four(t, l):
        return four_blocks(t, l, range(4))

    pre_five = None
    for first in (0, 2):
        if first:
            relay(ch_four)
            fill_four(2)
            ch_four[3].wait_recv()
            fill_four(3)
        for t in range(3):
            for l in range(3):
                blocks = four_blocks(t, l, range(first, first + 2))
                term = mm(blocks, kernel_rows(g.W5, 3 * t + l, first))
                pre_five = term if pre_five is None else pre_five + term
    g.PRE5[...] = pre_five
    st_five = narrow_send(3, *narrow_local(g.PRE5, 1))
    mean_five, spread_five = narrow_merge(3, st_five, 1)
    inv_five, scale_five = scale_of(spread_five, g.gm[3:4, :])
    narrow_feature(g.PRE5, mean_five, scale_five, g.bm[3:4, :], g.F5.at[0], 0, 0)
    ch_five = gather(lambda s: g.F5.at[s], 0, R)
    ld_w6.wait()
    ld_cot.wait()
    g.COTP[...] = mm_tn(g.po[...], g.COT[...])
    g.PRE6[...] = chip_product(ch_five, g.F5, g.W6)
    st_six = wide_send(2, *wide_local(g.PRE6))
    mean_six, spread_six = wide_merge(2, st_six)
    inv_six, scale_six = scale_of(spread_six, g.go[2:3, :])
    bias_six = g.bo[2:3, :]

    def last_body(at, carry):
        acc_b, acc_g = carry
        rows = pl.ds(at, WCH)
        m = bc(mask_rows(at, WCH), CO)
        hat = (g.PRE6[rows, :] - mean_six) * inv_six
        v = (g.PRE6[rows, :] - mean_six) * scale_six + bias_six + g.BM[rows, :]
        s = gate(v)
        g.OUT[rows, :] = v * s * m
        grad = g.COTP[rows, :] * m * (s * (1.0 + v * (1.0 - s)))
        g.GSB[rows, :] = grad
        return acc_b + fold(grad), acc_g + fold(grad * hat)

    zero_w = jnp.zeros((8, CO), F32)
    acc_b, acc_g = over(R, WCH, last_body, (zero_w, zero_w))

    def down(value):
        return jnp.sum(value, axis=0, keepdims=True)

    st = wide_send(3, down(acc_b), down(acc_g))

    out_block = net.local(g.OUT, g.block_out)

    def wide_sums(ref, copies, count):
        copies.wait_recv()
        return [
            wide_row(tree([ref[k, j * NW : (j + 1) * NW, :] for k in range(NB)]))
            for j in range(count)
        ]

    def narrow_sums(idx, copies):
        copies.wait_recv()
        return [tree([g.SN[idx, k, j : j + 1, :] for k in range(NB)]) for j in range(2)]

    bsum_six, gsum_six = wide_sums(g.SW.at[3], st, 2)
    inv_wide = bc(inv_out, CO)

    def wide_pre_grad(grad, pre, mean, inv, scale, bsum, gsum, out):
        mb, mg = bsum * inv_wide, gsum * inv_wide

        def body(at, carry):
            rows = pl.ds(at, WCH)
            hat = (pre[rows, :] - mean) * inv
            e = bc(mask_rows(at, WCH), CO) * scale * (grad[rows, :] - (mb + hat * mg))
            out[rows, :] = e.astype(BF)
            return carry

        over(R, WCH, body, 0)

    wide_pre_grad(
        g.GSB, g.PRE6, mean_six, inv_six, scale_six, bsum_six, gsum_six, g.E6.at[0]
    )
    for copy in rm_back:
        copy.wait_recv()

    def swap(ref):
        return net.push(ref.at[0], ref.at[1], core)

    def reduce_back(part, sent, got):
        sent[...] = part[:, MI:].astype(BF)
        return net.push(sent, got, far)

    def wide_back(e, own, other):
        near = lanes([own[0], other[0]])
        away = lanes([own[2], other[1]])
        return mm_nt(lanes([e[0], e[1]]), jnp.concatenate([near, away], axis=0))

    def narrow_back(idx, near, got, copy, phases, pre, mean, inv, scale, bias, order=None):
        acc_b = jnp.zeros((8, MI), F32)
        acc_g = jnp.zeros((8, MI), F32)
        for ph in range(phases):
            if copy is not None:
                copy[ph].wait_recv()

            def body(at, carry, ph=ph):
                b_acc, g_acc = carry
                rows = pl.ds(ph * R + at, NCH)
                hat = (pre[rows, :] - mean) * inv
                v = (pre[rows, :] - mean) * scale + bias
                s = gate(v)
                feat = near[rows, :]
                if got is not None:
                    feat = feat + got[rows, :].astype(F32)
                grad = feat * mask_rows(at, NCH) * (s * (1.0 + v * (1.0 - s)))
                near[rows, :] = grad
                return b_acc + fold(grad), g_acc + fold(grad * hat)

            acc_b, acc_g = over(R, NCH, body, (acc_b, acc_g))
        return narrow_send(idx, down(acc_b), down(acc_g))

    def narrow_pre_grad(grad, pre, mean, inv, scale, bsum, gsum, phases, ph, out, at0):
        inv_count = inv_out * (1.0 / phases)
        mb, mg = bsum * inv_count, gsum * inv_count

        def body(at, carry):
            rows = pl.ds(ph * R + at, NCH)
            hat = (pre[rows, :] - mean) * inv
            e = mask_rows(at, NCH) * scale * (grad[rows, :] - (mb + hat * mg))
            out[pl.ds(at0 + at, NCH), :] = e.astype(BF)
            return carry

        over(R, NCH, body, 0)

    outs = [out_block]

    def give(src, dst):
        outs.append(net.local(src, dst))

    cp = swap(g.E6)
    cp.wait_recv()
    part = wide_back(g.E6, g.W6, g.W6P)
    cp = [reduce_back(part, g.B5S, g.B5R)]
    g.GF5[...] = part[:, :MI]
    def rows_grad(part, value, s):
        half = value.shape[0] // 2
        for h in range(2):
            part[2 * s + h] = value[h * half : (h + 1) * half].astype(BF)

    def taps_grad(part, tap, value):
        half = MI // 2
        for p in range(8):
            part[p, tap] = value[p * half : (p + 1) * half].astype(BF)

    jobs = []

    def spilled(done, targets):
        sem = net.take()
        copies = [net.plan_local(source, place, sem) for source, place in targets]
        return copies, net.plan_local(done, done, sem)

    def job(part, got, done, targets, across=None):
        jobs.append(Summed(net, part, got, done, ring, spilled(done, targets), across))

    def pump(most=3):
        left = sorted((work for work in jobs if work.todo), key=lambda work: -len(work.todo))
        for work in left[:most]:
            work.step()

    def slots_to(part, place):
        return [(part.at[pl.ds(2 * s, 2)], place(ranks[s])) for s in range(4)]

    def chips_to(part, out, taps=None):
        def place(rank):
            return out.at[rank] if taps is None else out.at[rank, :, taps]

        return [
            (part.at[pl.ds(4 * s, 4), v], place(ranks[2 * v + s]))
            for s in range(2)
            for v in range(2)
        ]

    for s in range(4):
        rows_grad(g.K6, mm_tn(g.F5[s], g.E6[0]), s)
    job(g.K6, g.K6R, g.K6D, slots_to(g.K6D, lambda rank: g.k6.at[rank]))
    pump()
    st = narrow_back(
        4, g.GF5, g.B5R, cp, 1, g.PRE5, mean_five, inv_five, scale_five, g.bm[3:4, :]
    )
    pump()
    bsum_five, gsum_five = narrow_sums(4, st)
    narrow_pre_grad(
        g.GF5, g.PRE5, mean_five, inv_five, scale_five, bsum_five, gsum_five, 1, 0,
        g.E5.at[1, 0], QS,
    )
    cp = net.push(g.E5.at[1, 0, pl.ds(QS, R)], g.E5.at[1, 1, pl.ds(QS, R)], core)
    spread_rows(g.E5.at[1, 0], g.E5.at[0, 0], g.E5.at[2, 0])
    cp.wait_recv()
    spread_rows(g.E5.at[1, 1], g.E5.at[0, 1], g.E5.at[2, 1])
    pump()

    def taps_back(own, other, tap):
        near = lanes([own[tap, 0], other[tap, 0]])
        away = lanes([own[tap, 2], other[tap, 1]])
        return jnp.concatenate([near, away], axis=0)

    part = None
    for t in range(3):
        for l in range(3):
            rows = slice((2 - l) * QS, (2 - l) * QS + R)
            e = lanes([g.E5[2 - t, s, rows, :] for s in range(2)])
            term = mm_nt(e, taps_back(g.W5, g.W5P, 3 * t + l))
            part = term if part is None else part + term
    cp = [reduce_back(part, g.B4S, g.B4R)]
    g.GF4[...] = part[:, :MI]
    pump()
    own_five = g.E5[1, 0, QS : QS + R, :]

    def five_grad(part, first, last):
        for tap in range(first, last):
            taps_grad(part, tap - first, mm_tn(whole_four(tap // 3, tap % 3), own_five))

    five_grad(g.K5A, 0, 5)
    job(g.K5A, g.K5AR, g.K5AD, slots_to(g.K5AD, lambda rank: g.k5.at[rank, :, pl.ds(0, 5)]))
    five_grad(g.K5B, 5, 9)
    job(g.K5B, g.K5BR, g.K5BD, slots_to(g.K5BD, lambda rank: g.k5.at[rank, :, pl.ds(5, 4)]))
    pump()
    st = narrow_back(
        5, g.GF4, g.B4R, cp, 1, g.PRE4, mean_four, inv_four, scale_four, g.bm[2:3, :]
    )
    pump()
    bsum_four, gsum_four = narrow_sums(5, st)
    narrow_pre_grad(
        g.GF4, g.PRE4, mean_four, inv_four, scale_four, bsum_four, gsum_four, 1, 0,
        g.G4.at[0], 0,
    )
    ch = gather(lambda s: g.G4.at[s], 0, R)
    relay(ch)
    pump()
    landed(ch)
    mid_back = mm_nt(
        four(g.G4),
        lanes([g.W4C[0:CO, MI:], g.W4P[0], g.W4C[0:CO, :MI], g.W4P[1]]),
    )
    g.GMID[...] = mid_back

    def mid_back_body(at, carry):
        a_b, a_3, a_s = carry
        rows = pl.ds(at, WCH)
        v = mid_value(rows)
        s = gate(v)
        grad = (g.GSB[rows, :] + g.GMID[rows, :]) * bc(mask_rows(at, WCH), CO)
        grad = grad * (s * (1.0 + v * (1.0 - s)))
        g.GMID[rows, :] = grad
        hat3 = (g.PRE3[rows, :] - mean_three) * inv_three
        hats = (g.PRES[rows, :] - mean_side) * inv_side
        return a_b + fold(grad), a_3 + fold(grad * hat3), a_s + fold(grad * hats)

    a_b, a_3, a_s = over(R, WCH, mid_back_body, (zero_w, zero_w, zero_w))
    for j, value in enumerate((a_b, a_3, a_s, zero_w)):
        wide_put(g.SA, j * NW, down(value))
    st = exchange(g.SA, 4 * NW)
    e4 = lanes([g.G4[0], g.G4[2]])

    def chip_grad(part, s, value):
        size = value.shape[0] // 4
        for p in range(4):
            for w in range(2):
                block = value[p * size : (p + 1) * size, w * MI : (w + 1) * MI]
                part[4 * s + p, w] = block.astype(BF)

    for s in range(2):
        chip_grad(g.K4, s, mm_tn(g.MIDC[s], e4))
    job(g.K4, g.K4R, g.K4D, chips_to(g.K4D, g.k4), far)
    pump()
    bsum_a, gsum_three, gsum_side = wide_sums(g.SA, st, 3)
    wide_pre_grad(
        g.GMID, g.PRE3, mean_three, inv_three, scale_three, bsum_a, gsum_three,
        g.E3.at[0],
    )
    cp = swap(g.E3)
    wide_pre_grad(
        g.GMID, g.PRES, mean_side, inv_side, scale_side, bsum_a, gsum_side, g.ES.at[0]
    )
    cp_side = swap(g.ES)
    pump()
    cp.wait_recv()
    part = wide_back(g.E3, g.W3, g.W3P)
    cp = [reduce_back(part, g.B2S, g.B2R)]
    g.GF2[...] = part[:, :MI]
    for s in range(4):
        rows_grad(g.K3, mm_tn(g.F2[s], g.E3[0]), s)
    job(g.K3, g.K3R, g.K3D, slots_to(g.K3D, lambda rank: g.k3.at[rank]))
    pump()
    st = narrow_back(
        6, g.GF2, g.B2R, cp, 1, g.PRE2, mean_two, inv_two, scale_two, g.bm[1:2, :]
    )
    pump()
    cp_side.wait_recv()
    es = lanes([g.ES[0], g.ES[1]])
    g.IGS[...] = mm_nt(es, lanes([g.WS[0], g.WSP[0]]))
    half = CO // 2
    for s, block in enumerate(strided()):
        grad = mm_tn(block, g.ES[0])
        rows_grad(g.KSA, grad[:, :half], s)
        rows_grad(g.KSB, grad[:, half:], s)
    job(g.KSA, g.KSAR, g.KSAD, slots_to(g.KSAD, lambda rank: g.ks.at[rank, :, :, pl.ds(0, half)]))
    job(g.KSB, g.KSBR, g.KSBD, slots_to(g.KSBD, lambda rank: g.ks.at[rank, :, :, pl.ds(half, half)]))
    pump()
    pump()
    bsum_two, gsum_two = narrow_sums(6, st)
    narrow_pre_grad(
        g.GF2, g.PRE2, mean_two, inv_two, scale_two, bsum_two, gsum_two, 1, 0,
        g.E2.at[0, 0], 0,
    )
    ch = gather(lambda s: g.E2.at[0, s], 0, R)

    def lift(s):
        def body(at, carry):
            rows = pl.ds(at, QS)
            v = g.E2[0, s, rows, :].astype(F32)
            g.E2[1, s, rows, :] = shifted(v, 1).astype(BF)
            return carry

        over(R, QS, body, 0)

    def two_grad(w, slot):
        e = g.E2[0, slot, 0:R, :]
        for ph in range(4):
            for t, l in taps_two(ph):
                tap = 3 * t + l
                part, tap = (g.K2A, tap) if tap < 5 else (g.K2B, tap - 5)
                for s in range(2):
                    grad = mm_tn(chip_one(s, ph, t == 0, l == 0), e)
                    for p in range(4):
                        rows = grad[p * piece : (p + 1) * piece]
                        part[4 * s + p, w, tap] = rows.astype(BF)

    lift(0)
    pump()
    two_grad(0, 0)
    ch[0].wait_recv()
    lift(1)
    relay(ch)
    two_grad(1, 2)
    for name, first, count in (("K2A", 0, 5), ("K2B", 5, 4)):
        bufs = [getattr(g, name + end) for end in ("", "R", "D")]
        job(*bufs, chips_to(bufs[2], g.k2, pl.ds(first, count)), far)
    pump()
    lift(2)
    ch[3].wait_recv()
    lift(3)

    def own_two(tap):
        far_own = jnp.concatenate([g.W2F[k, tap] for k in range(4)], axis=0)
        far_other = jnp.concatenate([g.W2Q[k, tap] for k in range(4)], axis=0)
        return lanes([g.W2[tap, 0], g.W2P[tap], far_own, far_other])

    for ph in range(4):
        part = None
        for t, l in taps_two(ph):
            rows = slice(QS, QS + R) if l == 0 else slice(0, R)
            e = lanes([g.E2[1 if t == 0 else 0, s, rows, :] for s in range(4)])
            term = mm_nt(e, own_two(3 * t + l))
            part = term if part is None else part + term
        g.GF1[ph * R : (ph + 1) * R, :] = part
        if ph == 3:
            pump()
    st = narrow_back(
        7, g.GF1, None, None, 4, g.PRE1, mean_one, inv_one, scale_one, g.bm[0:1, :]
    )
    side_far = mm_nt(es, lanes([g.WS[2], g.WSP[1]]))
    g.BSS[...] = side_far.astype(BF)
    cp_bs = net.push(g.BSS, g.BSR, far)
    pump()
    bsum_one, gsum_one = narrow_sums(7, st)
    ch = []
    for ph in range(4):
        narrow_pre_grad(
            g.GF1, g.PRE1, mean_one, inv_one, scale_one, bsum_one, gsum_one, 4, ph,
            g.G1.at[0, ph], 0,
        )
        ch.append(gather(lambda s, ph=ph: g.G1.at[s, ph], 0, R))
    pump()
    w1_own = lanes([g.W1C[0:CI, MI:], g.W1P[0], g.W1C[0:CI, :MI], g.W1P[1]])
    relay(ch[0])
    for ph in range(4):
        if ph < 3:
            relay(ch[ph + 1])
        landed(ch[ph])
        pump()
        whole = lanes([g.G1[s, ph] for s in range(4)])
        g.IG[ph * R : (ph + 1) * R, :] = mm_nt(whole, w1_own)
    for s in range(2):
        k1 = None
        for ph in range(4):
            e1 = lanes([g.G1[0, ph], g.G1[2, ph]])
            term = mm_tn(g.SRC[s, ph * R : (ph + 1) * R, :], e1)
            k1 = term if k1 is None else k1 + term
        chip_grad(g.K1, s, k1)
    spill = spilled(g.K1D, chips_to(g.K1D, g.k1))
    jobs.append(Direct(net, g.K1, g.K1R, g.K1D, b, peers, spill, far))
    jobs[-1].step()
    pump()
    cp_bs.wait_recv()
    g.IG[0:R, :] = g.IG[0:R, :] + g.IGS[...] + g.BSR[...].astype(F32)
    for ph in range(4):
        rows = slice(ph * R, (ph + 1) * R)
        g.IG[rows, :] = g.IG[rows, :] * bc(g.mask[...], CI)
    give(g.IG, g.images_grad)
    while any(work.todo for work in jobs):
        if jobs[-1].todo:
            jobs[-1].step()
        pump()

    g.gain_mid_grad[...] = jnp.concatenate([gsum_one, gsum_two, gsum_four, gsum_five], axis=0)
    g.bias_mid_grad[...] = jnp.concatenate([bsum_one, bsum_two, bsum_four, bsum_five], axis=0)
    g.gain_out_grad[...] = jnp.concatenate([gsum_three, gsum_side, gsum_six], axis=0)
    g.bias_out_grad[...] = jnp.concatenate([bsum_a, bsum_a, bsum_six], axis=0)
    g.mean_mid[...] = jnp.concatenate([mean_one, mean_two, mean_four, mean_five], axis=0)
    g.var_mid[...] = jnp.concatenate(
        [spread_one * unb_in, spread_two * unb_out, spread_four * unb_out, spread_five * unb_out],
        axis=0,
    )
    g.mean_out[...] = jnp.concatenate([mean_three, mean_side, mean_six], axis=0)
    g.var_out[...] = jnp.concatenate([spread_three, spread_side, spread_six], axis=0) * bc(
        unb_out, CO
    )
    for copy in outs:
        copy.wait()
    for copy in net.sent:
        copy.wait_send()

    for work in jobs:
        work.drain()


def fused_on_device(
    images, heights, widths, reduce_first, spatial_first, expand_first, shortcut, reduce_second,
    spatial_second, expand_second, gain_mid, bias_mid, gain_out, bias_out, cotangent,
):
    n, rows, cols, CO = cotangent.shape
    CI, MI = images.shape[3], reduce_first.shape[1]
    NB = heights.shape[0] // n
    R, QS = n * rows * cols, n * rows
    q, p, i = np.meshgrid(np.arange(cols), np.arange(rows), np.arange(n), indexing="ij")
    q, p, i = (v.reshape(-1) for v in (q, p, i))
    pick_out = np.zeros((R, R), np.float32)
    pick_out[np.arange(R), (i * cols + q) * rows + p] = 1.0
    pick_in = np.zeros((2 * R, 2 * R), np.float32)
    for h in range(2):
        pick_in[h * R + np.arange(R), (i * rows + p) * 2 * cols + 2 * q + h] = 1.0
    po = jnp.asarray(pick_out.T.astype(ml_dtypes.bfloat16))
    pi = jnp.asarray(pick_in.T.astype(ml_dtypes.bfloat16))
    cot = cotangent.transpose(0, 2, 1, 3).reshape(R, CO)
    ANY, VM = pl.BlockSpec(memory_space=pl.ANY), pl.BlockSpec(memory_space=pltpu.VMEM)
    SM = pl.BlockSpec(memory_space=pltpu.SMEM)
    CM, MC = 4 * MI, 4 * CI
    ins = dict(
        img=(images.reshape(4 * R, CI), ANY),
        cot=(cot, ANY),
        w1=(reduce_first, ANY),
        w2=(spatial_first.reshape(9, CM, MI), ANY),
        w3=(expand_first, ANY),
        wsc=(shortcut, ANY),
        w4=(reduce_second, ANY),
        w5=(spatial_second.reshape(9, CM, MI), ANY),
        w6=(expand_second, ANY),
        heights=(heights, SM),
        widths=(widths, SM),
        po=(po, VM),
        gm=(gain_mid, VM),
        bm=(bias_mid, VM),
        go=(gain_out, VM),
        bo=(bias_out, VM),
    )
    outs = dict(
        block_out=((R, CO), F32, ANY),
        images_grad=((4 * R, CI), F32, ANY),
        k1=((4, 4, CI // 4, MI), BF, ANY),
        k2=((4, 4, 9, MI // 4, MI), BF, ANY),
        k3=((4, 2, MI // 2, CO), BF, ANY),
        ks=((4, 2, CI // 2, CO), BF, ANY),
        k4=((4, 4, CO // 4, MI), BF, ANY),
        k5=((4, 2, 9, MI // 2, MI), BF, ANY),
        k6=((4, 2, MI // 2, CO), BF, ANY),
        gain_mid_grad=((4, MI), F32, VM),
        bias_mid_grad=((4, MI), F32, VM),
        gain_out_grad=((3, CO), F32, VM),
        bias_out_grad=((3, CO), F32, VM),
        mean_mid=((4, MI), F32, VM),
        var_mid=((4, MI), F32, VM),
        mean_out=((3, CO), F32, VM),
        var_out=((3, CO), F32, VM),
    )
    NW = CO // 128
    scratch = dict(
        IMG=((4 * R, CI), BF),
        mask=((R, 128), F32),
        aux=((24, 128), F32),
        SRC=((2, 4 * R, CI), BF),
        XS=((2, R, CI), BF),
        W1C=((2 * CI, 2 * MI), BF),
        W1P=((2, CI, MI), BF),
        W2=((9, 2, MI, MI), BF),
        W2F=((NB, 9, MI // 4, MI), BF),
        W2P=((9, MI, MI), BF),
        W2Q=((4, 9, MI // 4, MI), BF),
        P2S=((R, MI), BF),
        P2R=((R, MI), BF),
        W3=((4, MI, CO), BF),
        W3P=((2, MI, CO), BF),
        WS=((4, CI, CO), BF),
        WSP=((2, CI, CO), BF),
        W4C=((2 * CO, 2 * MI), BF),
        W4P=((2, CO, MI), BF),
        W5=((9, 4, MI, MI), BF),
        W5P=((9, 2, MI, MI), BF),
        W6=((4, MI, CO), BF),
        W6P=((2, MI, CO), BF),
        COT=((R, CO), BF),
        COTP=((R, CO), F32),
        P1S=((4, R, MI), BF),
        P1R=((4, R, MI), BF),
        P4S=((R, MI), BF),
        P4R=((R, MI), BF),
        PRE1=((4 * R, MI), F32),
        PRE2=((R, MI), F32),
        PRE3=((R, CO), F32),
        PRES=((R, CO), F32),
        PRE4=((R, MI), F32),
        PRE5=((R, MI), F32),
        PRE6=((R, CO), F32),
        F1=((2, 4, QS + R, MI), BF),
        D1=((2, 2, QS + R, MI), BF),
        F2=((4, R, MI), BF),
        BM=((R, CO), F32),
        MIDC=((2, R, CO), BF),
        F4=((4, R + 2 * QS, MI), BF),
        D4=((2, 4, R + 2 * QS, MI), BF),
        F5=((4, R, MI), BF),
        OUT=((R, CO), F32),
        GSB=((R, CO), F32),
        E6=((2, R, CO), BF),
        B5S=((R, MI), BF),
        B5R=((R, MI), BF),
        GF5=((R, MI), F32),
        E5=((3, 2, R + 2 * QS, MI), BF),
        B4S=((R, MI), BF),
        B4R=((R, MI), BF),
        GF4=((R, MI), F32),
        G4=((4, R, MI), BF),
        GMID=((R, CO), F32),
        E3=((2, R, CO), BF),
        ES=((2, R, CO), BF),
        B2S=((R, MI), BF),
        B2R=((R, MI), BF),
        GF2=((R, MI), F32),
        E2=((2, 4, R + QS, MI), BF),
        GF1=((4 * R, MI), F32),
        G1=((4, 4, R, MI), BF),
        IGS=((R, CI), F32),
        BSS=((R, CI), BF),
        BSR=((R, CI), BF),
        IG=((4 * R, CI), F32),
        SN=((8, NB, 2, MI), F32),
        SW=((4, NB, 2 * NW, 128), F32),
        SA=((NB, 4 * NW, 128), F32),
    )
    for name, piece in dict(
        K1=(2, CI // 4, MI),
        K2A=(2, 5, MI // 4, MI),
        K2B=(2, 4, MI // 4, MI),
        K3=(MI // 2, CO),
        KSA=(CI // 2, CO // 2),
        KSB=(CI // 2, CO // 2),
        K4=(2, CO // 4, MI),
        K5A=(5, MI // 2, MI),
        K5B=(4, MI // 2, MI),
        K6=(MI // 2, CO),
    ).items():
        scratch[name] = ((8, *piece), BF)
        scratch[name + "D"] = ((8, *piece), BF)
        scratch[name + "R"] = ((8 if name == "K1" else 7, *piece), BF)
    names = [*ins, *outs, *scratch, "sems"]
    geo = types.SimpleNamespace(
        R=R, QS=QS, PS=n, CI=CI, MI=MI, CO=CO, NB=NB, rows=rows, cols=cols
    )
    got = pl.pallas_call(
        functools.partial(block_kernel, geo, names),
        out_shape=[jax.ShapeDtypeStruct(s, d) for s, d, _ in outs.values()],
        in_specs=[spec for _, spec in ins.values()],
        out_specs=[spec for _, _, spec in outs.values()],
        scratch_shapes=[pltpu.VMEM(s, d) for s, d in scratch.values()]
        + [pltpu.SemaphoreType.DMA((SEMS,))],
        compiler_params=pltpu.CompilerParams(
            collective_id=0, has_side_effects=True, vmem_limit_bytes=VMEM_LIMIT
        ),
    )(*[value for value, _ in ins.values()])
    o = types.SimpleNamespace(**dict(zip(outs, got)))
    passed = [
        o.gain_mid_grad, o.bias_mid_grad, o.gain_out_grad, o.bias_out_grad,
        o.mean_mid, o.var_mid, o.mean_out, o.var_out,
    ]
    finals = [
        jax.ShapeDtypeStruct(shape, F32)
        for shape in (
            (R, CO), (n, 2 * rows, 2 * cols, CI), (MC, MI), (3, 3, CM, MI), (CM, CO),
            (MC, CO), (4 * CO, MI), (3, 3, CM, MI), (CM, CO),
        )
    ]
    ks = (o.k1, o.k2, o.k3, o.ks, o.k4, o.k5, o.k6)
    res = pl.pallas_call(
        finish_kernel,
        out_shape=finals + [jax.ShapeDtypeStruct(v.shape, F32) for v in passed],
        in_specs=[ANY] * 9 + [VM] * 10,
        out_specs=[ANY] * 9 + [VM] * 8,
        scratch_shapes=[pltpu.VMEM((R, CO), F32), pltpu.VMEM((4 * R, CI), F32)]
        + [pltpu.VMEM(k.shape, BF) for k in ks]
        + [pltpu.VMEM(f.shape, F32) for f in finals]
        + [pltpu.SemaphoreType.DMA((18,))],
        compiler_params=pltpu.CompilerParams(vmem_limit_bytes=VMEM_LIMIT),
    )(o.block_out, o.images_grad, *ks, po, pi, *passed)
    block_out = res[0].reshape(n, cols, rows, CO).transpose(0, 2, 1, 3)
    return (block_out, *res[1:])


def exact(pick, value):
    high = value.astype(BF)
    low = (value - high.astype(F32)).astype(BF)
    return mm(pick, high) + mm(pick, low)


ORDER = (5, 3, 7, 6, 4, 8, 2, 1, 0)


def finish_kernel(*refs):
    ins, po, pi, small = refs[:9], refs[9], refs[10], refs[11:19]
    outs, small_outs = refs[19:28], refs[28:36]
    held, made, sems = refs[36:45], refs[45:54], refs[54]
    loads = [pltpu.make_async_copy(a, v, sems.at[k]) for k, (a, v) in enumerate(zip(ins, held))]
    stores = [
        pltpu.make_async_copy(v, a, sems.at[9 + k]) for k, (v, a) in enumerate(zip(made, outs))
    ]
    for k in ORDER:
        loads[k].start()
    for a, v in zip(small, small_outs):
        v[...] = a[...]

    def rows_of(k):
        src, dst = held[k], made[k]
        size = math.prod(src.shape[1:-1])
        for rank in range(4):
            dst[rank * size : (rank + 1) * size, :] = (
                src[rank].reshape(size, src.shape[-1]).astype(F32)
            )

    def taps_of(k):
        src, dst = held[k], made[k]
        size = src.shape[3]

        def tap(t):
            for rank in range(4):
                for h in range(src.shape[1]):
                    at = (src.shape[1] * rank + h) * size
                    dst[t // 3, t % 3, at : at + size, :] = src[rank, h, t].astype(F32)

        for t in range(src.shape[2]):
            tap(t)
            store = pltpu.make_async_copy(dst.at[t // 3, t % 3], outs[k].at[t // 3, t % 3], sems.at[9 + k])
            store.start()

    def block():
        made[0][...] = exact(po[...], held[0][...])

    def images():
        half = held[1].shape[0] // 2
        for a in range(2):
            value = exact(pi[...], held[1][a * half : (a + 1) * half, :])
            value = value.reshape(-1, *made[1].shape[2:])
            rows = made[1].shape[1] // 2
            for at in range(value.shape[0]):
                made[1][at // rows, 2 * (at % rows) + a] = value[at]

    for k in ORDER:
        loads[k].wait()
        if k == 0:
            block()
        elif k == 1:
            images()
        elif k in (3, 7):
            taps_of(k)
        else:
            rows_of(k)
        if k not in (3, 7):
            stores[k].start()
    for copy in stores:
        copy.wait()


def solution(mesh):
    in_specs = (
        P("batch", None, None, "chan"),
        P(),
        P(),
        P(None, "chan"),
        P(None, None, None, "chan"),
        P(None, "chan"),
        P(None, "chan"),
        P(None, "chan"),
        P(None, None, None, "chan"),
        P(None, "chan"),
        P(None, "chan"),
        P(None, "chan"),
        P(None, "chan"),
        P(None, "chan"),
        P("batch", None, None, "chan"),
    )
    out_specs = (
        P("batch", None, None, "chan"),
        P("batch", None, None, "chan"),
        P(None, "chan"),
        P(None, None, None, "chan"),
        P(None, "chan"),
        P(None, "chan"),
        P(None, "chan"),
        P(None, None, None, "chan"),
        P(None, "chan"),
        P(None, "chan"),
        P(None, "chan"),
        P(None, "chan"),
        P(None, "chan"),
        P(None, "chan"),
        P(None, "chan"),
        P(None, "chan"),
        P(None, "chan"),
    )
    fused = mesh.shape["chan"] == 4 and mesh.shape["batch"] == 8
    return jax.shard_map(
        fused_on_device if fused else on_device, mesh=mesh, in_specs=in_specs, out_specs=out_specs, check_vma=False
    )
```

```python
import functools
import math
import types

import jax
import jax.numpy as jnp
import ml_dtypes
import numpy as np
from jax import lax
from jax.experimental import pallas as pl
from jax.experimental.pallas import tpu as pltpu
from jax.sharding import PartitionSpec as P

EPS = 1e-05
VMEM_LIMIT = 60 * 1024 * 1024


def shortened(shard):
    return jax.tree.map(lambda a: a.astype(jnp.bfloat16) if a.dtype == jnp.float32 else a, shard)


def frame_masks(heights, widths, rows, cols):
    tall = heights[:, None, None]
    broad = widths[:, None, None]
    row_in = jnp.arange(2 * rows, dtype=jnp.int32)[None, :, None]
    col_in = jnp.arange(2 * cols, dtype=jnp.int32)[None, None, :]
    row_out = jnp.arange(rows, dtype=jnp.int32)[None, :, None]
    col_out = jnp.arange(cols, dtype=jnp.int32)[None, None, :]
    inner = ((row_in < 2 * tall) & (col_in < 2 * broad)).astype(jnp.float32)[..., None]
    outer = ((row_out < tall) & (col_out < broad)).astype(jnp.float32)[..., None]
    return (inner, outer)


def silu_slope(value):
    sig = jax.nn.sigmoid(value)
    return sig * (1.0 + value * (1.0 - sig))


def convolve(source, kernel, stride, rows, cols):
    taps = kernel.shape[0]
    margin = taps // 2
    padded = jnp.pad(source, ((0, 0), (margin, margin), (margin, margin), (0, 0)))
    total = None
    for top in range(taps):
        for left in range(taps):
            window = padded[
                :, top : top + stride * rows : stride, left : left + stride * cols : stride, :
            ]
            term = jnp.einsum(
                "nhwc,cd->nhwd", window, kernel[top, left], preferred_element_type=jnp.float32
            )
            total = term if total is None else total + term
    return total


def kernel_grad(source, grad, stride, taps):
    rows, cols = (grad.shape[1], grad.shape[2])
    margin = taps // 2
    padded = jnp.pad(source, ((0, 0), (margin, margin), (margin, margin), (0, 0)))
    return jnp.stack(
        [
            jnp.stack(
                [
                    jnp.einsum(
                        "nhwc,nhwd->cd",
                        padded[
                            :,
                            top : top + stride * rows : stride,
                            left : left + stride * cols : stride,
                            :,
                        ],
                        grad,
                        preferred_element_type=jnp.float32,
                    )
                    for left in range(taps)
                ]
            )
            for top in range(taps)
        ]
    )


def spread_back(grad, kernel, stride):
    taps = kernel.shape[0]
    margin = taps // 2
    total = None
    for top in range(taps):
        for left in range(taps):
            term = jnp.einsum(
                "nhwd,cd->nhwc", grad, kernel[top, left], preferred_element_type=jnp.float32
            )
            placed = lax.pad(
                term,
                jnp.float32(0.0),
                (
                    (0, 0, 0),
                    (top, 2 * margin - top + stride - 1, stride - 1),
                    (left, 2 * margin - left + stride - 1, stride - 1),
                    (0, 0, 0),
                ),
            )
            total = placed if total is None else total + placed
    rows, cols = (grad.shape[1], grad.shape[2])
    return total[:, margin : margin + stride * rows, margin : margin + stride * cols, :]


def norm_forward(pre, mask, count, gain, bias):
    mean = lax.psum(jnp.sum(pre * mask, axis=(0, 1, 2)), "batch") / count
    centered = (pre - mean) * mask
    spread = lax.psum(jnp.sum(centered * centered, axis=(0, 1, 2)), "batch") / count
    inv = lax.rsqrt(spread + EPS)
    hat = (pre - mean) * inv
    return (hat * gain + bias, hat, inv, mean, spread)


def norm_backward(grad, hat, mask, count, gain, inv):
    masked = grad * mask
    bias_grad, gain_grad = lax.psum(
        (jnp.sum(masked, axis=(0, 1, 2)), jnp.sum(masked * hat, axis=(0, 1, 2))), "batch"
    )
    pre_grad = mask * gain * inv * (grad - (bias_grad + hat * gain_grad) / count)
    return (pre_grad.astype(jnp.bfloat16), gain_grad, bias_grad)


def widen(feature):
    return lax.all_gather(feature, "chan", axis=3, tiled=True)


def input_grad(grad, kernel, stride):
    return jax.tree.map(
        lambda part: part.astype(jnp.float32),
        lax.psum_scatter(
            shortened(spread_back(grad, kernel, stride)), "chan", scatter_dimension=3, tiled=True
        ),
    )


def image_back(grad_one, grad_side, kernels):
    summands = spread_back(grad_one, kernels[0], 1) + spread_back(grad_side, kernels[3], 2)
    return lax.psum_scatter(
        summands.astype(jnp.bfloat16), "chan", scatter_dimension=3, tiled=True
    ).astype(jnp.float32)


def on_device(
    images,
    heights,
    widths,
    reduce_first,
    spatial_first,
    expand_first,
    shortcut,
    reduce_second,
    spatial_second,
    expand_second,
    gain_mid,
    bias_mid,
    gain_out,
    bias_out,
    cotangent,
):
    local = images.shape[0]
    rows, cols = (cotangent.shape[1], cotangent.shape[2])
    offset = lax.axis_index("batch") * local
    inner, outer = frame_masks(
        lax.dynamic_slice_in_dim(heights, offset, local),
        lax.dynamic_slice_in_dim(widths, offset, local),
        rows,
        cols,
    )
    count_out = jnp.sum(heights * widths).astype(jnp.float32)
    count_in = 4.0 * count_out
    kernels = (
        reduce_first[None, None],
        spatial_first,
        expand_first[None, None],
        shortcut[None, None],
        reduce_second[None, None],
        spatial_second,
        expand_second[None, None],
    )
    source = images * inner.astype(jnp.bfloat16)
    whole_source = lax.all_gather(source, "chan", axis=3, tiled=True)
    pre_one = convolve(whole_source, kernels[0], 1, 2 * rows, 2 * cols)
    normed_one, hat_one, inv_one, mean_one, spread_one = norm_forward(
        pre_one, inner, count_in, gain_mid[0], bias_mid[0]
    )
    whole_one = widen((jax.nn.silu(normed_one) * inner).astype(jnp.bfloat16))
    pre_two = convolve(whole_one, kernels[1], 2, rows, cols)
    normed_two, hat_two, inv_two, mean_two, spread_two = norm_forward(
        pre_two, outer, count_out, gain_mid[1], bias_mid[1]
    )
    whole_two = widen((jax.nn.silu(normed_two) * outer).astype(jnp.bfloat16))
    pre_three = convolve(whole_two, kernels[2], 1, rows, cols)
    normed_three, hat_three, inv_three, mean_three, spread_three = norm_forward(
        pre_three, outer, count_out, gain_out[0], bias_out[0]
    )
    pre_side = convolve(whole_source, kernels[3], 2, rows, cols)
    normed_side, hat_side, inv_side, mean_side, spread_side = norm_forward(
        pre_side, outer, count_out, gain_out[1], bias_out[1]
    )
    block_mid = jax.nn.silu(normed_three + normed_side) * outer
    whole_mid = widen(block_mid.astype(jnp.bfloat16))
    pre_four = convolve(whole_mid, kernels[4], 1, rows, cols)
    normed_four, hat_four, inv_four, mean_four, spread_four = norm_forward(
        pre_four, outer, count_out, gain_mid[2], bias_mid[2]
    )
    whole_four = widen((jax.nn.silu(normed_four) * outer).astype(jnp.bfloat16))
    pre_five = convolve(whole_four, kernels[5], 1, rows, cols)
    normed_five, hat_five, inv_five, mean_five, spread_five = norm_forward(
        pre_five, outer, count_out, gain_mid[3], bias_mid[3]
    )
    whole_five = widen((jax.nn.silu(normed_five) * outer).astype(jnp.bfloat16))
    pre_six = convolve(whole_five, kernels[6], 1, rows, cols)
    normed_six, hat_six, inv_six, mean_six, spread_six = norm_forward(
        pre_six, outer, count_out, gain_out[2], bias_out[2]
    )
    result = jax.nn.silu(normed_six + block_mid) * outer
    grad_sum_b = cotangent.astype(jnp.float32) * outer * silu_slope(normed_six + block_mid)
    grad_six, gain_six, bias_six = norm_backward(
        grad_sum_b, hat_six, outer, count_out, gain_out[2], inv_six
    )
    kern_six = kernel_grad(whole_five, grad_six, 1, 1)
    grad_feat_five = input_grad(grad_six, kernels[6], 1)
    grad_five, gain_five, bias_five = norm_backward(
        grad_feat_five * outer * silu_slope(normed_five),
        hat_five,
        outer,
        count_out,
        gain_mid[3],
        inv_five,
    )
    kern_five = kernel_grad(whole_four, grad_five, 1, 3)
    grad_feat_four = input_grad(grad_five, kernels[5], 1)
    grad_four, gain_four, bias_four = norm_backward(
        grad_feat_four * outer * silu_slope(normed_four),
        hat_four,
        outer,
        count_out,
        gain_mid[2],
        inv_four,
    )
    kern_four = kernel_grad(whole_mid, grad_four, 1, 1)
    grad_mid = grad_sum_b + input_grad(grad_four, kernels[4], 1)
    grad_sum_a = grad_mid * outer * silu_slope(normed_three + normed_side)
    grad_three, gain_three, bias_three = norm_backward(
        grad_sum_a, hat_three, outer, count_out, gain_out[0], inv_three
    )
    grad_side, gain_side, bias_side = norm_backward(
        grad_sum_a, hat_side, outer, count_out, gain_out[1], inv_side
    )
    kern_three = kernel_grad(whole_two, grad_three, 1, 1)
    kern_side = kernel_grad(whole_source, grad_side, 2, 1)
    grad_feat_two = input_grad(grad_three, kernels[2], 1)
    grad_two, gain_two, bias_two = norm_backward(
        grad_feat_two * outer * silu_slope(normed_two),
        hat_two,
        outer,
        count_out,
        gain_mid[1],
        inv_two,
    )
    kern_two = kernel_grad(whole_one, grad_two, 2, 3)
    grad_feat_one = input_grad(grad_two, kernels[1], 2)
    grad_one, gain_one, bias_one = norm_backward(
        grad_feat_one * inner * silu_slope(normed_one),
        hat_one,
        inner,
        count_in,
        gain_mid[0],
        inv_one,
    )
    kern_one = kernel_grad(whole_source, grad_one, 1, 1)
    images_grad = image_back(grad_one, grad_side, kernels) * inner
    summed = (
        lax.psum(kern_one.astype(jnp.bfloat16), "batch").astype(jnp.float32),
        lax.psum(kern_two.astype(jnp.bfloat16), "batch").astype(jnp.float32),
        lax.psum(kern_three.astype(jnp.bfloat16), "batch").astype(jnp.float32),
        lax.psum(kern_side.astype(jnp.bfloat16), "batch").astype(jnp.float32),
        lax.psum(kern_four.astype(jnp.bfloat16), "batch").astype(jnp.float32),
        lax.psum(kern_five.astype(jnp.bfloat16), "batch").astype(jnp.float32),
        lax.psum(kern_six.astype(jnp.bfloat16), "batch").astype(jnp.float32),
    )
    counts_mid = jnp.stack([count_in, count_out, count_out, count_out])[:, None]
    mean_mid_batch = jnp.stack([mean_one, mean_two, mean_four, mean_five])
    var_mid_batch = (
        jnp.stack([spread_one, spread_two, spread_four, spread_five])
        * counts_mid
        / (counts_mid - 1.0)
    )
    mean_out_batch = jnp.stack([mean_three, mean_side, mean_six])
    var_out_batch = (
        jnp.stack([spread_three, spread_side, spread_six]) * count_out / (count_out - 1.0)
    )
    return (
        result,
        images_grad,
        summed[0][0, 0],
        summed[1],
        summed[2][0, 0],
        summed[3][0, 0],
        summed[4][0, 0],
        summed[5],
        summed[6][0, 0],
        jnp.stack([gain_one, gain_two, gain_four, gain_five]),
        jnp.stack([bias_one, bias_two, bias_four, bias_five]),
        jnp.stack([gain_three, gain_side, gain_six]),
        jnp.stack([bias_three, bias_side, bias_six]),
        mean_mid_batch,
        var_mid_batch,
        mean_out_batch,
        var_out_batch,
    )


MESH = pl.DeviceIdType.MESH
BF = jnp.bfloat16
F32 = jnp.float32


def flip(value, bit):
    return value + bit - 2 * bit * lax.rem(lax.div(value, bit), 2)


def gate(value):
    return 0.5 * jnp.tanh(0.5 * value) + 0.5


def tree(parts):
    while len(parts) > 1:
        parts = [parts[k] + parts[k + 1] for k in range(0, len(parts), 2)]
    return parts[0]


def wide_row(block):
    return jnp.concatenate([block[j : j + 1] for j in range(block.shape[0])], axis=1)


def fold(value):
    return jnp.sum(value.reshape(value.shape[0] // 8, 8, value.shape[1]), axis=0)


def mm(a, b):
    return jnp.dot(a, b, preferred_element_type=F32)


def mm_nt(a, b):
    return lax.dot_general(a, b, (((1,), (1,)), ((), ())), preferred_element_type=F32)


def mm_tn(a, b):
    return lax.dot_general(a, b, (((0,), (0,)), ((), ())), preferred_element_type=F32)


class Traffic:
    def __init__(self, sems):
        self.sems, self.used, self.sent = sems, 0, []

    def take(self):
        self.used += 1
        assert self.used <= SEMS
        return self.sems.at[self.used - 1]

    def plan(self, src, dst, device, send_sem=None, recv_sem=None):
        return pltpu.make_async_remote_copy(
            src_ref=src,
            dst_ref=dst,
            send_sem=self.take() if send_sem is None else send_sem,
            recv_sem=self.take() if recv_sem is None else recv_sem,
            device_id=device,
            device_id_type=MESH,
        )

    def spread(self, src, dst, peers, all_of):
        sems = self.take(), self.take()
        copies = [self.plan(a, d, p, *sems) for a, d, p in zip(src, dst, peers)]
        return copies, self.plan(all_of, all_of, peers[0], *sems)

    def push(self, src, dst, device):
        copy = self.plan(src, dst, device)
        copy.start()
        self.sent.append(copy)
        return copy

    def plan_local(self, src, dst, sem=None):
        return pltpu.make_async_copy(src, dst, self.take() if sem is None else sem)

    def local(self, src, dst):
        copy = self.plan_local(src, dst)
        copy.start()
        return copy

    def load(self, pairs, all_of):
        sem = self.take()
        for src, dst in pairs:
            pltpu.make_async_copy(src, dst, sem).start()
        return pltpu.make_async_copy(all_of, all_of, sem)


class Summed:
    def __init__(self, net, part, got, done, ring, spill, across=None):
        at, ahead, behind = ring
        self.part, self.got, self.done, self.at = part, got, done, at
        self.spill, self.spill_wait = spill
        legs, legs_back = net.take(), net.take()
        up = [part.at[at(4)]] + [got.at[k] for k in range(4)]
        down = [part.at[at(-3)]] + [got.at[k] for k in range(4, 7)]
        self.out = [
            [net.plan(up[k], up[k + 1], ahead, legs)]
            + ([net.plan(down[k], down[k + 1], behind, legs)] if k < 3 else [])
            for k in range(4)
        ]
        self.back = [
            ([net.plan(done.at[at(-k)], done.at[at(-k)], ahead, legs_back)] if k < 3 else [])
            + [net.plan(done.at[at(k)], done.at[at(k)], behind, legs_back)]
            for k in range(4)
        ]
        self.left = [
            net.plan(got, got, ahead, legs, legs),
            net.plan(done.at[pl.ds(0, 7)], done.at[pl.ds(0, 7)], ahead, legs_back, legs_back),
        ]
        self.across = across is not None
        if self.across:
            self.crossing = net.plan(got.at[3, 1], done.at[at(0), 1], across)
            self.left.append(self.crossing)
        self.todo = [self.begin] + [functools.partial(self.add, k) for k in range(3)]
        self.todo += [self.finish] + ([self.crossed] if self.across else [])
        self.todo += [functools.partial(self.pass_on, k) for k in range(3)] + [self.last]

    def step(self):
        self.todo.pop(0)()

    def start(self, copies):
        for copy in copies:
            copy.start()

    def arrived(self, copies):
        for copy in copies:
            copy.wait_recv()

    def begin(self):
        self.start(self.out[0])

    def add(self, k):
        self.arrived(self.out[k])
        self.got[k] = self.got[k] + self.part[self.at(3 - k)]
        if k < 2:
            self.got[4 + k] = self.got[4 + k] + self.part[self.at(k - 2)]
        self.start(self.out[k + 1])

    def finish(self):
        self.arrived(self.out[3])
        total = self.got[3] + self.got[6] + self.part[self.at(0)]
        if self.across:
            self.done[self.at(0), 0] = total[0]
            self.got[3, 1] = total[1]
            self.crossing.start()
        else:
            self.done[self.at(0)] = total
            self.start(self.back[0])

    def crossed(self):
        self.crossing.wait_recv()
        self.start(self.back[0])

    def pass_on(self, k):
        self.arrived(self.back[k])
        self.start(self.back[k + 1])

    def last(self):
        self.arrived(self.back[3])
        self.start(self.spill)

    def drain(self):
        for copy in self.left:
            copy.wait_send()
        self.spill_wait.wait()


class Direct:
    def __init__(self, net, part, got, done, place, peers, spill, across):
        self.part, self.got, self.done, self.place = part, got, done, place
        self.spill, self.spill_wait = spill
        n = len(peers)
        self.out, self.whole = net.spread(
            [part.at[peer[0]] for peer in peers],
            [got.at[k] for k in range(n)],
            peers,
            got.at[pl.ds(0, n)],
        )
        self.back, self.whole_back = net.spread(
            [done.at[place]] * n, [done.at[place]] * n, peers, done.at[pl.ds(0, n)]
        )
        self.crossing = net.plan(got.at[n, 1], done.at[place, 1], across)
        self.todo = [self.begin, self.finish, self.crossed, self.last]

    def step(self):
        self.todo.pop(0)()

    def begin(self):
        for copy in self.out:
            copy.start()

    def finish(self):
        total = self.part[self.place].astype(F32)
        self.whole.wait_recv()
        for k in range(len(self.out)):
            total = total + self.got[k].astype(F32)
        self.done[self.place, 0] = total[0].astype(BF)
        self.got[len(self.out), 1] = total[1].astype(BF)
        self.crossing.start()

    def crossed(self):
        self.crossing.wait_recv()
        for copy in self.back:
            copy.start()

    def last(self):
        self.whole_back.wait_recv()
        for copy in self.spill:
            copy.start()

    def drain(self):
        for copy in (self.whole, self.whole_back, self.crossing):
            copy.wait_send()
        self.spill_wait.wait()


SEMS = 356


def block_kernel(geo, names, *refs):
    g = types.SimpleNamespace(**dict(zip(names, refs)))
    R, QS, PS = geo.R, geo.QS, geo.PS
    CI, MI, CO = geo.CI, geo.MI, geo.CO
    NB = geo.NB
    r = lax.axis_index("chan")
    b = lax.axis_index("batch")
    r1, r2 = flip(r, 1), flip(r, 2)
    r3 = flip(r1, 2)
    ranks = (r, r1, r2, r3)
    core, far = (b, r1), (b, r2)
    peers = []
    for k in range(1, NB):
        other = b
        bit = 1
        while bit < NB:
            if k & bit:
                other = flip(other, bit)
            bit *= 2
        peers.append((other, r))
    net = Traffic(g.sems)
    def seat(batch):
        x, z = lax.rem(batch, 2), lax.div(batch, 2)
        return z + x * (7 - 2 * z)

    def batch_at(place):
        x = lax.div(place, 4)
        return 2 * (place + x * (7 - 2 * place)) + x

    way = 1 - 2 * lax.rem(r, 2)
    places = {k: lax.rem(seat(b) + way * k + 16, 8) for k in range(-3, 5)}
    ring = (places.get, (batch_at(places[1]), r), (batch_at(places[-1]), r))

    bar = pltpu.get_barrier_semaphore()
    everyone = [core, far] + peers
    for device in everyone:
        pl.semaphore_signal(bar, 1, device_id=device, device_id_type=MESH)

    def everywhere(src, dst, all_of):
        copies, whole = net.spread(src, dst, peers, all_of)
        for copy in copies:
            copy.start()
        net.sent.append(whole)
        return whole

    def rows_of(ref, rank, size):
        return ref.at[pl.ds(pl.multiple_of(rank * size, size), size)]

    def taps_of(ref, rank, size):
        return ref.at[:, pl.ds(pl.multiple_of(rank * size, size), size), :]

    ld_img = net.local(g.img, g.IMG)
    ld_w1 = [
        net.local(rows_of(g.w1, rank, CI), g.W1C.at[pl.ds(s * CI, CI), pl.ds(MI, MI)])
        for s, rank in enumerate((r, r1))
    ]

    area = [g.heights[k] * g.widths[k] for k in range(NB * PS)]
    first = lax.broadcasted_iota(jnp.int32, (R, 128), 0)

    def of_image(ref, image):
        value = jnp.full(image.shape, ref[b * PS], jnp.int32)
        for k in range(1, PS):
            value = jnp.where(image == k, ref[b * PS + k], value)
        return value

    def pixel(m):
        image, row, column = lax.rem(m, PS), lax.rem(lax.div(m, PS), geo.rows), lax.div(m, QS)
        good = (row < of_image(g.heights, image)) & (column < of_image(g.widths, image))
        return column, row, image, good

    g.mask[...] = jnp.where(pixel(first)[3], 1.0, 0.0)

    def row(scalar):
        return jnp.full((1, 128), scalar.astype(F32), F32)

    for k in range(NB):
        other = b if k == 0 else peers[k - 1][0]
        own = 0
        for j in range(PS):
            own = own + g.heights[other * PS + j] * g.widths[other * PS + j]
        g.aux[k : k + 1, :] = row(own)
        g.aux[NB + k : NB + k + 1, :] = 1.0 / row(own)
    count = row(sum(area))
    g.aux[16:17, :] = 1.0 / count
    g.aux[17:18, :] = count / (count - 1.0)
    g.aux[18:19, :] = 4.0 * count / (4.0 * count - 1.0)

    ld_img.wait()
    lane = lax.broadcasted_iota(jnp.int32, (R, 4 * R), 1)
    column, line, image, good = pixel(lax.broadcasted_iota(jnp.int32, (R, 1), 0))
    corner = image * 4 * geo.rows * geo.cols + 2 * line * 2 * geo.cols + 2 * column
    for ph in range(4):
        source = jnp.where(good, corner + (ph // 2) * 2 * geo.cols + ph % 2, -1)
        pick = jnp.where(lane == source, 1.0, 0.0).astype(BF)
        g.SRC[0, ph * R : (ph + 1) * R, :] = mm(pick, g.IMG[...]).astype(BF)

    pl.semaphore_wait(bar, len(everyone))

    rm_src = net.push(g.SRC.at[0], g.SRC.at[1], core)
    rm_w1 = [
        net.push(rows_of(g.w1, rank, CI), g.W1C.at[pl.ds(s * CI, CI), pl.ds(0, MI)], far)
        for s, rank in enumerate((r2, r3))
    ]
    piece = MI // 4
    rank = jnp.where(b < 4, r2, r3)
    at = pl.multiple_of(rank * MI + lax.rem(b, 4) * piece, piece)
    rm_w2 = net.push(g.w2.at[:, pl.ds(at, piece), :], g.W2F.at[b], far)
    ld_sc = net.load([(rows_of(g.wsc, rank, CI), g.WS.at[s]) for s, rank in enumerate(ranks)], g.WS)
    ld_w2 = net.load([(taps_of(g.w2, rank, MI), g.W2.at[:, s]) for s, rank in enumerate((r, r1))], g.W2)
    ld_w3 = net.load([(rows_of(g.w3, rank, MI), g.W3.at[s]) for s, rank in enumerate(ranks)], g.W3)
    ld_w4 = [
        net.local(rows_of(g.w4, rank, CO), g.W4C.at[pl.ds(s * CO, CO), pl.ds(MI, MI)])
        for s, rank in enumerate((r, r1))
    ]
    ld_w5 = net.load([(taps_of(g.w5, rank, MI), g.W5.at[:, s]) for s, rank in enumerate(ranks)], g.W5)
    ld_w6 = net.load([(rows_of(g.w6, rank, MI), g.W6.at[s]) for s, rank in enumerate(ranks)], g.W6)
    ld_cot = net.local(g.cot, g.COT)

    for ph in (1, 3):
        for s in range(2):
            g.F1[s, ph, 0:QS, :] = jnp.zeros((QS, MI), BF)
    for s in range(2):
        g.D1[1, s, 0:QS, :] = jnp.zeros((QS, MI), BF)
    for s in range(4):
        g.F4[s, 0:QS, :] = jnp.zeros((QS, MI), BF)
        g.F4[s, QS + R :, :] = jnp.zeros((QS, MI), BF)
        for d in range(2):
            g.D4[d, s, 0:QS, :] = jnp.zeros((QS, MI), BF)
            g.D4[d, s, QS + R :, :] = jnp.zeros((QS, MI), BF)
    for d in range(3):
        for s in range(2):
            g.E5[d, s, 0:QS, :] = jnp.zeros((QS, MI), BF)
            g.E5[d, s, QS + R :, :] = jnp.zeros((QS, MI), BF)
    for d in range(2):
        for s in range(4):
            g.E2[d, s, R:, :] = jnp.zeros((QS, MI), BF)

    for copy in ld_w1:
        copy.wait()
    rm_src.wait_recv()
    for copy in rm_w1:
        copy.wait_recv()
    rm_p1 = []
    for ph in range(4):
        span = slice(ph * R, (ph + 1) * R)
        both = jnp.concatenate([g.SRC[0, span, :], g.SRC[1, span, :]], axis=1)
        part = mm(both, g.W1C[...])
        g.P1S[ph] = part[:, :MI].astype(BF)
        rm_p1.append(net.push(g.P1S.at[ph], g.P1R.at[ph], far))
        g.PRE1[span, :] = part[:, MI:]

    rm_w2.wait_recv()
    rm_w2s = everywhere([g.W2F.at[b]] * (NB - 1), [g.W2F.at[b]] * (NB - 1), g.W2F.at[pl.ds(0, NB - 1)])

    rm_back = []
    for s, rank in enumerate((r1, r3)):
        rm_back.append(net.push(rows_of(g.w6, rank, MI), g.W6P.at[s], core))
        rm_back.append(net.push(taps_of(g.w5, rank, MI), g.W5P.at[:, s], core))
        rm_back.append(net.push(rows_of(g.w3, rank, MI), g.W3P.at[s], core))
        rm_back.append(net.push(rows_of(g.wsc, rank, CI), g.WSP.at[s], core))
    rm_back.append(net.push(taps_of(g.w2, r1, MI), g.W2P, core))
    rm_back.append(net.push(rows_of(g.w4, r1, CO), g.W4P.at[0], core))
    rm_back.append(net.push(rows_of(g.w1, r1, CI), g.W1P.at[0], core))
    rm_back.append(
        net.push(g.W1C.at[pl.ds(CI, CI), pl.ds(0, MI)], g.W1P.at[1], core)
    )

    aux = g.aux
    inv_out = aux[16:17, :]
    unb_out, unb_in = aux[17:18, :], aux[18:19, :]

    def mask_rows(at, size):
        return g.mask[pl.ds(at, size), :]

    def over(total, size, body, init):
        def step(i, carry):
            return body(pl.multiple_of(i * size, size), carry)

        return lax.fori_loop(0, total // size, step, init)

    NCH = 128 if R % 128 == 0 else QS
    WCH = QS

    def bc(mask, width):
        return jnp.concatenate([mask] * (width // 128), axis=1)

    def exchange(slots, payload_rows):
        others = range(1, NB)
        return everywhere(
            [slots.at[0] for _ in others],
            [slots.at[k] for k in others],
            slots.at[pl.ds(1, NB - 1)],
        )

    def narrow_local(pre, phases, prepare=None):
        total = jnp.zeros((8, MI), F32)
        for ph in range(phases):
            if prepare is not None:
                prepare(ph)

            def add(at, acc, ph=ph):
                return acc + fold(pre[pl.ds(ph * R + at, NCH), :] * mask_rows(at, NCH))

            total = over(R, NCH, add, total)
        total = jnp.sum(total, axis=0, keepdims=True)
        mean = total * (aux[8:9, :] * (1.0 / phases))
        squares = jnp.zeros((8, MI), F32)
        for ph in range(phases):

            def add2(at, acc, ph=ph):
                d = (pre[pl.ds(ph * R + at, NCH), :] - mean) * mask_rows(at, NCH)
                return acc + fold(d * d)

            squares = over(R, NCH, add2, squares)
        return total, jnp.sum(squares, axis=0, keepdims=True)

    def narrow_send(idx, first, second):
        slots = g.SN.at[idx]
        g.SN[idx, 0, 0:1, :] = first
        g.SN[idx, 0, 1:2, :] = second
        return exchange(slots, 2)

    def narrow_merge(idx, copies, phases):
        copies.wait_recv()
        sums = [g.SN[idx, k, 0:1, :] for k in range(NB)]
        squares = [g.SN[idx, k, 1:2, :] for k in range(NB)]
        return moments(sums, squares, phases)

    def moments(sums, squares, phases):
        inv_count = inv_out * (1.0 / phases)
        mean = tree(list(sums)) * inv_count
        terms = []
        for k in range(NB):
            d = sums[k] * (aux[8 + k : 9 + k, :] * (1.0 / phases)) - mean
            terms.append(squares[k] + aux[k : k + 1, :] * float(phases) * d * d)
        spread = tree(terms) * inv_count
        return mean, spread

    def wide_local(pre):
        def add(at, acc):
            m = bc(mask_rows(at, WCH), CO)
            return acc + fold(pre[pl.ds(at, WCH), :] * m)

        total = jnp.sum(over(R, WCH, add, jnp.zeros((8, CO), F32)), axis=0, keepdims=True)
        mean = total * bc(aux[8:9, :], CO)

        def add2(at, acc):
            m = bc(mask_rows(at, WCH), CO)
            d = (pre[pl.ds(at, WCH), :] - mean) * m
            return acc + fold(d * d)

        squares = jnp.sum(over(R, WCH, add2, jnp.zeros((8, CO), F32)), axis=0, keepdims=True)
        return total, squares

    NW = CO // 128

    def wide_put(slots, row, value):
        for j in range(NW):
            slots[0, row + j : row + j + 1, :] = value[:, j * 128 : (j + 1) * 128]

    def wide_send(idx, first, second):
        slots = g.SW.at[idx]
        wide_put(slots, 0, first)
        wide_put(slots, NW, second)
        return exchange(slots, 2 * NW)

    def wide_merge(idx, copies):
        copies.wait_recv()
        sums = [g.SW[idx, k, 0:NW, :] for k in range(NB)]
        squares = [g.SW[idx, k, NW : 2 * NW, :] for k in range(NB)]
        mean, spread = moments(sums, squares, 1)
        return wide_row(mean), wide_row(spread)

    def gather(buf, at, size):
        here = [buf(s).at[pl.ds(at, size)] for s in range(4)]
        near = net.push(here[0], here[1], core)
        away = net.push(here[0], here[2], far)
        return [near, away, here]

    def relay(chunk):
        near, away, here = chunk
        away.wait_recv()
        chunk.append(net.push(here[2], here[3], core))

    def landed(chunk):
        chunk[0].wait_recv()
        chunk[3].wait_recv()

    def lanes(parts):
        return jnp.concatenate(parts, axis=1)

    place = lax.broadcasted_iota(jnp.int32, (QS, 128), 0)
    keep_down = place >= PS
    keep_up = place < QS - PS

    def shifted(value, step):
        if step < 0:
            return jnp.where(keep_down, pltpu.roll(value, PS, 0), 0.0)
        return jnp.where(keep_up, pltpu.roll(value, QS - PS, 0), 0.0)

    def take_p1(ph):
        rm_p1[ph].wait_recv()

        def add(at, carry):
            rows = pl.ds(ph * R + at, NCH)
            g.PRE1[rows, :] = g.PRE1[rows, :] + g.P1R[ph, pl.ds(at, NCH), :].astype(F32)
            return carry

        over(R, NCH, add, 0)

    sum_one, sq_one = narrow_local(g.PRE1, 4, take_p1)
    st_one = narrow_send(0, sum_one, sq_one)
    rm_xs = net.push(g.SRC.at[0, pl.ds(0, R)], g.XS.at[0], far)

    def scale_of(spread, gain):
        inv = lax.rsqrt(spread + EPS)
        return inv, inv * gain

    mean_one, spread_one = narrow_merge(0, st_one, 4)
    inv_one, scale_one = scale_of(spread_one, g.gm[0:1, :])

    def narrow_feature(pre, mean, scale, bias, out, ph, at0):
        def body(at, carry):
            v = (pre[pl.ds(ph * R + at, NCH), :] - mean) * scale + bias
            out[pl.ds(at0 + at, NCH), :] = (v * gate(v) * mask_rows(at, NCH)).astype(BF)
            return carry

        over(R, NCH, body, 0)

    ch_one = []
    for ph in range(4):
        narrow_feature(
            g.PRE1, mean_one, scale_one, g.bm[0:1, :], g.F1.at[0, ph], ph, QS
        )
        span = pl.ds(QS, R)
        ch_one.append(net.push(g.F1.at[0, ph, span], g.F1.at[1, ph, span], core))

    def taking(copy, pre, got):
        def take(ph):
            copy.wait_recv()

            def add(at, carry):
                rows = pl.ds(at, NCH)
                pre[rows, :] = pre[rows, :] + got[rows, :].astype(F32)
                return carry

            over(R, NCH, add, 0)

        return take

    rm_xs.wait_recv()
    rm_xs2 = net.push(g.XS.at[0], g.XS.at[1], core)
    ld_sc.wait()
    rm_xs2.wait_recv()

    def strided():
        return [g.SRC[0, 0:R, :], g.SRC[1, 0:R, :], g.XS[0], g.XS[1]]

    pre_side = None
    for s, block in enumerate(strided()):
        term = mm(block, g.WS[s])
        pre_side = term if pre_side is None else pre_side + term
    g.PRES[...] = pre_side
    st_side = wide_send(0, *wide_local(g.PRES))

    ld_w2.wait()

    def chip_one(s, ph, down, left):
        rows = slice(0, R) if left else slice(QS, QS + R)
        return g.D1[ph - 2, s, rows, :] if down else g.F1[s, ph, rows, :]

    def far_two(tap, first):
        return jnp.concatenate([g.W2F[first + k, tap] for k in range(4)], axis=0)

    def both_two(tap):
        near = jnp.concatenate([g.W2[tap, s] for s in range(2)], axis=0)
        away = jnp.concatenate([far_two(tap, 0), far_two(tap, 4)], axis=0)
        return lanes([away, near])

    def taps_two(ph):
        top = (1,) if ph < 2 else (0, 2)
        left = (1,) if ph % 2 == 0 else (0, 2)
        return [(t, l) for t in top for l in left]

    def lower(ph, s):
        def move(at, carry):
            v = g.F1[s, ph, pl.ds(QS + at, QS), :].astype(F32)
            g.D1[ph - 2, s, pl.ds(QS + at, QS), :] = shifted(v, -1).astype(BF)
            return carry

        over(R, QS, move, 0)

    rm_w2s.wait_recv()
    rm_back.append(net.push(g.W2F.at[pl.ds(4, 4)], g.W2Q, core))
    part = None
    for ph in range(4):
        if ph >= 2:
            lower(ph, 0)
        ch_one[ph].wait_recv()
        if ph >= 2:
            lower(ph, 1)
        for t, l in taps_two(ph):
            term = mm(lanes([chip_one(s, ph, t == 0, l == 0) for s in range(2)]), both_two(3 * t + l))
            part = term if part is None else part + term
    g.P2S[...] = part[:, :MI].astype(BF)
    rm_p2 = net.push(g.P2S, g.P2R, far)
    g.PRE2[...] = part[:, MI:]
    rm_w4 = [
        net.push(rows_of(g.w4, rank, CO), g.W4C.at[pl.ds(s * CO, CO), pl.ds(0, MI)], far)
        for s, rank in enumerate((r2, r3))
    ]
    st_two = narrow_send(1, *narrow_local(g.PRE2, 1, taking(rm_p2, g.PRE2, g.P2R)))
    mean_two, spread_two = narrow_merge(1, st_two, 1)
    inv_two, scale_two = scale_of(spread_two, g.gm[1:2, :])
    narrow_feature(g.PRE2, mean_two, scale_two, g.bm[1:2, :], g.F2.at[0], 0, 0)
    ch_two = gather(lambda s: g.F2.at[s], 0, R)
    ld_w3.wait()
    mean_side, spread_side = wide_merge(0, st_side)
    inv_side, scale_side = scale_of(spread_side, g.go[1:2, :])

    def four(ref):
        return lanes([ref[s] for s in range(4)])

    def chip_product(chunk, ref, weight):
        chunk[0].wait_recv()
        value = mm(lanes([ref[0], ref[1]]), weight[0:2].reshape(2 * MI, CO))
        relay(chunk)
        chunk[3].wait_recv()
        return value + mm(lanes([ref[2], ref[3]]), weight[2:4].reshape(2 * MI, CO))

    g.PRE3[...] = chip_product(ch_two, g.F2, g.W3)
    st_three = wide_send(1, *wide_local(g.PRE3))
    mean_three, spread_three = wide_merge(1, st_three)
    inv_three, scale_three = scale_of(spread_three, g.go[0:1, :])
    bias_three, bias_side = g.bo[0:1, :], g.bo[1:2, :]

    def mid_value(rows):
        return (
            (g.PRE3[rows, :] - mean_three) * scale_three
            + bias_three
            + (g.PRES[rows, :] - mean_side) * scale_side
            + bias_side
        )

    def mid_body(at, carry):
        rows = pl.ds(at, WCH)
        v = mid_value(rows)
        out = v * gate(v) * bc(mask_rows(at, WCH), CO)
        g.BM[rows, :] = out
        g.MIDC[0, rows, :] = out.astype(BF)
        return carry

    over(R, WCH, mid_body, 0)
    rm_mid = net.push(g.MIDC.at[0], g.MIDC.at[1], core)

    for copy in ld_w4:
        copy.wait()
    for copy in rm_w4:
        copy.wait_recv()
    rm_back.append(net.push(g.W4C.at[pl.ds(CO, CO), pl.ds(0, MI)], g.W4P.at[1], core))
    rm_mid.wait_recv()
    part = mm(lanes([g.MIDC[0], g.MIDC[1]]), g.W4C[...])
    g.P4S[...] = part[:, :MI].astype(BF)
    rm_p4 = net.push(g.P4S, g.P4R, far)
    g.PRE4[...] = part[:, MI:]

    st_four = narrow_send(2, *narrow_local(g.PRE4, 1, taking(rm_p4, g.PRE4, g.P4R)))
    mean_four, spread_four = narrow_merge(2, st_four, 1)
    inv_four, scale_four = scale_of(spread_four, g.gm[2:3, :])
    narrow_feature(g.PRE4, mean_four, scale_four, g.bm[2:3, :], g.F4.at[0], 0, QS)
    ch_four = gather(lambda s: g.F4.at[s], QS, R)
    ld_w5.wait()

    def kernel_rows(ref, tap, first=0):
        return jnp.concatenate([ref[tap, s] for s in range(first, first + 2)], axis=0)

    def spread_rows(src, dst_up, dst_down):
        def body(at, carry):
            rows = pl.ds(QS + at, QS)
            v = src[rows, :].astype(F32)
            dst_up[rows, :] = shifted(v, -1).astype(BF)
            dst_down[rows, :] = shifted(v, 1).astype(BF)
            return carry

        over(R, QS, body, 0)

    def fill_four(s):
        spread_rows(g.F4.at[s], g.D4.at[0, s], g.D4.at[1, s])

    fill_four(0)
    ch_four[0].wait_recv()
    fill_four(1)

    def four_blocks(t, l, slots):
        rows = slice(l * QS, l * QS + R)
        if t == 1:
            return lanes([g.F4[s, rows, :] for s in slots])
        return lanes([g.D4[t // 2, s, rows, :] for s in slots])

    def whole_four(t, l):
        return four_blocks(t, l, range(4))

    pre_five = None
    for first in (0, 2):
        if first:
            relay(ch_four)
            fill_four(2)
            ch_four[3].wait_recv()
            fill_four(3)
        for t in range(3):
            for l in range(3):
                blocks = four_blocks(t, l, range(first, first + 2))
                term = mm(blocks, kernel_rows(g.W5, 3 * t + l, first))
                pre_five = term if pre_five is None else pre_five + term
    g.PRE5[...] = pre_five
    st_five = narrow_send(3, *narrow_local(g.PRE5, 1))
    mean_five, spread_five = narrow_merge(3, st_five, 1)
    inv_five, scale_five = scale_of(spread_five, g.gm[3:4, :])
    narrow_feature(g.PRE5, mean_five, scale_five, g.bm[3:4, :], g.F5.at[0], 0, 0)
    ch_five = gather(lambda s: g.F5.at[s], 0, R)
    ld_w6.wait()
    ld_cot.wait()
    g.COTP[...] = mm_tn(g.po[...], g.COT[...])
    g.PRE6[...] = chip_product(ch_five, g.F5, g.W6)
    st_six = wide_send(2, *wide_local(g.PRE6))
    mean_six, spread_six = wide_merge(2, st_six)
    inv_six, scale_six = scale_of(spread_six, g.go[2:3, :])
    bias_six = g.bo[2:3, :]

    def last_body(at, carry):
        acc_b, acc_g = carry
        rows = pl.ds(at, WCH)
        m = bc(mask_rows(at, WCH), CO)
        hat = (g.PRE6[rows, :] - mean_six) * inv_six
        v = (g.PRE6[rows, :] - mean_six) * scale_six + bias_six + g.BM[rows, :]
        s = gate(v)
        g.OUT[rows, :] = v * s * m
        grad = g.COTP[rows, :] * m * (s * (1.0 + v * (1.0 - s)))
        g.GSB[rows, :] = grad
        return acc_b + fold(grad), acc_g + fold(grad * hat)

    zero_w = jnp.zeros((8, CO), F32)
    acc_b, acc_g = over(R, WCH, last_body, (zero_w, zero_w))

    def down(value):
        return jnp.sum(value, axis=0, keepdims=True)

    st = wide_send(3, down(acc_b), down(acc_g))

    out_block = net.local(g.OUT, g.block_out)

    def wide_sums(ref, copies, count):
        copies.wait_recv()
        return [
            wide_row(tree([ref[k, j * NW : (j + 1) * NW, :] for k in range(NB)]))
            for j in range(count)
        ]

    def narrow_sums(idx, copies):
        copies.wait_recv()
        return [tree([g.SN[idx, k, j : j + 1, :] for k in range(NB)]) for j in range(2)]

    bsum_six, gsum_six = wide_sums(g.SW.at[3], st, 2)
    inv_wide = bc(inv_out, CO)

    def wide_pre_grad(grad, pre, mean, inv, scale, bsum, gsum, out):
        mb, mg = bsum * inv_wide, gsum * inv_wide

        def body(at, carry):
            rows = pl.ds(at, WCH)
            hat = (pre[rows, :] - mean) * inv
            e = bc(mask_rows(at, WCH), CO) * scale * (grad[rows, :] - (mb + hat * mg))
            out[rows, :] = e.astype(BF)
            return carry

        over(R, WCH, body, 0)

    wide_pre_grad(
        g.GSB, g.PRE6, mean_six, inv_six, scale_six, bsum_six, gsum_six, g.E6.at[0]
    )
    for copy in rm_back:
        copy.wait_recv()

    def swap(ref):
        return net.push(ref.at[0], ref.at[1], core)

    def reduce_back(part, sent, got):
        sent[...] = part[:, MI:].astype(BF)
        return net.push(sent, got, far)

    def wide_back(e, own, other):
        near = lanes([own[0], other[0]])
        away = lanes([own[2], other[1]])
        return mm_nt(lanes([e[0], e[1]]), jnp.concatenate([near, away], axis=0))

    def narrow_back(idx, near, got, copy, phases, pre, mean, inv, scale, bias, order=None):
        acc_b = jnp.zeros((8, MI), F32)
        acc_g = jnp.zeros((8, MI), F32)
        for ph in range(phases):
            if copy is not None:
                copy[ph].wait_recv()

            def body(at, carry, ph=ph):
                b_acc, g_acc = carry
                rows = pl.ds(ph * R + at, NCH)
                hat = (pre[rows, :] - mean) * inv
                v = (pre[rows, :] - mean) * scale + bias
                s = gate(v)
                feat = near[rows, :]
                if got is not None:
                    feat = feat + got[rows, :].astype(F32)
                grad = feat * mask_rows(at, NCH) * (s * (1.0 + v * (1.0 - s)))
                near[rows, :] = grad
                return b_acc + fold(grad), g_acc + fold(grad * hat)

            acc_b, acc_g = over(R, NCH, body, (acc_b, acc_g))
        return narrow_send(idx, down(acc_b), down(acc_g))

    def narrow_pre_grad(grad, pre, mean, inv, scale, bsum, gsum, phases, ph, out, at0):
        inv_count = inv_out * (1.0 / phases)
        mb, mg = bsum * inv_count, gsum * inv_count

        def body(at, carry):
            rows = pl.ds(ph * R + at, NCH)
            hat = (pre[rows, :] - mean) * inv
            e = mask_rows(at, NCH) * scale * (grad[rows, :] - (mb + hat * mg))
            out[pl.ds(at0 + at, NCH), :] = e.astype(BF)
            return carry

        over(R, NCH, body, 0)

    outs = [out_block]

    def give(src, dst):
        outs.append(net.local(src, dst))

    cp = swap(g.E6)
    cp.wait_recv()
    part = wide_back(g.E6, g.W6, g.W6P)
    cp = [reduce_back(part, g.B5S, g.B5R)]
    g.GF5[...] = part[:, :MI]
    def rows_grad(part, value, s):
        half = value.shape[0] // 2
        for h in range(2):
            part[2 * s + h] = value[h * half : (h + 1) * half].astype(BF)

    def taps_grad(part, tap, value):
        half = MI // 2
        for p in range(8):
            part[p, tap] = value[p * half : (p + 1) * half].astype(BF)

    jobs = []

    def spilled(done, targets):
        sem = net.take()
        copies = [net.plan_local(source, place, sem) for source, place in targets]
        return copies, net.plan_local(done, done, sem)

    def job(part, got, done, targets, across=None):
        jobs.append(Summed(net, part, got, done, ring, spilled(done, targets), across))

    def pump(most=3):
        left = sorted((work for work in jobs if work.todo), key=lambda work: -len(work.todo))
        for work in left[:most]:
            work.step()

    def slots_to(part, place):
        return [(part.at[pl.ds(2 * s, 2)], place(ranks[s])) for s in range(4)]

    def chips_to(part, out, taps=None):
        def place(rank):
            return out.at[rank] if taps is None else out.at[rank, :, taps]

        return [
            (part.at[pl.ds(4 * s, 4), v], place(ranks[2 * v + s]))
            for s in range(2)
            for v in range(2)
        ]

    for s in range(4):
        rows_grad(g.K6, mm_tn(g.F5[s], g.E6[0]), s)
    job(g.K6, g.K6R, g.K6D, slots_to(g.K6D, lambda rank: g.k6.at[rank]))
    pump()
    st = narrow_back(
        4, g.GF5, g.B5R, cp, 1, g.PRE5, mean_five, inv_five, scale_five, g.bm[3:4, :]
    )
    pump()
    bsum_five, gsum_five = narrow_sums(4, st)
    narrow_pre_grad(
        g.GF5, g.PRE5, mean_five, inv_five, scale_five, bsum_five, gsum_five, 1, 0,
        g.E5.at[1, 0], QS,
    )
    cp = net.push(g.E5.at[1, 0, pl.ds(QS, R)], g.E5.at[1, 1, pl.ds(QS, R)], core)
    spread_rows(g.E5.at[1, 0], g.E5.at[0, 0], g.E5.at[2, 0])
    cp.wait_recv()
    spread_rows(g.E5.at[1, 1], g.E5.at[0, 1], g.E5.at[2, 1])
    pump()

    def taps_back(own, other, tap):
        near = lanes([own[tap, 0], other[tap, 0]])
        away = lanes([own[tap, 2], other[tap, 1]])
        return jnp.concatenate([near, away], axis=0)

    part = None
    for t in range(3):
        for l in range(3):
            rows = slice((2 - l) * QS, (2 - l) * QS + R)
            e = lanes([g.E5[2 - t, s, rows, :] for s in range(2)])
            term = mm_nt(e, taps_back(g.W5, g.W5P, 3 * t + l))
            part = term if part is None else part + term
    cp = [reduce_back(part, g.B4S, g.B4R)]
    g.GF4[...] = part[:, :MI]
    pump()
    own_five = g.E5[1, 0, QS : QS + R, :]

    def five_grad(part, first, last):
        for tap in range(first, last):
            taps_grad(part, tap - first, mm_tn(whole_four(tap // 3, tap % 3), own_five))

    five_grad(g.K5A, 0, 5)
    job(g.K5A, g.K5AR, g.K5AD, slots_to(g.K5AD, lambda rank: g.k5.at[rank, :, pl.ds(0, 5)]))
    five_grad(g.K5B, 5, 9)
    job(g.K5B, g.K5BR, g.K5BD, slots_to(g.K5BD, lambda rank: g.k5.at[rank, :, pl.ds(5, 4)]))
    pump()
    st = narrow_back(
        5, g.GF4, g.B4R, cp, 1, g.PRE4, mean_four, inv_four, scale_four, g.bm[2:3, :]
    )
    pump()
    bsum_four, gsum_four = narrow_sums(5, st)
    narrow_pre_grad(
        g.GF4, g.PRE4, mean_four, inv_four, scale_four, bsum_four, gsum_four, 1, 0,
        g.G4.at[0], 0,
    )
    ch = gather(lambda s: g.G4.at[s], 0, R)
    relay(ch)
    pump()
    landed(ch)
    mid_back = mm_nt(
        four(g.G4),
        lanes([g.W4C[0:CO, MI:], g.W4P[0], g.W4C[0:CO, :MI], g.W4P[1]]),
    )
    g.GMID[...] = mid_back

    def mid_back_body(at, carry):
        a_b, a_3, a_s = carry
        rows = pl.ds(at, WCH)
        v = mid_value(rows)
        s = gate(v)
        grad = (g.GSB[rows, :] + g.GMID[rows, :]) * bc(mask_rows(at, WCH), CO)
        grad = grad * (s * (1.0 + v * (1.0 - s)))
        g.GMID[rows, :] = grad
        hat3 = (g.PRE3[rows, :] - mean_three) * inv_three
        hats = (g.PRES[rows, :] - mean_side) * inv_side
        return a_b + fold(grad), a_3 + fold(grad * hat3), a_s + fold(grad * hats)

    a_b, a_3, a_s = over(R, WCH, mid_back_body, (zero_w, zero_w, zero_w))
    for j, value in enumerate((a_b, a_3, a_s, zero_w)):
        wide_put(g.SA, j * NW, down(value))
    st = exchange(g.SA, 4 * NW)
    e4 = lanes([g.G4[0], g.G4[2]])

    def chip_grad(part, s, value):
        size = value.shape[0] // 4
        for p in range(4):
            for w in range(2):
                block = value[p * size : (p + 1) * size, w * MI : (w + 1) * MI]
                part[4 * s + p, w] = block.astype(BF)

    for s in range(2):
        chip_grad(g.K4, s, mm_tn(g.MIDC[s], e4))
    job(g.K4, g.K4R, g.K4D, chips_to(g.K4D, g.k4), far)
    pump()
    bsum_a, gsum_three, gsum_side = wide_sums(g.SA, st, 3)
    wide_pre_grad(
        g.GMID, g.PRE3, mean_three, inv_three, scale_three, bsum_a, gsum_three,
        g.E3.at[0],
    )
    cp = swap(g.E3)
    wide_pre_grad(
        g.GMID, g.PRES, mean_side, inv_side, scale_side, bsum_a, gsum_side, g.ES.at[0]
    )
    cp_side = swap(g.ES)
    pump()
    cp.wait_recv()
    part = wide_back(g.E3, g.W3, g.W3P)
    cp = [reduce_back(part, g.B2S, g.B2R)]
    g.GF2[...] = part[:, :MI]
    for s in range(4):
        rows_grad(g.K3, mm_tn(g.F2[s], g.E3[0]), s)
    job(g.K3, g.K3R, g.K3D, slots_to(g.K3D, lambda rank: g.k3.at[rank]))
    pump()
    st = narrow_back(
        6, g.GF2, g.B2R, cp, 1, g.PRE2, mean_two, inv_two, scale_two, g.bm[1:2, :]
    )
    pump()
    cp_side.wait_recv()
    es = lanes([g.ES[0], g.ES[1]])
    g.IGS[...] = mm_nt(es, lanes([g.WS[0], g.WSP[0]]))
    half = CO // 2
    for s, block in enumerate(strided()):
        grad = mm_tn(block, g.ES[0])
        rows_grad(g.KSA, grad[:, :half], s)
        rows_grad(g.KSB, grad[:, half:], s)
    job(g.KSA, g.KSAR, g.KSAD, slots_to(g.KSAD, lambda rank: g.ks.at[rank, :, :, pl.ds(0, half)]))
    job(g.KSB, g.KSBR, g.KSBD, slots_to(g.KSBD, lambda rank: g.ks.at[rank, :, :, pl.ds(half, half)]))
    pump()
    pump()
    bsum_two, gsum_two = narrow_sums(6, st)
    narrow_pre_grad(
        g.GF2, g.PRE2, mean_two, inv_two, scale_two, bsum_two, gsum_two, 1, 0,
        g.E2.at[0, 0], 0,
    )
    ch = gather(lambda s: g.E2.at[0, s], 0, R)

    def lift(s):
        def body(at, carry):
            rows = pl.ds(at, QS)
            v = g.E2[0, s, rows, :].astype(F32)
            g.E2[1, s, rows, :] = shifted(v, 1).astype(BF)
            return carry

        over(R, QS, body, 0)

    def two_grad(w, slot):
        e = g.E2[0, slot, 0:R, :]
        for ph in range(4):
            for t, l in taps_two(ph):
                tap = 3 * t + l
                part, tap = (g.K2A, tap) if tap < 5 else (g.K2B, tap - 5)
                for s in range(2):
                    grad = mm_tn(chip_one(s, ph, t == 0, l == 0), e)
                    for p in range(4):
                        rows = grad[p * piece : (p + 1) * piece]
                        part[4 * s + p, w, tap] = rows.astype(BF)

    lift(0)
    pump()
    two_grad(0, 0)
    ch[0].wait_recv()
    lift(1)
    relay(ch)
    two_grad(1, 2)
    for name, first, count in (("K2A", 0, 5), ("K2B", 5, 4)):
        bufs = [getattr(g, name + end) for end in ("", "R", "D")]
        job(*bufs, chips_to(bufs[2], g.k2, pl.ds(first, count)), far)
    pump()
    lift(2)
    ch[3].wait_recv()
    lift(3)

    def own_two(tap):
        far_own = jnp.concatenate([g.W2F[k, tap] for k in range(4)], axis=0)
        far_other = jnp.concatenate([g.W2Q[k, tap] for k in range(4)], axis=0)
        return lanes([g.W2[tap, 0], g.W2P[tap], far_own, far_other])

    for ph in range(4):
        part = None
        for t, l in taps_two(ph):
            rows = slice(QS, QS + R) if l == 0 else slice(0, R)
            e = lanes([g.E2[1 if t == 0 else 0, s, rows, :] for s in range(4)])
            term = mm_nt(e, own_two(3 * t + l))
            part = term if part is None else part + term
        g.GF1[ph * R : (ph + 1) * R, :] = part
        if ph == 3:
            pump()
    st = narrow_back(
        7, g.GF1, None, None, 4, g.PRE1, mean_one, inv_one, scale_one, g.bm[0:1, :]
    )
    side_far = mm_nt(es, lanes([g.WS[2], g.WSP[1]]))
    g.BSS[...] = side_far.astype(BF)
    cp_bs = net.push(g.BSS, g.BSR, far)
    pump()
    bsum_one, gsum_one = narrow_sums(7, st)
    ch = []
    for ph in range(4):
        narrow_pre_grad(
            g.GF1, g.PRE1, mean_one, inv_one, scale_one, bsum_one, gsum_one, 4, ph,
            g.G1.at[0, ph], 0,
        )
        ch.append(gather(lambda s, ph=ph: g.G1.at[s, ph], 0, R))
    pump()
    k1 = [None, None]
    for ph in range(4):
        relay(ch[ph])
        if ph == 1:
            pump()
        e1 = lanes([g.G1[0, ph], g.G1[2, ph]])
        for s in range(2):
            term = mm_tn(g.SRC[s, ph * R : (ph + 1) * R, :], e1)
            k1[s] = term if k1[s] is None else k1[s] + term
    for s in range(2):
        chip_grad(g.K1, s, k1[s])
    job(g.K1, g.K1R, g.K1D, chips_to(g.K1D, g.k1), far)
    pump()
    w1_own = lanes([g.W1C[0:CI, MI:], g.W1P[0], g.W1C[0:CI, :MI], g.W1P[1]])
    for ph in range(4):
        landed(ch[ph])
        whole = lanes([g.G1[s, ph] for s in range(4)])
        g.IG[ph * R : (ph + 1) * R, :] = mm_nt(whole, w1_own)
        if ph % 2:
            pump()
    cp_bs.wait_recv()
    g.IG[0:R, :] = g.IG[0:R, :] + g.IGS[...] + g.BSR[...].astype(F32)
    for ph in range(4):
        rows = slice(ph * R, (ph + 1) * R)
        g.IG[rows, :] = g.IG[rows, :] * bc(g.mask[...], CI)
    give(g.IG, g.images_grad)
    while any(work.todo for work in jobs):
        pump()

    g.gain_mid_grad[...] = jnp.concatenate([gsum_one, gsum_two, gsum_four, gsum_five], axis=0)
    g.bias_mid_grad[...] = jnp.concatenate([bsum_one, bsum_two, bsum_four, bsum_five], axis=0)
    g.gain_out_grad[...] = jnp.concatenate([gsum_three, gsum_side, gsum_six], axis=0)
    g.bias_out_grad[...] = jnp.concatenate([bsum_a, bsum_a, bsum_six], axis=0)
    g.mean_mid[...] = jnp.concatenate([mean_one, mean_two, mean_four, mean_five], axis=0)
    g.var_mid[...] = jnp.concatenate(
        [spread_one * unb_in, spread_two * unb_out, spread_four * unb_out, spread_five * unb_out],
        axis=0,
    )
    g.mean_out[...] = jnp.concatenate([mean_three, mean_side, mean_six], axis=0)
    g.var_out[...] = jnp.concatenate([spread_three, spread_side, spread_six], axis=0) * bc(
        unb_out, CO
    )
    for copy in outs:
        copy.wait()
    for copy in net.sent:
        copy.wait_send()

    for work in jobs:
        work.drain()


def fused_on_device(
    images, heights, widths, reduce_first, spatial_first, expand_first, shortcut, reduce_second,
    spatial_second, expand_second, gain_mid, bias_mid, gain_out, bias_out, cotangent,
):
    n, rows, cols, CO = cotangent.shape
    CI, MI = images.shape[3], reduce_first.shape[1]
    NB = heights.shape[0] // n
    R, QS = n * rows * cols, n * rows
    q, p, i = np.meshgrid(np.arange(cols), np.arange(rows), np.arange(n), indexing="ij")
    q, p, i = (v.reshape(-1) for v in (q, p, i))
    pick_out = np.zeros((R, R), np.float32)
    pick_out[np.arange(R), (i * cols + q) * rows + p] = 1.0
    pick_in = np.zeros((2 * R, 2 * R), np.float32)
    for h in range(2):
        pick_in[h * R + np.arange(R), (i * rows + p) * 2 * cols + 2 * q + h] = 1.0
    po = jnp.asarray(pick_out.T.astype(ml_dtypes.bfloat16))
    pi = jnp.asarray(pick_in.T.astype(ml_dtypes.bfloat16))
    cot = cotangent.transpose(0, 2, 1, 3).reshape(R, CO)
    ANY, VM = pl.BlockSpec(memory_space=pl.ANY), pl.BlockSpec(memory_space=pltpu.VMEM)
    SM = pl.BlockSpec(memory_space=pltpu.SMEM)
    CM, MC = 4 * MI, 4 * CI
    ins = dict(
        img=(images.reshape(4 * R, CI), ANY),
        cot=(cot, ANY),
        w1=(reduce_first, ANY),
        w2=(spatial_first.reshape(9, CM, MI), ANY),
        w3=(expand_first, ANY),
        wsc=(shortcut, ANY),
        w4=(reduce_second, ANY),
        w5=(spatial_second.reshape(9, CM, MI), ANY),
        w6=(expand_second, ANY),
        heights=(heights, SM),
        widths=(widths, SM),
        po=(po, VM),
        gm=(gain_mid, VM),
        bm=(bias_mid, VM),
        go=(gain_out, VM),
        bo=(bias_out, VM),
    )
    outs = dict(
        block_out=((R, CO), F32, ANY),
        images_grad=((4 * R, CI), F32, ANY),
        k1=((4, 4, CI // 4, MI), BF, ANY),
        k2=((4, 4, 9, MI // 4, MI), BF, ANY),
        k3=((4, 2, MI // 2, CO), BF, ANY),
        ks=((4, 2, CI // 2, CO), BF, ANY),
        k4=((4, 4, CO // 4, MI), BF, ANY),
        k5=((4, 2, 9, MI // 2, MI), BF, ANY),
        k6=((4, 2, MI // 2, CO), BF, ANY),
        gain_mid_grad=((4, MI), F32, VM),
        bias_mid_grad=((4, MI), F32, VM),
        gain_out_grad=((3, CO), F32, VM),
        bias_out_grad=((3, CO), F32, VM),
        mean_mid=((4, MI), F32, VM),
        var_mid=((4, MI), F32, VM),
        mean_out=((3, CO), F32, VM),
        var_out=((3, CO), F32, VM),
    )
    NW = CO // 128
    scratch = dict(
        IMG=((4 * R, CI), BF),
        mask=((R, 128), F32),
        aux=((24, 128), F32),
        SRC=((2, 4 * R, CI), BF),
        XS=((2, R, CI), BF),
        W1C=((2 * CI, 2 * MI), BF),
        W1P=((2, CI, MI), BF),
        W2=((9, 2, MI, MI), BF),
        W2F=((NB, 9, MI // 4, MI), BF),
        W2P=((9, MI, MI), BF),
        W2Q=((4, 9, MI // 4, MI), BF),
        P2S=((R, MI), BF),
        P2R=((R, MI), BF),
        W3=((4, MI, CO), BF),
        W3P=((2, MI, CO), BF),
        WS=((4, CI, CO), BF),
        WSP=((2, CI, CO), BF),
        W4C=((2 * CO, 2 * MI), BF),
        W4P=((2, CO, MI), BF),
        W5=((9, 4, MI, MI), BF),
        W5P=((9, 2, MI, MI), BF),
        W6=((4, MI, CO), BF),
        W6P=((2, MI, CO), BF),
        COT=((R, CO), BF),
        COTP=((R, CO), F32),
        P1S=((4, R, MI), BF),
        P1R=((4, R, MI), BF),
        P4S=((R, MI), BF),
        P4R=((R, MI), BF),
        PRE1=((4 * R, MI), F32),
        PRE2=((R, MI), F32),
        PRE3=((R, CO), F32),
        PRES=((R, CO), F32),
        PRE4=((R, MI), F32),
        PRE5=((R, MI), F32),
        PRE6=((R, CO), F32),
        F1=((2, 4, QS + R, MI), BF),
        D1=((2, 2, QS + R, MI), BF),
        F2=((4, R, MI), BF),
        BM=((R, CO), F32),
        MIDC=((2, R, CO), BF),
        F4=((4, R + 2 * QS, MI), BF),
        D4=((2, 4, R + 2 * QS, MI), BF),
        F5=((4, R, MI), BF),
        OUT=((R, CO), F32),
        GSB=((R, CO), F32),
        E6=((2, R, CO), BF),
        B5S=((R, MI), BF),
        B5R=((R, MI), BF),
        GF5=((R, MI), F32),
        E5=((3, 2, R + 2 * QS, MI), BF),
        B4S=((R, MI), BF),
        B4R=((R, MI), BF),
        GF4=((R, MI), F32),
        G4=((4, R, MI), BF),
        GMID=((R, CO), F32),
        E3=((2, R, CO), BF),
        ES=((2, R, CO), BF),
        B2S=((R, MI), BF),
        B2R=((R, MI), BF),
        GF2=((R, MI), F32),
        E2=((2, 4, R + QS, MI), BF),
        GF1=((4 * R, MI), F32),
        G1=((4, 4, R, MI), BF),
        IGS=((R, CI), F32),
        BSS=((R, CI), BF),
        BSR=((R, CI), BF),
        IG=((4 * R, CI), F32),
        SN=((8, NB, 2, MI), F32),
        SW=((4, NB, 2 * NW, 128), F32),
        SA=((NB, 4 * NW, 128), F32),
    )
    for name, piece in dict(
        K1=(2, CI // 4, MI),
        K2A=(2, 5, MI // 4, MI),
        K2B=(2, 4, MI // 4, MI),
        K3=(MI // 2, CO),
        KSA=(CI // 2, CO // 2),
        KSB=(CI // 2, CO // 2),
        K4=(2, CO // 4, MI),
        K5A=(5, MI // 2, MI),
        K5B=(4, MI // 2, MI),
        K6=(MI // 2, CO),
    ).items():
        scratch[name] = ((8, *piece), BF)
        scratch[name + "D"] = ((8, *piece), BF)
        scratch[name + "R"] = ((7, *piece), BF)
    names = [*ins, *outs, *scratch, "sems"]
    geo = types.SimpleNamespace(
        R=R, QS=QS, PS=n, CI=CI, MI=MI, CO=CO, NB=NB, rows=rows, cols=cols
    )
    got = pl.pallas_call(
        functools.partial(block_kernel, geo, names),
        out_shape=[jax.ShapeDtypeStruct(s, d) for s, d, _ in outs.values()],
        in_specs=[spec for _, spec in ins.values()],
        out_specs=[spec for _, _, spec in outs.values()],
        scratch_shapes=[pltpu.VMEM(s, d) for s, d in scratch.values()]
        + [pltpu.SemaphoreType.DMA((SEMS,))],
        compiler_params=pltpu.CompilerParams(
            collective_id=0, has_side_effects=True, vmem_limit_bytes=VMEM_LIMIT
        ),
    )(*[value for value, _ in ins.values()])
    o = types.SimpleNamespace(**dict(zip(outs, got)))
    passed = [
        o.gain_mid_grad, o.bias_mid_grad, o.gain_out_grad, o.bias_out_grad,
        o.mean_mid, o.var_mid, o.mean_out, o.var_out,
    ]
    finals = [
        jax.ShapeDtypeStruct(shape, F32)
        for shape in (
            (R, CO), (n, 2 * rows, 2 * cols, CI), (MC, MI), (3, 3, CM, MI), (CM, CO),
            (MC, CO), (4 * CO, MI), (3, 3, CM, MI), (CM, CO),
        )
    ]
    ks = (o.k1, o.k2, o.k3, o.ks, o.k4, o.k5, o.k6)
    res = pl.pallas_call(
        finish_kernel,
        out_shape=finals + [jax.ShapeDtypeStruct(v.shape, F32) for v in passed],
        in_specs=[ANY] * 9 + [VM] * 10,
        out_specs=[ANY] * 9 + [VM] * 8,
        scratch_shapes=[pltpu.VMEM((R, CO), F32), pltpu.VMEM((4 * R, CI), F32)]
        + [pltpu.VMEM(k.shape, BF) for k in ks]
        + [pltpu.VMEM(f.shape, F32) for f in finals]
        + [pltpu.SemaphoreType.DMA((18,))],
        compiler_params=pltpu.CompilerParams(vmem_limit_bytes=VMEM_LIMIT),
    )(o.block_out, o.images_grad, *ks, po, pi, *passed)
    block_out = res[0].reshape(n, cols, rows, CO).transpose(0, 2, 1, 3)
    return (block_out, *res[1:])


def exact(pick, value):
    high = value.astype(BF)
    low = (value - high.astype(F32)).astype(BF)
    return mm(pick, high) + mm(pick, low)


ORDER = (5, 3, 7, 6, 4, 8, 2, 1, 0)


def finish_kernel(*refs):
    ins, po, pi, small = refs[:9], refs[9], refs[10], refs[11:19]
    outs, small_outs = refs[19:28], refs[28:36]
    held, made, sems = refs[36:45], refs[45:54], refs[54]
    loads = [pltpu.make_async_copy(a, v, sems.at[k]) for k, (a, v) in enumerate(zip(ins, held))]
    stores = [
        pltpu.make_async_copy(v, a, sems.at[9 + k]) for k, (v, a) in enumerate(zip(made, outs))
    ]
    for k in ORDER:
        loads[k].start()
    for a, v in zip(small, small_outs):
        v[...] = a[...]

    def rows_of(k):
        src, dst = held[k], made[k]
        size = math.prod(src.shape[1:-1])
        for rank in range(4):
            dst[rank * size : (rank + 1) * size, :] = (
                src[rank].reshape(size, src.shape[-1]).astype(F32)
            )

    def taps_of(k):
        src, dst = held[k], made[k]
        size = src.shape[3]

        def tap(t):
            for rank in range(4):
                for h in range(src.shape[1]):
                    at = (src.shape[1] * rank + h) * size
                    dst[t // 3, t % 3, at : at + size, :] = src[rank, h, t].astype(F32)

        for t in range(src.shape[2]):
            tap(t)
            store = pltpu.make_async_copy(dst.at[t // 3, t % 3], outs[k].at[t // 3, t % 3], sems.at[9 + k])
            store.start()

    def block():
        made[0][...] = exact(po[...], held[0][...])

    def images():
        half = held[1].shape[0] // 2
        for a in range(2):
            value = exact(pi[...], held[1][a * half : (a + 1) * half, :])
            value = value.reshape(-1, *made[1].shape[2:])
            rows = made[1].shape[1] // 2
            for at in range(value.shape[0]):
                made[1][at // rows, 2 * (at % rows) + a] = value[at]

    for k in ORDER:
        loads[k].wait()
        if k == 0:
            block()
        elif k == 1:
            images()
        elif k in (3, 7):
            taps_of(k)
        else:
            rows_of(k)
        if k not in (3, 7):
            stores[k].start()
    for copy in stores:
        copy.wait()


def solution(mesh):
    in_specs = (
        P("batch", None, None, "chan"),
        P(),
        P(),
        P(None, "chan"),
        P(None, None, None, "chan"),
        P(None, "chan"),
        P(None, "chan"),
        P(None, "chan"),
        P(None, None, None, "chan"),
        P(None, "chan"),
        P(None, "chan"),
        P(None, "chan"),
        P(None, "chan"),
        P(None, "chan"),
        P("batch", None, None, "chan"),
    )
    out_specs = (
        P("batch", None, None, "chan"),
        P("batch", None, None, "chan"),
        P(None, "chan"),
        P(None, None, None, "chan"),
        P(None, "chan"),
        P(None, "chan"),
        P(None, "chan"),
        P(None, None, None, "chan"),
        P(None, "chan"),
        P(None, "chan"),
        P(None, "chan"),
        P(None, "chan"),
        P(None, "chan"),
        P(None, "chan"),
        P(None, "chan"),
        P(None, "chan"),
        P(None, "chan"),
    )
    fused = mesh.shape["chan"] == 4 and mesh.shape["batch"] == 8
    return jax.shard_map(
        fused_on_device if fused else on_device, mesh=mesh, in_specs=in_specs, out_specs=out_specs, check_vma=False
    )
```

```python
import functools
import math
import types

import jax
import jax.numpy as jnp
import ml_dtypes
import numpy as np
from jax import lax
from jax.experimental import pallas as pl
from jax.experimental.pallas import tpu as pltpu
from jax.sharding import PartitionSpec as P

EPS = 1e-05
VMEM_LIMIT = 60 * 1024 * 1024


def shortened(shard):
    return jax.tree.map(lambda a: a.astype(jnp.bfloat16) if a.dtype == jnp.float32 else a, shard)


def frame_masks(heights, widths, rows, cols):
    tall = heights[:, None, None]
    broad = widths[:, None, None]
    row_in = jnp.arange(2 * rows, dtype=jnp.int32)[None, :, None]
    col_in = jnp.arange(2 * cols, dtype=jnp.int32)[None, None, :]
    row_out = jnp.arange(rows, dtype=jnp.int32)[None, :, None]
    col_out = jnp.arange(cols, dtype=jnp.int32)[None, None, :]
    inner = ((row_in < 2 * tall) & (col_in < 2 * broad)).astype(jnp.float32)[..., None]
    outer = ((row_out < tall) & (col_out < broad)).astype(jnp.float32)[..., None]
    return (inner, outer)


def silu_slope(value):
    sig = jax.nn.sigmoid(value)
    return sig * (1.0 + value * (1.0 - sig))


def convolve(source, kernel, stride, rows, cols):
    taps = kernel.shape[0]
    margin = taps // 2
    padded = jnp.pad(source, ((0, 0), (margin, margin), (margin, margin), (0, 0)))
    total = None
    for top in range(taps):
        for left in range(taps):
            window = padded[
                :, top : top + stride * rows : stride, left : left + stride * cols : stride, :
            ]
            term = jnp.einsum(
                "nhwc,cd->nhwd", window, kernel[top, left], preferred_element_type=jnp.float32
            )
            total = term if total is None else total + term
    return total


def kernel_grad(source, grad, stride, taps):
    rows, cols = (grad.shape[1], grad.shape[2])
    margin = taps // 2
    padded = jnp.pad(source, ((0, 0), (margin, margin), (margin, margin), (0, 0)))
    return jnp.stack(
        [
            jnp.stack(
                [
                    jnp.einsum(
                        "nhwc,nhwd->cd",
                        padded[
                            :,
                            top : top + stride * rows : stride,
                            left : left + stride * cols : stride,
                            :,
                        ],
                        grad,
                        preferred_element_type=jnp.float32,
                    )
                    for left in range(taps)
                ]
            )
            for top in range(taps)
        ]
    )


def spread_back(grad, kernel, stride):
    taps = kernel.shape[0]
    margin = taps // 2
    total = None
    for top in range(taps):
        for left in range(taps):
            term = jnp.einsum(
                "nhwd,cd->nhwc", grad, kernel[top, left], preferred_element_type=jnp.float32
            )
            placed = lax.pad(
                term,
                jnp.float32(0.0),
                (
                    (0, 0, 0),
                    (top, 2 * margin - top + stride - 1, stride - 1),
                    (left, 2 * margin - left + stride - 1, stride - 1),
                    (0, 0, 0),
                ),
            )
            total = placed if total is None else total + placed
    rows, cols = (grad.shape[1], grad.shape[2])
    return total[:, margin : margin + stride * rows, margin : margin + stride * cols, :]


def norm_forward(pre, mask, count, gain, bias):
    mean = lax.psum(jnp.sum(pre * mask, axis=(0, 1, 2)), "batch") / count
    centered = (pre - mean) * mask
    spread = lax.psum(jnp.sum(centered * centered, axis=(0, 1, 2)), "batch") / count
    inv = lax.rsqrt(spread + EPS)
    hat = (pre - mean) * inv
    return (hat * gain + bias, hat, inv, mean, spread)


def norm_backward(grad, hat, mask, count, gain, inv):
    masked = grad * mask
    bias_grad, gain_grad = lax.psum(
        (jnp.sum(masked, axis=(0, 1, 2)), jnp.sum(masked * hat, axis=(0, 1, 2))), "batch"
    )
    pre_grad = mask * gain * inv * (grad - (bias_grad + hat * gain_grad) / count)
    return (pre_grad.astype(jnp.bfloat16), gain_grad, bias_grad)


def widen(feature):
    return lax.all_gather(feature, "chan", axis=3, tiled=True)


def input_grad(grad, kernel, stride):
    return jax.tree.map(
        lambda part: part.astype(jnp.float32),
        lax.psum_scatter(
            shortened(spread_back(grad, kernel, stride)), "chan", scatter_dimension=3, tiled=True
        ),
    )


def image_back(grad_one, grad_side, kernels):
    summands = spread_back(grad_one, kernels[0], 1) + spread_back(grad_side, kernels[3], 2)
    return lax.psum_scatter(
        summands.astype(jnp.bfloat16), "chan", scatter_dimension=3, tiled=True
    ).astype(jnp.float32)


def on_device(
    images,
    heights,
    widths,
    reduce_first,
    spatial_first,
    expand_first,
    shortcut,
    reduce_second,
    spatial_second,
    expand_second,
    gain_mid,
    bias_mid,
    gain_out,
    bias_out,
    cotangent,
):
    local = images.shape[0]
    rows, cols = (cotangent.shape[1], cotangent.shape[2])
    offset = lax.axis_index("batch") * local
    inner, outer = frame_masks(
        lax.dynamic_slice_in_dim(heights, offset, local),
        lax.dynamic_slice_in_dim(widths, offset, local),
        rows,
        cols,
    )
    count_out = jnp.sum(heights * widths).astype(jnp.float32)
    count_in = 4.0 * count_out
    kernels = (
        reduce_first[None, None],
        spatial_first,
        expand_first[None, None],
        shortcut[None, None],
        reduce_second[None, None],
        spatial_second,
        expand_second[None, None],
    )
    source = images * inner.astype(jnp.bfloat16)
    whole_source = lax.all_gather(source, "chan", axis=3, tiled=True)
    pre_one = convolve(whole_source, kernels[0], 1, 2 * rows, 2 * cols)
    normed_one, hat_one, inv_one, mean_one, spread_one = norm_forward(
        pre_one, inner, count_in, gain_mid[0], bias_mid[0]
    )
    whole_one = widen((jax.nn.silu(normed_one) * inner).astype(jnp.bfloat16))
    pre_two = convolve(whole_one, kernels[1], 2, rows, cols)
    normed_two, hat_two, inv_two, mean_two, spread_two = norm_forward(
        pre_two, outer, count_out, gain_mid[1], bias_mid[1]
    )
    whole_two = widen((jax.nn.silu(normed_two) * outer).astype(jnp.bfloat16))
    pre_three = convolve(whole_two, kernels[2], 1, rows, cols)
    normed_three, hat_three, inv_three, mean_three, spread_three = norm_forward(
        pre_three, outer, count_out, gain_out[0], bias_out[0]
    )
    pre_side = convolve(whole_source, kernels[3], 2, rows, cols)
    normed_side, hat_side, inv_side, mean_side, spread_side = norm_forward(
        pre_side, outer, count_out, gain_out[1], bias_out[1]
    )
    block_mid = jax.nn.silu(normed_three + normed_side) * outer
    whole_mid = widen(block_mid.astype(jnp.bfloat16))
    pre_four = convolve(whole_mid, kernels[4], 1, rows, cols)
    normed_four, hat_four, inv_four, mean_four, spread_four = norm_forward(
        pre_four, outer, count_out, gain_mid[2], bias_mid[2]
    )
    whole_four = widen((jax.nn.silu(normed_four) * outer).astype(jnp.bfloat16))
    pre_five = convolve(whole_four, kernels[5], 1, rows, cols)
    normed_five, hat_five, inv_five, mean_five, spread_five = norm_forward(
        pre_five, outer, count_out, gain_mid[3], bias_mid[3]
    )
    whole_five = widen((jax.nn.silu(normed_five) * outer).astype(jnp.bfloat16))
    pre_six = convolve(whole_five, kernels[6], 1, rows, cols)
    normed_six, hat_six, inv_six, mean_six, spread_six = norm_forward(
        pre_six, outer, count_out, gain_out[2], bias_out[2]
    )
    result = jax.nn.silu(normed_six + block_mid) * outer
    grad_sum_b = cotangent.astype(jnp.float32) * outer * silu_slope(normed_six + block_mid)
    grad_six, gain_six, bias_six = norm_backward(
        grad_sum_b, hat_six, outer, count_out, gain_out[2], inv_six
    )
    kern_six = kernel_grad(whole_five, grad_six, 1, 1)
    grad_feat_five = input_grad(grad_six, kernels[6], 1)
    grad_five, gain_five, bias_five = norm_backward(
        grad_feat_five * outer * silu_slope(normed_five),
        hat_five,
        outer,
        count_out,
        gain_mid[3],
        inv_five,
    )
    kern_five = kernel_grad(whole_four, grad_five, 1, 3)
    grad_feat_four = input_grad(grad_five, kernels[5], 1)
    grad_four, gain_four, bias_four = norm_backward(
        grad_feat_four * outer * silu_slope(normed_four),
        hat_four,
        outer,
        count_out,
        gain_mid[2],
        inv_four,
    )
    kern_four = kernel_grad(whole_mid, grad_four, 1, 1)
    grad_mid = grad_sum_b + input_grad(grad_four, kernels[4], 1)
    grad_sum_a = grad_mid * outer * silu_slope(normed_three + normed_side)
    grad_three, gain_three, bias_three = norm_backward(
        grad_sum_a, hat_three, outer, count_out, gain_out[0], inv_three
    )
    grad_side, gain_side, bias_side = norm_backward(
        grad_sum_a, hat_side, outer, count_out, gain_out[1], inv_side
    )
    kern_three = kernel_grad(whole_two, grad_three, 1, 1)
    kern_side = kernel_grad(whole_source, grad_side, 2, 1)
    grad_feat_two = input_grad(grad_three, kernels[2], 1)
    grad_two, gain_two, bias_two = norm_backward(
        grad_feat_two * outer * silu_slope(normed_two),
        hat_two,
        outer,
        count_out,
        gain_mid[1],
        inv_two,
    )
    kern_two = kernel_grad(whole_one, grad_two, 2, 3)
    grad_feat_one = input_grad(grad_two, kernels[1], 2)
    grad_one, gain_one, bias_one = norm_backward(
        grad_feat_one * inner * silu_slope(normed_one),
        hat_one,
        inner,
        count_in,
        gain_mid[0],
        inv_one,
    )
    kern_one = kernel_grad(whole_source, grad_one, 1, 1)
    images_grad = image_back(grad_one, grad_side, kernels) * inner
    summed = (
        lax.psum(kern_one.astype(jnp.bfloat16), "batch").astype(jnp.float32),
        lax.psum(kern_two.astype(jnp.bfloat16), "batch").astype(jnp.float32),
        lax.psum(kern_three.astype(jnp.bfloat16), "batch").astype(jnp.float32),
        lax.psum(kern_side.astype(jnp.bfloat16), "batch").astype(jnp.float32),
        lax.psum(kern_four.astype(jnp.bfloat16), "batch").astype(jnp.float32),
        lax.psum(kern_five.astype(jnp.bfloat16), "batch").astype(jnp.float32),
        lax.psum(kern_six.astype(jnp.bfloat16), "batch").astype(jnp.float32),
    )
    counts_mid = jnp.stack([count_in, count_out, count_out, count_out])[:, None]
    mean_mid_batch = jnp.stack([mean_one, mean_two, mean_four, mean_five])
    var_mid_batch = (
        jnp.stack([spread_one, spread_two, spread_four, spread_five])
        * counts_mid
        / (counts_mid - 1.0)
    )
    mean_out_batch = jnp.stack([mean_three, mean_side, mean_six])
    var_out_batch = (
        jnp.stack([spread_three, spread_side, spread_six]) * count_out / (count_out - 1.0)
    )
    return (
        result,
        images_grad,
        summed[0][0, 0],
        summed[1],
        summed[2][0, 0],
        summed[3][0, 0],
        summed[4][0, 0],
        summed[5],
        summed[6][0, 0],
        jnp.stack([gain_one, gain_two, gain_four, gain_five]),
        jnp.stack([bias_one, bias_two, bias_four, bias_five]),
        jnp.stack([gain_three, gain_side, gain_six]),
        jnp.stack([bias_three, bias_side, bias_six]),
        mean_mid_batch,
        var_mid_batch,
        mean_out_batch,
        var_out_batch,
    )


MESH = pl.DeviceIdType.MESH
BF = jnp.bfloat16
F32 = jnp.float32


def flip(value, bit):
    return value + bit - 2 * bit * lax.rem(lax.div(value, bit), 2)


def gate(value):
    return 0.5 * jnp.tanh(0.5 * value) + 0.5


def tree(parts):
    while len(parts) > 1:
        parts = [parts[k] + parts[k + 1] for k in range(0, len(parts), 2)]
    return parts[0]


def wide_row(block):
    return jnp.concatenate([block[j : j + 1] for j in range(block.shape[0])], axis=1)


def fold(value):
    return jnp.sum(value.reshape(value.shape[0] // 8, 8, value.shape[1]), axis=0)


def mm(a, b):
    return jnp.dot(a, b, preferred_element_type=F32)


def mm_nt(a, b):
    return lax.dot_general(a, b, (((1,), (1,)), ((), ())), preferred_element_type=F32)


def mm_tn(a, b):
    return lax.dot_general(a, b, (((0,), (0,)), ((), ())), preferred_element_type=F32)


class Traffic:
    def __init__(self, sems):
        self.sems, self.used, self.sent = sems, 0, []

    def take(self):
        self.used += 1
        assert self.used <= SEMS
        return self.sems.at[self.used - 1]

    def plan(self, src, dst, device, send_sem=None, recv_sem=None):
        return pltpu.make_async_remote_copy(
            src_ref=src,
            dst_ref=dst,
            send_sem=self.take() if send_sem is None else send_sem,
            recv_sem=self.take() if recv_sem is None else recv_sem,
            device_id=device,
            device_id_type=MESH,
        )

    def spread(self, src, dst, peers, all_of):
        sems = self.take(), self.take()
        copies = [self.plan(a, d, p, *sems) for a, d, p in zip(src, dst, peers)]
        return copies, self.plan(all_of, all_of, peers[0], *sems)

    def push(self, src, dst, device):
        copy = self.plan(src, dst, device)
        copy.start()
        self.sent.append(copy)
        return copy

    def plan_local(self, src, dst, sem=None):
        return pltpu.make_async_copy(src, dst, self.take() if sem is None else sem)

    def local(self, src, dst):
        copy = self.plan_local(src, dst)
        copy.start()
        return copy

    def load(self, pairs, all_of):
        sem = self.take()
        for src, dst in pairs:
            pltpu.make_async_copy(src, dst, sem).start()
        return pltpu.make_async_copy(all_of, all_of, sem)


class Summed:
    def __init__(self, net, part, got, done, ring, spill, across=None):
        at, ahead, behind = ring
        self.part, self.got, self.done, self.at = part, got, done, at
        self.spill, self.spill_wait = spill
        legs, legs_back = net.take(), net.take()
        up = [part.at[at(4)]] + [got.at[k] for k in range(4)]
        down = [part.at[at(-3)]] + [got.at[k] for k in range(4, 7)]
        ends, ends_back = [[net.take() for k in range(4)] for _ in range(2)]
        self.out = [
            [net.plan(up[k], up[k + 1], ahead, legs, ends[k])]
            + ([net.plan(down[k], down[k + 1], behind, legs, ends[k])] if k < 3 else [])
            for k in range(4)
        ]
        self.back = [
            ([net.plan(done.at[at(-k)], done.at[at(-k)], ahead, legs_back, ends_back[k])] if k < 3 else [])
            + [net.plan(done.at[at(k)], done.at[at(k)], behind, legs_back, ends_back[k])]
            for k in range(4)
        ]
        self.pair, self.pair_back = (
            [
                net.plan(got.at[pl.ds(0, 1 + (k < 3))], got.at[pl.ds(0, 1 + (k < 3))], ahead, legs, end)
                for k, end in enumerate(some)
            ]
            for some in (ends, ends_back)
        )
        self.left = [
            net.plan(got, got, ahead, legs, legs),
            net.plan(done.at[pl.ds(0, 7)], done.at[pl.ds(0, 7)], ahead, legs_back, legs_back),
        ]
        self.across = across is not None
        if self.across:
            self.crossing = net.plan(got.at[3, 1], done.at[at(0), 1], across)
            self.left.append(self.crossing)
        self.todo = [self.begin] + [functools.partial(self.add, k) for k in range(3)]
        self.todo += [self.finish] + ([self.crossed] if self.across else [])
        self.todo += [functools.partial(self.pass_on, k) for k in range(3)] + [self.last]

    def step(self):
        self.todo.pop(0)()

    def start(self, copies):
        for copy in copies:
            copy.start()

    def begin(self):
        self.start(self.out[0])

    def add(self, k):
        self.pair[k].wait_recv()
        self.got[k] = self.got[k] + self.part[self.at(3 - k)]
        if k < 2:
            self.got[4 + k] = self.got[4 + k] + self.part[self.at(k - 2)]
        self.start(self.out[k + 1])

    def finish(self):
        self.pair[3].wait_recv()
        total = self.got[3] + self.got[6] + self.part[self.at(0)]
        if self.across:
            self.done[self.at(0), 0] = total[0]
            self.got[3, 1] = total[1]
            self.crossing.start()
        else:
            self.done[self.at(0)] = total
            self.start(self.back[0])

    def crossed(self):
        self.crossing.wait_recv()
        self.start(self.back[0])

    def pass_on(self, k):
        self.pair_back[k].wait_recv()
        self.start(self.back[k + 1])

    def last(self):
        self.pair_back[3].wait_recv()
        self.start(self.spill)

    def drain(self):
        for copy in self.left:
            copy.wait_send()
        self.spill_wait.wait()


class Direct:
    def __init__(self, net, part, got, done, place, peers, spill, across):
        self.part, self.got, self.done, self.place = part, got, done, place
        self.spill, self.spill_wait = spill
        n = len(peers)
        self.out, self.whole = net.spread(
            [part.at[peer[0]] for peer in peers],
            [got.at[k] for k in range(n)],
            peers,
            got.at[pl.ds(0, n)],
        )
        self.back, self.whole_back = net.spread(
            [done.at[place]] * n, [done.at[place]] * n, peers, done.at[pl.ds(0, n)]
        )
        self.crossing = net.plan(got.at[n, 1], done.at[place, 1], across)
        self.todo = [self.begin, self.finish, self.crossed, self.last]

    def step(self):
        self.todo.pop(0)()

    def begin(self):
        for copy in self.out:
            copy.start()

    def finish(self):
        total = self.part[self.place].astype(F32)
        self.whole.wait_recv()
        for k in range(len(self.out)):
            total = total + self.got[k].astype(F32)
        self.done[self.place, 0] = total[0].astype(BF)
        self.got[len(self.out), 1] = total[1].astype(BF)
        self.crossing.start()

    def crossed(self):
        self.crossing.wait_recv()
        for copy in self.back:
            copy.start()

    def last(self):
        self.whole_back.wait_recv()
        for copy in self.spill:
            copy.start()

    def drain(self):
        for copy in (self.whole, self.whole_back, self.crossing):
            copy.wait_send()
        self.spill_wait.wait()


SEMS = 296


def block_kernel(geo, names, *refs):
    g = types.SimpleNamespace(**dict(zip(names, refs)))
    R, QS, PS = geo.R, geo.QS, geo.PS
    CI, MI, CO = geo.CI, geo.MI, geo.CO
    NB = geo.NB
    r = lax.axis_index("chan")
    b = lax.axis_index("batch")
    r1, r2 = flip(r, 1), flip(r, 2)
    r3 = flip(r1, 2)
    ranks = (r, r1, r2, r3)
    core, far = (b, r1), (b, r2)
    peers = []
    for k in range(1, NB):
        other = b
        bit = 1
        while bit < NB:
            if k & bit:
                other = flip(other, bit)
            bit *= 2
        peers.append((other, r))
    net = Traffic(g.sems)
    def seat(batch):
        x, z = lax.rem(batch, 2), lax.div(batch, 2)
        return z + x * (7 - 2 * z)

    def batch_at(place):
        x = lax.div(place, 4)
        return 2 * (place + x * (7 - 2 * place)) + x

    way = 1 - 2 * lax.rem(r, 2)
    places = {k: lax.rem(seat(b) + way * k + 16, 8) for k in range(-3, 5)}
    ring = (places.get, (batch_at(places[1]), r), (batch_at(places[-1]), r))

    bar = pltpu.get_barrier_semaphore()
    everyone = [core, far] + peers
    for device in everyone:
        pl.semaphore_signal(bar, 1, device_id=device, device_id_type=MESH)

    def everywhere(src, dst, all_of):
        copies, whole = net.spread(src, dst, peers, all_of)
        for copy in copies:
            copy.start()
        net.sent.append(whole)
        return whole

    def rows_of(ref, rank, size):
        return ref.at[pl.ds(pl.multiple_of(rank * size, size), size)]

    def taps_of(ref, rank, size):
        return ref.at[:, pl.ds(pl.multiple_of(rank * size, size), size), :]

    ld_img = net.local(g.img, g.IMG)
    ld_w1 = [
        net.local(rows_of(g.w1, rank, CI), g.W1C.at[pl.ds(s * CI, CI), pl.ds(MI, MI)])
        for s, rank in enumerate((r, r1))
    ]

    area = [g.heights[k] * g.widths[k] for k in range(NB * PS)]
    first = lax.broadcasted_iota(jnp.int32, (R, 128), 0)

    def of_image(ref, image):
        value = jnp.full(image.shape, ref[b * PS], jnp.int32)
        for k in range(1, PS):
            value = jnp.where(image == k, ref[b * PS + k], value)
        return value

    def pixel(m):
        image, row, column = lax.rem(m, PS), lax.rem(lax.div(m, PS), geo.rows), lax.div(m, QS)
        good = (row < of_image(g.heights, image)) & (column < of_image(g.widths, image))
        return column, row, image, good

    g.mask[...] = jnp.where(pixel(first)[3], 1.0, 0.0)

    def row(scalar):
        return jnp.full((1, 128), scalar.astype(F32), F32)

    for k in range(NB):
        other = b if k == 0 else peers[k - 1][0]
        own = 0
        for j in range(PS):
            own = own + g.heights[other * PS + j] * g.widths[other * PS + j]
        g.aux[k : k + 1, :] = row(own)
        g.aux[NB + k : NB + k + 1, :] = 1.0 / row(own)
    count = row(sum(area))
    g.aux[16:17, :] = 1.0 / count
    g.aux[17:18, :] = count / (count - 1.0)
    g.aux[18:19, :] = 4.0 * count / (4.0 * count - 1.0)

    ld_img.wait()
    lane = lax.broadcasted_iota(jnp.int32, (R, 4 * R), 1)
    column, line, image, good = pixel(lax.broadcasted_iota(jnp.int32, (R, 1), 0))
    corner = image * 4 * geo.rows * geo.cols + 2 * line * 2 * geo.cols + 2 * column
    for ph in range(4):
        source = jnp.where(good, corner + (ph // 2) * 2 * geo.cols + ph % 2, -1)
        pick = jnp.where(lane == source, 1.0, 0.0).astype(BF)
        g.SRC[0, ph * R : (ph + 1) * R, :] = mm(pick, g.IMG[...]).astype(BF)

    pl.semaphore_wait(bar, len(everyone))

    rm_src = net.push(g.SRC.at[0], g.SRC.at[1], core)
    rm_w1 = [
        net.push(rows_of(g.w1, rank, CI), g.W1C.at[pl.ds(s * CI, CI), pl.ds(0, MI)], far)
        for s, rank in enumerate((r2, r3))
    ]
    rm_gain = [net.push(g.gm, g.GMF, far), net.push(g.bm, g.BMF, far)]
    piece = MI // 4
    rank = jnp.where(b < 4, r2, r3)
    at = pl.multiple_of(rank * MI + lax.rem(b, 4) * piece, piece)
    rm_w2 = net.push(g.w2.at[:, pl.ds(at, piece), :], g.W2F.at[b], far)
    ld_sc = net.load([(rows_of(g.wsc, rank, CI), g.WS.at[s]) for s, rank in enumerate(ranks)], g.WS)
    ld_w2 = net.load([(taps_of(g.w2, rank, MI), g.W2.at[:, s]) for s, rank in enumerate((r, r1))], g.W2)
    ld_w3 = net.load([(rows_of(g.w3, rank, MI), g.W3.at[s]) for s, rank in enumerate(ranks)], g.W3)
    ld_w4 = [
        net.local(rows_of(g.w4, rank, CO), g.W4C.at[pl.ds(s * CO, CO), pl.ds(MI, MI)])
        for s, rank in enumerate((r, r1))
    ]
    ld_w5 = net.load([(taps_of(g.w5, rank, MI), g.W5.at[:, s]) for s, rank in enumerate(ranks)], g.W5)
    ld_w6 = net.load([(rows_of(g.w6, rank, MI), g.W6.at[s]) for s, rank in enumerate(ranks)], g.W6)
    ld_cot = net.local(g.cot, g.COT)

    for ph in (1, 3):
        for s in range(2):
            g.F1[s, ph, 0:QS, :] = jnp.zeros((QS, MI), BF)
    for s in range(2):
        g.D1[1, s, 0:QS, :] = jnp.zeros((QS, MI), BF)
    for s in range(4):
        g.F4[s, 0:QS, :] = jnp.zeros((QS, MI), BF)
        g.F4[s, QS + R :, :] = jnp.zeros((QS, MI), BF)
        for d in range(2):
            g.D4[d, s, 0:QS, :] = jnp.zeros((QS, MI), BF)
            g.D4[d, s, QS + R :, :] = jnp.zeros((QS, MI), BF)
    for d in range(3):
        for s in range(2):
            g.E5[d, s, 0:QS, :] = jnp.zeros((QS, MI), BF)
            g.E5[d, s, QS + R :, :] = jnp.zeros((QS, MI), BF)
    for d in range(2):
        for s in range(4):
            g.E2[d, s, R:, :] = jnp.zeros((QS, MI), BF)

    for copy in ld_w1:
        copy.wait()
    rm_src.wait_recv()
    for copy in rm_w1:
        copy.wait_recv()
    rm_p1 = []
    for ph in range(4):
        span = slice(ph * R, (ph + 1) * R)
        both = jnp.concatenate([g.SRC[0, span, :], g.SRC[1, span, :]], axis=1)
        part = mm(both, g.W1C[...])
        g.P1S[ph] = part[:, :MI].astype(BF)
        rm_p1.append(net.push(g.P1S.at[ph], g.P1R.at[ph], far))
        g.PRE1[span, :] = part[:, MI:]

    rm_w2.wait_recv()
    rm_w2s = everywhere([g.W2F.at[b]] * (NB - 1), [g.W2F.at[b]] * (NB - 1), g.W2F.at[pl.ds(0, NB - 1)])

    rm_back = []
    for s, rank in enumerate((r1, r3)):
        rm_back.append(net.push(rows_of(g.w6, rank, MI), g.W6P.at[s], core))
        rm_back.append(net.push(taps_of(g.w5, rank, MI), g.W5P.at[:, s], core))
        rm_back.append(net.push(rows_of(g.w3, rank, MI), g.W3P.at[s], core))
        rm_back.append(net.push(rows_of(g.wsc, rank, CI), g.WSP.at[s], core))
    rm_back.append(net.push(taps_of(g.w2, r1, MI), g.W2P, core))
    rm_back.append(net.push(rows_of(g.w4, r1, CO), g.W4P.at[0], core))
    rm_back.append(net.push(rows_of(g.w1, r1, CI), g.W1P.at[0], core))
    rm_back.append(
        net.push(g.W1C.at[pl.ds(CI, CI), pl.ds(0, MI)], g.W1P.at[1], core)
    )

    aux = g.aux
    inv_out = aux[16:17, :]
    unb_out, unb_in = aux[17:18, :], aux[18:19, :]

    def mask_rows(at, size):
        return g.mask[pl.ds(at, size), :]

    def over(total, size, body, init):
        def step(i, carry):
            return body(pl.multiple_of(i * size, size), carry)

        return lax.fori_loop(0, total // size, step, init)

    NCH = 128 if R % 128 == 0 else QS
    WCH = QS

    def bc(mask, width):
        return jnp.concatenate([mask] * (width // 128), axis=1)

    def exchange(slots, payload_rows):
        others = range(1, NB)
        return everywhere(
            [slots.at[0] for _ in others],
            [slots.at[k] for k in others],
            slots.at[pl.ds(1, NB - 1)],
        )

    def narrow_local(pre, phases, prepare=None):
        total = jnp.zeros((8, MI), F32)
        for ph in range(phases):
            if prepare is not None:
                prepare(ph)

            def add(at, acc, ph=ph):
                return acc + fold(pre[pl.ds(ph * R + at, NCH), :] * mask_rows(at, NCH))

            total = over(R, NCH, add, total)
        total = jnp.sum(total, axis=0, keepdims=True)
        mean = total * (aux[8:9, :] * (1.0 / phases))
        squares = jnp.zeros((8, MI), F32)
        for ph in range(phases):

            def add2(at, acc, ph=ph):
                d = (pre[pl.ds(ph * R + at, NCH), :] - mean) * mask_rows(at, NCH)
                return acc + fold(d * d)

            squares = over(R, NCH, add2, squares)
        return total, jnp.sum(squares, axis=0, keepdims=True)

    def narrow_send(idx, first, second):
        slots = g.SN.at[idx]
        g.SN[idx, 0, 0:1, :] = first
        g.SN[idx, 0, 1:2, :] = second
        return exchange(slots, 2)

    def narrow_merge(idx, copies, phases):
        copies.wait_recv()
        sums = [g.SN[idx, k, 0:1, :] for k in range(NB)]
        squares = [g.SN[idx, k, 1:2, :] for k in range(NB)]
        return moments(sums, squares, phases)

    def moments(sums, squares, phases):
        inv_count = inv_out * (1.0 / phases)
        mean = tree(list(sums)) * inv_count
        terms = []
        for k in range(NB):
            d = sums[k] * (aux[8 + k : 9 + k, :] * (1.0 / phases)) - mean
            terms.append(squares[k] + aux[k : k + 1, :] * float(phases) * d * d)
        spread = tree(terms) * inv_count
        return mean, spread

    def wide_local(pre):
        def add(at, acc):
            m = bc(mask_rows(at, WCH), CO)
            return acc + fold(pre[pl.ds(at, WCH), :] * m)

        total = jnp.sum(over(R, WCH, add, jnp.zeros((8, CO), F32)), axis=0, keepdims=True)
        mean = total * bc(aux[8:9, :], CO)

        def add2(at, acc):
            m = bc(mask_rows(at, WCH), CO)
            d = (pre[pl.ds(at, WCH), :] - mean) * m
            return acc + fold(d * d)

        squares = jnp.sum(over(R, WCH, add2, jnp.zeros((8, CO), F32)), axis=0, keepdims=True)
        return total, squares

    NW = CO // 128

    def wide_put(slots, row, value):
        for j in range(NW):
            slots[0, row + j : row + j + 1, :] = value[:, j * 128 : (j + 1) * 128]

    def wide_send(idx, first, second):
        slots = g.SW.at[idx]
        wide_put(slots, 0, first)
        wide_put(slots, NW, second)
        return exchange(slots, 2 * NW)

    def wide_merge(idx, copies):
        copies.wait_recv()
        sums = [g.SW[idx, k, 0:NW, :] for k in range(NB)]
        squares = [g.SW[idx, k, NW : 2 * NW, :] for k in range(NB)]
        mean, spread = moments(sums, squares, 1)
        return wide_row(mean), wide_row(spread)

    def gather(buf, at, size):
        here = [buf(s).at[pl.ds(at, size)] for s in range(4)]
        near = net.push(here[0], here[1], core)
        away = net.push(here[0], here[2], far)
        return [near, away, here]

    def relay(chunk):
        near, away, here = chunk
        away.wait_recv()
        chunk.append(net.push(here[2], here[3], core))

    def landed(chunk):
        chunk[0].wait_recv()
        chunk[3].wait_recv()

    def lanes(parts):
        return jnp.concatenate(parts, axis=1)

    place = lax.broadcasted_iota(jnp.int32, (QS, 128), 0)
    keep_down = place >= PS
    keep_up = place < QS - PS

    def shifted(value, step):
        if step < 0:
            return jnp.where(keep_down, pltpu.roll(value, PS, 0), 0.0)
        return jnp.where(keep_up, pltpu.roll(value, QS - PS, 0), 0.0)

    def take_p1(ph):
        rm_p1[ph].wait_recv()

        def add(at, carry):
            rows = pl.ds(ph * R + at, NCH)
            g.PRE1[rows, :] = g.PRE1[rows, :] + g.P1R[ph, pl.ds(at, NCH), :].astype(F32)
            return carry

        over(R, NCH, add, 0)

    sum_one, sq_one = narrow_local(g.PRE1, 4, take_p1)
    st_one = narrow_send(0, sum_one, sq_one)
    rm_xs = net.push(g.SRC.at[0, pl.ds(0, R)], g.XS.at[0], far)

    def scale_of(spread, gain):
        inv = lax.rsqrt(spread + EPS)
        return inv, inv * gain

    mean_one, spread_one = narrow_merge(0, st_one, 4)
    inv_one, scale_one = scale_of(spread_one, g.gm[0:1, :])

    def narrow_feature(pre, mean, scale, bias, out, ph, at0):
        def body(at, carry):
            v = (pre[pl.ds(ph * R + at, NCH), :] - mean) * scale + bias
            out[pl.ds(at0 + at, NCH), :] = (v * gate(v) * mask_rows(at, NCH)).astype(BF)
            return carry

        over(R, NCH, body, 0)

    ch_one = []
    for ph in range(4):
        narrow_feature(
            g.PRE1, mean_one, scale_one, g.bm[0:1, :], g.F1.at[0, ph], ph, QS
        )
        span = pl.ds(QS, R)
        ch_one.append(net.push(g.F1.at[0, ph, span], g.F1.at[1, ph, span], core))

    def both_chips(part, sent, got, pre, pre_far):
        sent[...] = part.astype(BF)
        copy = net.push(sent, got, far)
        pre[...] = part[:, MI:]
        pre_far[...] = part[:, :MI]
        return copy

    def both_norms(idx, copy, got, pre, pre_far, row, feature, at0):
        copy.wait_recv()

        def add(at, carry):
            rows = pl.ds(at, NCH)
            pre[rows, :] = pre[rows, :] + got[rows, 0:MI].astype(F32)
            pre_far[rows, :] = pre_far[rows, :] + got[rows, MI : 2 * MI].astype(F32)
            return carry

        over(R, NCH, add, 0)
        slots = g.SB.at[idx]
        for k, value in enumerate((*narrow_local(pre, 1), *narrow_local(pre_far, 1))):
            g.SB[idx, 0, k : k + 1, :] = value
        exchange(slots, 4).wait_recv()
        results = []
        for k, gains, biases in ((0, g.gm, g.bm), (2, g.GMF, g.BMF)):
            sums = [g.SB[idx, j, k : k + 1, :] for j in range(NB)]
            squares = [g.SB[idx, j, k + 1 : k + 2, :] for j in range(NB)]
            mean, spread = moments(sums, squares, 1)
            inv, scale = scale_of(spread, gains[row : row + 1, :])
            here = pl.ds(at0, R)
            source = pre_far if k else pre
            narrow_feature(source, mean, scale, biases[row : row + 1, :], feature.at[k], 0, at0)
            results.append(
                net.push(feature.at[k, here], feature.at[k + 1, here], core)
            )
            if k == 0:
                kept = mean, spread, inv, scale
        return kept, results

    rm_xs.wait_recv()
    rm_xs2 = net.push(g.XS.at[0], g.XS.at[1], core)
    ld_sc.wait()
    rm_xs2.wait_recv()

    def strided():
        return [g.SRC[0, 0:R, :], g.SRC[1, 0:R, :], g.XS[0], g.XS[1]]

    pre_side = None
    for s, block in enumerate(strided()):
        term = mm(block, g.WS[s])
        pre_side = term if pre_side is None else pre_side + term
    g.PRES[...] = pre_side
    st_side = wide_send(0, *wide_local(g.PRES))

    ld_w2.wait()

    def chip_one(s, ph, down, left):
        rows = slice(0, R) if left else slice(QS, QS + R)
        return g.D1[ph - 2, s, rows, :] if down else g.F1[s, ph, rows, :]

    def far_two(tap, first):
        return jnp.concatenate([g.W2F[first + k, tap] for k in range(4)], axis=0)

    def both_two(tap):
        near = jnp.concatenate([g.W2[tap, s] for s in range(2)], axis=0)
        away = jnp.concatenate([far_two(tap, 0), far_two(tap, 4)], axis=0)
        return lanes([away, near])

    def taps_two(ph):
        top = (1,) if ph < 2 else (0, 2)
        left = (1,) if ph % 2 == 0 else (0, 2)
        return [(t, l) for t in top for l in left]

    def lower(ph, s):
        def move(at, carry):
            v = g.F1[s, ph, pl.ds(QS + at, QS), :].astype(F32)
            g.D1[ph - 2, s, pl.ds(QS + at, QS), :] = shifted(v, -1).astype(BF)
            return carry

        over(R, QS, move, 0)

    rm_w2s.wait_recv()
    rm_back.append(net.push(g.W2F.at[pl.ds(4, 4)], g.W2Q, core))
    part = None
    for ph in range(4):
        if ph >= 2:
            lower(ph, 0)
        ch_one[ph].wait_recv()
        if ph >= 2:
            lower(ph, 1)
        for t, l in taps_two(ph):
            term = mm(lanes([chip_one(s, ph, t == 0, l == 0) for s in range(2)]), both_two(3 * t + l))
            part = term if part is None else part + term
    rm_p2 = both_chips(part, g.P2S, g.P2R, g.PRE2, g.PRE2F)
    rm_w4 = [
        net.push(rows_of(g.w4, rank, CO), g.W4C.at[pl.ds(s * CO, CO), pl.ds(0, MI)], far)
        for s, rank in enumerate((r2, r3))
    ]
    for copy in rm_gain:
        copy.wait_recv()
    kept, ch_two = both_norms(0, rm_p2, g.P2R, g.PRE2, g.PRE2F, 1, g.F2, 0)
    mean_two, spread_two, inv_two, scale_two = kept
    ld_w3.wait()
    mean_side, spread_side = wide_merge(0, st_side)
    inv_side, scale_side = scale_of(spread_side, g.go[1:2, :])

    def four(ref):
        return lanes([ref[s] for s in range(4)])

    def half_product(ref, weight, a, b):
        return mm(lanes([ref[a], ref[b]]), jnp.concatenate([weight[a], weight[b]], axis=0))

    pre_three = half_product(g.F2, g.W3, 0, 2)
    for copy in ch_two:
        copy.wait_recv()
    g.PRE3[...] = pre_three + half_product(g.F2, g.W3, 1, 3)
    st_three = wide_send(1, *wide_local(g.PRE3))
    mean_three, spread_three = wide_merge(1, st_three)
    inv_three, scale_three = scale_of(spread_three, g.go[0:1, :])
    bias_three, bias_side = g.bo[0:1, :], g.bo[1:2, :]

    def mid_value(rows):
        return (
            (g.PRE3[rows, :] - mean_three) * scale_three
            + bias_three
            + (g.PRES[rows, :] - mean_side) * scale_side
            + bias_side
        )

    def mid_body(at, carry):
        rows = pl.ds(at, WCH)
        v = mid_value(rows)
        out = v * gate(v) * bc(mask_rows(at, WCH), CO)
        g.BM[rows, :] = out
        g.MIDC[0, rows, :] = out.astype(BF)
        return carry

    over(R, WCH, mid_body, 0)
    rm_mid = net.push(g.MIDC.at[0], g.MIDC.at[1], core)

    for copy in ld_w4:
        copy.wait()
    for copy in rm_w4:
        copy.wait_recv()
    rm_back.append(net.push(g.W4C.at[pl.ds(CO, CO), pl.ds(0, MI)], g.W4P.at[1], core))
    rm_mid.wait_recv()
    part = mm(lanes([g.MIDC[0], g.MIDC[1]]), g.W4C[...])
    rm_p4 = both_chips(part, g.P4S, g.P4R, g.PRE4, g.PRE4F)

    kept, ch_four = both_norms(1, rm_p4, g.P4R, g.PRE4, g.PRE4F, 2, g.F4, QS)
    mean_four, spread_four, inv_four, scale_four = kept
    ld_w5.wait()

    def kernel_rows(ref, tap, slots):
        return jnp.concatenate([ref[tap, s] for s in slots], axis=0)

    def spread_rows(src, dst_up, dst_down):
        def body(at, carry):
            rows = pl.ds(QS + at, QS)
            v = src[rows, :].astype(F32)
            dst_up[rows, :] = shifted(v, -1).astype(BF)
            dst_down[rows, :] = shifted(v, 1).astype(BF)
            return carry

        over(R, QS, body, 0)

    def fill_four(s):
        spread_rows(g.F4.at[s], g.D4.at[0, s], g.D4.at[1, s])

    fill_four(0)
    fill_four(2)

    def four_blocks(t, l, slots):
        rows = slice(l * QS, l * QS + R)
        if t == 1:
            return lanes([g.F4[s, rows, :] for s in slots])
        return lanes([g.D4[t // 2, s, rows, :] for s in slots])

    def whole_four(t, l):
        return four_blocks(t, l, range(4))

    pre_five = None
    for slots in ((0, 2), (1, 3)):
        if slots[0]:
            for s, copy in zip(slots, ch_four):
                copy.wait_recv()
                fill_four(s)
        for t in range(3):
            for l in range(3):
                term = mm(four_blocks(t, l, slots), kernel_rows(g.W5, 3 * t + l, slots))
                pre_five = term if pre_five is None else pre_five + term
    g.PRE5[...] = pre_five
    st_five = narrow_send(3, *narrow_local(g.PRE5, 1))
    mean_five, spread_five = narrow_merge(3, st_five, 1)
    inv_five, scale_five = scale_of(spread_five, g.gm[3:4, :])
    narrow_feature(g.PRE5, mean_five, scale_five, g.bm[3:4, :], g.F5.at[0], 0, 0)
    ch_five = gather(lambda s: g.F5.at[s], 0, R)
    ld_w6.wait()
    ld_cot.wait()
    g.COTP[...] = mm_tn(g.po[...], g.COT[...])
    ch_five[0].wait_recv()
    pre_six = half_product(g.F5, g.W6, 0, 1)
    relay(ch_five)
    ch_five[3].wait_recv()
    g.PRE6[...] = pre_six + half_product(g.F5, g.W6, 2, 3)
    st_six = wide_send(2, *wide_local(g.PRE6))
    mean_six, spread_six = wide_merge(2, st_six)
    inv_six, scale_six = scale_of(spread_six, g.go[2:3, :])
    bias_six = g.bo[2:3, :]

    def last_body(at, carry):
        acc_b, acc_g = carry
        rows = pl.ds(at, WCH)
        m = bc(mask_rows(at, WCH), CO)
        hat = (g.PRE6[rows, :] - mean_six) * inv_six
        v = (g.PRE6[rows, :] - mean_six) * scale_six + bias_six + g.BM[rows, :]
        s = gate(v)
        g.OUT[rows, :] = v * s * m
        grad = g.COTP[rows, :] * m * (s * (1.0 + v * (1.0 - s)))
        g.GSB[rows, :] = grad
        return acc_b + fold(grad), acc_g + fold(grad * hat)

    zero_w = jnp.zeros((8, CO), F32)
    acc_b, acc_g = over(R, WCH, last_body, (zero_w, zero_w))

    def down(value):
        return jnp.sum(value, axis=0, keepdims=True)

    st = wide_send(3, down(acc_b), down(acc_g))

    out_block = net.local(g.OUT, g.block_out)

    def wide_sums(ref, copies, count):
        copies.wait_recv()
        return [
            wide_row(tree([ref[k, j * NW : (j + 1) * NW, :] for k in range(NB)]))
            for j in range(count)
        ]

    def narrow_sums(idx, copies):
        copies.wait_recv()
        return [tree([g.SN[idx, k, j : j + 1, :] for k in range(NB)]) for j in range(2)]

    bsum_six, gsum_six = wide_sums(g.SW.at[3], st, 2)
    inv_wide = bc(inv_out, CO)

    def wide_pre_grad(grad, pre, mean, inv, scale, bsum, gsum, out):
        mb, mg = bsum * inv_wide, gsum * inv_wide

        def body(at, carry):
            rows = pl.ds(at, WCH)
            hat = (pre[rows, :] - mean) * inv
            e = bc(mask_rows(at, WCH), CO) * scale * (grad[rows, :] - (mb + hat * mg))
            out[rows, :] = e.astype(BF)
            return carry

        over(R, WCH, body, 0)

    wide_pre_grad(
        g.GSB, g.PRE6, mean_six, inv_six, scale_six, bsum_six, gsum_six, g.E6.at[0]
    )
    for copy in rm_back:
        copy.wait_recv()

    def swap(ref):
        return net.push(ref.at[0], ref.at[1], core)

    def reduce_back(part, sent, got):
        sent[...] = part[:, MI:].astype(BF)
        return net.push(sent, got, far)

    def wide_back(e, own, other):
        near = lanes([own[0], other[0]])
        away = lanes([own[2], other[1]])
        return mm_nt(lanes([e[0], e[1]]), jnp.concatenate([near, away], axis=0))

    def narrow_back(idx, near, got, copy, phases, pre, mean, inv, scale, bias, order=None):
        acc_b = jnp.zeros((8, MI), F32)
        acc_g = jnp.zeros((8, MI), F32)
        for ph in range(phases):
            if copy is not None:
                copy[ph].wait_recv()

            def body(at, carry, ph=ph):
                b_acc, g_acc = carry
                rows = pl.ds(ph * R + at, NCH)
                hat = (pre[rows, :] - mean) * inv
                v = (pre[rows, :] - mean) * scale + bias
                s = gate(v)
                feat = near[rows, :]
                if got is not None:
                    feat = feat + got[rows, :].astype(F32)
                grad = feat * mask_rows(at, NCH) * (s * (1.0 + v * (1.0 - s)))
                near[rows, :] = grad
                return b_acc + fold(grad), g_acc + fold(grad * hat)

            acc_b, acc_g = over(R, NCH, body, (acc_b, acc_g))
        return narrow_send(idx, down(acc_b), down(acc_g))

    def narrow_pre_grad(grad, pre, mean, inv, scale, bsum, gsum, phases, ph, out, at0):
        inv_count = inv_out * (1.0 / phases)
        mb, mg = bsum * inv_count, gsum * inv_count

        def body(at, carry):
            rows = pl.ds(ph * R + at, NCH)
            hat = (pre[rows, :] - mean) * inv
            e = mask_rows(at, NCH) * scale * (grad[rows, :] - (mb + hat * mg))
            out[pl.ds(at0 + at, NCH), :] = e.astype(BF)
            return carry

        over(R, NCH, body, 0)

    outs = [out_block]

    def give(src, dst):
        outs.append(net.local(src, dst))

    cp = swap(g.E6)
    cp.wait_recv()
    part = wide_back(g.E6, g.W6, g.W6P)
    cp = [reduce_back(part, g.B5S, g.B5R)]
    g.GF5[...] = part[:, :MI]
    def rows_grad(part, value, s):
        half = value.shape[0] // 2
        for h in range(2):
            part[2 * s + h] = value[h * half : (h + 1) * half].astype(BF)

    def taps_grad(part, tap, value):
        half = MI // 2
        for p in range(8):
            part[p, tap] = value[p * half : (p + 1) * half].astype(BF)

    jobs = []

    def spilled(done, targets):
        sem = net.take()
        copies = [net.plan_local(source, place, sem) for source, place in targets]
        return copies, net.plan_local(done, done, sem)

    def job(part, got, done, targets, across=None):
        jobs.append(Summed(net, part, got, done, ring, spilled(done, targets), across))

    def pump(most=3):
        left = sorted((work for work in jobs if work.todo), key=lambda work: -len(work.todo))
        for work in left[:most]:
            work.step()

    def slots_to(part, place):
        return [(part.at[pl.ds(2 * s, 2)], place(ranks[s])) for s in range(4)]

    def chips_to(part, out, taps=None):
        def place(rank):
            return out.at[rank] if taps is None else out.at[rank, :, taps]

        return [
            (part.at[pl.ds(4 * s, 4), v], place(ranks[2 * v + s]))
            for s in range(2)
            for v in range(2)
        ]

    for s in range(4):
        rows_grad(g.K6, mm_tn(g.F5[s], g.E6[0]), s)
    job(g.K6, g.K6R, g.K6D, slots_to(g.K6D, lambda rank: g.k6.at[rank]))
    pump()
    st = narrow_back(
        4, g.GF5, g.B5R, cp, 1, g.PRE5, mean_five, inv_five, scale_five, g.bm[3:4, :]
    )
    pump()
    bsum_five, gsum_five = narrow_sums(4, st)
    narrow_pre_grad(
        g.GF5, g.PRE5, mean_five, inv_five, scale_five, bsum_five, gsum_five, 1, 0,
        g.E5.at[1, 0], QS,
    )
    cp = net.push(g.E5.at[1, 0, pl.ds(QS, R)], g.E5.at[1, 1, pl.ds(QS, R)], core)
    spread_rows(g.E5.at[1, 0], g.E5.at[0, 0], g.E5.at[2, 0])
    cp.wait_recv()
    spread_rows(g.E5.at[1, 1], g.E5.at[0, 1], g.E5.at[2, 1])
    pump()

    def taps_back(own, other, tap):
        near = lanes([own[tap, 0], other[tap, 0]])
        away = lanes([own[tap, 2], other[tap, 1]])
        return jnp.concatenate([near, away], axis=0)

    part = None
    for t in range(3):
        for l in range(3):
            rows = slice((2 - l) * QS, (2 - l) * QS + R)
            e = lanes([g.E5[2 - t, s, rows, :] for s in range(2)])
            term = mm_nt(e, taps_back(g.W5, g.W5P, 3 * t + l))
            part = term if part is None else part + term
    cp = [reduce_back(part, g.B4S, g.B4R)]
    g.GF4[...] = part[:, :MI]
    pump()
    own_five = g.E5[1, 0, QS : QS + R, :]

    def five_grad(part, first, last):
        for tap in range(first, last):
            taps_grad(part, tap - first, mm_tn(whole_four(tap // 3, tap % 3), own_five))

    five_grad(g.K5A, 0, 5)
    job(g.K5A, g.K5AR, g.K5AD, slots_to(g.K5AD, lambda rank: g.k5.at[rank, :, pl.ds(0, 5)]))
    five_grad(g.K5B, 5, 9)
    job(g.K5B, g.K5BR, g.K5BD, slots_to(g.K5BD, lambda rank: g.k5.at[rank, :, pl.ds(5, 4)]))
    pump()
    st = narrow_back(
        5, g.GF4, g.B4R, cp, 1, g.PRE4, mean_four, inv_four, scale_four, g.bm[2:3, :]
    )
    pump()
    bsum_four, gsum_four = narrow_sums(5, st)
    narrow_pre_grad(
        g.GF4, g.PRE4, mean_four, inv_four, scale_four, bsum_four, gsum_four, 1, 0,
        g.G4.at[0], 0,
    )
    ch = gather(lambda s: g.G4.at[s], 0, R)
    relay(ch)
    pump()
    landed(ch)
    mid_back = mm_nt(
        four(g.G4),
        lanes([g.W4C[0:CO, MI:], g.W4P[0], g.W4C[0:CO, :MI], g.W4P[1]]),
    )
    g.GMID[...] = mid_back

    def mid_back_body(at, carry):
        a_b, a_3, a_s = carry
        rows = pl.ds(at, WCH)
        v = mid_value(rows)
        s = gate(v)
        grad = (g.GSB[rows, :] + g.GMID[rows, :]) * bc(mask_rows(at, WCH), CO)
        grad = grad * (s * (1.0 + v * (1.0 - s)))
        g.GMID[rows, :] = grad
        hat3 = (g.PRE3[rows, :] - mean_three) * inv_three
        hats = (g.PRES[rows, :] - mean_side) * inv_side
        return a_b + fold(grad), a_3 + fold(grad * hat3), a_s + fold(grad * hats)

    a_b, a_3, a_s = over(R, WCH, mid_back_body, (zero_w, zero_w, zero_w))
    for j, value in enumerate((a_b, a_3, a_s, zero_w)):
        wide_put(g.SA, j * NW, down(value))
    st = exchange(g.SA, 4 * NW)
    e4 = lanes([g.G4[0], g.G4[2]])

    def chip_grad(part, s, value):
        size = value.shape[0] // 4
        for p in range(4):
            for w in range(2):
                block = value[p * size : (p + 1) * size, w * MI : (w + 1) * MI]
                part[4 * s + p, w] = block.astype(BF)

    for s in range(2):
        chip_grad(g.K4, s, mm_tn(g.MIDC[s], e4))
    job(g.K4, g.K4R, g.K4D, chips_to(g.K4D, g.k4), far)
    pump()
    bsum_a, gsum_three, gsum_side = wide_sums(g.SA, st, 3)
    wide_pre_grad(
        g.GMID, g.PRE3, mean_three, inv_three, scale_three, bsum_a, gsum_three,
        g.E3.at[0],
    )
    cp = swap(g.E3)
    wide_pre_grad(
        g.GMID, g.PRES, mean_side, inv_side, scale_side, bsum_a, gsum_side, g.ES.at[0]
    )
    cp_side = swap(g.ES)
    pump()
    cp.wait_recv()
    part = wide_back(g.E3, g.W3, g.W3P)
    cp = [reduce_back(part, g.B2S, g.B2R)]
    g.GF2[...] = part[:, :MI]
    for s in range(4):
        rows_grad(g.K3, mm_tn(g.F2[s], g.E3[0]), s)
    job(g.K3, g.K3R, g.K3D, slots_to(g.K3D, lambda rank: g.k3.at[rank]))
    pump()
    st = narrow_back(
        6, g.GF2, g.B2R, cp, 1, g.PRE2, mean_two, inv_two, scale_two, g.bm[1:2, :]
    )
    pump()
    cp_side.wait_recv()
    es = lanes([g.ES[0], g.ES[1]])
    g.IGS[...] = mm_nt(es, lanes([g.WS[0], g.WSP[0]]))
    half = CO // 2
    for s, block in enumerate(strided()):
        grad = mm_tn(block, g.ES[0])
        rows_grad(g.KSA, grad[:, :half], s)
        rows_grad(g.KSB, grad[:, half:], s)
    job(g.KSA, g.KSAR, g.KSAD, slots_to(g.KSAD, lambda rank: g.ks.at[rank, :, :, pl.ds(0, half)]))
    job(g.KSB, g.KSBR, g.KSBD, slots_to(g.KSBD, lambda rank: g.ks.at[rank, :, :, pl.ds(half, half)]))
    pump()
    pump()
    bsum_two, gsum_two = narrow_sums(6, st)
    narrow_pre_grad(
        g.GF2, g.PRE2, mean_two, inv_two, scale_two, bsum_two, gsum_two, 1, 0,
        g.E2.at[0, 0], 0,
    )
    ch = gather(lambda s: g.E2.at[0, s], 0, R)

    def lift(s):
        def body(at, carry):
            rows = pl.ds(at, QS)
            v = g.E2[0, s, rows, :].astype(F32)
            g.E2[1, s, rows, :] = shifted(v, 1).astype(BF)
            return carry

        over(R, QS, body, 0)

    def two_grad(w, slot):
        e = g.E2[0, slot, 0:R, :]
        for ph in range(4):
            for t, l in taps_two(ph):
                tap = 3 * t + l
                part, tap = (g.K2A, tap) if tap < 5 else (g.K2B, tap - 5)
                for s in range(2):
                    grad = mm_tn(chip_one(s, ph, t == 0, l == 0), e)
                    for p in range(4):
                        rows = grad[p * piece : (p + 1) * piece]
                        part[4 * s + p, w, tap] = rows.astype(BF)

    lift(0)
    pump()
    two_grad(0, 0)
    ch[0].wait_recv()
    lift(1)
    relay(ch)
    two_grad(1, 2)
    for name, first, count in (("K2A", 0, 5), ("K2B", 5, 4)):
        bufs = [getattr(g, name + end) for end in ("", "R", "D")]
        job(*bufs, chips_to(bufs[2], g.k2, pl.ds(first, count)), far)
    pump()
    lift(2)
    ch[3].wait_recv()
    lift(3)

    def own_two(tap):
        far_own = jnp.concatenate([g.W2F[k, tap] for k in range(4)], axis=0)
        far_other = jnp.concatenate([g.W2Q[k, tap] for k in range(4)], axis=0)
        return lanes([g.W2[tap, 0], g.W2P[tap], far_own, far_other])

    for ph in range(4):
        part = None
        for t, l in taps_two(ph):
            rows = slice(QS, QS + R) if l == 0 else slice(0, R)
            e = lanes([g.E2[1 if t == 0 else 0, s, rows, :] for s in range(4)])
            term = mm_nt(e, own_two(3 * t + l))
            part = term if part is None else part + term
        g.GF1[ph * R : (ph + 1) * R, :] = part
        if ph == 3:
            pump()
    st = narrow_back(
        7, g.GF1, None, None, 4, g.PRE1, mean_one, inv_one, scale_one, g.bm[0:1, :]
    )
    side_far = mm_nt(es, lanes([g.WS[2], g.WSP[1]]))
    g.BSS[...] = side_far.astype(BF)
    cp_bs = net.push(g.BSS, g.BSR, far)
    pump()
    bsum_one, gsum_one = narrow_sums(7, st)
    ch = []
    for ph in range(4):
        narrow_pre_grad(
            g.GF1, g.PRE1, mean_one, inv_one, scale_one, bsum_one, gsum_one, 4, ph,
            g.G1.at[0, ph], 0,
        )
        ch.append(gather(lambda s, ph=ph: g.G1.at[s, ph], 0, R))
    pump()
    k1 = [None, None]
    for ph in range(4):
        relay(ch[ph])
        if ph == 1:
            pump()
        e1 = lanes([g.G1[0, ph], g.G1[2, ph]])
        for s in range(2):
            term = mm_tn(g.SRC[s, ph * R : (ph + 1) * R, :], e1)
            k1[s] = term if k1[s] is None else k1[s] + term
    for s in range(2):
        chip_grad(g.K1, s, k1[s])
    job(g.K1, g.K1R, g.K1D, chips_to(g.K1D, g.k1), far)
    pump()
    w1_own = lanes([g.W1C[0:CI, MI:], g.W1P[0], g.W1C[0:CI, :MI], g.W1P[1]])
    for ph in range(4):
        landed(ch[ph])
        whole = lanes([g.G1[s, ph] for s in range(4)])
        g.IG[ph * R : (ph + 1) * R, :] = mm_nt(whole, w1_own)
        if ph % 2:
            pump()
    cp_bs.wait_recv()
    g.IG[0:R, :] = g.IG[0:R, :] + g.IGS[...] + g.BSR[...].astype(F32)
    for ph in range(4):
        rows = slice(ph * R, (ph + 1) * R)
        g.IG[rows, :] = g.IG[rows, :] * bc(g.mask[...], CI)
    give(g.IG, g.images_grad)
    while any(work.todo for work in jobs):
        pump()

    g.gain_mid_grad[...] = jnp.concatenate([gsum_one, gsum_two, gsum_four, gsum_five], axis=0)
    g.bias_mid_grad[...] = jnp.concatenate([bsum_one, bsum_two, bsum_four, bsum_five], axis=0)
    g.gain_out_grad[...] = jnp.concatenate([gsum_three, gsum_side, gsum_six], axis=0)
    g.bias_out_grad[...] = jnp.concatenate([bsum_a, bsum_a, bsum_six], axis=0)
    g.mean_mid[...] = jnp.concatenate([mean_one, mean_two, mean_four, mean_five], axis=0)
    g.var_mid[...] = jnp.concatenate(
        [spread_one * unb_in, spread_two * unb_out, spread_four * unb_out, spread_five * unb_out],
        axis=0,
    )
    g.mean_out[...] = jnp.concatenate([mean_three, mean_side, mean_six], axis=0)
    g.var_out[...] = jnp.concatenate([spread_three, spread_side, spread_six], axis=0) * bc(
        unb_out, CO
    )
    for copy in outs:
        copy.wait()
    for copy in net.sent:
        copy.wait_send()

    for work in jobs:
        work.drain()


def fused_on_device(
    images, heights, widths, reduce_first, spatial_first, expand_first, shortcut, reduce_second,
    spatial_second, expand_second, gain_mid, bias_mid, gain_out, bias_out, cotangent,
):
    n, rows, cols, CO = cotangent.shape
    CI, MI = images.shape[3], reduce_first.shape[1]
    NB = heights.shape[0] // n
    R, QS = n * rows * cols, n * rows
    q, p, i = np.meshgrid(np.arange(cols), np.arange(rows), np.arange(n), indexing="ij")
    q, p, i = (v.reshape(-1) for v in (q, p, i))
    pick_out = np.zeros((R, R), np.float32)
    pick_out[np.arange(R), (i * cols + q) * rows + p] = 1.0
    pick_in = np.zeros((2 * R, 2 * R), np.float32)
    for h in range(2):
        pick_in[h * R + np.arange(R), (i * rows + p) * 2 * cols + 2 * q + h] = 1.0
    po = jnp.asarray(pick_out.T.astype(ml_dtypes.bfloat16))
    pi = jnp.asarray(pick_in.T.astype(ml_dtypes.bfloat16))
    cot = cotangent.transpose(0, 2, 1, 3).reshape(R, CO)
    ANY, VM = pl.BlockSpec(memory_space=pl.ANY), pl.BlockSpec(memory_space=pltpu.VMEM)
    SM = pl.BlockSpec(memory_space=pltpu.SMEM)
    CM, MC = 4 * MI, 4 * CI
    ins = dict(
        img=(images.reshape(4 * R, CI), ANY),
        cot=(cot, ANY),
        w1=(reduce_first, ANY),
        w2=(spatial_first.reshape(9, CM, MI), ANY),
        w3=(expand_first, ANY),
        wsc=(shortcut, ANY),
        w4=(reduce_second, ANY),
        w5=(spatial_second.reshape(9, CM, MI), ANY),
        w6=(expand_second, ANY),
        heights=(heights, SM),
        widths=(widths, SM),
        po=(po, VM),
        gm=(gain_mid, VM),
        bm=(bias_mid, VM),
        go=(gain_out, VM),
        bo=(bias_out, VM),
    )
    outs = dict(
        block_out=((R, CO), F32, ANY),
        images_grad=((4 * R, CI), F32, ANY),
        k1=((4, 4, CI // 4, MI), BF, ANY),
        k2=((4, 4, 9, MI // 4, MI), BF, ANY),
        k3=((4, 2, MI // 2, CO), BF, ANY),
        ks=((4, 2, CI // 2, CO), BF, ANY),
        k4=((4, 4, CO // 4, MI), BF, ANY),
        k5=((4, 2, 9, MI // 2, MI), BF, ANY),
        k6=((4, 2, MI // 2, CO), BF, ANY),
        gain_mid_grad=((4, MI), F32, VM),
        bias_mid_grad=((4, MI), F32, VM),
        gain_out_grad=((3, CO), F32, VM),
        bias_out_grad=((3, CO), F32, VM),
        mean_mid=((4, MI), F32, VM),
        var_mid=((4, MI), F32, VM),
        mean_out=((3, CO), F32, VM),
        var_out=((3, CO), F32, VM),
    )
    NW = CO // 128
    scratch = dict(
        IMG=((4 * R, CI), BF),
        mask=((R, 128), F32),
        aux=((24, 128), F32),
        SRC=((2, 4 * R, CI), BF),
        XS=((2, R, CI), BF),
        W1C=((2 * CI, 2 * MI), BF),
        W1P=((2, CI, MI), BF),
        W2=((9, 2, MI, MI), BF),
        W2F=((NB, 9, MI // 4, MI), BF),
        W2P=((9, MI, MI), BF),
        W2Q=((4, 9, MI // 4, MI), BF),
        P2S=((R, 2 * MI), BF),
        P2R=((R, 2 * MI), BF),
        PRE2F=((R, MI), F32),
        PRE4F=((R, MI), F32),
        GMF=((4, MI), F32),
        BMF=((4, MI), F32),
        SB=((2, NB, 4, MI), F32),
        W3=((4, MI, CO), BF),
        W3P=((2, MI, CO), BF),
        WS=((4, CI, CO), BF),
        WSP=((2, CI, CO), BF),
        W4C=((2 * CO, 2 * MI), BF),
        W4P=((2, CO, MI), BF),
        W5=((9, 4, MI, MI), BF),
        W5P=((9, 2, MI, MI), BF),
        W6=((4, MI, CO), BF),
        W6P=((2, MI, CO), BF),
        COT=((R, CO), BF),
        COTP=((R, CO), F32),
        P1S=((4, R, MI), BF),
        P1R=((4, R, MI), BF),
        P4S=((R, 2 * MI), BF),
        P4R=((R, 2 * MI), BF),
        PRE1=((4 * R, MI), F32),
        PRE2=((R, MI), F32),
        PRE3=((R, CO), F32),
        PRES=((R, CO), F32),
        PRE4=((R, MI), F32),
        PRE5=((R, MI), F32),
        PRE6=((R, CO), F32),
        F1=((2, 4, QS + R, MI), BF),
        D1=((2, 2, QS + R, MI), BF),
        F2=((4, R, MI), BF),
        BM=((R, CO), F32),
        MIDC=((2, R, CO), BF),
        F4=((4, R + 2 * QS, MI), BF),
        D4=((2, 4, R + 2 * QS, MI), BF),
        F5=((4, R, MI), BF),
        OUT=((R, CO), F32),
        GSB=((R, CO), F32),
        E6=((2, R, CO), BF),
        B5S=((R, MI), BF),
        B5R=((R, MI), BF),
        GF5=((R, MI), F32),
        E5=((3, 2, R + 2 * QS, MI), BF),
        B4S=((R, MI), BF),
        B4R=((R, MI), BF),
        GF4=((R, MI), F32),
        G4=((4, R, MI), BF),
        GMID=((R, CO), F32),
        E3=((2, R, CO), BF),
        ES=((2, R, CO), BF),
        B2S=((R, MI), BF),
        B2R=((R, MI), BF),
        GF2=((R, MI), F32),
        E2=((2, 4, R + QS, MI), BF),
        GF1=((4 * R, MI), F32),
        G1=((4, 4, R, MI), BF),
        IGS=((R, CI), F32),
        BSS=((R, CI), BF),
        BSR=((R, CI), BF),
        IG=((4 * R, CI), F32),
        SN=((8, NB, 2, MI), F32),
        SW=((4, NB, 2 * NW, 128), F32),
        SA=((NB, 4 * NW, 128), F32),
    )
    for name, piece in dict(
        K1=(2, CI // 4, MI),
        K2A=(2, 5, MI // 4, MI),
        K2B=(2, 4, MI // 4, MI),
        K3=(MI // 2, CO),
        KSA=(CI // 2, CO // 2),
        KSB=(CI // 2, CO // 2),
        K4=(2, CO // 4, MI),
        K5A=(5, MI // 2, MI),
        K5B=(4, MI // 2, MI),
        K6=(MI // 2, CO),
    ).items():
        scratch[name] = ((8, *piece), BF)
        scratch[name + "D"] = ((8, *piece), BF)
        scratch[name + "R"] = ((7, *piece), BF)
    names = [*ins, *outs, *scratch, "sems"]
    geo = types.SimpleNamespace(
        R=R, QS=QS, PS=n, CI=CI, MI=MI, CO=CO, NB=NB, rows=rows, cols=cols
    )
    got = pl.pallas_call(
        functools.partial(block_kernel, geo, names),
        out_shape=[jax.ShapeDtypeStruct(s, d) for s, d, _ in outs.values()],
        in_specs=[spec for _, spec in ins.values()],
        out_specs=[spec for _, _, spec in outs.values()],
        scratch_shapes=[pltpu.VMEM(s, d) for s, d in scratch.values()]
        + [pltpu.SemaphoreType.DMA((SEMS,))],
        compiler_params=pltpu.CompilerParams(
            collective_id=0, has_side_effects=True, vmem_limit_bytes=VMEM_LIMIT
        ),
    )(*[value for value, _ in ins.values()])
    o = types.SimpleNamespace(**dict(zip(outs, got)))
    passed = [
        o.gain_mid_grad, o.bias_mid_grad, o.gain_out_grad, o.bias_out_grad,
        o.mean_mid, o.var_mid, o.mean_out, o.var_out,
    ]
    finals = [
        jax.ShapeDtypeStruct(shape, F32)
        for shape in (
            (R, CO), (n, 2 * rows, 2 * cols, CI), (MC, MI), (3, 3, CM, MI), (CM, CO),
            (MC, CO), (4 * CO, MI), (3, 3, CM, MI), (CM, CO),
        )
    ]
    ks = (o.k1, o.k2, o.k3, o.ks, o.k4, o.k5, o.k6)
    res = pl.pallas_call(
        finish_kernel,
        out_shape=finals + [jax.ShapeDtypeStruct(v.shape, F32) for v in passed],
        in_specs=[ANY] * 9 + [VM] * 10,
        out_specs=[ANY] * 9 + [VM] * 8,
        scratch_shapes=[pltpu.VMEM((R, CO), F32), pltpu.VMEM((4 * R, CI), F32)]
        + [pltpu.VMEM(k.shape, BF) for k in ks]
        + [pltpu.VMEM(f.shape, F32) for f in finals]
        + [pltpu.SemaphoreType.DMA((18,))],
        compiler_params=pltpu.CompilerParams(vmem_limit_bytes=VMEM_LIMIT),
    )(o.block_out, o.images_grad, *ks, po, pi, *passed)
    block_out = res[0].reshape(n, cols, rows, CO).transpose(0, 2, 1, 3)
    return (block_out, *res[1:])


def exact(pick, value):
    high = value.astype(BF)
    low = (value - high.astype(F32)).astype(BF)
    return mm(pick, high) + mm(pick, low)


ORDER = (5, 3, 7, 6, 4, 8, 2, 1, 0)


def finish_kernel(*refs):
    ins, po, pi, small = refs[:9], refs[9], refs[10], refs[11:19]
    outs, small_outs = refs[19:28], refs[28:36]
    held, made, sems = refs[36:45], refs[45:54], refs[54]
    loads = [pltpu.make_async_copy(a, v, sems.at[k]) for k, (a, v) in enumerate(zip(ins, held))]
    stores = [
        pltpu.make_async_copy(v, a, sems.at[9 + k]) for k, (v, a) in enumerate(zip(made, outs))
    ]
    for k in ORDER:
        loads[k].start()
    for a, v in zip(small, small_outs):
        v[...] = a[...]

    def rows_of(k):
        src, dst = held[k], made[k]
        size = math.prod(src.shape[1:-1])
        for rank in range(4):
            dst[rank * size : (rank + 1) * size, :] = (
                src[rank].reshape(size, src.shape[-1]).astype(F32)
            )

    def taps_of(k):
        src, dst = held[k], made[k]
        size = src.shape[3]

        def tap(t):
            for rank in range(4):
                for h in range(src.shape[1]):
                    at = (src.shape[1] * rank + h) * size
                    dst[t // 3, t % 3, at : at + size, :] = src[rank, h, t].astype(F32)

        for t in range(src.shape[2]):
            tap(t)
            store = pltpu.make_async_copy(dst.at[t // 3, t % 3], outs[k].at[t // 3, t % 3], sems.at[9 + k])
            store.start()

    def block():
        made[0][...] = exact(po[...], held[0][...])

    def images():
        half = held[1].shape[0] // 2
        for a in range(2):
            value = exact(pi[...], held[1][a * half : (a + 1) * half, :])
            value = value.reshape(-1, *made[1].shape[2:])
            rows = made[1].shape[1] // 2
            for at in range(value.shape[0]):
                made[1][at // rows, 2 * (at % rows) + a] = value[at]

    for k in ORDER:
        loads[k].wait()
        if k == 0:
            block()
        elif k == 1:
            images()
        elif k in (3, 7):
            taps_of(k)
        else:
            rows_of(k)
        if k not in (3, 7):
            stores[k].start()
    for copy in stores:
        copy.wait()


def solution(mesh):
    in_specs = (
        P("batch", None, None, "chan"),
        P(),
        P(),
        P(None, "chan"),
        P(None, None, None, "chan"),
        P(None, "chan"),
        P(None, "chan"),
        P(None, "chan"),
        P(None, None, None, "chan"),
        P(None, "chan"),
        P(None, "chan"),
        P(None, "chan"),
        P(None, "chan"),
        P(None, "chan"),
        P("batch", None, None, "chan"),
    )
    out_specs = (
        P("batch", None, None, "chan"),
        P("batch", None, None, "chan"),
        P(None, "chan"),
        P(None, None, None, "chan"),
        P(None, "chan"),
        P(None, "chan"),
        P(None, "chan"),
        P(None, None, None, "chan"),
        P(None, "chan"),
        P(None, "chan"),
        P(None, "chan"),
        P(None, "chan"),
        P(None, "chan"),
        P(None, "chan"),
        P(None, "chan"),
        P(None, "chan"),
        P(None, "chan"),
    )
    fused = mesh.shape["chan"] == 4 and mesh.shape["batch"] == 8
    return jax.shard_map(
        fused_on_device if fused else on_device, mesh=mesh, in_specs=in_specs, out_specs=out_specs, check_vma=False
    )
```

```python
import functools
import math
import types

import jax
import jax.numpy as jnp
import ml_dtypes
import numpy as np
from jax import lax
from jax.experimental import pallas as pl
from jax.experimental.pallas import tpu as pltpu
from jax.sharding import PartitionSpec as P

EPS = 1e-05
VMEM_LIMIT = 60 * 1024 * 1024


def shortened(shard):
    return jax.tree.map(lambda a: a.astype(jnp.bfloat16) if a.dtype == jnp.float32 else a, shard)


def frame_masks(heights, widths, rows, cols):
    tall = heights[:, None, None]
    broad = widths[:, None, None]
    row_in = jnp.arange(2 * rows, dtype=jnp.int32)[None, :, None]
    col_in = jnp.arange(2 * cols, dtype=jnp.int32)[None, None, :]
    row_out = jnp.arange(rows, dtype=jnp.int32)[None, :, None]
    col_out = jnp.arange(cols, dtype=jnp.int32)[None, None, :]
    inner = ((row_in < 2 * tall) & (col_in < 2 * broad)).astype(jnp.float32)[..., None]
    outer = ((row_out < tall) & (col_out < broad)).astype(jnp.float32)[..., None]
    return (inner, outer)


def silu_slope(value):
    sig = jax.nn.sigmoid(value)
    return sig * (1.0 + value * (1.0 - sig))


def convolve(source, kernel, stride, rows, cols):
    taps = kernel.shape[0]
    margin = taps // 2
    padded = jnp.pad(source, ((0, 0), (margin, margin), (margin, margin), (0, 0)))
    total = None
    for top in range(taps):
        for left in range(taps):
            window = padded[
                :, top : top + stride * rows : stride, left : left + stride * cols : stride, :
            ]
            term = jnp.einsum(
                "nhwc,cd->nhwd", window, kernel[top, left], preferred_element_type=jnp.float32
            )
            total = term if total is None else total + term
    return total


def kernel_grad(source, grad, stride, taps):
    rows, cols = (grad.shape[1], grad.shape[2])
    margin = taps // 2
    padded = jnp.pad(source, ((0, 0), (margin, margin), (margin, margin), (0, 0)))
    return jnp.stack(
        [
            jnp.stack(
                [
                    jnp.einsum(
                        "nhwc,nhwd->cd",
                        padded[
                            :,
                            top : top + stride * rows : stride,
                            left : left + stride * cols : stride,
                            :,
                        ],
                        grad,
                        preferred_element_type=jnp.float32,
                    )
                    for left in range(taps)
                ]
            )
            for top in range(taps)
        ]
    )


def spread_back(grad, kernel, stride):
    taps = kernel.shape[0]
    margin = taps // 2
    total = None
    for top in range(taps):
        for left in range(taps):
            term = jnp.einsum(
                "nhwd,cd->nhwc", grad, kernel[top, left], preferred_element_type=jnp.float32
            )
            placed = lax.pad(
                term,
                jnp.float32(0.0),
                (
                    (0, 0, 0),
                    (top, 2 * margin - top + stride - 1, stride - 1),
                    (left, 2 * margin - left + stride - 1, stride - 1),
                    (0, 0, 0),
                ),
            )
            total = placed if total is None else total + placed
    rows, cols = (grad.shape[1], grad.shape[2])
    return total[:, margin : margin + stride * rows, margin : margin + stride * cols, :]


def norm_forward(pre, mask, count, gain, bias):
    mean = lax.psum(jnp.sum(pre * mask, axis=(0, 1, 2)), "batch") / count
    centered = (pre - mean) * mask
    spread = lax.psum(jnp.sum(centered * centered, axis=(0, 1, 2)), "batch") / count
    inv = lax.rsqrt(spread + EPS)
    hat = (pre - mean) * inv
    return (hat * gain + bias, hat, inv, mean, spread)


def norm_backward(grad, hat, mask, count, gain, inv):
    masked = grad * mask
    bias_grad, gain_grad = lax.psum(
        (jnp.sum(masked, axis=(0, 1, 2)), jnp.sum(masked * hat, axis=(0, 1, 2))), "batch"
    )
    pre_grad = mask * gain * inv * (grad - (bias_grad + hat * gain_grad) / count)
    return (pre_grad.astype(jnp.bfloat16), gain_grad, bias_grad)


def widen(feature):
    return lax.all_gather(feature, "chan", axis=3, tiled=True)


def input_grad(grad, kernel, stride):
    return jax.tree.map(
        lambda part: part.astype(jnp.float32),
        lax.psum_scatter(
            shortened(spread_back(grad, kernel, stride)), "chan", scatter_dimension=3, tiled=True
        ),
    )


def image_back(grad_one, grad_side, kernels):
    summands = spread_back(grad_one, kernels[0], 1) + spread_back(grad_side, kernels[3], 2)
    return lax.psum_scatter(
        summands.astype(jnp.bfloat16), "chan", scatter_dimension=3, tiled=True
    ).astype(jnp.float32)


def on_device(
    images,
    heights,
    widths,
    reduce_first,
    spatial_first,
    expand_first,
    shortcut,
    reduce_second,
    spatial_second,
    expand_second,
    gain_mid,
    bias_mid,
    gain_out,
    bias_out,
    cotangent,
):
    local = images.shape[0]
    rows, cols = (cotangent.shape[1], cotangent.shape[2])
    offset = lax.axis_index("batch") * local
    inner, outer = frame_masks(
        lax.dynamic_slice_in_dim(heights, offset, local),
        lax.dynamic_slice_in_dim(widths, offset, local),
        rows,
        cols,
    )
    count_out = jnp.sum(heights * widths).astype(jnp.float32)
    count_in = 4.0 * count_out
    kernels = (
        reduce_first[None, None],
        spatial_first,
        expand_first[None, None],
        shortcut[None, None],
        reduce_second[None, None],
        spatial_second,
        expand_second[None, None],
    )
    source = images * inner.astype(jnp.bfloat16)
    whole_source = lax.all_gather(source, "chan", axis=3, tiled=True)
    pre_one = convolve(whole_source, kernels[0], 1, 2 * rows, 2 * cols)
    normed_one, hat_one, inv_one, mean_one, spread_one = norm_forward(
        pre_one, inner, count_in, gain_mid[0], bias_mid[0]
    )
    whole_one = widen((jax.nn.silu(normed_one) * inner).astype(jnp.bfloat16))
    pre_two = convolve(whole_one, kernels[1], 2, rows, cols)
    normed_two, hat_two, inv_two, mean_two, spread_two = norm_forward(
        pre_two, outer, count_out, gain_mid[1], bias_mid[1]
    )
    whole_two = widen((jax.nn.silu(normed_two) * outer).astype(jnp.bfloat16))
    pre_three = convolve(whole_two, kernels[2], 1, rows, cols)
    normed_three, hat_three, inv_three, mean_three, spread_three = norm_forward(
        pre_three, outer, count_out, gain_out[0], bias_out[0]
    )
    pre_side = convolve(whole_source, kernels[3], 2, rows, cols)
    normed_side, hat_side, inv_side, mean_side, spread_side = norm_forward(
        pre_side, outer, count_out, gain_out[1], bias_out[1]
    )
    block_mid = jax.nn.silu(normed_three + normed_side) * outer
    whole_mid = widen(block_mid.astype(jnp.bfloat16))
    pre_four = convolve(whole_mid, kernels[4], 1, rows, cols)
    normed_four, hat_four, inv_four, mean_four, spread_four = norm_forward(
        pre_four, outer, count_out, gain_mid[2], bias_mid[2]
    )
    whole_four = widen((jax.nn.silu(normed_four) * outer).astype(jnp.bfloat16))
    pre_five = convolve(whole_four, kernels[5], 1, rows, cols)
    normed_five, hat_five, inv_five, mean_five, spread_five = norm_forward(
        pre_five, outer, count_out, gain_mid[3], bias_mid[3]
    )
    whole_five = widen((jax.nn.silu(normed_five) * outer).astype(jnp.bfloat16))
    pre_six = convolve(whole_five, kernels[6], 1, rows, cols)
    normed_six, hat_six, inv_six, mean_six, spread_six = norm_forward(
        pre_six, outer, count_out, gain_out[2], bias_out[2]
    )
    result = jax.nn.silu(normed_six + block_mid) * outer
    grad_sum_b = cotangent.astype(jnp.float32) * outer * silu_slope(normed_six + block_mid)
    grad_six, gain_six, bias_six = norm_backward(
        grad_sum_b, hat_six, outer, count_out, gain_out[2], inv_six
    )
    kern_six = kernel_grad(whole_five, grad_six, 1, 1)
    grad_feat_five = input_grad(grad_six, kernels[6], 1)
    grad_five, gain_five, bias_five = norm_backward(
        grad_feat_five * outer * silu_slope(normed_five),
        hat_five,
        outer,
        count_out,
        gain_mid[3],
        inv_five,
    )
    kern_five = kernel_grad(whole_four, grad_five, 1, 3)
    grad_feat_four = input_grad(grad_five, kernels[5], 1)
    grad_four, gain_four, bias_four = norm_backward(
        grad_feat_four * outer * silu_slope(normed_four),
        hat_four,
        outer,
        count_out,
        gain_mid[2],
        inv_four,
    )
    kern_four = kernel_grad(whole_mid, grad_four, 1, 1)
    grad_mid = grad_sum_b + input_grad(grad_four, kernels[4], 1)
    grad_sum_a = grad_mid * outer * silu_slope(normed_three + normed_side)
    grad_three, gain_three, bias_three = norm_backward(
        grad_sum_a, hat_three, outer, count_out, gain_out[0], inv_three
    )
    grad_side, gain_side, bias_side = norm_backward(
        grad_sum_a, hat_side, outer, count_out, gain_out[1], inv_side
    )
    kern_three = kernel_grad(whole_two, grad_three, 1, 1)
    kern_side = kernel_grad(whole_source, grad_side, 2, 1)
    grad_feat_two = input_grad(grad_three, kernels[2], 1)
    grad_two, gain_two, bias_two = norm_backward(
        grad_feat_two * outer * silu_slope(normed_two),
        hat_two,
        outer,
        count_out,
        gain_mid[1],
        inv_two,
    )
    kern_two = kernel_grad(whole_one, grad_two, 2, 3)
    grad_feat_one = input_grad(grad_two, kernels[1], 2)
    grad_one, gain_one, bias_one = norm_backward(
        grad_feat_one * inner * silu_slope(normed_one),
        hat_one,
        inner,
        count_in,
        gain_mid[0],
        inv_one,
    )
    kern_one = kernel_grad(whole_source, grad_one, 1, 1)
    images_grad = image_back(grad_one, grad_side, kernels) * inner
    summed = (
        lax.psum(kern_one.astype(jnp.bfloat16), "batch").astype(jnp.float32),
        lax.psum(kern_two.astype(jnp.bfloat16), "batch").astype(jnp.float32),
        lax.psum(kern_three.astype(jnp.bfloat16), "batch").astype(jnp.float32),
        lax.psum(kern_side.astype(jnp.bfloat16), "batch").astype(jnp.float32),
        lax.psum(kern_four.astype(jnp.bfloat16), "batch").astype(jnp.float32),
        lax.psum(kern_five.astype(jnp.bfloat16), "batch").astype(jnp.float32),
        lax.psum(kern_six.astype(jnp.bfloat16), "batch").astype(jnp.float32),
    )
    counts_mid = jnp.stack([count_in, count_out, count_out, count_out])[:, None]
    mean_mid_batch = jnp.stack([mean_one, mean_two, mean_four, mean_five])
    var_mid_batch = (
        jnp.stack([spread_one, spread_two, spread_four, spread_five])
        * counts_mid
        / (counts_mid - 1.0)
    )
    mean_out_batch = jnp.stack([mean_three, mean_side, mean_six])
    var_out_batch = (
        jnp.stack([spread_three, spread_side, spread_six]) * count_out / (count_out - 1.0)
    )
    return (
        result,
        images_grad,
        summed[0][0, 0],
        summed[1],
        summed[2][0, 0],
        summed[3][0, 0],
        summed[4][0, 0],
        summed[5],
        summed[6][0, 0],
        jnp.stack([gain_one, gain_two, gain_four, gain_five]),
        jnp.stack([bias_one, bias_two, bias_four, bias_five]),
        jnp.stack([gain_three, gain_side, gain_six]),
        jnp.stack([bias_three, bias_side, bias_six]),
        mean_mid_batch,
        var_mid_batch,
        mean_out_batch,
        var_out_batch,
    )


MESH = pl.DeviceIdType.MESH
BF = jnp.bfloat16
F32 = jnp.float32


def flip(value, bit):
    return value + bit - 2 * bit * lax.rem(lax.div(value, bit), 2)


def gate(value):
    return 0.5 * jnp.tanh(0.5 * value) + 0.5


def tree(parts):
    while len(parts) > 1:
        parts = [parts[k] + parts[k + 1] for k in range(0, len(parts), 2)]
    return parts[0]


def wide_row(block):
    return jnp.concatenate([block[j : j + 1] for j in range(block.shape[0])], axis=1)


def fold(value):
    return jnp.sum(value.reshape(value.shape[0] // 8, 8, value.shape[1]), axis=0)


def mm(a, b):
    return jnp.dot(a, b, preferred_element_type=F32)


def mm_nt(a, b):
    return lax.dot_general(a, b, (((1,), (1,)), ((), ())), preferred_element_type=F32)


def mm_tn(a, b):
    return lax.dot_general(a, b, (((0,), (0,)), ((), ())), preferred_element_type=F32)


class Traffic:
    def __init__(self, sems):
        self.sems, self.used, self.sent = sems, 0, []

    def take(self):
        self.used += 1
        assert self.used <= SEMS
        return self.sems.at[self.used - 1]

    def plan(self, src, dst, device, send_sem=None, recv_sem=None):
        return pltpu.make_async_remote_copy(
            src_ref=src,
            dst_ref=dst,
            send_sem=self.take() if send_sem is None else send_sem,
            recv_sem=self.take() if recv_sem is None else recv_sem,
            device_id=device,
            device_id_type=MESH,
        )

    def spread(self, src, dst, peers, all_of):
        sems = self.take(), self.take()
        copies = [self.plan(a, d, p, *sems) for a, d, p in zip(src, dst, peers)]
        return copies, self.plan(all_of, all_of, peers[0], *sems)

    def push(self, src, dst, device):
        copy = self.plan(src, dst, device)
        copy.start()
        self.sent.append(copy)
        return copy

    def plan_local(self, src, dst, sem=None):
        return pltpu.make_async_copy(src, dst, self.take() if sem is None else sem)

    def local(self, src, dst):
        copy = self.plan_local(src, dst)
        copy.start()
        return copy

    def load(self, pairs, all_of):
        sem = self.take()
        for src, dst in pairs:
            pltpu.make_async_copy(src, dst, sem).start()
        return pltpu.make_async_copy(all_of, all_of, sem)


class Summed:
    def __init__(self, net, part, got, done, ring, spill, across=None):
        at, ahead, behind = ring
        self.part, self.got, self.done, self.at = part, got, done, at
        self.spill, self.spill_wait = spill
        legs, legs_back = net.take(), net.take()
        up = [part.at[at(4)]] + [got.at[k] for k in range(4)]
        down = [part.at[at(-3)]] + [got.at[k] for k in range(4, 7)]
        ends, ends_back = [[net.take() for k in range(4)] for _ in range(2)]
        self.out = [
            [net.plan(up[k], up[k + 1], ahead, legs, ends[k])]
            + ([net.plan(down[k], down[k + 1], behind, legs, ends[k])] if k < 3 else [])
            for k in range(4)
        ]
        self.back = [
            ([net.plan(done.at[at(-k)], done.at[at(-k)], ahead, legs_back, ends_back[k])] if k < 3 else [])
            + [net.plan(done.at[at(k)], done.at[at(k)], behind, legs_back, ends_back[k])]
            for k in range(4)
        ]
        self.pair, self.pair_back = (
            [
                net.plan(got.at[pl.ds(0, 1 + (k < 3))], got.at[pl.ds(0, 1 + (k < 3))], ahead, legs, end)
                for k, end in enumerate(some)
            ]
            for some in (ends, ends_back)
        )
        self.left = [
            net.plan(got, got, ahead, legs, legs),
            net.plan(done.at[pl.ds(0, 7)], done.at[pl.ds(0, 7)], ahead, legs_back, legs_back),
        ]
        self.across = across is not None
        if self.across:
            self.crossing = net.plan(got.at[3, 1], done.at[at(0), 1], across)
            self.left.append(self.crossing)
        self.todo = [self.begin] + [functools.partial(self.add, k) for k in range(3)]
        self.todo += [self.finish] + ([self.crossed] if self.across else [])
        self.todo += [functools.partial(self.pass_on, k) for k in range(3)] + [self.last]

    def step(self):
        self.todo.pop(0)()

    def start(self, copies):
        for copy in copies:
            copy.start()

    def begin(self):
        self.start(self.out[0])

    def add(self, k):
        self.pair[k].wait_recv()
        self.got[k] = self.got[k] + self.part[self.at(3 - k)]
        if k < 2:
            self.got[4 + k] = self.got[4 + k] + self.part[self.at(k - 2)]
        self.start(self.out[k + 1])

    def finish(self):
        self.pair[3].wait_recv()
        total = self.got[3] + self.got[6] + self.part[self.at(0)]
        if self.across:
            self.done[self.at(0), 0] = total[0]
            self.got[3, 1] = total[1]
            self.crossing.start()
        else:
            self.done[self.at(0)] = total
            self.start(self.back[0])

    def crossed(self):
        self.crossing.wait_recv()
        self.start(self.back[0])

    def pass_on(self, k):
        self.pair_back[k].wait_recv()
        self.start(self.back[k + 1])

    def last(self):
        self.pair_back[3].wait_recv()
        self.start(self.spill)

    def drain(self):
        for copy in self.left:
            copy.wait_send()
        self.spill_wait.wait()


class Direct:
    def __init__(self, net, part, got, done, place, peers, spill, across):
        self.part, self.got, self.done, self.place = part, got, done, place
        self.spill, self.spill_wait = spill
        n = len(peers)
        self.out, self.whole = net.spread(
            [part.at[peer[0]] for peer in peers],
            [got.at[k] for k in range(n)],
            peers,
            got.at[pl.ds(0, n)],
        )
        self.back, self.whole_back = net.spread(
            [done.at[place]] * n, [done.at[place]] * n, peers, done.at[pl.ds(0, n)]
        )
        self.crossing = net.plan(got.at[n, 1], done.at[place, 1], across)
        self.todo = [self.begin, self.finish, self.crossed, self.last]

    def step(self):
        self.todo.pop(0)()

    def begin(self):
        for copy in self.out:
            copy.start()

    def finish(self):
        total = self.part[self.place].astype(F32)
        self.whole.wait_recv()
        for k in range(len(self.out)):
            total = total + self.got[k].astype(F32)
        self.done[self.place, 0] = total[0].astype(BF)
        self.got[len(self.out), 1] = total[1].astype(BF)
        self.crossing.start()

    def crossed(self):
        self.crossing.wait_recv()
        for copy in self.back:
            copy.start()

    def last(self):
        self.whole_back.wait_recv()
        for copy in self.spill:
            copy.start()

    def drain(self):
        for copy in (self.whole, self.whole_back, self.crossing):
            copy.wait_send()
        self.spill_wait.wait()


SEMS = 296


def block_kernel(geo, names, *refs):
    g = types.SimpleNamespace(**dict(zip(names, refs)))
    R, QS, PS = geo.R, geo.QS, geo.PS
    CI, MI, CO = geo.CI, geo.MI, geo.CO
    NB = geo.NB
    r = lax.axis_index("chan")
    b = lax.axis_index("batch")
    r1, r2 = flip(r, 1), flip(r, 2)
    r3 = flip(r1, 2)
    ranks = (r, r1, r2, r3)
    core, far = (b, r1), (b, r2)
    peers = []
    for k in range(1, NB):
        other = b
        bit = 1
        while bit < NB:
            if k & bit:
                other = flip(other, bit)
            bit *= 2
        peers.append((other, r))
    net = Traffic(g.sems)
    def seat(batch):
        x, z = lax.rem(batch, 2), lax.div(batch, 2)
        return z + x * (7 - 2 * z)

    def batch_at(place):
        x = lax.div(place, 4)
        return 2 * (place + x * (7 - 2 * place)) + x

    way = 1 - 2 * lax.rem(r, 2)
    places = {k: lax.rem(seat(b) + way * k + 16, 8) for k in range(-3, 5)}
    ring = (places.get, (batch_at(places[1]), r), (batch_at(places[-1]), r))

    bar = pltpu.get_barrier_semaphore()
    everyone = [core, far] + peers
    for device in everyone:
        pl.semaphore_signal(bar, 1, device_id=device, device_id_type=MESH)

    def everywhere(src, dst, all_of):
        copies, whole = net.spread(src, dst, peers, all_of)
        for copy in copies:
            copy.start()
        net.sent.append(whole)
        return whole

    def rows_of(ref, rank, size):
        return ref.at[pl.ds(pl.multiple_of(rank * size, size), size)]

    def taps_of(ref, rank, size):
        return ref.at[:, pl.ds(pl.multiple_of(rank * size, size), size), :]

    ld_img = net.local(g.img, g.IMG)
    ld_w1 = [
        net.local(rows_of(g.w1, rank, CI), g.W1C.at[pl.ds(s * CI, CI), pl.ds(MI, MI)])
        for s, rank in enumerate((r, r1))
    ]

    area = [g.heights[k] * g.widths[k] for k in range(NB * PS)]
    first = lax.broadcasted_iota(jnp.int32, (R, 128), 0)

    def of_image(ref, image):
        value = jnp.full(image.shape, ref[b * PS], jnp.int32)
        for k in range(1, PS):
            value = jnp.where(image == k, ref[b * PS + k], value)
        return value

    def pixel(m):
        image, row, column = lax.rem(m, PS), lax.rem(lax.div(m, PS), geo.rows), lax.div(m, QS)
        good = (row < of_image(g.heights, image)) & (column < of_image(g.widths, image))
        return column, row, image, good

    g.mask[...] = jnp.where(pixel(first)[3], 1.0, 0.0)

    def row(scalar):
        return jnp.full((1, 128), scalar.astype(F32), F32)

    for k in range(NB):
        other = b if k == 0 else peers[k - 1][0]
        own = 0
        for j in range(PS):
            own = own + g.heights[other * PS + j] * g.widths[other * PS + j]
        g.aux[k : k + 1, :] = row(own)
        g.aux[NB + k : NB + k + 1, :] = 1.0 / row(own)
    count = row(sum(area))
    g.aux[16:17, :] = 1.0 / count
    g.aux[17:18, :] = count / (count - 1.0)
    g.aux[18:19, :] = 4.0 * count / (4.0 * count - 1.0)

    ld_img.wait()
    lane = lax.broadcasted_iota(jnp.int32, (R, 4 * R), 1)
    column, line, image, good = pixel(lax.broadcasted_iota(jnp.int32, (R, 1), 0))
    corner = image * 4 * geo.rows * geo.cols + 2 * line * 2 * geo.cols + 2 * column
    for ph in range(4):
        source = jnp.where(good, corner + (ph // 2) * 2 * geo.cols + ph % 2, -1)
        pick = jnp.where(lane == source, 1.0, 0.0).astype(BF)
        g.SRC[0, ph * R : (ph + 1) * R, :] = mm(pick, g.IMG[...]).astype(BF)

    pl.semaphore_wait(bar, len(everyone))

    rm_src = net.push(g.SRC.at[0], g.SRC.at[1], core)
    rm_w1 = [
        net.push(rows_of(g.w1, rank, CI), g.W1C.at[pl.ds(s * CI, CI), pl.ds(0, MI)], far)
        for s, rank in enumerate((r2, r3))
    ]
    rm_gain = [net.push(g.gm, g.GMF, far), net.push(g.bm, g.BMF, far)]
    piece = MI // 4
    rank = jnp.where(b < 4, r2, r3)
    at = pl.multiple_of(rank * MI + lax.rem(b, 4) * piece, piece)
    rm_w2 = net.push(g.w2.at[:, pl.ds(at, piece), :], g.W2F.at[b], far)
    ld_sc = net.load([(rows_of(g.wsc, rank, CI), g.WS.at[s]) for s, rank in enumerate(ranks)], g.WS)
    ld_w2 = net.load([(taps_of(g.w2, rank, MI), g.W2.at[:, s]) for s, rank in enumerate((r, r1))], g.W2)
    ld_w3 = net.load([(rows_of(g.w3, rank, MI), g.W3.at[s]) for s, rank in enumerate(ranks)], g.W3)
    ld_w4 = [
        net.local(rows_of(g.w4, rank, CO), g.W4C.at[pl.ds(s * CO, CO), pl.ds(MI, MI)])
        for s, rank in enumerate((r, r1))
    ]
    ld_w5 = net.load([(taps_of(g.w5, rank, MI), g.W5.at[:, s]) for s, rank in enumerate(ranks)], g.W5)
    ld_w6 = net.load([(rows_of(g.w6, rank, MI), g.W6.at[s]) for s, rank in enumerate(ranks)], g.W6)
    ld_cot = net.local(g.cot, g.COT)

    for ph in (1, 3):
        for s in range(2):
            g.F1[s, ph, 0:QS, :] = jnp.zeros((QS, MI), BF)
    for s in range(2):
        g.D1[1, s, 0:QS, :] = jnp.zeros((QS, MI), BF)
    for s in range(4):
        g.F4[s, 0:QS, :] = jnp.zeros((QS, MI), BF)
        g.F4[s, QS + R :, :] = jnp.zeros((QS, MI), BF)
        for d in range(2):
            g.D4[d, s, 0:QS, :] = jnp.zeros((QS, MI), BF)
            g.D4[d, s, QS + R :, :] = jnp.zeros((QS, MI), BF)
    for d in range(3):
        for s in range(2):
            g.E5[d, s, 0:QS, :] = jnp.zeros((QS, MI), BF)
            g.E5[d, s, QS + R :, :] = jnp.zeros((QS, MI), BF)
    for d in range(2):
        for s in range(4):
            g.E2[d, s, R:, :] = jnp.zeros((QS, MI), BF)

    for copy in ld_w1:
        copy.wait()
    rm_src.wait_recv()
    for copy in rm_w1:
        copy.wait_recv()
    rm_p1 = []
    for ph in range(4):
        span = slice(ph * R, (ph + 1) * R)
        both = jnp.concatenate([g.SRC[0, span, :], g.SRC[1, span, :]], axis=1)
        part = mm(both, g.W1C[...])
        g.P1S[ph] = part[:, :MI].astype(BF)
        rm_p1.append(net.push(g.P1S.at[ph], g.P1R.at[ph], far))
        g.PRE1[span, :] = part[:, MI:]

    rm_w2.wait_recv()
    rm_w2s = everywhere([g.W2F.at[b]] * (NB - 1), [g.W2F.at[b]] * (NB - 1), g.W2F.at[pl.ds(0, NB - 1)])

    rm_back = []
    for s, rank in enumerate((r1, r3)):
        rm_back.append(net.push(rows_of(g.w6, rank, MI), g.W6P.at[s], core))
        rm_back.append(net.push(taps_of(g.w5, rank, MI), g.W5P.at[:, s], core))
        rm_back.append(net.push(rows_of(g.w3, rank, MI), g.W3P.at[s], core))
        rm_back.append(net.push(rows_of(g.wsc, rank, CI), g.WSP.at[s], core))
    rm_back.append(net.push(taps_of(g.w2, r1, MI), g.W2P, core))
    rm_back.append(net.push(rows_of(g.w4, r1, CO), g.W4P.at[0], core))
    rm_back.append(net.push(rows_of(g.w1, r1, CI), g.W1P.at[0], core))
    rm_back.append(
        net.push(g.W1C.at[pl.ds(CI, CI), pl.ds(0, MI)], g.W1P.at[1], core)
    )

    aux = g.aux
    inv_out = aux[16:17, :]
    unb_out, unb_in = aux[17:18, :], aux[18:19, :]

    def mask_rows(at, size):
        return g.mask[pl.ds(at, size), :]

    def over(total, size, body, init):
        def step(i, carry):
            return body(pl.multiple_of(i * size, size), carry)

        return lax.fori_loop(0, total // size, step, init)

    NCH = 128 if R % 128 == 0 else QS
    WCH = QS

    def bc(mask, width):
        return jnp.concatenate([mask] * (width // 128), axis=1)

    def exchange(slots, payload_rows):
        others = range(1, NB)
        return everywhere(
            [slots.at[0] for _ in others],
            [slots.at[k] for k in others],
            slots.at[pl.ds(1, NB - 1)],
        )

    def narrow_local(pre, phases, prepare=None):
        total = jnp.zeros((8, MI), F32)
        for ph in range(phases):
            if prepare is not None:
                prepare(ph)

            def add(at, acc, ph=ph):
                return acc + fold(pre[pl.ds(ph * R + at, NCH), :] * mask_rows(at, NCH))

            total = over(R, NCH, add, total)
        total = jnp.sum(total, axis=0, keepdims=True)
        mean = total * (aux[8:9, :] * (1.0 / phases))
        squares = jnp.zeros((8, MI), F32)
        for ph in range(phases):

            def add2(at, acc, ph=ph):
                d = (pre[pl.ds(ph * R + at, NCH), :] - mean) * mask_rows(at, NCH)
                return acc + fold(d * d)

            squares = over(R, NCH, add2, squares)
        return total, jnp.sum(squares, axis=0, keepdims=True)

    def narrow_send(idx, first, second):
        slots = g.SN.at[idx]
        g.SN[idx, 0, 0:1, :] = first
        g.SN[idx, 0, 1:2, :] = second
        return exchange(slots, 2)

    def narrow_merge(idx, copies, phases):
        copies.wait_recv()
        sums = [g.SN[idx, k, 0:1, :] for k in range(NB)]
        squares = [g.SN[idx, k, 1:2, :] for k in range(NB)]
        return moments(sums, squares, phases)

    def moments(sums, squares, phases):
        inv_count = inv_out * (1.0 / phases)
        mean = tree(list(sums)) * inv_count
        terms = []
        for k in range(NB):
            d = sums[k] * (aux[8 + k : 9 + k, :] * (1.0 / phases)) - mean
            terms.append(squares[k] + aux[k : k + 1, :] * float(phases) * d * d)
        spread = tree(terms) * inv_count
        return mean, spread

    def wide_local(pre):
        def add(at, acc):
            m = bc(mask_rows(at, WCH), CO)
            return acc + fold(pre[pl.ds(at, WCH), :] * m)

        total = jnp.sum(over(R, WCH, add, jnp.zeros((8, CO), F32)), axis=0, keepdims=True)
        mean = total * bc(aux[8:9, :], CO)

        def add2(at, acc):
            m = bc(mask_rows(at, WCH), CO)
            d = (pre[pl.ds(at, WCH), :] - mean) * m
            return acc + fold(d * d)

        squares = jnp.sum(over(R, WCH, add2, jnp.zeros((8, CO), F32)), axis=0, keepdims=True)
        return total, squares

    NW = CO // 128

    def wide_put(slots, row, value):
        for j in range(NW):
            slots[0, row + j : row + j + 1, :] = value[:, j * 128 : (j + 1) * 128]

    def wide_send(idx, first, second):
        slots = g.SW.at[idx]
        wide_put(slots, 0, first)
        wide_put(slots, NW, second)
        return exchange(slots, 2 * NW)

    def wide_merge(idx, copies):
        copies.wait_recv()
        sums = [g.SW[idx, k, 0:NW, :] for k in range(NB)]
        squares = [g.SW[idx, k, NW : 2 * NW, :] for k in range(NB)]
        mean, spread = moments(sums, squares, 1)
        return wide_row(mean), wide_row(spread)

    def gather(buf, at, size):
        here = [buf(s).at[pl.ds(at, size)] for s in range(4)]
        near = net.push(here[0], here[1], core)
        away = net.push(here[0], here[2], far)
        return [near, away, here]

    def relay(chunk):
        near, away, here = chunk
        away.wait_recv()
        chunk.append(net.push(here[2], here[3], core))

    def landed(chunk):
        chunk[0].wait_recv()
        chunk[3].wait_recv()

    def lanes(parts):
        return jnp.concatenate(parts, axis=1)

    place = lax.broadcasted_iota(jnp.int32, (QS, 128), 0)
    keep_down = place >= PS
    keep_up = place < QS - PS

    def shifted(value, step):
        if step < 0:
            return jnp.where(keep_down, pltpu.roll(value, PS, 0), 0.0)
        return jnp.where(keep_up, pltpu.roll(value, QS - PS, 0), 0.0)

    def take_p1(ph):
        rm_p1[ph].wait_recv()

        def add(at, carry):
            rows = pl.ds(ph * R + at, NCH)
            g.PRE1[rows, :] = g.PRE1[rows, :] + g.P1R[ph, pl.ds(at, NCH), :].astype(F32)
            return carry

        over(R, NCH, add, 0)

    sum_one, sq_one = narrow_local(g.PRE1, 4, take_p1)
    st_one = narrow_send(0, sum_one, sq_one)
    rm_xs = net.push(g.SRC.at[0, pl.ds(0, R)], g.XS.at[0], far)

    def scale_of(spread, gain):
        inv = lax.rsqrt(spread + EPS)
        return inv, inv * gain

    mean_one, spread_one = narrow_merge(0, st_one, 4)
    inv_one, scale_one = scale_of(spread_one, g.gm[0:1, :])

    def narrow_feature(pre, mean, scale, bias, out, ph, at0):
        def body(at, carry):
            v = (pre[pl.ds(ph * R + at, NCH), :] - mean) * scale + bias
            out[pl.ds(at0 + at, NCH), :] = (v * gate(v) * mask_rows(at, NCH)).astype(BF)
            return carry

        over(R, NCH, body, 0)

    ch_one = []
    for ph in range(4):
        narrow_feature(
            g.PRE1, mean_one, scale_one, g.bm[0:1, :], g.F1.at[0, ph], ph, QS
        )
        span = pl.ds(QS, R)
        ch_one.append(net.push(g.F1.at[0, ph, span], g.F1.at[1, ph, span], core))

    def both_chips(part, sent, got, pre, pre_far):
        sent[...] = part.astype(BF)
        copy = net.push(sent, got, far)
        pre[...] = part[:, MI:]
        pre_far[...] = part[:, :MI]
        return copy

    def both_norms(idx, copy, got, pre, pre_far, row, feature, at0):
        copy.wait_recv()

        def add(at, carry):
            rows = pl.ds(at, NCH)
            pre[rows, :] = pre[rows, :] + got[rows, 0:MI].astype(F32)
            pre_far[rows, :] = pre_far[rows, :] + got[rows, MI : 2 * MI].astype(F32)
            return carry

        over(R, NCH, add, 0)
        slots = g.SB.at[idx]
        for k, value in enumerate((*narrow_local(pre, 1), *narrow_local(pre_far, 1))):
            g.SB[idx, 0, k : k + 1, :] = value
        exchange(slots, 4).wait_recv()
        results = []
        for k, gains, biases in ((0, g.gm, g.bm), (2, g.GMF, g.BMF)):
            sums = [g.SB[idx, j, k : k + 1, :] for j in range(NB)]
            squares = [g.SB[idx, j, k + 1 : k + 2, :] for j in range(NB)]
            mean, spread = moments(sums, squares, 1)
            inv, scale = scale_of(spread, gains[row : row + 1, :])
            here = pl.ds(at0, R)
            source = pre_far if k else pre
            narrow_feature(source, mean, scale, biases[row : row + 1, :], feature.at[k], 0, at0)
            results.append(
                net.push(feature.at[k, here], feature.at[k + 1, here], core)
            )
            if k == 0:
                kept = mean, spread, inv, scale
        return kept, results

    rm_xs.wait_recv()
    rm_xs2 = net.push(g.XS.at[0], g.XS.at[1], core)
    ld_sc.wait()
    rm_xs2.wait_recv()

    def strided():
        return [g.SRC[0, 0:R, :], g.SRC[1, 0:R, :], g.XS[0], g.XS[1]]

    pre_side = None
    for s, block in enumerate(strided()):
        term = mm(block, g.WS[s])
        pre_side = term if pre_side is None else pre_side + term
    g.PRES[...] = pre_side
    st_side = wide_send(0, *wide_local(g.PRES))

    ld_w2.wait()

    def chip_one(s, ph, down, left):
        rows = slice(0, R) if left else slice(QS, QS + R)
        return g.D1[ph - 2, s, rows, :] if down else g.F1[s, ph, rows, :]

    def far_two(tap, first):
        return jnp.concatenate([g.W2F[first + k, tap] for k in range(4)], axis=0)

    def both_two(tap):
        near = jnp.concatenate([g.W2[tap, s] for s in range(2)], axis=0)
        away = jnp.concatenate([far_two(tap, 0), far_two(tap, 4)], axis=0)
        return lanes([away, near])

    def taps_two(ph):
        top = (1,) if ph < 2 else (0, 2)
        left = (1,) if ph % 2 == 0 else (0, 2)
        return [(t, l) for t in top for l in left]

    def lower(ph, s):
        def move(at, carry):
            v = g.F1[s, ph, pl.ds(QS + at, QS), :].astype(F32)
            g.D1[ph - 2, s, pl.ds(QS + at, QS), :] = shifted(v, -1).astype(BF)
            return carry

        over(R, QS, move, 0)

    rm_w2s.wait_recv()
    rm_back.append(net.push(g.W2F.at[pl.ds(4, 4)], g.W2Q, core))
    part = None
    for ph in range(4):
        if ph >= 2:
            lower(ph, 0)
        ch_one[ph].wait_recv()
        if ph >= 2:
            lower(ph, 1)
        for t, l in taps_two(ph):
            term = mm(lanes([chip_one(s, ph, t == 0, l == 0) for s in range(2)]), both_two(3 * t + l))
            part = term if part is None else part + term
    rm_p2 = both_chips(part, g.P2S, g.P2R, g.PRE2, g.PRE2F)
    rm_w4 = [
        net.push(rows_of(g.w4, rank, CO), g.W4C.at[pl.ds(s * CO, CO), pl.ds(0, MI)], far)
        for s, rank in enumerate((r2, r3))
    ]
    for copy in rm_gain:
        copy.wait_recv()
    kept, ch_two = both_norms(0, rm_p2, g.P2R, g.PRE2, g.PRE2F, 1, g.F2, 0)
    mean_two, spread_two, inv_two, scale_two = kept
    ld_w3.wait()
    mean_side, spread_side = wide_merge(0, st_side)
    inv_side, scale_side = scale_of(spread_side, g.go[1:2, :])

    def four(ref):
        return lanes([ref[s] for s in range(4)])

    def half_product(ref, weight, a, b):
        return mm(lanes([ref[a], ref[b]]), jnp.concatenate([weight[a], weight[b]], axis=0))

    pre_three = half_product(g.F2, g.W3, 0, 2)
    for copy in ch_two:
        copy.wait_recv()
    g.PRE3[...] = pre_three + half_product(g.F2, g.W3, 1, 3)
    st_three = wide_send(1, *wide_local(g.PRE3))
    mean_three, spread_three = wide_merge(1, st_three)
    inv_three, scale_three = scale_of(spread_three, g.go[0:1, :])
    bias_three, bias_side = g.bo[0:1, :], g.bo[1:2, :]

    def mid_value(rows):
        return (
            (g.PRE3[rows, :] - mean_three) * scale_three
            + bias_three
            + (g.PRES[rows, :] - mean_side) * scale_side
            + bias_side
        )

    def mid_body(at, carry):
        rows = pl.ds(at, WCH)
        v = mid_value(rows)
        out = v * gate(v) * bc(mask_rows(at, WCH), CO)
        g.BM[rows, :] = out
        g.MIDC[0, rows, :] = out.astype(BF)
        return carry

    over(R, WCH, mid_body, 0)
    rm_mid = net.push(g.MIDC.at[0], g.MIDC.at[1], core)

    for copy in ld_w4:
        copy.wait()
    for copy in rm_w4:
        copy.wait_recv()
    rm_back.append(net.push(g.W4C.at[pl.ds(CO, CO), pl.ds(0, MI)], g.W4P.at[1], core))
    rm_mid.wait_recv()
    part = mm(lanes([g.MIDC[0], g.MIDC[1]]), g.W4C[...])
    rm_p4 = both_chips(part, g.P4S, g.P4R, g.PRE4, g.PRE4F)

    kept, ch_four = both_norms(1, rm_p4, g.P4R, g.PRE4, g.PRE4F, 2, g.F4, QS)
    mean_four, spread_four, inv_four, scale_four = kept
    ld_w5.wait()

    def kernel_rows(ref, tap, slots):
        return jnp.concatenate([ref[tap, s] for s in slots], axis=0)

    def spread_rows(src, dst_up, dst_down):
        def body(at, carry):
            rows = pl.ds(QS + at, QS)
            v = src[rows, :].astype(F32)
            dst_up[rows, :] = shifted(v, -1).astype(BF)
            dst_down[rows, :] = shifted(v, 1).astype(BF)
            return carry

        over(R, QS, body, 0)

    def fill_four(s):
        spread_rows(g.F4.at[s], g.D4.at[0, s], g.D4.at[1, s])

    fill_four(0)
    fill_four(2)

    def four_blocks(t, l, slots):
        rows = slice(l * QS, l * QS + R)
        if t == 1:
            return lanes([g.F4[s, rows, :] for s in slots])
        return lanes([g.D4[t // 2, s, rows, :] for s in slots])

    def whole_four(t, l):
        return four_blocks(t, l, range(4))

    pre_five = None
    for slots in ((0, 2), (1, 3)):
        if slots[0]:
            for s, copy in zip(slots, ch_four):
                copy.wait_recv()
                fill_four(s)
        for t in range(3):
            for l in range(3):
                term = mm(four_blocks(t, l, slots), kernel_rows(g.W5, 3 * t + l, slots))
                pre_five = term if pre_five is None else pre_five + term
    g.PRE5[...] = pre_five
    st_five = narrow_send(3, *narrow_local(g.PRE5, 1))
    mean_five, spread_five = narrow_merge(3, st_five, 1)
    inv_five, scale_five = scale_of(spread_five, g.gm[3:4, :])
    narrow_feature(g.PRE5, mean_five, scale_five, g.bm[3:4, :], g.F5.at[0], 0, 0)
    ch_five = gather(lambda s: g.F5.at[s], 0, R)
    ld_w6.wait()
    ld_cot.wait()
    g.COTP[...] = mm_tn(g.po[...], g.COT[...])
    ch_five[0].wait_recv()
    pre_six = half_product(g.F5, g.W6, 0, 1)
    relay(ch_five)
    ch_five[3].wait_recv()
    g.PRE6[...] = pre_six + half_product(g.F5, g.W6, 2, 3)
    st_six = wide_send(2, *wide_local(g.PRE6))
    mean_six, spread_six = wide_merge(2, st_six)
    inv_six, scale_six = scale_of(spread_six, g.go[2:3, :])
    bias_six = g.bo[2:3, :]

    def last_body(at, carry):
        acc_b, acc_g = carry
        rows = pl.ds(at, WCH)
        m = bc(mask_rows(at, WCH), CO)
        hat = (g.PRE6[rows, :] - mean_six) * inv_six
        v = (g.PRE6[rows, :] - mean_six) * scale_six + bias_six + g.BM[rows, :]
        s = gate(v)
        g.OUT[rows, :] = v * s * m
        grad = g.COTP[rows, :] * m * (s * (1.0 + v * (1.0 - s)))
        g.GSB[rows, :] = grad
        return acc_b + fold(grad), acc_g + fold(grad * hat)

    zero_w = jnp.zeros((8, CO), F32)
    acc_b, acc_g = over(R, WCH, last_body, (zero_w, zero_w))

    def down(value):
        return jnp.sum(value, axis=0, keepdims=True)

    st = wide_send(3, down(acc_b), down(acc_g))

    out_block = net.local(g.OUT, g.block_out)

    def wide_sums(ref, copies, count):
        copies.wait_recv()
        return [
            wide_row(tree([ref[k, j * NW : (j + 1) * NW, :] for k in range(NB)]))
            for j in range(count)
        ]

    def narrow_sums(idx, copies):
        copies.wait_recv()
        return [tree([g.SN[idx, k, j : j + 1, :] for k in range(NB)]) for j in range(2)]

    bsum_six, gsum_six = wide_sums(g.SW.at[3], st, 2)
    inv_wide = bc(inv_out, CO)

    def wide_pre_grad(grad, pre, mean, inv, scale, bsum, gsum, out):
        mb, mg = bsum * inv_wide, gsum * inv_wide

        def body(at, carry):
            rows = pl.ds(at, WCH)
            hat = (pre[rows, :] - mean) * inv
            e = bc(mask_rows(at, WCH), CO) * scale * (grad[rows, :] - (mb + hat * mg))
            out[rows, :] = e.astype(BF)
            return carry

        over(R, WCH, body, 0)

    wide_pre_grad(
        g.GSB, g.PRE6, mean_six, inv_six, scale_six, bsum_six, gsum_six, g.E6.at[0]
    )
    for copy in rm_back:
        copy.wait_recv()

    def swap(ref):
        return net.push(ref.at[0], ref.at[1], core)

    def reduce_back(part, sent, got):
        sent[...] = part[:, MI:].astype(BF)
        return net.push(sent, got, far)

    def wide_back(e, own, other):
        near = lanes([own[0], other[0]])
        away = lanes([own[2], other[1]])
        return mm_nt(lanes([e[0], e[1]]), jnp.concatenate([near, away], axis=0))

    def narrow_back(idx, near, got, copy, phases, pre, mean, inv, scale, bias, order=None):
        acc_b = jnp.zeros((8, MI), F32)
        acc_g = jnp.zeros((8, MI), F32)
        for ph in range(phases):
            if copy is not None:
                copy[ph].wait_recv()

            def body(at, carry, ph=ph):
                b_acc, g_acc = carry
                rows = pl.ds(ph * R + at, NCH)
                hat = (pre[rows, :] - mean) * inv
                v = (pre[rows, :] - mean) * scale + bias
                s = gate(v)
                feat = near[rows, :]
                if got is not None:
                    feat = feat + got[rows, :].astype(F32)
                grad = feat * mask_rows(at, NCH) * (s * (1.0 + v * (1.0 - s)))
                near[rows, :] = grad
                return b_acc + fold(grad), g_acc + fold(grad * hat)

            acc_b, acc_g = over(R, NCH, body, (acc_b, acc_g))
        return narrow_send(idx, down(acc_b), down(acc_g))

    def narrow_pre_grad(grad, pre, mean, inv, scale, bsum, gsum, phases, ph, out, at0):
        inv_count = inv_out * (1.0 / phases)
        mb, mg = bsum * inv_count, gsum * inv_count

        def body(at, carry):
            rows = pl.ds(ph * R + at, NCH)
            hat = (pre[rows, :] - mean) * inv
            e = mask_rows(at, NCH) * scale * (grad[rows, :] - (mb + hat * mg))
            out[pl.ds(at0 + at, NCH), :] = e.astype(BF)
            return carry

        over(R, NCH, body, 0)

    outs = [out_block]

    def give(src, dst):
        outs.append(net.local(src, dst))

    cp = swap(g.E6)
    cp.wait_recv()
    part = wide_back(g.E6, g.W6, g.W6P)
    cp = [reduce_back(part, g.B5S, g.B5R)]
    g.GF5[...] = part[:, :MI]
    def rows_grad(part, value, s):
        half = value.shape[0] // 2
        for h in range(2):
            part[2 * s + h] = value[h * half : (h + 1) * half].astype(BF)

    def taps_grad(part, tap, value):
        half = MI // 2
        for p in range(8):
            part[p, tap] = value[p * half : (p + 1) * half].astype(BF)

    jobs = []

    def spilled(done, targets):
        sem = net.take()
        copies = [net.plan_local(source, place, sem) for source, place in targets]
        return copies, net.plan_local(done, done, sem)

    def job(part, got, done, targets, across=None):
        jobs.append(Summed(net, part, got, done, ring, spilled(done, targets), across))

    def pump(most=3):
        left = sorted((work for work in jobs if work.todo), key=lambda work: -len(work.todo))
        for work in left[:most]:
            work.step()

    def slots_to(part, place):
        return [(part.at[pl.ds(2 * s, 2)], place(ranks[s])) for s in range(4)]

    def chips_to(part, out, taps=None):
        def place(rank):
            return out.at[rank] if taps is None else out.at[rank, :, taps]

        return [
            (part.at[pl.ds(4 * s, 4), v], place(ranks[2 * v + s]))
            for s in range(2)
            for v in range(2)
        ]

    for s in range(4):
        rows_grad(g.K6, mm_tn(g.F5[s], g.E6[0]), s)
    job(g.K6, g.K6R, g.K6D, slots_to(g.K6D, lambda rank: g.k6.at[rank]))
    pump()
    st = narrow_back(
        4, g.GF5, g.B5R, cp, 1, g.PRE5, mean_five, inv_five, scale_five, g.bm[3:4, :]
    )
    pump()
    bsum_five, gsum_five = narrow_sums(4, st)
    narrow_pre_grad(
        g.GF5, g.PRE5, mean_five, inv_five, scale_five, bsum_five, gsum_five, 1, 0,
        g.E5.at[1, 0], QS,
    )
    cp = net.push(g.E5.at[1, 0, pl.ds(QS, R)], g.E5.at[1, 1, pl.ds(QS, R)], core)
    spread_rows(g.E5.at[1, 0], g.E5.at[0, 0], g.E5.at[2, 0])
    cp.wait_recv()
    spread_rows(g.E5.at[1, 1], g.E5.at[0, 1], g.E5.at[2, 1])
    pump()

    def taps_back(own, other, tap):
        near = lanes([own[tap, 0], other[tap, 0]])
        away = lanes([own[tap, 2], other[tap, 1]])
        return jnp.concatenate([near, away], axis=0)

    part = None
    for t in range(3):
        for l in range(3):
            rows = slice((2 - l) * QS, (2 - l) * QS + R)
            e = lanes([g.E5[2 - t, s, rows, :] for s in range(2)])
            term = mm_nt(e, taps_back(g.W5, g.W5P, 3 * t + l))
            part = term if part is None else part + term
    cp = [reduce_back(part, g.B4S, g.B4R)]
    g.GF4[...] = part[:, :MI]
    pump()
    own_five = g.E5[1, 0, QS : QS + R, :]

    def five_grad(part, first, last):
        for tap in range(first, last):
            taps_grad(part, tap - first, mm_tn(whole_four(tap // 3, tap % 3), own_five))

    five_grad(g.K5A, 0, 5)
    job(g.K5A, g.K5AR, g.K5AD, slots_to(g.K5AD, lambda rank: g.k5.at[rank, :, pl.ds(0, 5)]))
    five_grad(g.K5B, 5, 9)
    job(g.K5B, g.K5BR, g.K5BD, slots_to(g.K5BD, lambda rank: g.k5.at[rank, :, pl.ds(5, 4)]))
    pump()
    st = narrow_back(
        5, g.GF4, g.B4R, cp, 1, g.PRE4, mean_four, inv_four, scale_four, g.bm[2:3, :]
    )
    pump()
    bsum_four, gsum_four = narrow_sums(5, st)
    narrow_pre_grad(
        g.GF4, g.PRE4, mean_four, inv_four, scale_four, bsum_four, gsum_four, 1, 0,
        g.G4.at[0], 0,
    )
    ch = gather(lambda s: g.G4.at[s], 0, R)
    relay(ch)
    pump()
    landed(ch)
    mid_back = mm_nt(
        four(g.G4),
        lanes([g.W4C[0:CO, MI:], g.W4P[0], g.W4C[0:CO, :MI], g.W4P[1]]),
    )
    g.GMID[...] = mid_back

    def mid_back_body(at, carry):
        a_b, a_3, a_s = carry
        rows = pl.ds(at, WCH)
        v = mid_value(rows)
        s = gate(v)
        grad = (g.GSB[rows, :] + g.GMID[rows, :]) * bc(mask_rows(at, WCH), CO)
        grad = grad * (s * (1.0 + v * (1.0 - s)))
        g.GMID[rows, :] = grad
        hat3 = (g.PRE3[rows, :] - mean_three) * inv_three
        hats = (g.PRES[rows, :] - mean_side) * inv_side
        return a_b + fold(grad), a_3 + fold(grad * hat3), a_s + fold(grad * hats)

    a_b, a_3, a_s = over(R, WCH, mid_back_body, (zero_w, zero_w, zero_w))
    for j, value in enumerate((a_b, a_3, a_s, zero_w)):
        wide_put(g.SA, j * NW, down(value))
    st = exchange(g.SA, 4 * NW)
    e4 = lanes([g.G4[0], g.G4[2]])

    def chip_grad(part, s, value):
        size = value.shape[0] // 4
        for p in range(4):
            for w in range(2):
                block = value[p * size : (p + 1) * size, w * MI : (w + 1) * MI]
                part[4 * s + p, w] = block.astype(BF)

    for s in range(2):
        chip_grad(g.K4, s, mm_tn(g.MIDC[s], e4))
    job(g.K4, g.K4R, g.K4D, chips_to(g.K4D, g.k4), far)
    pump()
    bsum_a, gsum_three, gsum_side = wide_sums(g.SA, st, 3)
    wide_pre_grad(
        g.GMID, g.PRE3, mean_three, inv_three, scale_three, bsum_a, gsum_three,
        g.E3.at[0],
    )
    cp = swap(g.E3)
    wide_pre_grad(
        g.GMID, g.PRES, mean_side, inv_side, scale_side, bsum_a, gsum_side, g.ES.at[0]
    )
    cp_side = swap(g.ES)
    pump()
    cp.wait_recv()
    part = wide_back(g.E3, g.W3, g.W3P)
    cp = [reduce_back(part, g.B2S, g.B2R)]
    g.GF2[...] = part[:, :MI]
    for s in range(4):
        rows_grad(g.K3, mm_tn(g.F2[s], g.E3[0]), s)
    job(g.K3, g.K3R, g.K3D, slots_to(g.K3D, lambda rank: g.k3.at[rank]))
    pump()
    st = narrow_back(
        6, g.GF2, g.B2R, cp, 1, g.PRE2, mean_two, inv_two, scale_two, g.bm[1:2, :]
    )
    pump()
    cp_side.wait_recv()
    es = lanes([g.ES[0], g.ES[1]])
    g.IGS[...] = mm_nt(es, lanes([g.WS[0], g.WSP[0]]))
    half = CO // 2
    for s, block in enumerate(strided()):
        grad = mm_tn(block, g.ES[0])
        rows_grad(g.KSA, grad[:, :half], s)
        rows_grad(g.KSB, grad[:, half:], s)
    job(g.KSA, g.KSAR, g.KSAD, slots_to(g.KSAD, lambda rank: g.ks.at[rank, :, :, pl.ds(0, half)]))
    job(g.KSB, g.KSBR, g.KSBD, slots_to(g.KSBD, lambda rank: g.ks.at[rank, :, :, pl.ds(half, half)]))
    pump()
    pump()
    bsum_two, gsum_two = narrow_sums(6, st)
    narrow_pre_grad(
        g.GF2, g.PRE2, mean_two, inv_two, scale_two, bsum_two, gsum_two, 1, 0,
        g.E2.at[0, 0], 0,
    )
    ch = gather(lambda s: g.E2.at[0, s], 0, R)

    def lift(s):
        def body(at, carry):
            rows = pl.ds(at, QS)
            v = g.E2[0, s, rows, :].astype(F32)
            g.E2[1, s, rows, :] = shifted(v, 1).astype(BF)
            return carry

        over(R, QS, body, 0)

    def two_grad(w, slot):
        e = g.E2[0, slot, 0:R, :]
        for ph in range(4):
            for t, l in taps_two(ph):
                tap = 3 * t + l
                part, tap = (g.K2A, tap) if tap < 5 else (g.K2B, tap - 5)
                for s in range(2):
                    grad = mm_tn(chip_one(s, ph, t == 0, l == 0), e)
                    for p in range(4):
                        rows = grad[p * piece : (p + 1) * piece]
                        part[4 * s + p, w, tap] = rows.astype(BF)

    lift(0)
    pump()
    two_grad(0, 0)
    ch[0].wait_recv()
    lift(1)
    relay(ch)
    two_grad(1, 2)
    for name, first, count in (("K2A", 0, 5), ("K2B", 5, 4)):
        bufs = [getattr(g, name + end) for end in ("", "R", "D")]
        job(*bufs, chips_to(bufs[2], g.k2, pl.ds(first, count)), far)
    pump()
    lift(2)
    ch[3].wait_recv()
    lift(3)

    def own_two(tap):
        far_own = jnp.concatenate([g.W2F[k, tap] for k in range(4)], axis=0)
        far_other = jnp.concatenate([g.W2Q[k, tap] for k in range(4)], axis=0)
        return lanes([g.W2[tap, 0], g.W2P[tap], far_own, far_other])

    for ph in range(4):
        part = None
        for t, l in taps_two(ph):
            rows = slice(QS, QS + R) if l == 0 else slice(0, R)
            e = lanes([g.E2[1 if t == 0 else 0, s, rows, :] for s in range(4)])
            term = mm_nt(e, own_two(3 * t + l))
            part = term if part is None else part + term
        g.GF1[ph * R : (ph + 1) * R, :] = part
        if ph == 3:
            pump()
    st = narrow_back(
        7, g.GF1, None, None, 4, g.PRE1, mean_one, inv_one, scale_one, g.bm[0:1, :]
    )
    side_far = mm_nt(es, lanes([g.WS[2], g.WSP[1]]))
    g.BSS[...] = side_far.astype(BF)
    cp_bs = net.push(g.BSS, g.BSR, far)
    pump()
    bsum_one, gsum_one = narrow_sums(7, st)
    ch = []
    for ph in range(4):
        narrow_pre_grad(
            g.GF1, g.PRE1, mean_one, inv_one, scale_one, bsum_one, gsum_one, 4, ph,
            g.G1.at[0, ph], 0,
        )
        ch.append(gather(lambda s, ph=ph: g.G1.at[s, ph], 0, R))
    pump()
    k1 = [None, None]
    for ph in range(4):
        relay(ch[ph])
        if ph == 1:
            pump()
        e1 = lanes([g.G1[0, ph], g.G1[2, ph]])
        for s in range(2):
            term = mm_tn(g.SRC[s, ph * R : (ph + 1) * R, :], e1)
            k1[s] = term if k1[s] is None else k1[s] + term
    for s in range(2):
        chip_grad(g.K1, s, k1[s])
    job(g.K1, g.K1R, g.K1D, chips_to(g.K1D, g.k1), far)
    pump()
    w1_own = lanes([g.W1C[0:CI, MI:], g.W1P[0], g.W1C[0:CI, :MI], g.W1P[1]])
    for ph in range(4):
        landed(ch[ph])
        whole = lanes([g.G1[s, ph] for s in range(4)])
        g.IG[ph * R : (ph + 1) * R, :] = mm_nt(whole, w1_own)
        if ph % 2:
            pump()
    cp_bs.wait_recv()
    g.IG[0:R, :] = g.IG[0:R, :] + g.IGS[...] + g.BSR[...].astype(F32)
    for ph in range(4):
        rows = slice(ph * R, (ph + 1) * R)
        g.IGB[rows, :] = (g.IG[rows, :] * bc(g.mask[...], CI)).astype(BF)
    give(g.IGB, g.images_grad)
    while any(work.todo for work in jobs):
        pump()

    g.gain_mid_grad[...] = jnp.concatenate([gsum_one, gsum_two, gsum_four, gsum_five], axis=0)
    g.bias_mid_grad[...] = jnp.concatenate([bsum_one, bsum_two, bsum_four, bsum_five], axis=0)
    g.gain_out_grad[...] = jnp.concatenate([gsum_three, gsum_side, gsum_six], axis=0)
    g.bias_out_grad[...] = jnp.concatenate([bsum_a, bsum_a, bsum_six], axis=0)
    g.mean_mid[...] = jnp.concatenate([mean_one, mean_two, mean_four, mean_five], axis=0)
    g.var_mid[...] = jnp.concatenate(
        [spread_one * unb_in, spread_two * unb_out, spread_four * unb_out, spread_five * unb_out],
        axis=0,
    )
    g.mean_out[...] = jnp.concatenate([mean_three, mean_side, mean_six], axis=0)
    g.var_out[...] = jnp.concatenate([spread_three, spread_side, spread_six], axis=0) * bc(
        unb_out, CO
    )
    for copy in outs:
        copy.wait()
    for copy in net.sent:
        copy.wait_send()

    for work in jobs:
        work.drain()


def fused_on_device(
    images, heights, widths, reduce_first, spatial_first, expand_first, shortcut, reduce_second,
    spatial_second, expand_second, gain_mid, bias_mid, gain_out, bias_out, cotangent,
):
    n, rows, cols, CO = cotangent.shape
    CI, MI = images.shape[3], reduce_first.shape[1]
    NB = heights.shape[0] // n
    R, QS = n * rows * cols, n * rows
    q, p, i = np.meshgrid(np.arange(cols), np.arange(rows), np.arange(n), indexing="ij")
    q, p, i = (v.reshape(-1) for v in (q, p, i))
    pick_out = np.zeros((R, R), np.float32)
    pick_out[np.arange(R), (i * cols + q) * rows + p] = 1.0
    pick_in = np.zeros((2 * R, 2 * R), np.float32)
    for h in range(2):
        pick_in[h * R + np.arange(R), (i * rows + p) * 2 * cols + 2 * q + h] = 1.0
    po = jnp.asarray(pick_out.T.astype(ml_dtypes.bfloat16))
    pi = jnp.asarray(pick_in.T.astype(ml_dtypes.bfloat16))
    cot = cotangent.transpose(0, 2, 1, 3).reshape(R, CO)
    ANY, VM = pl.BlockSpec(memory_space=pl.ANY), pl.BlockSpec(memory_space=pltpu.VMEM)
    SM = pl.BlockSpec(memory_space=pltpu.SMEM)
    CM, MC = 4 * MI, 4 * CI
    ins = dict(
        img=(images.reshape(4 * R, CI), ANY),
        cot=(cot, ANY),
        w1=(reduce_first, ANY),
        w2=(spatial_first.reshape(9, CM, MI), ANY),
        w3=(expand_first, ANY),
        wsc=(shortcut, ANY),
        w4=(reduce_second, ANY),
        w5=(spatial_second.reshape(9, CM, MI), ANY),
        w6=(expand_second, ANY),
        heights=(heights, SM),
        widths=(widths, SM),
        po=(po, VM),
        gm=(gain_mid, VM),
        bm=(bias_mid, VM),
        go=(gain_out, VM),
        bo=(bias_out, VM),
    )
    outs = dict(
        block_out=((R, CO), F32, ANY),
        images_grad=((4 * R, CI), BF, ANY),
        k1=((4, 4, CI // 4, MI), BF, ANY),
        k2=((4, 4, 9, MI // 4, MI), BF, ANY),
        k3=((4, 2, MI // 2, CO), BF, ANY),
        ks=((4, 2, CI // 2, CO), BF, ANY),
        k4=((4, 4, CO // 4, MI), BF, ANY),
        k5=((4, 2, 9, MI // 2, MI), BF, ANY),
        k6=((4, 2, MI // 2, CO), BF, ANY),
        gain_mid_grad=((4, MI), F32, VM),
        bias_mid_grad=((4, MI), F32, VM),
        gain_out_grad=((3, CO), F32, VM),
        bias_out_grad=((3, CO), F32, VM),
        mean_mid=((4, MI), F32, VM),
        var_mid=((4, MI), F32, VM),
        mean_out=((3, CO), F32, VM),
        var_out=((3, CO), F32, VM),
    )
    NW = CO // 128
    scratch = dict(
        IMG=((4 * R, CI), BF),
        mask=((R, 128), F32),
        aux=((24, 128), F32),
        SRC=((2, 4 * R, CI), BF),
        XS=((2, R, CI), BF),
        W1C=((2 * CI, 2 * MI), BF),
        W1P=((2, CI, MI), BF),
        W2=((9, 2, MI, MI), BF),
        W2F=((NB, 9, MI // 4, MI), BF),
        W2P=((9, MI, MI), BF),
        W2Q=((4, 9, MI // 4, MI), BF),
        P2S=((R, 2 * MI), BF),
        P2R=((R, 2 * MI), BF),
        PRE2F=((R, MI), F32),
        PRE4F=((R, MI), F32),
        GMF=((4, MI), F32),
        BMF=((4, MI), F32),
        SB=((2, NB, 4, MI), F32),
        W3=((4, MI, CO), BF),
        W3P=((2, MI, CO), BF),
        WS=((4, CI, CO), BF),
        WSP=((2, CI, CO), BF),
        W4C=((2 * CO, 2 * MI), BF),
        W4P=((2, CO, MI), BF),
        W5=((9, 4, MI, MI), BF),
        W5P=((9, 2, MI, MI), BF),
        W6=((4, MI, CO), BF),
        W6P=((2, MI, CO), BF),
        COT=((R, CO), BF),
        COTP=((R, CO), F32),
        P1S=((4, R, MI), BF),
        P1R=((4, R, MI), BF),
        P4S=((R, 2 * MI), BF),
        P4R=((R, 2 * MI), BF),
        PRE1=((4 * R, MI), F32),
        PRE2=((R, MI), F32),
        PRE3=((R, CO), F32),
        PRES=((R, CO), F32),
        PRE4=((R, MI), F32),
        PRE5=((R, MI), F32),
        PRE6=((R, CO), F32),
        F1=((2, 4, QS + R, MI), BF),
        D1=((2, 2, QS + R, MI), BF),
        F2=((4, R, MI), BF),
        BM=((R, CO), F32),
        MIDC=((2, R, CO), BF),
        F4=((4, R + 2 * QS, MI), BF),
        D4=((2, 4, R + 2 * QS, MI), BF),
        F5=((4, R, MI), BF),
        OUT=((R, CO), F32),
        GSB=((R, CO), F32),
        E6=((2, R, CO), BF),
        B5S=((R, MI), BF),
        B5R=((R, MI), BF),
        GF5=((R, MI), F32),
        E5=((3, 2, R + 2 * QS, MI), BF),
        B4S=((R, MI), BF),
        B4R=((R, MI), BF),
        GF4=((R, MI), F32),
        G4=((4, R, MI), BF),
        GMID=((R, CO), F32),
        E3=((2, R, CO), BF),
        ES=((2, R, CO), BF),
        B2S=((R, MI), BF),
        B2R=((R, MI), BF),
        GF2=((R, MI), F32),
        E2=((2, 4, R + QS, MI), BF),
        GF1=((4 * R, MI), F32),
        G1=((4, 4, R, MI), BF),
        IGS=((R, CI), F32),
        BSS=((R, CI), BF),
        BSR=((R, CI), BF),
        IG=((4 * R, CI), F32),
        IGB=((4 * R, CI), BF),
        SN=((8, NB, 2, MI), F32),
        SW=((4, NB, 2 * NW, 128), F32),
        SA=((NB, 4 * NW, 128), F32),
    )
    for name, piece in dict(
        K1=(2, CI // 4, MI),
        K2A=(2, 5, MI // 4, MI),
        K2B=(2, 4, MI // 4, MI),
        K3=(MI // 2, CO),
        KSA=(CI // 2, CO // 2),
        KSB=(CI // 2, CO // 2),
        K4=(2, CO // 4, MI),
        K5A=(5, MI // 2, MI),
        K5B=(4, MI // 2, MI),
        K6=(MI // 2, CO),
    ).items():
        scratch[name] = ((8, *piece), BF)
        scratch[name + "D"] = ((8, *piece), BF)
        scratch[name + "R"] = ((7, *piece), BF)
    names = [*ins, *outs, *scratch, "sems"]
    geo = types.SimpleNamespace(
        R=R, QS=QS, PS=n, CI=CI, MI=MI, CO=CO, NB=NB, rows=rows, cols=cols
    )
    got = pl.pallas_call(
        functools.partial(block_kernel, geo, names),
        out_shape=[jax.ShapeDtypeStruct(s, d) for s, d, _ in outs.values()],
        in_specs=[spec for _, spec in ins.values()],
        out_specs=[spec for _, _, spec in outs.values()],
        scratch_shapes=[pltpu.VMEM(s, d) for s, d in scratch.values()]
        + [pltpu.SemaphoreType.DMA((SEMS,))],
        compiler_params=pltpu.CompilerParams(
            collective_id=0, has_side_effects=True, vmem_limit_bytes=VMEM_LIMIT
        ),
    )(*[value for value, _ in ins.values()])
    o = types.SimpleNamespace(**dict(zip(outs, got)))
    passed = [
        o.gain_mid_grad, o.bias_mid_grad, o.gain_out_grad, o.bias_out_grad,
        o.mean_mid, o.var_mid, o.mean_out, o.var_out,
    ]
    finals = [
        jax.ShapeDtypeStruct(shape, F32)
        for shape in (
            (R, CO), (n, 2 * rows, 2 * cols, CI), (MC, MI), (3, 3, CM, MI), (CM, CO),
            (MC, CO), (4 * CO, MI), (3, 3, CM, MI), (CM, CO),
        )
    ]
    ks = (o.k1, o.k2, o.k3, o.ks, o.k4, o.k5, o.k6)
    res = pl.pallas_call(
        finish_kernel,
        out_shape=finals + [jax.ShapeDtypeStruct(v.shape, F32) for v in passed],
        in_specs=[ANY] * 9 + [VM] * 10,
        out_specs=[ANY] * 9 + [VM] * 8,
        scratch_shapes=[pltpu.VMEM((R, CO), F32), pltpu.VMEM((4 * R, CI), BF)]
        + [pltpu.VMEM(k.shape, BF) for k in ks]
        + [pltpu.VMEM(f.shape, F32) for f in finals]
        + [pltpu.SemaphoreType.DMA((18,))],
        compiler_params=pltpu.CompilerParams(vmem_limit_bytes=VMEM_LIMIT),
    )(o.block_out, o.images_grad, *ks, po, pi, *passed)
    block_out = res[0].reshape(n, cols, rows, CO).transpose(0, 2, 1, 3)
    return (block_out, *res[1:])


def exact(pick, value):
    high = value.astype(BF)
    low = (value - high.astype(F32)).astype(BF)
    return mm(pick, high) + mm(pick, low)


ORDER = (5, 3, 7, 6, 4, 8, 2, 1, 0)


def finish_kernel(*refs):
    ins, po, pi, small = refs[:9], refs[9], refs[10], refs[11:19]
    outs, small_outs = refs[19:28], refs[28:36]
    held, made, sems = refs[36:45], refs[45:54], refs[54]
    loads = [pltpu.make_async_copy(a, v, sems.at[k]) for k, (a, v) in enumerate(zip(ins, held))]
    stores = [
        pltpu.make_async_copy(v, a, sems.at[9 + k]) for k, (v, a) in enumerate(zip(made, outs))
    ]
    for k in ORDER:
        loads[k].start()
    for a, v in zip(small, small_outs):
        v[...] = a[...]

    def rows_of(k):
        src, dst = held[k], made[k]
        size = math.prod(src.shape[1:-1])
        for rank in range(4):
            dst[rank * size : (rank + 1) * size, :] = (
                src[rank].reshape(size, src.shape[-1]).astype(F32)
            )

    def taps_of(k):
        src, dst = held[k], made[k]
        size = src.shape[3]

        def tap(t):
            for rank in range(4):
                for h in range(src.shape[1]):
                    at = (src.shape[1] * rank + h) * size
                    dst[t // 3, t % 3, at : at + size, :] = src[rank, h, t].astype(F32)

        for t in range(src.shape[2]):
            tap(t)
            store = pltpu.make_async_copy(dst.at[t // 3, t % 3], outs[k].at[t // 3, t % 3], sems.at[9 + k])
            store.start()

    def block():
        made[0][...] = exact(po[...], held[0][...])

    def images():
        half = held[1].shape[0] // 2
        for a in range(2):
            value = mm(pi[...], held[1][a * half : (a + 1) * half, :])
            value = value.reshape(-1, *made[1].shape[2:])
            rows = made[1].shape[1] // 2
            for at in range(value.shape[0]):
                made[1][at // rows, 2 * (at % rows) + a] = value[at]

    for k in ORDER:
        loads[k].wait()
        if k == 0:
            block()
        elif k == 1:
            images()
        elif k in (3, 7):
            taps_of(k)
        else:
            rows_of(k)
        if k not in (3, 7):
            stores[k].start()
    for copy in stores:
        copy.wait()


def solution(mesh):
    in_specs = (
        P("batch", None, None, "chan"),
        P(),
        P(),
        P(None, "chan"),
        P(None, None, None, "chan"),
        P(None, "chan"),
        P(None, "chan"),
        P(None, "chan"),
        P(None, None, None, "chan"),
        P(None, "chan"),
        P(None, "chan"),
        P(None, "chan"),
        P(None, "chan"),
        P(None, "chan"),
        P("batch", None, None, "chan"),
    )
    out_specs = (
        P("batch", None, None, "chan"),
        P("batch", None, None, "chan"),
        P(None, "chan"),
        P(None, None, None, "chan"),
        P(None, "chan"),
        P(None, "chan"),
        P(None, "chan"),
        P(None, None, None, "chan"),
        P(None, "chan"),
        P(None, "chan"),
        P(None, "chan"),
        P(None, "chan"),
        P(None, "chan"),
        P(None, "chan"),
        P(None, "chan"),
        P(None, "chan"),
        P(None, "chan"),
    )
    fused = mesh.shape["chan"] == 4 and mesh.shape["batch"] == 8
    return jax.shard_map(
        fused_on_device if fused else on_device, mesh=mesh, in_specs=in_specs, out_specs=out_specs, check_vma=False
    )
```
